32 devices in a mesh: groups: 2 (over y), gx: 4 (over z), gy: 4 (over x, core).
Axes of the slice: x: 2, y: 2, z: 4, core: 2. Of those that a mesh axis runs over, the one named last changes fastest.
Arguments:
- courant: float32 [32, 256, 128], P('gx', 'gy'), may hold values from 0.04 to 0.16
- state_prev: float32 [64, 256, 128], P(('groups', 'gx'), 'gy'), parts along dimension 0, may hold values from -6 to 6
- state_now: float32 [64, 256, 128], P(('groups', 'gx'), 'gy'), parts along dimension 0, may hold values from -6 to 6
- adjoint_now: float32 [64, 256, 128], P(('groups', 'gx'), 'gy'), parts along dimension 0, may hold values from -6 to 6
- adjoint_next: float32 [64, 256, 128], P(('groups', 'gx'), 'gy'), parts along dimension 0, may hold values from -6 to 6
- source_cell: int32 [32], P('groups'), parts along dimension 0, may hold values from 0 to 1048575
- wavelet: float32 [12, 32], P(None, 'groups'), parts along dimension 1, may hold values from -24 to 24
- observed: float32 [24, 4, 4, 4, 128], P('groups', 'gx', 'gy'), parts along dimension 0, may hold values from -6 to 6
- receiver_cell: int32 [4, 4, 4, 128], P('gx', 'gy'), may hold values from 0 to 65535
- receiver_count: int32 [4, 4, 4], P('gx', 'gy'), may hold values from 0 to 128, as said below
Outputs:
- gradient: float32 [64, 256, 128], P(('groups', 'gx'), 'gy'), parts along dimension 0
- trace_residual: float32 [24, 4, 4, 4, 128], P('groups', 'gx', 'gy'), parts along dimension 0
The draws below stay inside these ranges and needn't reach their ends.
There are 2 independent parts, one for each index of `groups`. The reference program is written for one: setup_inputs(seed, part) draws one part's arguments, and reference() takes and returns one part's arrays. A program takes and returns all parts, laid end to end along the dimension named above; an argument that names none is the same for every part. Nothing has to cross between parts.
Inputs may be any that keep to these rules, and one draw needn't show every extreme that they name: receiver_count[k, j, i] counts the used slots that trace tile (i, j) holds for slab k; in every draw one slab k takes 128 from every tile i of strip 0.
All inputs are finite; a program needn't handle non-finite values.
Results may differ from the reference program's by a relative error of at most 0.00002.
Values sent between devices are 32-bit elements; how exact they have to be, the bound alone decides.
No kernel may reach another device: no remote copies, remote signals or barrier semaphores. Data moves between devices by JAX's collectives and lax.ppermute only.
A program may use at most 64 MiB of HBM per device.

```python
import math
import jax
import jax.numpy as jnp

CX = 8
CY = 64
NZ = 128
STEPS = 12
CAP = 128
SOURCES = 16
SPONGE = 8
NX = 32
NY = 256
N_GX = 4
N_GY = 4


def draw_receiver_count(key, part):
    key = jax.random.fold_in(key, 7)
    level_key, drop_key, pick_key = jax.random.split(key, 3)
    level = jax.random.randint(level_key, (N_GX, 1, 1), 1, 5)
    dropped = jax.random.randint(drop_key, (N_GX, N_GY, N_GX), 0, CAP // 4 + 1)
    counts = jnp.maximum(CAP * level // 4 - dropped, 0)
    full_slab = jax.random.randint(pick_key, (), 0, N_GX)
    slab_index = jnp.arange(N_GX)[:, None, None]
    strip_index = jnp.arange(N_GY)[None, :, None]
    counts = jnp.where((slab_index == full_slab) & (strip_index == 0), CAP, counts)
    return counts.astype(jnp.int32)


def place_ends(entries, own_key, low, top_value):
    longest = entries.shape.index(max(entries.shape))
    spots = []
    for shift in (0, 1):
        where = [jax.random.randint(jax.random.fold_in(own_key, axis), (), 0, length) for axis, length in enumerate(entries.shape)]
        where[longest] = (where[longest] + shift) % entries.shape[longest]
        spots.append(tuple(where))
    return entries.at[spots[0]].set(low).at[spots[1]].set(top_value)


def level_of(stream_key, extent, cuts, low, largest):
    loudness, own = 1.0, jax.random.fold_in(stream_key, 6)
    for axis_at, parts in cuts:
        draws = jnp.exp(jax.random.uniform(jax.random.fold_in(own, axis_at), (parts,), jnp.float32, low / len(cuts), largest / len(cuts)))
        loudness = loudness * jnp.repeat(draws, extent[axis_at] // parts).reshape([-1 if axis == axis_at else 1 for axis in range(len(extent))])
    return loudness


def noise(rng, dims, scale, bound, shards=(), kind=jnp.bfloat16):
    result = scale * jax.random.normal(rng, dims, jnp.float32)
    if shards:
        result = result * level_of(rng, dims, shards, -0.22, 0.18)
    return jnp.clip(result, -bound, bound).astype(kind)


def setup_inputs(seed: int = 0, part: int = 0) -> dict:
    key_of = jax.random.split(jax.random.key(seed), 11)
    part_keys = jax.random.split(jax.random.fold_in(key_of[10], part), 11)
    courant = jnp.clip(jnp.exp(math.log(0.16) - 1.3862944 * jax.random.uniform(key_of[0], (NX, NY, NZ), jnp.float32) ** level_of(key_of[0], (NX, NY, NZ), ((0, 4), (1, 4)), -0.2, 0.2)), 0.04, 0.16)
    state_prev = noise(part_keys[1], (NX, NY, NZ), 1.0, 6.0, ((0, 4), (1, 4)), jnp.float32)
    state_now = noise(part_keys[2], (NX, NY, NZ), 1.0, 6.0, ((0, 4), (1, 4)), jnp.float32)
    adjoint_now = noise(part_keys[3], (NX, NY, NZ), 1.0, 6.0, ((0, 4), (1, 4)), jnp.float32)
    adjoint_next = noise(part_keys[4], (NX, NY, NZ), 1.0, 6.0, ((0, 4), (1, 4)), jnp.float32)
    source_cell = place_ends(jax.random.randint(part_keys[5], (SOURCES,), 0, NX * NY * NZ), jax.random.fold_in(part_keys[5], 1), 0, (NX * NY * NZ) - 1).astype(jnp.int32)
    wavelet = noise(part_keys[6], (STEPS, SOURCES), 4.0, 24.0, (), jnp.float32)
    observed = noise(part_keys[7], (STEPS, N_GX, N_GY, N_GX, CAP), 1.0, 6.0, ((1, 4), (2, 4)), jnp.float32)
    receiver_cell = place_ends(jax.random.randint(key_of[8], (N_GX, N_GY, N_GX, CAP), 0, CX * CY * NZ), jax.random.fold_in(key_of[8], 1), 0, (CX * CY * NZ) - 1).astype(jnp.int32)
    receiver_count = draw_receiver_count(jax.random.fold_in(key_of[10], 71), part)
    return {"courant": courant, "state_prev": state_prev, "state_now": state_now, "adjoint_now": adjoint_now, "adjoint_next": adjoint_next, "source_cell": source_cell, "wavelet": wavelet, "observed": observed, "receiver_cell": receiver_cell, "receiver_count": receiver_count}


stencil = (-205.0 / 72.0, 8.0 / 5.0, -1.0 / 5.0, 8.0 / 315.0, -1.0 / 560.0)
damping_peak = 0.3


def laplace(values):
    width_x, width_y, depth_z = values.shape
    padded = jnp.pad(values, ((4, 4), (4, 4), (0, 0)))
    z_padded = jnp.pad(values, ((0, 0), (0, 0), (4, 4)))
    summed = 3.0 * stencil[0] * values
    for offset in range(1, 5):
        paired = padded[4 + offset:4 + offset + width_x, 4:4 + width_y] + padded[4 - offset:4 - offset + width_x, 4:4 + width_y]
        paired = paired + padded[4:4 + width_x, 4 + offset:4 + offset + width_y] + padded[4:4 + width_x, 4 - offset:4 - offset + width_y]
        paired = paired + z_padded[:, :, 4 + offset:4 + offset + depth_z] + z_padded[:, :, 4 - offset:4 - offset + depth_z]
        summed = summed + stencil[offset] * paired
    return summed


def sponge(count):
    position = jnp.arange(count, dtype=jnp.int32)
    edge_gap = jnp.minimum(position, count - 1 - position)
    profile = jnp.maximum(SPONGE - edge_gap, 0).astype(jnp.float32) / SPONGE
    return profile * profile


def place_sum(indices, amounts):
    flat = jnp.zeros((NX * NY * NZ,), jnp.float32).at[indices].add(amounts)
    return flat.reshape(NX, NY, NZ)


def reference(courant, state_prev, state_now, adjoint_now, adjoint_next, source_cell, wavelet, observed, receiver_cell, receiver_count):
    damping = damping_peak * (sponge(NX)[:, None, None] + sponge(NY)[None, :, None])
    slab_index = jnp.arange(N_GX, dtype=jnp.int32)[:, None, None, None]
    strip_index = jnp.arange(N_GY, dtype=jnp.int32)[None, :, None, None]
    local_x = receiver_cell // (CY * NZ)
    local_y = (receiver_cell // NZ) % CY
    local_z = receiver_cell % NZ
    global_cell = ((slab_index * CX + local_x) * NY + strip_index * CY + local_y) * NZ + local_z
    global_cell = global_cell.reshape(-1).astype(jnp.int32)
    active = (jnp.arange(CAP, dtype=jnp.int32)[None, None, None, :] < receiver_count[..., None]).astype(jnp.float32)
    former, current = state_prev, state_now
    accels = []
    recorded = []
    for moment in range(STEPS):
        drive = laplace(current) + place_sum(source_cell, wavelet[moment])
        following = (2.0 * current - (1.0 - damping) * former + courant * drive) / (1.0 + damping)
        accels.append(following - 2.0 * current + former)
        recorded.append(following.reshape(-1)[global_cell].reshape(active.shape) * active)
        former, current = current, following
    synthetic = jnp.stack(recorded)
    misfit = active[None] * (synthetic - observed.transpose(0, 3, 2, 1, 4))
    trace_residual = misfit.transpose(0, 3, 2, 1, 4)
    later, current = adjoint_next, adjoint_now
    gradient = jnp.zeros((NX, NY, NZ), jnp.float32)
    for moment in reversed(range(STEPS)):
        drive = laplace(current) + place_sum(global_cell, misfit[moment].reshape(-1))
        earlier = (2.0 * current - (1.0 - damping) * later + courant * drive) / (1.0 + damping)
        gradient = gradient + earlier * accels[moment]
        later, current = current, earlier
    return gradient, trace_residual
```

```python
import functools

import jax
import jax.numpy as jnp
from jax import lax
from jax.experimental import pallas as pl
from jax.experimental.pallas import tpu as pltpu
from jax.sharding import PartitionSpec as P

STEPS = 12
SPONGE = 8
REACH = 4
DEPTH = 4
LANES = 128
PAD = 8


stencil = (-205.0 / 72.0, 8.0 / 5.0, -1.0 / 5.0, 8.0 / 315.0, -1.0 / 560.0)
damping_peak = 0.3


class Layout:
    def __init__(self, count_x, count_y, width_x, width_y):
        self.count_x, self.count_y = count_x, count_y
        self.width_x, self.width_y = width_x, width_y
        self.chunk = width_y // count_x
        self.whole_x = width_x * count_x
        self.whole_y = width_y * count_y
        self.margin = REACH * DEPTH
        self.extent = self.chunk + 2 * self.margin
        self.stride = self.whole_x + PAD
        self.padded_rows = self.extent * self.stride + PAD
        self.kept = self.margin - REACH
        self.inner = self.extent - 2 * REACH

    def at(self, place):
        pair, rest = divmod(place, 2 * self.count_x)
        chip, core = divmod(rest, 2)
        slab = chip if pair % 2 == 0 else self.count_x - 1 - chip
        return slab * self.count_y + 2 * pair + core

    def to_chunks(self, turn):
        moves = []
        for slab in range(self.count_x):
            for strip in range(self.count_y):
                moves.append((slab * self.count_y + strip, self.at(strip * self.count_x + (slab ^ turn))))
        return moves

    def to_slabs(self, turn):
        return [(target, source) for source, target in self.to_chunks(turn)]

    def onward(self):
        last = self.count_x * self.count_y - 1
        return [(self.at(place), self.at(place + 1)) for place in range(last)]

    def backward(self):
        return [(target, source) for source, target in self.onward()]


def fits(count_x, count_y, width_x, width_y, depth_z):
    return (
        count_x & (count_x - 1) == 0
        and count_y % 2 == 0
        and width_x == 8
        and depth_z == LANES
        and width_y == count_x * REACH * DEPTH
    )


def smem():
    return pl.BlockSpec(memory_space=pltpu.SMEM)


def vmem():
    return pl.BlockSpec(memory_space=pltpu.VMEM)


def f32(*shape):
    return jax.ShapeDtypeStruct(shape, jnp.float32)


def call(kernel, ints, arrays, outs, scratch=(), flops=1_000_000):
    moved = 4 * (sum(a.size for a in arrays) + sum(o.size for o in outs))
    return pl.pallas_call(
        kernel,
        out_shape=tuple(outs),
        in_specs=[smem()] * len(ints) + [vmem()] * len(arrays),
        out_specs=tuple(vmem() for _ in outs),
        scratch_shapes=list(scratch),
        compiler_params=pltpu.CompilerParams(vmem_limit_bytes=40 * 1024 * 1024),
        cost_estimate=pl.CostEstimate(flops=flops, bytes_accessed=moved, transcendentals=0),
    )(*ints, *arrays)


def cut_fields(lay, slab, fields, fill, target, first_row):
    for turn in range(lay.count_x):
        start = (slab ^ turn) * lay.chunk
        row = 0
        for field in fields:
            for y in range(lay.chunk):
                target[turn][row : row + 8, :] = field[pl.ds(start + y, 8, stride=lay.width_y), :]
                row += 8
        fill(target[turn], row)


def cut_forward(lay, slab_ref, count_ref, now, prev, courant, cell, *sends):
    slots = lax.broadcasted_iota(jnp.int32, (1, LANES), 1)

    def fill(target, row):
        for tile in range(lay.count_x):
            used = jnp.where(slots < count_ref[tile], cell[tile : tile + 1, :], -1)
            target[row + tile : row + tile + 1, :] = used.astype(jnp.float32)

    cut_fields(lay, slab_ref[0], (now, prev, courant), fill, sends, 0)


def cut_adjoint(lay, slab_ref, now, prev, observed, *sends):
    def fill(target, row):
        target[row : row + observed.shape[0], :] = observed[...]

    cut_fields(lay, slab_ref[0], (now, prev), fill, sends, 0)


def place_rows(lay, ref, layer, start_x, tile):
    first = pl.multiple_of(layer * lay.whole_x + start_x, 8)
    ref[pl.ds(first, 8), :] = tile


def join_fields(lay, own_slot, pieces, names, state, courant, send_back, send_on):
    for turn, piece in enumerate(pieces):
        start_x = pl.multiple_of((own_slot ^ turn) * 8, 8)
        row = 0
        for index, name in enumerate(names):
            first = 0 if index == 0 else lay.chunk + (index - 1) * lay.kept
            for y in range(lay.chunk):
                tile = piece[row : row + 8, :]
                row += 8
                if name == "courant":
                    place_rows(lay, courant, y, start_x, tile)
                else:
                    place_rows(lay, state, index * lay.chunk + y, start_x, tile)
                if index == 0:
                    place_rows(lay, send_back, y, start_x, tile)
                    place_rows(lay, send_on, y, start_x, tile)
                    continue
                if y < lay.kept:
                    place_rows(lay, send_back, first + y, start_x, tile)
                if y >= lay.chunk - lay.kept:
                    place_rows(lay, send_on, first + y - (lay.chunk - lay.kept), start_x, tile)


def join_forward(lay, slot_ref, *refs):
    pieces, (state, courant, send_back, send_on, codes) = refs[: lay.count_x], refs[lay.count_x :]
    own_slot = slot_ref[0]
    join_fields(lay, own_slot, pieces, ("now", "prev", "courant"), state, courant, send_back, send_on)
    first = 3 * lay.chunk * 8
    strip_cells = lay.width_y * LANES
    slab_row = lax.broadcasted_iota(jnp.int32, codes.shape, 0)
    found = jnp.full(codes.shape, -1.0, jnp.float32)
    for turn, piece in enumerate(pieces):
        cell = piece[first : first + lay.count_x, :].astype(jnp.int32)
        used = cell >= 0
        cell = jnp.maximum(cell, 0)
        x = lax.div(cell, jnp.int32(strip_cells))
        y = lax.rem(lax.div(cell, jnp.int32(LANES)), jnp.int32(lay.width_y)) - own_slot * lay.chunk
        inside = used & (y >= 0) & (y < lay.chunk)
        code = jnp.where(inside, (y * 8 + x) * LANES + lax.rem(cell, jnp.int32(LANES)), -1)
        code = code.astype(jnp.float32)
        line = jnp.concatenate([code[tile : tile + 1, :] for tile in range(lay.count_x)], axis=1)
        found = jnp.where(slab_row == (own_slot ^ turn), jnp.broadcast_to(line, codes.shape), found)
    codes[...] = found


def join_adjoint(lay, slot_ref, *refs):
    pieces, (state, send_back, send_on) = refs[: lay.count_x], refs[lay.count_x :]
    join_fields(lay, slot_ref[0], pieces, ("now", "prev"), state, None, send_back, send_on)


def zero_pads(lay, buffers):
    zeros = jnp.zeros((PAD, LANES), jnp.float32)
    for y in range(lay.extent + 1):
        for buffer in buffers:
            buffer[y * lay.stride : y * lay.stride + PAD, :] = zeros


def load_state(lay, now, prev, state, from_back, from_on):
    wide, own = lay.whole_x, lay.margin

    def put(buffer, layer, ref, source):
        first = layer * lay.stride + PAD
        buffer[first : first + wide, :] = ref[source * wide : (source + 1) * wide, :]

    for y in range(lay.chunk):
        put(now, own + y, state, y)
        put(prev, own + y, state, lay.chunk + y)
        put(now, y, from_back, y)
        put(now, own + lay.chunk + y, from_on, y)
    for y in range(lay.kept):
        put(prev, REACH + y, from_back, lay.chunk + y)
        put(prev, own + lay.chunk + y, from_on, lay.chunk + y)


def store_state(lay, now, prev, state, send_back, send_on):
    wide, own = lay.whole_x, lay.margin
    skipped = lay.chunk - lay.kept

    def put(ref, target, values):
        ref[target * wide : (target + 1) * wide, :] = values

    for y in range(lay.chunk):
        first = (own + y) * lay.stride + PAD
        values = now[first : first + wide, :]
        put(state, y, values)
        put(send_back, y, values)
        put(send_on, y, values)
        values = prev[first : first + wide, :]
        put(state, lay.chunk + y, values)
        if y < lay.kept:
            put(send_back, lay.chunk + y, values)
        if y >= skipped:
            put(send_on, lay.chunk + y - skipped, values)


def fill_gain(lay, first_y, gain):
    x = lax.broadcasted_iota(jnp.int32, (lay.whole_x, LANES), 0)
    gap_x = jnp.minimum(x, lay.whole_x - 1 - x)
    ramp_x = jnp.maximum(SPONGE - gap_x, 0).astype(jnp.float32) / SPONGE
    part_x = ramp_x * ramp_x

    def layer(y, carry):
        global_y = jnp.full((lay.whole_x, LANES), first_y + REACH + y, jnp.int32)
        gap_y = jnp.minimum(global_y, lay.whole_y - 1 - global_y)
        ramp_y = jnp.maximum(SPONGE - gap_y, 0).astype(jnp.float32) / SPONGE
        first = pl.multiple_of(y * lay.whole_x, 8)
        gain[pl.ds(first, lay.whole_x), :] = 2.0 / (1.0 + damping_peak * (part_x + ramp_y * ramp_y))
        return carry

    lax.fori_loop(0, lay.inner, layer, 0)


def sweep(lay, step, now, prev, following, courant, gain, inject=None):
    wide, stride = lay.whole_x, lay.stride
    first_layer = REACH * (step + 1)
    group = 8
    z = lax.broadcasted_iota(jnp.int32, (wide, LANES), 1)
    up = [jnp.where(z >= k, stencil[k], 0.0).astype(jnp.float32) for k in range(REACH + 1)]
    down = [jnp.where(z < LANES - k, stencil[k], 0.0).astype(jnp.float32) for k in range(REACH + 1)]

    def layers(block, carry):
        for inner in range(group):
            y = first_layer + group * block + inner
            base = pl.multiple_of(y * stride + PAD, 8)
            flat = pl.multiple_of((y - REACH) * wide, 8)
            center = now[pl.ds(base, wide), :]
            total = (3.0 * stencil[0]) * center
            for k in range(1, REACH + 1):
                pair = now[pl.ds(base + k, wide), :] + now[pl.ds(base - k, wide), :]
                pair = pair + (now[pl.ds(base + stride * k, wide), :] + now[pl.ds(base - stride * k, wide), :])
                total = total + stencil[k] * pair
                total = total + up[k] * pltpu.roll(center, k, 1)
                total = total + down[k] * pltpu.roll(center, LANES - k, 1)
            if inject is not None:
                total = total + inject[step, pl.ds(flat, wide), :]
            former = prev[pl.ds(base, wide), :]
            change = (center - former) + (0.5 * courant[pl.ds(flat, wide), :]) * total
            following[pl.ds(base, wide), :] = former + gain[pl.ds(flat, wide), :] * change
        return carry

    lax.fori_loop(0, (lay.extent - 2 * first_layer) // group, layers, 0)


def split(values):
    high = values.astype(jnp.bfloat16)
    rest = values - high.astype(jnp.float32)
    middle = rest.astype(jnp.bfloat16)
    low = (rest - middle.astype(jnp.float32)).astype(jnp.bfloat16)
    return high, middle, low


def slot_rows(codes, slab):
    code = codes[slab : slab + 1, :].astype(jnp.int32)
    row = jnp.where(code >= 0, lax.shift_right_arithmetic(code, 7), -1)
    return row, jnp.where(code >= 0, code & (LANES - 1), -1)


def forward(lay, phase, sources, ints, wavelet, state, from_back, from_on, courant_in, codes, *refs):
    first, last = phase == 0, phase == STEPS // DEPTH - 1
    rows = lay.chunk * lay.whole_x
    refs = list(refs)
    earlier, observed = [], []
    if last:
        earlier = [refs.pop(0) for _ in range(phase)]
        observed = [refs.pop(0) for _ in range(lay.count_x)]
    accel = refs.pop(0)
    if first:
        courant = refs.pop(0)
    else:
        courant = courant_in
    if last:
        misfit = refs.pop(0)
    else:
        state_out, send_back, send_on, record = [refs.pop(0) for _ in range(4)]
    buffers = [refs.pop(0) for _ in range(3)]
    gain, pulse, stash = refs.pop(0), refs.pop(0), refs.pop(0)
    if last:
        record = refs.pop(0)
    now, prev, following = buffers

    zero_pads(lay, buffers)
    load_state(lay, now, prev, state, from_back, from_on)
    if first:
        tail = (lay.chunk + lay.kept) * lay.whole_x
        part = lay.kept * lay.whole_x
        courant[0:part, :] = from_back[tail : tail + part, :]
        courant[part : part + rows, :] = courant_in[...]
        courant[part + rows : part + rows + part, :] = from_on[tail : tail + part, :]
    fill_gain(lay, ints[0], gain)
    lane = lax.broadcasted_iota(jnp.int32, (1, LANES), 1)
    for source in range(sources):
        flat = pl.ds(ints[1 + sources + source], 1)
        strength = 0.5 * courant[flat, :] * gain[flat, :]
        pulse[source : source + 1, :] = jnp.where(lane == ints[1 + 2 * sources + source], strength, 0.0)

    for step in range(DEPTH):
        sweep(lay, step, now, prev, following, courant, gain)
        for source in range(sources):
            row = pl.ds(ints[1 + source], 1)
            weight = wavelet[phase * DEPTH + step, source]
            following[row, :] = following[row, :] + weight * pulse[source : source + 1, :]

        def own_layers(index, carry):
            pair = []
            for y in (2 * index, 2 * index + 1):
                base = pl.multiple_of((lay.margin + y) * lay.stride + PAD, 8)
                later, center = following[pl.ds(base, lay.whole_x), :], now[pl.ds(base, lay.whole_x), :]
                change = (later - center) - (center - prev[pl.ds(base, lay.whole_x), :])
                target = pl.multiple_of((step * lay.chunk + y) * lay.whole_x, 8)
                accel[pl.ds(target, lay.whole_x), :] = change
                pair.append(later)
            for slab in range(lay.count_x):
                both = jnp.concatenate([part[slab * 8 : slab * 8 + 8, :] for part in pair], axis=0)
                target = pl.multiple_of((slab * DEPTH + step) * lay.chunk * 8 + index * 16, 16)
                for place, values in enumerate(split(both)):
                    stash[pl.ds(target, 16), place * LANES : (place + 1) * LANES] = values
            return carry

        lax.fori_loop(0, lay.chunk // 2, own_layers, 0)
        now, prev, following = following, now, prev

    slots = codes.shape[1]
    cells = lay.chunk * 8
    width = 2 * LANES
    for slab in range(lay.count_x):
        cell_row, cell_z = slot_rows(codes, slab)
        for start in range(0, slots, width):
            here = slice(start, start + width)
            z = lax.broadcasted_iota(jnp.int32, (LANES, width), 0)
            pick = jnp.where(z == cell_z[:, here], 1.0, 0.0).astype(jnp.bfloat16)
            pick = jnp.concatenate([pick] * 3, axis=0)
            found = jnp.dot(
                stash[slab * DEPTH * cells : (slab + 1) * DEPTH * cells, :],
                pick,
                preferred_element_type=jnp.float32,
            )
            wanted = lax.broadcasted_iota(jnp.int32, (cells, width), 0) == cell_row[:, here]
            for step in range(DEPTH):
                part = jnp.where(wanted, found[step * cells : (step + 1) * cells, :], 0.0)
                row = step * lay.count_x + slab
                record[row : row + 1, here] = jnp.sum(part, axis=0, keepdims=True)

    if not last:
        store_state(lay, now, prev, state_out, send_back, send_on)
        return
    block = DEPTH * lay.count_x
    for index, part in enumerate(earlier + [record]):
        misfit[index * block : (index + 1) * block, :] = part[...]
    total = STEPS * lay.count_x
    for slab in range(lay.count_x):
        misfit[total + slab : total + slab + 1, :] = codes[slab : slab + 1, :]
    own_slot = ints[1 + 3 * sources]
    for turn, piece in enumerate(observed):
        place = pl.ds(pl.multiple_of((own_slot ^ turn) * LANES, LANES), LANES)
        used = jnp.concatenate([codes[:, place]] * STEPS, axis=0) >= 0
        seen = piece[2 * lay.chunk * 8 : 2 * lay.chunk * 8 + total, :]
        misfit[0:total, place] = jnp.where(used, misfit[0:total, place] - seen, 0.0)


def spread(lay, phase, misfits, inject):
    cells = lay.chunk * 8
    for slab in range(lay.count_x):
        for side, misfit in zip((-1, 0, 1), misfits):
            codes = misfit[STEPS * lay.count_x : (STEPS + 1) * lay.count_x, :]
            cell_row, cell_z = slot_rows(codes, slab)
            slots = cell_row.shape[1]
            z = lax.broadcasted_iota(jnp.int32, (LANES, slots), 0)
            pick = jnp.where(z == cell_z, 1.0, 0.0).astype(jnp.bfloat16)
            pick = jnp.concatenate([pick] * 3, axis=1)
            hit = lax.broadcasted_iota(jnp.int32, (cells, slots), 0) == cell_row
            hit = jnp.where(hit, 1.0, 0.0).astype(jnp.bfloat16)
            left, spans = [], []
            for step in range(DEPTH):
                low, high = 0, lay.chunk
                if side < 0:
                    low = REACH * (step + 1) - lay.margin + lay.chunk
                if side > 0:
                    high = lay.margin - REACH * (step + 1)
                if low >= high:
                    continue
                moment = STEPS - 1 - phase * DEPTH - step
                row = moment * lay.count_x + slab
                parts = split(misfit[row : row + 1, :])
                left.append(jnp.concatenate([hit[low * 8 : high * 8, :] * part for part in parts], axis=1))
                spans.append((step, low, high))
            placed = lax.dot_general(
                jnp.concatenate(left, axis=0),
                pick,
                (((1,), (1,)), ((), ())),
                preferred_element_type=jnp.float32,
            )
            at = 0
            for step, low, high in spans:
                for y in range(low, high):
                    layer = lay.margin + side * lay.chunk + y - REACH
                    target = layer * lay.whole_x + slab * 8
                    inject[step, target : target + 8, :] = placed[at : at + 8, :]
                    at += 8


def backward(lay, phase, ints, state, from_back, from_on, courant, accel, misfit, misfit_back, misfit_on, *refs):
    first, last = phase == 0, phase == STEPS // DEPTH - 1
    refs = list(refs)
    if not first:
        gradient_in = refs.pop(0)
    if last:
        sends = [refs.pop(0) for _ in range(lay.count_x)]
    else:
        gradient, state_out, send_back, send_on = [refs.pop(0) for _ in range(4)]
    buffers = [refs.pop(0) for _ in range(3)]
    gain, inject = refs.pop(0), refs.pop(0)
    if last:
        gradient = refs.pop(0)
    now, prev, following = buffers

    zero_pads(lay, buffers)
    load_state(lay, now, prev, state, from_back, from_on)
    fill_gain(lay, ints[0], gain)
    spread(lay, phase, (misfit_back, misfit, misfit_on), inject)
    for step in range(DEPTH):
        sweep(lay, step, now, prev, following, courant, gain, inject)

        def own_layers(y, carry):
            base = pl.multiple_of((lay.margin + y) * lay.stride + PAD, 8)
            source = pl.multiple_of(((DEPTH - 1 - step) * lay.chunk + y) * lay.whole_x, 8)
            target = pl.ds(pl.multiple_of(y * lay.whole_x, 8), lay.whole_x)
            term = following[pl.ds(base, lay.whole_x), :] * accel[pl.ds(source, lay.whole_x), :]
            if step > 0:
                term = gradient[target, :] + term
            elif not first:
                term = gradient_in[target, :] + term
            gradient[target, :] = term
            return carry

        lax.fori_loop(0, lay.chunk, own_layers, 0)
        now, prev, following = following, now, prev

    if not last:
        store_state(lay, now, prev, state_out, send_back, send_on)
        return
    own_slot = ints[1]
    total = STEPS * lay.count_x
    for turn, send in enumerate(sends):
        other = own_slot ^ turn
        for y in range(lay.chunk):
            source = pl.ds(pl.multiple_of(y * lay.whole_x + other * 8, 8), 8)
            send[y * 8 : y * 8 + 8, :] = gradient[source, :]
        tile = pl.ds(pl.multiple_of(other * LANES, LANES), LANES)
        send[lay.chunk * 8 : lay.chunk * 8 + total, :] = misfit[0:total, tile]


def finish(lay, slab_ref, *refs):
    pieces, (gradient, residual) = refs[: lay.count_x], refs[lay.count_x :]
    slab = slab_ref[0]
    total = None
    for turn, piece in enumerate(pieces):
        start = (slab ^ turn) * lay.chunk
        for x in range(8):
            target = pl.ds(pl.multiple_of(x * lay.width_y + start, 8), lay.chunk)
            gradient[target, :] = piece[pl.ds(x, lay.chunk, stride=8), :]
        part = piece[lay.chunk * 8 : lay.chunk * 8 + residual.shape[0], :]
        total = part if total is None else total + part
    residual[...] = total


def local_tiles(
    lay,
    courant,
    state_prev,
    state_now,
    adjoint_now,
    adjoint_next,
    source_cell,
    wavelet,
    observed,
    receiver_cell,
    receiver_count,
):
    axes = ("gx", "gy")
    slab = lax.axis_index("gx")
    strip = lax.axis_index("gy")
    pair = strip // 2
    chip = jnp.where(pair % 2 == 0, slab, lay.count_x - 1 - slab)
    place = (pair * lay.count_x + chip) * 2 + strip % 2
    own_slot = place % lay.count_x
    first_y = place * lay.chunk - lay.margin
    slab_int = slab.reshape(1).astype(jnp.int32)
    slot_int = own_slot.reshape(1).astype(jnp.int32)

    count = lay.count_x
    wide = lay.whole_x
    rows = lay.chunk * wide
    cells = lay.chunk * 8
    sources = source_cell.shape[0]
    slots = count * receiver_cell.shape[3]
    flat = lambda values: values.reshape(-1, LANES)

    source_x = source_cell // (lay.whole_y * LANES)
    source_y = source_cell // LANES % lay.whole_y - first_y
    source_z = source_cell % LANES
    inside = (source_y >= REACH) & (source_y < lay.extent - REACH)
    source_row = jnp.where(inside, source_y * lay.stride + PAD + source_x, REACH * lay.stride + PAD)
    source_flat = jnp.where(inside, (source_y - REACH) * wide + source_x, 0)
    source_z = jnp.where(inside, source_z, -1)
    ints = jnp.concatenate(
        [first_y.reshape(1), source_row, source_flat, source_z, own_slot.reshape(1)]
    ).astype(jnp.int32)
    back_ints = jnp.stack([first_y, own_slot]).astype(jnp.int32)

    def exchange(send_back, send_on):
        return (
            lax.ppermute(send_on, axes, lay.onward()),
            lax.ppermute(send_back, axes, lay.backward()),
        )

    tail = -(-count // 8) * 8
    cuts = call(
        functools.partial(cut_forward, lay),
        (slab_int, receiver_count.reshape(-1)),
        (flat(state_now), flat(state_prev), flat(courant), receiver_cell.reshape(count, LANES)),
        [f32(3 * cells + tail, LANES)] * count,
    )
    pieces = [lax.ppermute(cut, axes, lay.to_chunks(turn)) for turn, cut in enumerate(cuts)]
    kept_rows = lay.kept * wide
    state, own_courant, send_back, send_on, codes = call(
        functools.partial(join_forward, lay),
        (slot_int,),
        pieces,
        [f32(2 * rows, LANES), f32(rows, LANES)]
        + [f32(rows + 2 * kept_rows, LANES)] * 2
        + [f32(count, slots)],
    )
    from_back, from_on = exchange(send_back, send_on)

    traces = flat(observed)
    cuts = call(
        functools.partial(cut_adjoint, lay),
        (slab_int,),
        (flat(adjoint_now), flat(adjoint_next), traces),
        [f32(2 * cells + traces.shape[0], LANES)] * count,
    )
    back_pieces = [lax.ppermute(cut, axes, lay.to_chunks(turn)) for turn, cut in enumerate(cuts)]
    state_shapes = [f32(2 * rows, LANES)] + [f32(rows + kept_rows, LANES)] * 2
    back_state, back_send_back, back_send_on = call(
        functools.partial(join_adjoint, lay), (slot_int,), back_pieces, state_shapes
    )
    back_from_back, back_from_on = exchange(back_send_back, back_send_on)

    phases = STEPS // DEPTH
    block = DEPTH * count
    buffers = [pltpu.VMEM((lay.padded_rows, LANES), jnp.float32)] * 3
    inner = lay.inner * wide
    gain = pltpu.VMEM((inner, LANES), jnp.float32)
    accels, records = [], []
    courant_all = own_courant
    for phase in range(phases):
        first, last = phase == 0, phase == phases - 1
        arrays = [state, from_back, from_on, courant_all, codes]
        outs = [f32(DEPTH * rows, LANES)]
        scratch = buffers + [
            gain,
            pltpu.VMEM((sources, LANES), jnp.float32),
            pltpu.VMEM((count * DEPTH * cells, 3 * LANES), jnp.bfloat16),
        ]
        if first:
            outs.append(f32(inner, LANES))
        if last:
            arrays += records + back_pieces
            outs.append(f32(-(-(STEPS + 1) * count // 8) * 8, slots))
            scratch.append(pltpu.VMEM((block, slots), jnp.float32))
        else:
            outs += state_shapes + [f32(block, slots)]
        results = list(
            call(
                functools.partial(forward, lay, phase, sources),
                (ints, wavelet),
                arrays,
                outs,
                scratch,
                flops=20_000_000,
            )
        )
        accels.append(results.pop(0))
        if first:
            courant_all = results.pop(0)
        if last:
            misfit = results.pop(0)
        else:
            state, send_back, send_on, record = results
            records.append(record)
            from_back, from_on = exchange(send_back, send_on)

    misfit_back, misfit_on = exchange(misfit, misfit)
    state, from_back, from_on = back_state, back_from_back, back_from_on
    gradient = None
    for phase in range(phases):
        first, last = phase == 0, phase == phases - 1
        arrays = [state, from_back, from_on, courant_all, accels[phases - 1 - phase]]
        arrays += [misfit, misfit_back, misfit_on]
        scratch = buffers + [gain, pltpu.VMEM((DEPTH, inner, LANES), jnp.float32)]
        if not first:
            arrays.append(gradient)
        if last:
            outs = [f32(cells + traces.shape[0], LANES)] * count
            scratch.append(pltpu.VMEM((rows, LANES), jnp.float32))
        else:
            outs = [f32(rows, LANES)] + state_shapes
        results = call(
            functools.partial(backward, lay, phase), (back_ints,), arrays, outs, scratch, flops=20_000_000
        )
        if not last:
            gradient, state, send_back, send_on = results
            from_back, from_on = exchange(send_back, send_on)
    pieces = [lax.ppermute(send, axes, lay.to_slabs(turn)) for turn, send in enumerate(results)]
    gradient, residual = call(
        functools.partial(finish, lay),
        (slab_int,),
        pieces,
        [f32(lay.width_x * lay.width_y, LANES), f32(*traces.shape)],
    )
    return gradient.reshape(courant.shape), residual.reshape(observed.shape)


def local(courant, *rest):
    width_x, width_y, depth_z = courant.shape
    count_x, count_y = lax.axis_size("gx"), lax.axis_size("gy")
    if fits(count_x, count_y, width_x, width_y, depth_z):
        return local_tiles(Layout(count_x, count_y, width_x, width_y), courant, *rest)
    return local_blocks(courant, *rest)


def padded_2(cells, sides, width):
    for axis, dim in sides:
        count = lax.axis_size(axis)
        ends = count - 1
        head = lax.slice_in_dim(cells, 0, width, axis=dim)
        tail = lax.slice_in_dim(cells, cells.shape[dim] - width, cells.shape[dim], axis=dim)
        cells = jnp.concatenate(
            [
                lax.ppermute(tail, axis, [(i, (i + 1) % count) for i in range(ends)]),
                cells,
                lax.ppermute(head, axis, [((i + 1) % count, i) for i in range(ends)]),
            ],
            axis=dim,
        )
    return cells


def laplace(values):
    width_x, width_y, depth_z = values.shape
    padded = padded_2(values, (("gx", 0), ("gy", 1)), 4)
    z_padded = jnp.pad(values, ((0, 0), (0, 0), (4, 4)))
    summed = 3.0 * stencil[0] * values
    for offset in range(1, 5):
        paired = (
            padded[4 + offset : 4 + offset + width_x, 4 : 4 + width_y]
            + padded[4 - offset : 4 - offset + width_x, 4 : 4 + width_y]
        )
        paired = (
            paired
            + padded[4 : 4 + width_x, 4 + offset : 4 + offset + width_y]
            + padded[4 : 4 + width_x, 4 - offset : 4 - offset + width_y]
        )
        paired = (
            paired
            + z_padded[:, :, 4 + offset : 4 + offset + depth_z]
            + z_padded[:, :, 4 - offset : 4 - offset + depth_z]
        )
        summed = summed + stencil[offset] * paired
    return summed


def sponge(start, count, whole):
    position = start + jnp.arange(count, dtype=jnp.int32)
    edge_gap = jnp.minimum(position, whole - 1 - position)
    profile = jnp.maximum(SPONGE - edge_gap, 0).astype(jnp.float32) / SPONGE
    return profile * profile


def place_sum(indices, amounts, shape):
    flat = jnp.zeros((shape[0] * shape[1] * shape[2],), jnp.float32).at[indices].add(amounts)
    return flat.reshape(shape)


def local_blocks(
    courant,
    state_prev,
    state_now,
    adjoint_now,
    adjoint_next,
    source_cell,
    wavelet,
    observed,
    receiver_cell,
    receiver_count,
):
    shape = courant.shape
    width_x, width_y, depth_z = shape
    slab = lax.axis_index("gx")
    strip = lax.axis_index("gy")
    whole_x = width_x * lax.axis_size("gx")
    whole_y = width_y * lax.axis_size("gy")
    damping = damping_peak * (
        sponge(slab * width_x, width_x, whole_x)[:, None, None]
        + sponge(strip * width_y, width_y, whole_y)[None, :, None]
    )
    source_x = source_cell // (whole_y * depth_z) - slab * width_x
    source_y = source_cell // depth_z % whole_y - strip * width_y
    source_z = source_cell % depth_z
    inside = (source_x >= 0) & (source_x < width_x) & (source_y >= 0) & (source_y < width_y)
    source_flat = jnp.where(inside, (source_x * width_y + source_y) * depth_z + source_z, 0)
    source_weight = wavelet * inside.astype(jnp.float32)[None, :]
    senders = receiver_cell.shape[2]
    slots = receiver_cell.shape[3]
    cells = receiver_cell.reshape(-1)
    active = (
        jnp.arange(slots, dtype=jnp.int32)[None, :] < receiver_count.reshape(senders, 1)
    ).astype(jnp.float32)
    active_flat = active.reshape(-1)

    def advance(carry, weights):
        former, current = carry
        drive = laplace(current) + place_sum(source_flat, weights, shape)
        following = (2.0 * current - (1.0 - damping) * former + courant * drive) / (1.0 + damping)
        return (
            (current, following),
            (following - 2.0 * current + former, following.reshape(-1)[cells] * active_flat),
        )

    final_states, (accels, recorded) = lax.scan(advance, (state_prev, state_now), source_weight)
    recorded_tiles = recorded.reshape(STEPS, senders, 1, 1, slots)
    active_tiles = active.reshape(1, senders, 1, 1, slots)
    synthetic, mask_back = (
        lax.all_to_all(recorded_tiles, "gx", split_axis=1, concat_axis=3, tiled=True),
        lax.all_to_all(active_tiles, "gx", split_axis=1, concat_axis=3, tiled=True),
    )
    trace_residual = mask_back * (synthetic - observed)
    misfit = lax.all_to_all(trace_residual, "gx", split_axis=3, concat_axis=1, tiled=True)
    misfit_rows = misfit.reshape(STEPS, senders * slots)

    def retreat(carry, inputs):
        later, current, gradient = carry
        acceleration, residual_row = inputs
        drive = laplace(current) + place_sum(cells, residual_row, shape)
        earlier = (2.0 * current - (1.0 - damping) * later + courant * drive) / (1.0 + damping)
        return ((current, earlier, gradient + earlier * acceleration), None)

    start_gradient = jnp.zeros(shape, jnp.float32)
    (last_later, last_current, gradient), unused = lax.scan(
        retreat, (adjoint_next, adjoint_now, start_gradient), (accels, misfit_rows), reverse=True
    )
    return (gradient, trace_residual)


def solution(mesh):
    placed = (
        P("gx", "gy", None),
        P(("groups", "gx"), "gy", None),
        P(("groups", "gx"), "gy", None),
        P(("groups", "gx"), "gy", None),
        P(("groups", "gx"), "gy", None),
        P("groups"),
        P(None, "groups"),
        P("groups", "gx", "gy", None, None),
        P("gx", "gy", None, None),
        P("gx", "gy", None),
    )
    return jax.shard_map(
        local,
        mesh=mesh,
        in_specs=placed,
        out_specs=(P(("groups", "gx"), "gy", None), P("groups", "gx", "gy", None, None)),
        check_vma=False,
    )
```

```python
import functools

import jax
import jax.numpy as jnp
from jax import lax
from jax.experimental import pallas as pl
from jax.experimental.pallas import tpu as pltpu
from jax.sharding import PartitionSpec as P

STEPS = 12
SPONGE = 8
REACH = 4
DEPTH = 4
LANES = 128
ROWS = 8


stencil = (-205.0 / 72.0, 8.0 / 5.0, -1.0 / 5.0, 8.0 / 315.0, -1.0 / 560.0)
damping_peak = 0.3


class Layout:
    def __init__(self, count_x, count_y, width_x, width_y):
        self.count_x, self.count_y = count_x, count_y
        self.width_x, self.width_y = width_x, width_y
        self.chunk = width_y // count_x
        self.wide = width_x * count_x
        self.tiles = self.wide // ROWS
        self.whole_y = width_y * count_y
        self.margin = REACH * DEPTH
        self.extent = self.chunk + 2 * self.margin
        self.stride = self.tiles * 2 * ROWS
        self.padded_rows = self.extent * self.stride + ROWS
        self.kept = self.margin - REACH
        self.inner = self.extent - 2 * REACH
        self.rows = self.chunk * self.wide
        self.cells = self.chunk * width_x
        self.near = self.chunk + 2 * REACH
        self.state_rows = (self.chunk + self.near) * self.wide
        self.lacking = range(REACH, self.chunk - REACH)
        self.send_rows = (self.chunk + len(self.lacking)) * self.wide

    def at(self, place):
        pair, rest = divmod(place, 2 * self.count_x)
        chip, core = divmod(rest, 2)
        slab = chip if pair % 2 == 0 else self.count_x - 1 - chip
        return slab * self.count_y + 2 * pair + core

    def to_chunks(self, turn):
        moves = []
        for slab in range(self.count_x):
            for strip in range(self.count_y):
                moves.append((slab * self.count_y + strip, self.at(strip * self.count_x + (slab ^ turn))))
        return moves

    def to_slabs(self, turn):
        return [(target, source) for source, target in self.to_chunks(turn)]

    def swaps(self, first):
        moves = []
        for place in range(first, self.count_x * self.count_y - 1, 2):
            moves += [(self.at(place), self.at(place + 1)), (self.at(place + 1), self.at(place))]
        return moves


def fits(count_x, count_y, width_x, width_y, depth_z):
    return (
        count_x & (count_x - 1) == 0
        and count_y % 2 == 0
        and width_x == ROWS
        and width_x * count_x == ROWS * REACH
        and depth_z == LANES
        and width_y == count_x * REACH * DEPTH
    )


def f32(*shape):
    return jax.ShapeDtypeStruct(shape, jnp.float32)


def call(kernel, ints, arrays, outs, scratch=(), cost=1_000_000, space=pltpu.VMEM, aliases=None):
    return pl.pallas_call(
        kernel,
        out_shape=tuple(outs),
        in_specs=[pl.BlockSpec(memory_space=pltpu.SMEM)] * len(ints)
        + [pl.BlockSpec(memory_space=space)] * len(arrays),
        out_specs=tuple(pl.BlockSpec(memory_space=pltpu.VMEM) for _ in outs),
        scratch_shapes=list(scratch),
        input_output_aliases=aliases or {},
        compiler_params=pltpu.CompilerParams(vmem_limit_bytes=32 * 1024 * 1024),
        cost_estimate=pl.CostEstimate(flops=cost, bytes_accessed=cost, transcendentals=0),
    )(*ints, *arrays)


def aligned(value, to=ROWS):
    return pl.multiple_of(value, to)


def cut_fields(lay, slab, fields, fill, targets):
    for turn, target in enumerate(targets):
        start = (slab ^ turn) * lay.chunk
        row = 0
        for field in fields:
            for y in range(lay.chunk):
                target[row : row + ROWS, :] = field[pl.ds(start + y, ROWS, stride=lay.width_y), :]
                row += ROWS
        fill(target, row)


def cut_forward(lay, slab_ref, count_ref, now, prev, courant, cell, *refs):
    sends, (held, held_cell, done) = refs[: lay.count_x], refs[lay.count_x :]
    copies = []
    for index, (source, target) in enumerate(
        [(cell, held_cell)] + [(field, held.at[place]) for place, field in enumerate((now, prev, courant))]
    ):
        copies.append(pltpu.make_async_copy(source, target, done.at[index]))
        copies[-1].start()
    for copy in copies:
        copy.wait()
    slots = lax.broadcasted_iota(jnp.int32, (1, LANES), 1)

    def fill(target, row):
        for tile in range(lay.count_x):
            used = jnp.where(slots < count_ref[tile], held_cell[tile : tile + 1, :], -1)
            target[row + tile : row + tile + 1, :] = used.astype(jnp.float32)

    cut_fields(lay, slab_ref[0], [held.at[place] for place in range(3)], fill, sends)


def cut_adjoint(lay, slab_ref, now, prev, observed, *sends):
    def fill(target, row):
        target[row : row + observed.shape[0], :] = observed[...]

    cut_fields(lay, slab_ref[0], (now, prev), fill, sends)


def join_fields(lay, own_slot, odd, pieces, joined, state, courant, send_next, send_twin):
    fields = joined.shape[0]
    for turn, piece in enumerate(pieces):
        start_x = (own_slot ^ turn) * ROWS
        for field in range(fields):
            for y in range(lay.chunk):
                row = (field * lay.chunk + y) * ROWS
                joined[field, pl.ds(aligned(y * lay.wide + start_x), ROWS), :] = piece[row : row + ROWS, :]
    kept_rows = lay.kept * lay.wide
    for field in range(fields):
        target, first = (state, 0) if field == 0 else (state, (lay.chunk + REACH) * lay.wide)
        if field == 2:
            target, first = courant, 0
        for y in range(lay.chunk):
            for tile in range(lay.tiles):
                values = joined[field, pl.ds(y * lay.wide + tile, ROWS, stride=lay.tiles), :]
                row = y * lay.wide + tile * ROWS
                target[first + row : first + row + ROWS, :] = values
                if field == 0:
                    send_next[row : row + ROWS, :] = values
                    send_twin[row : row + ROWS, :] = values
    for field in range(1, fields):
        source, first = (state, (lay.chunk + REACH) * lay.wide) if field == 1 else (courant, 0)
        place = lay.rows + (field - 1) * kept_rows
        skipped = (lay.chunk - lay.kept) * lay.wide
        ahead = source[pl.ds(aligned(first + odd * skipped), kept_rows), :]
        send_next[place : place + kept_rows, :] = ahead
        behind = source[pl.ds(aligned(first + (1 - odd) * skipped), kept_rows), :]
        send_twin[place : place + kept_rows, :] = behind


def join_forward(lay, where_ref, *refs):
    pieces, (state, courant, send_next, send_twin, codes, joined) = refs[: lay.count_x], refs[lay.count_x :]
    own_slot, odd = where_ref[0], where_ref[1]
    join_fields(lay, own_slot, odd, pieces, joined, state, courant, send_next, send_twin)
    first = 3 * lay.cells
    strip_cells = lay.width_y * LANES
    slab_row = lax.broadcasted_iota(jnp.int32, codes.shape, 0)
    found = jnp.full(codes.shape, -1.0, jnp.float32)
    for turn, piece in enumerate(pieces):
        cell = piece[first : first + lay.count_x, :].astype(jnp.int32)
        used = cell >= 0
        cell = jnp.maximum(cell, 0)
        x = lax.div(cell, jnp.int32(strip_cells))
        y = lax.rem(lax.div(cell, jnp.int32(LANES)), jnp.int32(lay.width_y)) - own_slot * lay.chunk
        inside = used & (y >= 0) & (y < lay.chunk)
        code = jnp.where(inside, (y * ROWS + x) * LANES + lax.rem(cell, jnp.int32(LANES)), -1)
        code = code.astype(jnp.float32)
        line = jnp.concatenate([code[tile : tile + 1, :] for tile in range(lay.count_x)], axis=1)
        found = jnp.where(slab_row == (own_slot ^ turn), jnp.broadcast_to(line, codes.shape), found)
    codes[...] = found


def join_adjoint(lay, where_ref, *refs):
    pieces, (state, send_next, send_twin, joined) = refs[: lay.count_x], refs[lay.count_x :]
    join_fields(lay, where_ref[0], where_ref[1], pieces, joined, state, None, send_next, send_twin)


def load_state(lay, odd, first, now, prev, state, from_next, from_twin):
    zeros = jnp.zeros((ROWS, LANES), jnp.float32)
    for row in range(0, lay.padded_rows, 2 * ROWS):
        now[row : row + ROWS, :] = zeros
        prev[row : row + ROWS, :] = zeros

    def put(buffer, layer, ref, source):
        for tile in range(lay.tiles):
            row = layer * lay.stride + (2 * tile + 1) * ROWS
            values = ref[source * lay.wide + tile * ROWS : source * lay.wide + (tile + 1) * ROWS, :]
            buffer[pl.ds(row if isinstance(row, int) else aligned(row), ROWS), :] = values

    ahead = lay.margin + lay.chunk
    for y in range(lay.chunk):
        put(now, lay.margin + y, state, y)
        put(now, odd * ahead + y, from_next, y)
        put(now, (1 - odd) * ahead + y, from_twin, y)
    if first:
        for y in range(lay.chunk):
            put(prev, lay.margin + y, state, lay.chunk + REACH + y)
        for y in range(lay.kept):
            put(prev, odd * ahead + (1 - odd) * REACH + y, from_next, lay.chunk + y)
            put(prev, (1 - odd) * ahead + odd * REACH + y, from_twin, lay.chunk + y)
        return
    for y in range(lay.near):
        put(prev, lay.margin - REACH + y, state, lay.chunk + y)
    for index, y in enumerate(lay.lacking):
        put(prev, odd * ahead + y, from_next, lay.chunk + index)
        put(prev, (1 - odd) * ahead + y, from_twin, lay.chunk + index)


def store_state(lay, now, prev, state, send):
    def put(refs, target, buffer, layer):
        for tile in range(lay.tiles):
            row = layer * lay.stride + (2 * tile + 1) * ROWS
            values = buffer[row : row + ROWS, :]
            for ref, place in refs:
                ref[place * lay.wide + tile * ROWS : place * lay.wide + (tile + 1) * ROWS, :] = values

    for y in range(lay.chunk):
        put([(state, y), (send, y)], y, now, lay.margin + y)
    for y in range(lay.near):
        refs = [(state, lay.chunk + y)]
        if y - REACH in lay.lacking:
            refs.append((send, lay.chunk + y - REACH - lay.lacking[0]))
        put(refs, y, prev, lay.margin - REACH + y)


def split(values):
    high = values.astype(jnp.bfloat16)
    rest = values - high.astype(jnp.float32)
    middle = rest.astype(jnp.bfloat16)
    low = (rest - middle.astype(jnp.float32)).astype(jnp.bfloat16)
    return high, middle, low


def fill_band(band):
    apart = lax.broadcasted_iota(jnp.int32, (LANES, LANES), 0) - lax.broadcasted_iota(
        jnp.int32, (LANES, LANES), 1
    )
    weights = jnp.where(apart == 0, 3.0 * stencil[0], 0.0).astype(jnp.float32)
    for k in range(1, REACH + 1):
        weights = jnp.where(jnp.abs(apart) == k, stencil[k], weights)
    high, middle, low = split(weights)
    for index, part in enumerate((high, high, high, middle, middle, low)):
        band[index * LANES : (index + 1) * LANES, :] = part


def sweep(lay, step, now, prev, following, half, gain, band, inject=None):
    first_layer = REACH * (step + 1)
    group = 8

    def layers(block, carry):
        start = first_layer + group * block

        def rows_of(y, tile, shift=0):
            return pl.ds(aligned(y * lay.stride + (2 * tile + 1) * ROWS) + shift, ROWS)

        centers = [
            [now[rows_of(start + inner, tile), :] for tile in range(lay.tiles)] for inner in range(group)
        ]
        stacked = jnp.concatenate([tile for layer in centers for tile in layer], axis=0)
        high, middle, low = split(stacked)
        along_z = jnp.dot(
            jnp.concatenate([high, middle, low, high, middle, high], axis=1),
            band[...],
            preferred_element_type=jnp.float32,
        )
        for inner in range(group):
            y = start + inner
            lower = [now[rows_of(y, tile, -1), :] for tile in range(lay.tiles)]
            upper = [now[rows_of(y, tile, 1), :] for tile in range(lay.tiles)]

            def at_x(tile):
                if tile < 0:
                    return lower[tile + lay.tiles]
                if tile >= lay.tiles:
                    return upper[tile - lay.tiles]
                return centers[inner][tile]

            for tile in range(lay.tiles):
                place = (inner * lay.tiles + tile) * ROWS
                total = along_z[place : place + ROWS, :]
                for k in range(1, REACH + 1):
                    pair = now[rows_of(y + k, tile), :] + now[rows_of(y - k, tile), :]
                    total = total + stencil[k] * (pair + (at_x(tile - k) + at_x(tile + k)))
                flat = aligned((y - REACH) * lay.wide + tile * ROWS)
                if inject is not None:
                    spread_rows = pl.ds((y - REACH) * lay.wide + tile, ROWS, stride=lay.tiles)
                    total = total + inject[step, spread_rows, :]
                former = prev[rows_of(y, tile), :]
                change = (centers[inner][tile] - former) + half[pl.ds(flat, ROWS), :] * total
                following[rows_of(y, tile), :] = former + gain[pl.ds(flat, ROWS), :] * change
        return carry

    lax.fori_loop(0, (lay.extent - 2 * first_layer) // group, layers, 0)


def zero_between(lay, buffer):
    zeros = jnp.zeros((ROWS, LANES), jnp.float32)
    for row in range(0, lay.padded_rows, 2 * ROWS):
        buffer[row : row + ROWS, :] = zeros


def keep_own(lay, step, following, history):
    for y in range(lay.chunk):
        for tile in range(lay.tiles):
            row = (lay.margin + y) * lay.stride + (2 * tile + 1) * ROWS
            place = step * lay.rows + y * lay.wide + tile * ROWS
            history[place : place + ROWS, :] = following[row : row + ROWS, :]


def forward(lay, phase, sources, ints, state, from_next, from_twin, courant, gain, drive, *refs):
    first, last = phase == 0, phase == STEPS // DEPTH - 1
    refs = list(refs)
    history = refs.pop(0)
    half = refs.pop(0) if first else courant
    if not last:
        state_out, send = refs.pop(0), refs.pop(0)
    now, prev, following, band, pulse = refs
    odd = ints[0]

    fill_band(band)
    load_state(lay, odd, first, now, prev, state, from_next, from_twin)
    zero_between(lay, following)
    if first:
        tail = (lay.chunk + lay.kept) * lay.wide
        part = lay.kept * lay.wide
        half[part : part + lay.rows, :] = 0.5 * courant[...]
        ahead = part + lay.rows
        half[pl.ds(aligned(odd * ahead), part), :] = 0.5 * from_next[tail : tail + part, :]
        half[pl.ds(aligned((1 - odd) * ahead), part), :] = 0.5 * from_twin[tail : tail + part, :]
    for source in range(sources):
        flat = pl.ds(ints[1 + sources + source], 1)
        pulse[source : source + 1, :] = half[flat, :] * gain[flat, :]

    for step in range(DEPTH):
        sweep(lay, step, now, prev, following, half, gain, band)
        added = pulse[...] * drive[phase * DEPTH + step]
        places = [pl.ds(ints[1 + source], 1) for source in range(sources)]
        lines = [following[place, :] for place in places]
        for source, (place, line) in enumerate(zip(places, lines)):
            following[place, :] = line + added[source : source + 1, :]
        keep_own(lay, step, following, history)
        now, prev, following = following, now, prev

    if not last:
        store_state(lay, now, prev, state_out, send)


def slot_rows(codes, slab):
    code = codes[slab : slab + 1, :].astype(jnp.int32)
    row = jnp.where(code >= 0, lax.shift_right_arithmetic(code, 7), -1)
    return row, jnp.where(code >= 0, code & (LANES - 1), -1)


def record_slots(lay, history, codes, plain, stash, record):
    for step in range(DEPTH):
        for y in range(lay.chunk):
            for tile in range(lay.tiles):
                row = step * lay.rows + y * lay.wide
                values = history[row + tile * ROWS : row + (tile + 1) * ROWS, :]
                plain[pl.ds(row + tile, ROWS, stride=lay.tiles), :] = values
    for slab in range(lay.count_x):
        for step in range(DEPTH):
            for y in range(lay.chunk):
                row = step * lay.rows + y * lay.wide + slab * ROWS
                target = ((slab * DEPTH + step) * lay.chunk + y) * ROWS
                stash[target : target + ROWS, :] = plain[row : row + ROWS, :]
    slots = codes.shape[1]
    width = 2 * LANES
    for slab in range(lay.count_x):
        cell_row, cell_z = slot_rows(codes, slab)
        parts = split(stash[slab * DEPTH * lay.cells : (slab + 1) * DEPTH * lay.cells, :])
        parts = jnp.concatenate(parts, axis=1)
        for start in range(0, slots, width):
            here = slice(start, start + width)
            z = lax.broadcasted_iota(jnp.int32, (LANES, width), 0)
            pick = jnp.where(z == cell_z[:, here], 1.0, 0.0).astype(jnp.bfloat16)
            found = jnp.dot(parts, jnp.concatenate([pick] * 3, axis=0), preferred_element_type=jnp.float32)
            wanted = lax.broadcasted_iota(jnp.int32, (lay.cells, width), 0) == cell_row[:, here]
            for step in range(DEPTH):
                part = jnp.where(wanted, found[step * lay.cells : (step + 1) * lay.cells, :], 0.0)
                row = step * lay.count_x + slab
                record[row : row + 1, here] = jnp.sum(part, axis=0, keepdims=True)


def record_phase(lay, history, codes, record, plain, stash):
    record_slots(lay, history, codes, plain, stash, record)


def record_last(lay, phases, where_ref, history, codes, *refs):
    earlier, refs = refs[: phases - 1], refs[phases - 1 :]
    observed, (misfit, plain, stash, record) = refs[: lay.count_x], refs[lay.count_x :]
    record_slots(lay, history, codes, plain, stash, record)
    block = DEPTH * lay.count_x
    for index, part in enumerate(list(earlier) + [record]):
        misfit[index * block : (index + 1) * block, :] = part[...]
    total = STEPS * lay.count_x
    for slab in range(lay.count_x):
        misfit[total + slab : total + slab + 1, :] = codes[slab : slab + 1, :]
    for turn, piece in enumerate(observed):
        place = pl.ds(aligned((where_ref[0] ^ turn) * LANES, LANES), LANES)
        used = jnp.concatenate([codes[:, place]] * STEPS, axis=0) >= 0
        seen = piece[2 * lay.cells : 2 * lay.cells + total, :]
        misfit[0:total, place] = jnp.where(used, misfit[0:total, place] - seen, 0.0)


def spread(lay, phase, side, misfit, inject):
    codes = misfit[STEPS * lay.count_x : (STEPS + 1) * lay.count_x, :]
    for slab in range(lay.count_x):
        cell_row, cell_z = slot_rows(codes, slab)
        slots = cell_row.shape[1]
        z = lax.broadcasted_iota(jnp.int32, (LANES, slots), 0)
        pick = jnp.where(z == cell_z, 1.0, 0.0).astype(jnp.bfloat16)
        hit = lax.broadcasted_iota(jnp.int32, (lay.cells, slots), 0) == cell_row
        hit = jnp.where(hit, 1.0, 0.0).astype(jnp.bfloat16)
        left, spans = [], []
        for step in range(DEPTH):
            low, high = 0, lay.chunk
            if side < 0:
                low = REACH * (step + 1) - lay.margin + lay.chunk
            if side > 0:
                high = lay.margin - REACH * (step + 1)
            if low >= high:
                continue
            row = (STEPS - 1 - phase * DEPTH - step) * lay.count_x + slab
            parts = split(misfit[row : row + 1, :])
            left.append(jnp.concatenate([hit[low * ROWS : high * ROWS, :] * part for part in parts], axis=1))
            spans.append((step, low, high))
        placed = lax.dot_general(
            jnp.concatenate(left, axis=0),
            jnp.concatenate([pick] * 3, axis=1),
            (((1,), (1,)), ((), ())),
            preferred_element_type=jnp.float32,
        )
        at = 0
        for step, low, high in spans:
            for y in range(low, high):
                layer = lay.margin + side * lay.chunk + y - REACH
                target = layer * lay.wide + slab * ROWS
                inject[step, target : target + ROWS, :] = placed[at : at + ROWS, :]
                at += ROWS


def spread_own(lay, phase, misfit, inject):
    spread(lay, phase, 0, misfit, inject)


def spread_sides(lay, phase, where_ref, own, misfit_next, misfit_twin, inject):
    odd = where_ref[1]

    @pl.when(odd == 1)
    def ahead_is_next():
        spread(lay, phase, 1, misfit_next, inject)
        spread(lay, phase, -1, misfit_twin, inject)

    @pl.when(odd == 0)
    def behind_is_next():
        spread(lay, phase, -1, misfit_next, inject)
        spread(lay, phase, 1, misfit_twin, inject)


def backward(lay, phase, where_ref, state, from_next, from_twin, half, gain, inject, *refs):
    first, last = phase == 0, phase == STEPS // DEPTH - 1
    refs = list(refs)
    history = refs.pop(0)
    if not last:
        state_out, send = refs.pop(0), refs.pop(0)
    now, prev, following, band = refs

    fill_band(band)
    load_state(lay, where_ref[1], first, now, prev, state, from_next, from_twin)
    zero_between(lay, following)
    for step in range(DEPTH):
        sweep(lay, step, now, prev, following, half, gain, band, inject)
        keep_own(lay, step, following, history)
        now, prev, following = following, now, prev
    if not last:
        store_state(lay, now, prev, state_out, send)


def add_gradient(lay, before, adjoint, history, state, gradient):
    def layer(y, carry):
        place = aligned(y * lay.wide)
        own = pl.ds(place, lay.wide)
        fields = [state[pl.ds(aligned(place + (lay.chunk + REACH) * lay.wide), lay.wide), :], state[own, :]]
        fields += [history[pl.ds(aligned(place + step * lay.rows), lay.wide), :] for step in range(DEPTH)]
        total = None if before is None else before[own, :]
        for step in range(DEPTH):
            index = DEPTH - 1 - step
            accel = (fields[index + 2] - fields[index + 1]) - (fields[index + 1] - fields[index])
            term = adjoint[pl.ds(aligned(place + step * lay.rows), lay.wide), :] * accel
            total = term if total is None else total + term
        gradient[own, :] = total
        return carry

    lax.fori_loop(0, lay.chunk, layer, 0)


def gradient_first(lay, adjoint, history, state, gradient):
    add_gradient(lay, None, adjoint, history, state, gradient)


def gradient_later(lay, adjoint, history, state, before, gradient):
    add_gradient(lay, before, adjoint, history, state, gradient)


def gradient_last(lay, where_ref, adjoint, history, state, before, misfit, *refs):
    sends, (gradient, plain) = refs[: lay.count_x], refs[lay.count_x :]
    add_gradient(lay, before, adjoint, history, state, gradient)
    for y in range(lay.chunk):
        for tile in range(lay.tiles):
            row = y * lay.wide + tile * ROWS
            plain[pl.ds(y * lay.wide + tile, ROWS, stride=lay.tiles), :] = gradient[row : row + ROWS, :]
    total = STEPS * lay.count_x
    for turn, send in enumerate(sends):
        other = where_ref[0] ^ turn
        for y in range(lay.chunk):
            source = pl.ds(aligned(y * lay.wide + other * ROWS), ROWS)
            send[y * ROWS : (y + 1) * ROWS, :] = plain[source, :]
        tile = pl.ds(aligned(other * LANES, LANES), LANES)
        send[lay.cells : lay.cells + total, :] = misfit[0:total, tile]


def finish(lay, slab_ref, *refs):
    pieces, (gradient, residual) = refs[: lay.count_x], refs[lay.count_x :]
    slab = slab_ref[0]
    total = None
    for turn, piece in enumerate(pieces):
        start = (slab ^ turn) * lay.chunk
        for x in range(ROWS):
            target = pl.ds(aligned(x * lay.width_y + start), lay.chunk)
            gradient[target, :] = piece[pl.ds(x, lay.chunk, stride=ROWS), :]
        part = piece[lay.cells : lay.cells + residual.shape[0], :]
        total = part if total is None else total + part
    residual[...] = total


def gain_rows(lay, first_y):
    x = jnp.arange(ROWS)[None, :] * lay.tiles + jnp.arange(lay.tiles)[:, None]
    y = first_y + REACH + jnp.arange(lay.inner)

    def ramp(position, count):
        gap = jnp.minimum(position, count - 1 - position)
        profile = jnp.maximum(SPONGE - gap, 0).astype(jnp.float32) / SPONGE
        return profile * profile

    damping = damping_peak * (ramp(x, lay.wide)[None] + ramp(y, lay.whole_y)[:, None, None])
    gain = (2.0 / (1.0 + damping)).reshape(lay.inner * lay.wide, 1)
    return jnp.broadcast_to(gain, (lay.inner * lay.wide, LANES))


def source_rows(lay, first_y, source_cell, wavelet):
    x = source_cell // (lay.whole_y * LANES)
    y = source_cell // LANES % lay.whole_y - first_y
    z = source_cell % LANES
    inside = (y >= REACH) & (y < lay.extent - REACH)
    tile, row = x % lay.tiles, x // lay.tiles
    padded = jnp.where(inside, y * lay.stride + (2 * tile + 1) * ROWS + row, ROWS // 2)
    flat = jnp.where(inside, (y - REACH) * lay.wide + tile * ROWS + row, 0)
    same = (padded[:, None] == padded[None, :]) & inside[None, :]
    spot = (z[:, None] == jnp.arange(LANES)[None, :]).astype(jnp.float32)
    lines = jnp.where(same[None, :, :, None], wavelet[:, None, :, None] * spot[None, None], 0.0)
    return padded, flat, jnp.sum(lines, axis=2)


def local_tiles(
    lay,
    courant,
    state_prev,
    state_now,
    adjoint_now,
    adjoint_next,
    source_cell,
    wavelet,
    observed,
    receiver_cell,
    receiver_count,
):
    axes = ("gx", "gy")
    slab = lax.axis_index("gx")
    strip = lax.axis_index("gy")
    pair = strip // 2
    chip = jnp.where(pair % 2 == 0, slab, lay.count_x - 1 - slab)
    place = (pair * lay.count_x + chip) * 2 + strip % 2
    odd = strip % 2
    first_y = place * lay.chunk - lay.margin
    slab_int = slab.reshape(1).astype(jnp.int32)
    where = jnp.stack([place % lay.count_x, odd]).astype(jnp.int32)

    count = lay.count_x
    sources = source_cell.shape[0]
    slots = count * receiver_cell.shape[3]
    flat = lambda values: values.reshape(-1, LANES)
    part = functools.partial

    def swap(to_next, to_twin):
        return (
            lax.ppermute(to_next, axes, lay.swaps(1)),
            lax.ppermute(to_twin, axes, lay.swaps(0)),
        )

    padded, flat_row, drive = source_rows(lay, first_y, source_cell, wavelet)
    gain = gain_rows(lay, first_y)
    ints = jnp.concatenate([odd.reshape(1), padded, flat_row]).astype(jnp.int32)

    tail = -(-count // ROWS) * ROWS
    cuts = call(
        part(cut_forward, lay),
        (slab_int, receiver_count.reshape(-1)),
        (flat(state_now), flat(state_prev), flat(courant), receiver_cell.reshape(count, LANES)),
        [f32(3 * lay.cells + tail, LANES)] * count,
        [
            pltpu.VMEM((3, lay.width_x * lay.width_y, LANES), jnp.float32),
            pltpu.VMEM((count, LANES), jnp.int32),
            pltpu.SemaphoreType.DMA((4,)),
        ],
        space=pltpu.HBM,
    )
    pieces = [lax.ppermute(cut, axes, lay.to_chunks(turn)) for turn, cut in enumerate(cuts)]
    kept_rows = lay.kept * lay.wide
    state, own_courant, to_next, to_twin, codes = call(
        part(join_forward, lay),
        (where,),
        pieces,
        [f32(lay.state_rows, LANES), f32(lay.rows, LANES)]
        + [f32(lay.rows + 2 * kept_rows, LANES)] * 2
        + [f32(count, slots)],
        [pltpu.VMEM((3, lay.rows, LANES), jnp.float32)],
    )
    from_next, from_twin = swap(to_next, to_twin)

    traces = flat(observed)
    cuts = call(
        part(cut_adjoint, lay),
        (slab_int,),
        (flat(adjoint_now), flat(adjoint_next), traces),
        [f32(2 * lay.cells + traces.shape[0], LANES)] * count,
    )
    back_pieces = [lax.ppermute(cut, axes, lay.to_chunks(turn)) for turn, cut in enumerate(cuts)]
    back_state, to_next, to_twin = call(
        part(join_adjoint, lay),
        (where,),
        back_pieces,
        [f32(lay.state_rows, LANES)] + [f32(lay.rows + kept_rows, LANES)] * 2,
        [pltpu.VMEM((2, lay.rows, LANES), jnp.float32)],
    )
    back_from_next, back_from_twin = swap(to_next, to_twin)

    phases = STEPS // DEPTH
    step_cost = 8_000_000
    side_cost = 4_000_000
    history_shape = f32(DEPTH * lay.rows, LANES)
    state_shapes = [f32(lay.state_rows, LANES), f32(lay.send_rows, LANES)]
    buffers = [pltpu.VMEM((lay.padded_rows, LANES), jnp.float32)] * 3
    buffers += [pltpu.VMEM((6 * LANES, LANES), jnp.bfloat16)]
    record_scratch = [pltpu.VMEM((DEPTH * lay.rows, LANES), jnp.float32)] * 2
    record_shape = (DEPTH * count, slots)
    histories, states, records = [], [], []
    half = own_courant
    for phase in range(phases):
        first, last = phase == 0, phase == phases - 1
        outs = [history_shape]
        if first:
            outs.append(f32(lay.inner * lay.wide, LANES))
        if not last:
            outs += state_shapes
        results = list(
            call(
                part(forward, lay, phase, sources),
                (ints,),
                [state, from_next, from_twin, half, gain, drive],
                outs,
                buffers + [pltpu.VMEM((sources, LANES), jnp.float32)],
                cost=step_cost,
            )
        )
        histories.append(results.pop(0))
        states.append(state)
        if first:
            half = results.pop(0)
        if last:
            (misfit,) = call(
                part(record_last, lay, phases),
                (where,),
                [histories[-1], codes] + records + back_pieces,
                [f32(-(-(STEPS + 1) * count // ROWS) * ROWS, slots)],
                record_scratch + [pltpu.VMEM(record_shape, jnp.float32)],
                cost=side_cost,
            )
        else:
            state, send = results
            from_next, from_twin = swap(send, send)
            records += call(
                part(record_phase, lay),
                (),
                [histories[-1], codes],
                [f32(*record_shape)],
                record_scratch,
                cost=side_cost,
            )

    misfit_next, misfit_twin = swap(misfit, misfit)
    state, from_next, from_twin = back_state, back_from_next, back_from_twin
    gradient = None
    inject_shape = f32(DEPTH, lay.inner * lay.wide, LANES)
    for phase in range(phases):
        first, last = phase == 0, phase == phases - 1
        (inject,) = call(part(spread_own, lay, phase), (), [misfit], [inject_shape], cost=side_cost)
        (inject,) = call(
            part(spread_sides, lay, phase),
            (where,),
            [inject, misfit_next, misfit_twin],
            [inject_shape],
            cost=side_cost,
            aliases={1: 0},
        )
        results = call(
            part(backward, lay, phase),
            (where,),
            [state, from_next, from_twin, half, gain, inject],
            [history_shape] + ([] if last else state_shapes),
            buffers,
            cost=step_cost,
        )
        arrays = [results[0], histories[phases - 1 - phase], states[phases - 1 - phase]]
        if last:
            sends = call(
                part(gradient_last, lay),
                (where,),
                arrays + [gradient, misfit],
                [f32(lay.cells + traces.shape[0], LANES)] * count,
                [pltpu.VMEM((lay.rows, LANES), jnp.float32)] * 2,
            )
            continue
        _, state, send = results
        from_next, from_twin = swap(send, send)
        kernel = gradient_first if first else gradient_later
        (gradient,) = call(
            part(kernel, lay), (), arrays + ([] if first else [gradient]), [f32(lay.rows, LANES)], cost=side_cost
        )
    pieces = [lax.ppermute(send, axes, lay.to_slabs(turn)) for turn, send in enumerate(sends)]
    gradient, residual = call(
        part(finish, lay),
        (slab_int,),
        pieces,
        [f32(lay.width_x * lay.width_y, LANES), f32(*traces.shape)],
    )
    return gradient.reshape(courant.shape), residual.reshape(observed.shape)


def local(courant, *rest):
    width_x, width_y, depth_z = courant.shape
    count_x, count_y = lax.axis_size("gx"), lax.axis_size("gy")
    if fits(count_x, count_y, width_x, width_y, depth_z):
        return local_tiles(Layout(count_x, count_y, width_x, width_y), courant, *rest)
    return local_blocks(courant, *rest)


def padded_2(cells, sides, width):
    for axis, dim in sides:
        count = lax.axis_size(axis)
        ends = count - 1
        head = lax.slice_in_dim(cells, 0, width, axis=dim)
        tail = lax.slice_in_dim(cells, cells.shape[dim] - width, cells.shape[dim], axis=dim)
        cells = jnp.concatenate(
            [
                lax.ppermute(tail, axis, [(i, (i + 1) % count) for i in range(ends)]),
                cells,
                lax.ppermute(head, axis, [((i + 1) % count, i) for i in range(ends)]),
            ],
            axis=dim,
        )
    return cells


def laplace(values):
    width_x, width_y, depth_z = values.shape
    padded = padded_2(values, (("gx", 0), ("gy", 1)), 4)
    z_padded = jnp.pad(values, ((0, 0), (0, 0), (4, 4)))
    summed = 3.0 * stencil[0] * values
    for offset in range(1, 5):
        paired = (
            padded[4 + offset : 4 + offset + width_x, 4 : 4 + width_y]
            + padded[4 - offset : 4 - offset + width_x, 4 : 4 + width_y]
        )
        paired = (
            paired
            + padded[4 : 4 + width_x, 4 + offset : 4 + offset + width_y]
            + padded[4 : 4 + width_x, 4 - offset : 4 - offset + width_y]
        )
        paired = (
            paired
            + z_padded[:, :, 4 + offset : 4 + offset + depth_z]
            + z_padded[:, :, 4 - offset : 4 - offset + depth_z]
        )
        summed = summed + stencil[offset] * paired
    return summed


def sponge(start, count, whole):
    position = start + jnp.arange(count, dtype=jnp.int32)
    edge_gap = jnp.minimum(position, whole - 1 - position)
    profile = jnp.maximum(SPONGE - edge_gap, 0).astype(jnp.float32) / SPONGE
    return profile * profile


def place_sum(indices, amounts, shape):
    flat = jnp.zeros((shape[0] * shape[1] * shape[2],), jnp.float32).at[indices].add(amounts)
    return flat.reshape(shape)


def local_blocks(
    courant,
    state_prev,
    state_now,
    adjoint_now,
    adjoint_next,
    source_cell,
    wavelet,
    observed,
    receiver_cell,
    receiver_count,
):
    shape = courant.shape
    width_x, width_y, depth_z = shape
    slab = lax.axis_index("gx")
    strip = lax.axis_index("gy")
    whole_x = width_x * lax.axis_size("gx")
    whole_y = width_y * lax.axis_size("gy")
    damping = damping_peak * (
        sponge(slab * width_x, width_x, whole_x)[:, None, None]
        + sponge(strip * width_y, width_y, whole_y)[None, :, None]
    )
    source_x = source_cell // (whole_y * depth_z) - slab * width_x
    source_y = source_cell // depth_z % whole_y - strip * width_y
    source_z = source_cell % depth_z
    inside = (source_x >= 0) & (source_x < width_x) & (source_y >= 0) & (source_y < width_y)
    source_flat = jnp.where(inside, (source_x * width_y + source_y) * depth_z + source_z, 0)
    source_weight = wavelet * inside.astype(jnp.float32)[None, :]
    senders = receiver_cell.shape[2]
    slots = receiver_cell.shape[3]
    cells = receiver_cell.reshape(-1)
    active = (
        jnp.arange(slots, dtype=jnp.int32)[None, :] < receiver_count.reshape(senders, 1)
    ).astype(jnp.float32)
    active_flat = active.reshape(-1)

    def advance(carry, weights):
        former, current = carry
        drive = laplace(current) + place_sum(source_flat, weights, shape)
        following = (2.0 * current - (1.0 - damping) * former + courant * drive) / (1.0 + damping)
        return (
            (current, following),
            (following - 2.0 * current + former, following.reshape(-1)[cells] * active_flat),
        )

    final_states, (accels, recorded) = lax.scan(advance, (state_prev, state_now), source_weight)
    recorded_tiles = recorded.reshape(STEPS, senders, 1, 1, slots)
    active_tiles = active.reshape(1, senders, 1, 1, slots)
    synthetic, mask_back = (
        lax.all_to_all(recorded_tiles, "gx", split_axis=1, concat_axis=3, tiled=True),
        lax.all_to_all(active_tiles, "gx", split_axis=1, concat_axis=3, tiled=True),
    )
    trace_residual = mask_back * (synthetic - observed)
    misfit = lax.all_to_all(trace_residual, "gx", split_axis=3, concat_axis=1, tiled=True)
    misfit_rows = misfit.reshape(STEPS, senders * slots)

    def retreat(carry, inputs):
        later, current, gradient = carry
        acceleration, residual_row = inputs
        drive = laplace(current) + place_sum(cells, residual_row, shape)
        earlier = (2.0 * current - (1.0 - damping) * later + courant * drive) / (1.0 + damping)
        return ((current, earlier, gradient + earlier * acceleration), None)

    start_gradient = jnp.zeros(shape, jnp.float32)
    (last_later, last_current, gradient), unused = lax.scan(
        retreat, (adjoint_next, adjoint_now, start_gradient), (accels, misfit_rows), reverse=True
    )
    return (gradient, trace_residual)


def solution(mesh):
    placed = (
        P("gx", "gy", None),
        P(("groups", "gx"), "gy", None),
        P(("groups", "gx"), "gy", None),
        P(("groups", "gx"), "gy", None),
        P(("groups", "gx"), "gy", None),
        P("groups"),
        P(None, "groups"),
        P("groups", "gx", "gy", None, None),
        P("gx", "gy", None, None),
        P("gx", "gy", None),
    )
    return jax.shard_map(
        local,
        mesh=mesh,
        in_specs=placed,
        out_specs=(P(("groups", "gx"), "gy", None), P("groups", "gx", "gy", None, None)),
        check_vma=False,
    )
```

```python
import functools

import jax
import jax.numpy as jnp
from jax import lax
from jax.experimental import pallas as pl
from jax.experimental.pallas import tpu as pltpu
from jax.sharding import PartitionSpec as P

STEPS = 12
SPONGE = 8
REACH = 4
DEPTH = 4
LANES = 128
ROWS = 8


stencil = (-205.0 / 72.0, 8.0 / 5.0, -1.0 / 5.0, 8.0 / 315.0, -1.0 / 560.0)
damping_peak = 0.3


class Layout:
    def __init__(self, count_x, count_y, width_x, width_y):
        self.count_x, self.count_y = count_x, count_y
        self.width_x, self.width_y = width_x, width_y
        self.chunk = width_y // count_x
        self.wide = width_x * count_x
        self.tiles = self.wide // ROWS
        self.whole_y = width_y * count_y
        self.margin = REACH * DEPTH
        self.extent = self.chunk + 2 * self.margin
        self.stride = self.tiles * 2 * ROWS
        self.padded_rows = self.extent * self.stride + ROWS
        self.kept = self.margin - REACH
        self.inner = self.extent - 2 * REACH
        self.rows = self.chunk * self.wide
        self.cells = self.chunk * width_x
        self.near = self.chunk + 2 * REACH
        self.state_rows = (self.chunk + self.near) * self.wide
        self.lacking = range(REACH, self.chunk - REACH)
        self.send_rows = (self.chunk + len(self.lacking)) * self.wide

    def at(self, place):
        pair, rest = divmod(place, 2 * self.count_x)
        chip, core = divmod(rest, 2)
        slab = chip if pair % 2 == 0 else self.count_x - 1 - chip
        return slab * self.count_y + 2 * pair + core

    def to_chunks(self, turn):
        moves = []
        for slab in range(self.count_x):
            for strip in range(self.count_y):
                moves.append((slab * self.count_y + strip, self.at(strip * self.count_x + (slab ^ turn))))
        return moves

    def to_slabs(self, turn):
        return [(target, source) for source, target in self.to_chunks(turn)]

    def swaps(self, first):
        moves = []
        for place in range(first, self.count_x * self.count_y - 1, 2):
            moves += [(self.at(place), self.at(place + 1)), (self.at(place + 1), self.at(place))]
        return moves


def fits(count_x, count_y, width_x, width_y, depth_z):
    return (
        count_x & (count_x - 1) == 0
        and count_y % 2 == 0
        and width_x == ROWS
        and width_x * count_x == ROWS * REACH
        and depth_z == LANES
        and width_y == count_x * REACH * DEPTH
    )


def f32(*shape):
    return jax.ShapeDtypeStruct(shape, jnp.float32)


def call(kernel, ints, arrays, outs, scratch=(), cost=1_000_000, space=pltpu.VMEM, aliases=None):
    return pl.pallas_call(
        kernel,
        out_shape=tuple(outs),
        in_specs=[pl.BlockSpec(memory_space=pltpu.SMEM)] * len(ints)
        + [pl.BlockSpec(memory_space=space)] * len(arrays),
        out_specs=tuple(pl.BlockSpec(memory_space=pltpu.VMEM) for _ in outs),
        scratch_shapes=list(scratch),
        input_output_aliases=aliases or {},
        compiler_params=pltpu.CompilerParams(vmem_limit_bytes=32 * 1024 * 1024),
        cost_estimate=pl.CostEstimate(flops=cost, bytes_accessed=cost, transcendentals=0),
    )(*ints, *arrays)


def aligned(value, to=ROWS):
    return pl.multiple_of(value, to)


def cut_fields(lay, slab, fields, fill, targets):
    for turn, target in targets:
        start = (slab ^ turn) * lay.chunk
        row = 0
        for field in fields:
            for y in range(lay.chunk):
                target[row : row + ROWS, :] = field[pl.ds(start + y, ROWS, stride=lay.width_y), :]
                row += ROWS
        if fill is not None:
            fill(target, row)


def cut_forward(lay, slab_ref, now, prev, courant, *sends):
    cut_fields(lay, slab_ref[0], (now, prev, courant), None, enumerate(sends))


def cut_adjoint(lay, turns, slab_ref, count_ref, now, prev, observed, cell, tie, *sends):
    slots = lax.broadcasted_iota(jnp.int32, (1, LANES), 1)

    def fill(target, row):
        target[row : row + observed.shape[0], :] = observed[...]
        row += observed.shape[0]
        for tile in range(lay.count_x):
            used = jnp.where(slots < count_ref[tile], cell[tile : tile + 1, :], -1)
            target[row + tile : row + tile + 1, :] = used.astype(jnp.float32)

    cut_fields(lay, slab_ref[0], (now, prev), fill, zip(turns, sends))


def join_fields(lay, own_slot, odd, pieces, joined, state, courant, send_next, send_twin):
    fields = joined.shape[0]
    for turn, piece in enumerate(pieces):
        start_x = (own_slot ^ turn) * ROWS
        for field in range(fields):
            for y in range(lay.chunk):
                row = (field * lay.chunk + y) * ROWS
                joined[field, pl.ds(aligned(y * lay.wide + start_x), ROWS), :] = piece[row : row + ROWS, :]
    kept_rows = lay.kept * lay.wide
    for field in range(fields):
        target, first = (state, 0) if field == 0 else (state, (lay.chunk + REACH) * lay.wide)
        if field == 2:
            target, first = courant, 0
        for y in range(lay.chunk):
            for tile in range(lay.tiles):
                values = joined[field, pl.ds(y * lay.wide + tile, ROWS, stride=lay.tiles), :]
                row = y * lay.wide + tile * ROWS
                target[first + row : first + row + ROWS, :] = values
                if field == 0:
                    send_next[row : row + ROWS, :] = values
                    send_twin[row : row + ROWS, :] = values
    for field in range(1, fields):
        source, first = (state, (lay.chunk + REACH) * lay.wide) if field == 1 else (courant, 0)
        place = lay.rows + (field - 1) * kept_rows
        skipped = (lay.chunk - lay.kept) * lay.wide
        ahead = source[pl.ds(aligned(first + odd * skipped), kept_rows), :]
        send_next[place : place + kept_rows, :] = ahead
        behind = source[pl.ds(aligned(first + (1 - odd) * skipped), kept_rows), :]
        send_twin[place : place + kept_rows, :] = behind


def join_forward(lay, where_ref, *refs):
    pieces, (state, courant, send_next, send_twin, tie, joined) = refs[: lay.count_x], refs[lay.count_x :]
    join_fields(lay, where_ref[0], where_ref[1], pieces, joined, state, courant, send_next, send_twin)
    tie[...] = jnp.zeros_like(tie)


def join_adjoint(lay, where_ref, *refs):
    pieces, (tie, state, send_next, send_twin, codes, joined) = refs[: lay.count_x], refs[lay.count_x :]
    own_slot = where_ref[0]
    join_fields(lay, own_slot, where_ref[1], pieces, joined, state, None, send_next, send_twin)
    first = 2 * lay.cells + STEPS * lay.count_x
    strip_cells = lay.width_y * LANES
    slab_row = lax.broadcasted_iota(jnp.int32, codes.shape, 0)
    found = jnp.full(codes.shape, -1.0, jnp.float32)
    for turn, piece in enumerate(pieces):
        cell = piece[first : first + lay.count_x, :].astype(jnp.int32)
        used = cell >= 0
        cell = jnp.maximum(cell, 0)
        x = lax.div(cell, jnp.int32(strip_cells))
        y = lax.rem(lax.div(cell, jnp.int32(LANES)), jnp.int32(lay.width_y)) - own_slot * lay.chunk
        inside = used & (y >= 0) & (y < lay.chunk)
        code = jnp.where(inside, (y * ROWS + x) * LANES + lax.rem(cell, jnp.int32(LANES)), -1)
        code = code.astype(jnp.float32)
        line = jnp.concatenate([code[tile : tile + 1, :] for tile in range(lay.count_x)], axis=1)
        found = jnp.where(slab_row == (own_slot ^ turn), jnp.broadcast_to(line, codes.shape), found)
    codes[...] = found


def load_state(lay, odd, first, now, prev, state, from_next, from_twin):
    def put(buffer, layer, ref, source):
        for tile in range(lay.tiles):
            row = layer * lay.stride + (2 * tile + 1) * ROWS
            values = ref[source * lay.wide + tile * ROWS : source * lay.wide + (tile + 1) * ROWS, :]
            buffer[pl.ds(row if isinstance(row, int) else aligned(row), ROWS), :] = values

    ahead = lay.margin + lay.chunk
    for y in range(lay.chunk):
        put(now, lay.margin + y, state, y)
        put(now, odd * ahead + y, from_next, y)
        put(now, (1 - odd) * ahead + y, from_twin, y)
    if first:
        for y in range(lay.chunk):
            put(prev, lay.margin + y, state, lay.chunk + REACH + y)
        for y in range(lay.kept):
            put(prev, odd * ahead + (1 - odd) * REACH + y, from_next, lay.chunk + y)
            put(prev, (1 - odd) * ahead + odd * REACH + y, from_twin, lay.chunk + y)
        return
    for y in range(lay.near):
        put(prev, lay.margin - REACH + y, state, lay.chunk + y)
    for index, y in enumerate(lay.lacking):
        put(prev, odd * ahead + y, from_next, lay.chunk + index)
        put(prev, (1 - odd) * ahead + y, from_twin, lay.chunk + index)


def store_state(lay, now, prev, state, send):
    def put(refs, target, buffer, layer):
        for tile in range(lay.tiles):
            row = layer * lay.stride + (2 * tile + 1) * ROWS
            values = buffer[row : row + ROWS, :]
            for ref, place in refs:
                ref[place * lay.wide + tile * ROWS : place * lay.wide + (tile + 1) * ROWS, :] = values

    for y in range(lay.chunk):
        put([(state, y), (send, y)], y, now, lay.margin + y)
    for y in range(lay.near):
        refs = [(state, lay.chunk + y)]
        if y - REACH in lay.lacking:
            refs.append((send, lay.chunk + y - REACH - lay.lacking[0]))
        put(refs, y, prev, lay.margin - REACH + y)


def split(values):
    high = values.astype(jnp.bfloat16)
    rest = values - high.astype(jnp.float32)
    middle = rest.astype(jnp.bfloat16)
    low = (rest - middle.astype(jnp.float32)).astype(jnp.bfloat16)
    return high, middle, low


def fill_band(band):
    apart = lax.broadcasted_iota(jnp.int32, (LANES, LANES), 0) - lax.broadcasted_iota(
        jnp.int32, (LANES, LANES), 1
    )
    weights = jnp.where(apart == 0, 3.0 * stencil[0], 0.0).astype(jnp.float32)
    for k in range(1, REACH + 1):
        weights = jnp.where(jnp.abs(apart) == k, stencil[k], weights)
    high, middle, low = split(weights)
    for index, part in enumerate((high, high, high, middle, middle, low)):
        band[index * LANES : (index + 1) * LANES, :] = part


def multiply_z(lay, first_layer, count, now, band, along_z):
    most = 16
    for start in range(0, count, most):
        tiles = []
        for y in range(start, min(start + most, count)):
            for tile in range(lay.tiles):
                row = (first_layer + y) * lay.stride + (2 * tile + 1) * ROWS
                tiles.append(now[row : row + ROWS, :])
        high, middle, low = split(jnp.concatenate(tiles, axis=0))
        along_z[start * lay.wide : start * lay.wide + len(tiles) * ROWS, :] = jnp.dot(
            jnp.concatenate([high, middle, low, high, middle, high], axis=1),
            band[...],
            preferred_element_type=jnp.float32,
        )


def sweep(lay, step, now, prev, following, half, gain, band, along_z, inject=None):
    first_layer = REACH * (step + 1)
    count = lay.extent - 2 * first_layer
    group, quad = 8, 4
    multiply_z(lay, first_layer, count, now, band, along_z)

    def rows_of(y, tile, shift=0):
        return pl.ds(aligned(y * lay.stride + (2 * tile + 1) * ROWS) + shift, ROWS)

    def quad_layers(start):
        centers = [[None] * lay.tiles for _ in range(quad)]
        totals = [[None] * lay.tiles for _ in range(quad)]
        for tile in range(lay.tiles):
            column = [now[rows_of(start + y, tile), :] for y in range(-REACH, quad + REACH)]
            for inner in range(quad):
                here = inner + REACH
                centers[inner][tile] = column[here]
                total = stencil[1] * (column[here - 1] + column[here + 1])
                for k in range(2, REACH + 1):
                    total = total + stencil[k] * (column[here - k] + column[here + k])
                totals[inner][tile] = total
        for inner in range(quad):
            y = start + inner
            lower = [now[rows_of(y, tile, -1), :] for tile in range(lay.tiles)]
            upper = [now[rows_of(y, tile, 1), :] for tile in range(lay.tiles)]
            line = lower + centers[inner] + upper
            for tile in range(lay.tiles):
                total = totals[inner][tile]
                for k in range(1, REACH + 1):
                    total = total + stencil[k] * (line[lay.tiles + tile - k] + line[lay.tiles + tile + k])
                place = (y - first_layer) * lay.wide + tile * ROWS
                total = total + along_z[pl.ds(aligned(place), ROWS), :]
                if inject is not None:
                    spread_rows = pl.ds((y - REACH) * lay.wide + tile, ROWS, stride=lay.tiles)
                    total = total + inject[step, spread_rows, :]
                flat = pl.ds(aligned((y - REACH) * lay.wide + tile * ROWS), ROWS)
                former = prev[rows_of(y, tile), :]
                change = (centers[inner][tile] - former) + half[flat, :] * total
                following[rows_of(y, tile), :] = former + gain[flat, :] * change

    def layers(block, carry):
        start = first_layer + group * block
        for offset in range(0, group, quad):
            quad_layers(start + offset)
        return carry

    lax.fori_loop(0, count // group, layers, 0)


def zero_between(lay, step, buffer):
    zeros = jnp.zeros((ROWS, LANES), jnp.float32)
    first = REACH * (step + 1)
    for row in range(first * lay.stride, (lay.extent - first) * lay.stride + 1, 2 * ROWS):
        buffer[row : row + ROWS, :] = zeros


def zero_buffers(lay, now, prev, following):
    zero_between(lay, 0, now)
    zero_between(lay, 1, following)
    zero_between(lay, 2, prev)


def keep_own(lay, step, following, history):
    for y in range(lay.chunk):
        for tile in range(lay.tiles):
            row = (lay.margin + y) * lay.stride + (2 * tile + 1) * ROWS
            place = step * lay.rows + y * lay.wide + tile * ROWS
            history[place : place + ROWS, :] = following[row : row + ROWS, :]


def forward(lay, phase, sources, ints, state, from_next, from_twin, courant, gain, drive, *refs):
    first, last = phase == 0, phase == STEPS // DEPTH - 1
    refs = list(refs)
    history = refs.pop(0)
    half = refs.pop(0) if first else courant
    if not last:
        state_out, send, tie = [refs.pop(0) for _ in range(3)]
        tie[...] = jnp.zeros_like(tie)
    now, prev, following, band, along_z, pulse = refs
    odd = ints[0]

    fill_band(band)
    load_state(lay, odd, first, now, prev, state, from_next, from_twin)
    zero_buffers(lay, now, prev, following)
    if first:
        tail = (lay.chunk + lay.kept) * lay.wide
        part = lay.kept * lay.wide
        half[part : part + lay.rows, :] = 0.5 * courant[...]
        ahead = part + lay.rows
        half[pl.ds(aligned(odd * ahead), part), :] = 0.5 * from_next[tail : tail + part, :]
        half[pl.ds(aligned((1 - odd) * ahead), part), :] = 0.5 * from_twin[tail : tail + part, :]
    for source in range(sources):
        flat = pl.ds(ints[1 + sources + source], 1)
        pulse[source : source + 1, :] = half[flat, :] * gain[flat, :]

    for step in range(DEPTH):
        sweep(lay, step, now, prev, following, half, gain, band, along_z)
        added = pulse[...] * drive[phase * DEPTH + step]
        places = [pl.ds(ints[1 + source], 1) for source in range(sources)]
        lines = [following[place, :] for place in places]
        for source, (place, line) in enumerate(zip(places, lines)):
            following[place, :] = line + added[source : source + 1, :]
        keep_own(lay, step, following, history)
        now, prev, following = following, now, prev

    if not last:
        store_state(lay, now, prev, state_out, send)


def slot_rows(codes, slab):
    code = codes[slab : slab + 1, :].astype(jnp.int32)
    row = jnp.where(code >= 0, lax.shift_right_arithmetic(code, 7), -1)
    return row, jnp.where(code >= 0, code & (LANES - 1), -1)


def record_slots(lay, history, codes, plain, record):
    for step in range(DEPTH):
        for y in range(lay.chunk):
            for tile in range(lay.tiles):
                row = step * lay.rows + y * lay.wide
                values = history[row + tile * ROWS : row + (tile + 1) * ROWS, :]
                plain[pl.ds(row + tile, ROWS, stride=lay.tiles), :] = values
    slots = codes.shape[1]
    width = 2 * LANES
    for slab in range(lay.count_x):
        cell_row, cell_z = slot_rows(codes, slab)
        tiles = []
        for step in range(DEPTH):
            for y in range(lay.chunk):
                row = step * lay.rows + y * lay.wide + slab * ROWS
                tiles.append(plain[row : row + ROWS, :])
        parts = jnp.concatenate(split(jnp.concatenate(tiles, axis=0)), axis=1)
        for start in range(0, slots, width):
            here = slice(start, start + width)
            z = lax.broadcasted_iota(jnp.int32, (LANES, width), 0)
            pick = jnp.where(z == cell_z[:, here], 1.0, 0.0).astype(jnp.bfloat16)
            found = jnp.dot(parts, jnp.concatenate([pick] * 3, axis=0), preferred_element_type=jnp.float32)
            wanted = lax.broadcasted_iota(jnp.int32, (lay.cells, width), 0) == cell_row[:, here]
            for step in range(DEPTH):
                part = jnp.where(wanted, found[step * lay.cells : (step + 1) * lay.cells, :], 0.0)
                row = step * lay.count_x + slab
                record[row : row + 1, here] = jnp.sum(part, axis=0, keepdims=True)


def record_phase(lay, history, codes, record, plain):
    record_slots(lay, history, codes, plain, record)


def record_last(lay, phases, where_ref, history, codes, *refs):
    earlier, refs = refs[: phases - 1], refs[phases - 1 :]
    observed, (misfit, plain, record) = refs[: lay.count_x], refs[lay.count_x :]
    record_slots(lay, history, codes, plain, record)
    block = DEPTH * lay.count_x
    for index, part in enumerate(list(earlier) + [record]):
        misfit[index * block : (index + 1) * block, :] = part[...]
    total = STEPS * lay.count_x
    for slab in range(lay.count_x):
        misfit[total + slab : total + slab + 1, :] = codes[slab : slab + 1, :]
    for turn, piece in enumerate(observed):
        place = pl.ds(aligned((where_ref[0] ^ turn) * LANES, LANES), LANES)
        used = jnp.concatenate([codes[:, place]] * STEPS, axis=0) >= 0
        seen = piece[2 * lay.cells : 2 * lay.cells + total, :]
        misfit[0:total, place] = jnp.where(used, misfit[0:total, place] - seen, 0.0)


def spread(lay, phase, side, misfit, inject):
    codes = misfit[STEPS * lay.count_x : (STEPS + 1) * lay.count_x, :]
    for slab in range(lay.count_x):
        cell_row, cell_z = slot_rows(codes, slab)
        slots = cell_row.shape[1]
        z = lax.broadcasted_iota(jnp.int32, (LANES, slots), 0)
        pick = jnp.where(z == cell_z, 1.0, 0.0).astype(jnp.bfloat16)
        hit = lax.broadcasted_iota(jnp.int32, (lay.cells, slots), 0) == cell_row
        hit = jnp.where(hit, 1.0, 0.0).astype(jnp.bfloat16)
        left, spans = [], []
        for step in range(DEPTH):
            low, high = 0, lay.chunk
            if side < 0:
                low = REACH * (step + 1) - lay.margin + lay.chunk
            if side > 0:
                high = lay.margin - REACH * (step + 1)
            if low >= high:
                continue
            row = (STEPS - 1 - phase * DEPTH - step) * lay.count_x + slab
            parts = split(misfit[row : row + 1, :])
            left.append(jnp.concatenate([hit[low * ROWS : high * ROWS, :] * part for part in parts], axis=1))
            spans.append((step, low, high))
        placed = lax.dot_general(
            jnp.concatenate(left, axis=0),
            jnp.concatenate([pick] * 3, axis=1),
            (((1,), (1,)), ((), ())),
            preferred_element_type=jnp.float32,
        )
        at = 0
        for step, low, high in spans:
            for y in range(low, high):
                layer = lay.margin + side * lay.chunk + y - REACH
                target = layer * lay.wide + slab * ROWS
                inject[step, target : target + ROWS, :] = placed[at : at + ROWS, :]
                at += ROWS


def spread_own(lay, phase, misfit, inject):
    spread(lay, phase, 0, misfit, inject)


def spread_sides(lay, phase, where_ref, own, misfit_next, misfit_twin, inject):
    odd = where_ref[1]

    @pl.when(odd == 1)
    def ahead_is_next():
        spread(lay, phase, 1, misfit_next, inject)
        spread(lay, phase, -1, misfit_twin, inject)

    @pl.when(odd == 0)
    def behind_is_next():
        spread(lay, phase, -1, misfit_next, inject)
        spread(lay, phase, 1, misfit_twin, inject)


def backward(lay, phase, where_ref, state, from_next, from_twin, half, gain, inject, *refs):
    first, last = phase == 0, phase == STEPS // DEPTH - 1
    refs = list(refs)
    history = refs.pop(0)
    if not last:
        state_out, send = refs.pop(0), refs.pop(0)
    now, prev, following, band, along_z = refs

    fill_band(band)
    load_state(lay, where_ref[1], first, now, prev, state, from_next, from_twin)
    zero_buffers(lay, now, prev, following)
    for step in range(DEPTH):
        sweep(lay, step, now, prev, following, half, gain, band, along_z, inject)
        keep_own(lay, step, following, history)
        now, prev, following = following, now, prev
    if not last:
        store_state(lay, now, prev, state_out, send)


def add_gradient(lay, before, adjoint, history, state, gradient):
    def layer(y, carry):
        place = aligned(y * lay.wide)
        own = pl.ds(place, lay.wide)
        fields = [state[pl.ds(aligned(place + (lay.chunk + REACH) * lay.wide), lay.wide), :], state[own, :]]
        fields += [history[pl.ds(aligned(place + step * lay.rows), lay.wide), :] for step in range(DEPTH)]
        total = None if before is None else before[own, :]
        for step in range(DEPTH):
            index = DEPTH - 1 - step
            accel = (fields[index + 2] - fields[index + 1]) - (fields[index + 1] - fields[index])
            term = adjoint[pl.ds(aligned(place + step * lay.rows), lay.wide), :] * accel
            total = term if total is None else total + term
        gradient[own, :] = total
        return carry

    lax.fori_loop(0, lay.chunk, layer, 0)


def gradient_first(lay, adjoint, history, state, gradient):
    add_gradient(lay, None, adjoint, history, state, gradient)


def gradient_later(lay, adjoint, history, state, before, gradient):
    add_gradient(lay, before, adjoint, history, state, gradient)


def gradient_last(lay, where_ref, adjoint, history, state, before, *refs):
    sends, (gradient, plain) = refs[: lay.count_x], refs[lay.count_x :]
    add_gradient(lay, before, adjoint, history, state, gradient)
    for y in range(lay.chunk):
        for tile in range(lay.tiles):
            row = y * lay.wide + tile * ROWS
            plain[pl.ds(y * lay.wide + tile, ROWS, stride=lay.tiles), :] = gradient[row : row + ROWS, :]
    for turn, send in enumerate(sends):
        other = where_ref[0] ^ turn
        for y in range(lay.chunk):
            source = pl.ds(aligned(y * lay.wide + other * ROWS), ROWS)
            send[y * ROWS : (y + 1) * ROWS, :] = plain[source, :]


def cut_residual(lay, where_ref, misfit, *sends):
    total = STEPS * lay.count_x
    for turn, send in enumerate(sends):
        tile = pl.ds(aligned((where_ref[0] ^ turn) * LANES, LANES), LANES)
        send[...] = misfit[0:total, tile]


def join_residual(*refs):
    total = refs[0][...]
    for piece in refs[1:-1]:
        total = total + piece[...]
    refs[-1][...] = total


def finish(lay, slab_ref, *refs):
    pieces, gradient = refs[: lay.count_x], refs[lay.count_x]
    for turn, piece in enumerate(pieces):
        start = (slab_ref[0] ^ turn) * lay.chunk
        for x in range(ROWS):
            target = pl.ds(aligned(x * lay.width_y + start), lay.chunk)
            gradient[target, :] = piece[pl.ds(x, lay.chunk, stride=ROWS), :]


def gain_rows(lay, first_y):
    x = jnp.arange(ROWS)[None, :] * lay.tiles + jnp.arange(lay.tiles)[:, None]
    y = first_y + REACH + jnp.arange(lay.inner)

    def ramp(position, count):
        gap = jnp.minimum(position, count - 1 - position)
        profile = jnp.maximum(SPONGE - gap, 0).astype(jnp.float32) / SPONGE
        return profile * profile

    damping = damping_peak * (ramp(x, lay.wide)[None] + ramp(y, lay.whole_y)[:, None, None])
    gain = (2.0 / (1.0 + damping)).reshape(lay.inner * lay.wide, 1)
    return jnp.broadcast_to(gain, (lay.inner * lay.wide, LANES))


def source_rows(lay, first_y, source_cell, wavelet):
    x = source_cell // (lay.whole_y * LANES)
    y = source_cell // LANES % lay.whole_y - first_y
    z = source_cell % LANES
    inside = (y >= REACH) & (y < lay.extent - REACH)
    tile, row = x % lay.tiles, x // lay.tiles
    padded = jnp.where(inside, y * lay.stride + (2 * tile + 1) * ROWS + row, ROWS // 2)
    flat = jnp.where(inside, (y - REACH) * lay.wide + tile * ROWS + row, 0)
    same = (padded[:, None] == padded[None, :]) & inside[None, :]
    spot = (z[:, None] == jnp.arange(LANES)[None, :]).astype(jnp.float32)
    lines = jnp.where(same[None, :, :, None], wavelet[:, None, :, None] * spot[None, None], 0.0)
    return padded, flat, jnp.sum(lines, axis=2)


def local_tiles(
    lay,
    courant,
    state_prev,
    state_now,
    adjoint_now,
    adjoint_next,
    source_cell,
    wavelet,
    observed,
    receiver_cell,
    receiver_count,
):
    axes = ("gx", "gy")
    slab = lax.axis_index("gx")
    strip = lax.axis_index("gy")
    pair = strip // 2
    chip = jnp.where(pair % 2 == 0, slab, lay.count_x - 1 - slab)
    place = (pair * lay.count_x + chip) * 2 + strip % 2
    odd = strip % 2
    first_y = place * lay.chunk - lay.margin
    slab_int = slab.reshape(1).astype(jnp.int32)
    where = jnp.stack([place % lay.count_x, odd]).astype(jnp.int32)

    count = lay.count_x
    sources = source_cell.shape[0]
    slots = count * receiver_cell.shape[3]
    flat = lambda values: values.reshape(-1, LANES)
    part = functools.partial

    def swap(to_next, to_twin):
        return (
            lax.ppermute(to_next, axes, lay.swaps(1)),
            lax.ppermute(to_twin, axes, lay.swaps(0)),
        )

    def after(value, others):
        return lax.optimization_barrier((value, others))[0]

    padded, flat_row, drive = source_rows(lay, first_y, source_cell, wavelet)
    gain = gain_rows(lay, first_y)
    ints = jnp.concatenate([odd.reshape(1), padded, flat_row]).astype(jnp.int32)

    cuts = call(
        part(cut_forward, lay),
        (slab_int,),
        (flat(state_now), flat(state_prev), flat(courant)),
        [f32(3 * lay.cells, LANES)] * count,
    )
    pieces = [lax.ppermute(cut, axes, lay.to_chunks(turn)) for turn, cut in enumerate(cuts)]
    kept_rows = lay.kept * lay.wide
    tie_shape = f32(ROWS, LANES)
    state, own_courant, to_next, to_twin, tie = call(
        part(join_forward, lay),
        (where,),
        pieces,
        [f32(lay.state_rows, LANES), f32(lay.rows, LANES)]
        + [f32(lay.rows + 2 * kept_rows, LANES)] * 2
        + [tie_shape],
        [pltpu.VMEM((3, lay.rows, LANES), jnp.float32)],
    )
    from_next, from_twin = swap(to_next, to_twin)

    traces = flat(observed)
    cut_cells = receiver_cell.reshape(count, LANES)
    back_pieces = []

    def move_adjoint(turns, tie):
        cuts = call(
            part(cut_adjoint, lay, turns),
            (slab_int, receiver_count.reshape(-1)),
            (flat(adjoint_now), flat(adjoint_next), traces, cut_cells, tie),
            [f32(2 * lay.cells + traces.shape[0] + -(-count // ROWS) * ROWS, LANES)] * len(turns),
        )
        for turn, cut in zip(turns, cuts):
            back_pieces.append(lax.ppermute(cut, axes, lay.to_chunks(turn)))

    move_adjoint(range(count // 2), tie)

    phases = STEPS // DEPTH
    step_cost = 8_000_000
    side_cost = 4_000_000
    history_shape = f32(DEPTH * lay.rows, LANES)
    state_shapes = [f32(lay.state_rows, LANES), f32(lay.send_rows, LANES)]
    buffers = [pltpu.VMEM((lay.padded_rows, LANES), jnp.float32)] * 3
    buffers += [pltpu.VMEM((6 * LANES, LANES), jnp.bfloat16)]
    buffers += [pltpu.VMEM((lay.inner * lay.wide, LANES), jnp.float32)]
    record_scratch = [pltpu.VMEM((DEPTH * lay.rows, LANES), jnp.float32)]
    record_shape = (DEPTH * count, slots)
    histories, states, records = [], [], []
    half = own_courant
    for phase in range(phases):
        first, last = phase == 0, phase == phases - 1
        outs = [history_shape]
        if first:
            outs.append(f32(lay.inner * lay.wide, LANES))
        if not last:
            outs += state_shapes + [tie_shape]
        results = list(
            call(
                part(forward, lay, phase, sources),
                (ints,),
                [state, from_next, from_twin, half, gain, drive],
                outs,
                buffers + [pltpu.VMEM((sources, LANES), jnp.float32)],
                cost=step_cost,
            )
        )
        histories.append(results.pop(0))
        states.append(state)
        if first:
            half = results.pop(0)
        if last:
            continue
        state, send, tie = results
        send = after(send, back_pieces[-(count // 2) :])
        from_next, from_twin = swap(send, send)
        if first:
            move_adjoint(range(count // 2, count), tie)
    back_state, to_next, to_twin, codes = call(
        part(join_adjoint, lay),
        (where,),
        back_pieces + [tie],
        [f32(lay.state_rows, LANES)] + [f32(lay.rows + kept_rows, LANES)] * 2 + [f32(count, slots)],
        [pltpu.VMEM((2, lay.rows, LANES), jnp.float32)],
    )
    for history in histories[:-1]:
        records += call(
            part(record_phase, lay),
            (),
            [history, codes],
            [f32(*record_shape)],
            record_scratch,
            cost=side_cost,
        )
    arrived = (from_next, from_twin, records)
    back_from_next, back_from_twin = swap(after(to_next, arrived), after(to_twin, arrived))
    (misfit,) = call(
        part(record_last, lay, phases),
        (where,),
        [histories[-1], codes] + records + back_pieces,
        [f32(-(-(STEPS + 1) * count // ROWS) * ROWS, slots)],
        record_scratch + [pltpu.VMEM(record_shape, jnp.float32)],
        cost=side_cost,
    )

    misfit = after(misfit, [back_from_next, back_from_twin])
    misfit_next, misfit_twin = swap(misfit, misfit)
    cuts = call(part(cut_residual, lay), (where,), [misfit], [f32(*traces.shape)] * count)
    parts = [lax.ppermute(cut, axes, lay.to_slabs(turn)) for turn, cut in enumerate(cuts)]
    (residual,) = call(join_residual, (), parts, [f32(*traces.shape)])
    state, from_next, from_twin = back_state, back_from_next, back_from_twin
    gradient = None
    inject_shape = f32(DEPTH, lay.inner * lay.wide, LANES)
    for phase in range(phases):
        first, last = phase == 0, phase == phases - 1
        (inject,) = call(part(spread_own, lay, phase), (), [misfit], [inject_shape], cost=side_cost)
        (inject,) = call(
            part(spread_sides, lay, phase),
            (where,),
            [inject, misfit_next, misfit_twin],
            [inject_shape],
            cost=side_cost,
            aliases={1: 0},
        )
        results = call(
            part(backward, lay, phase),
            (where,),
            [state, from_next, from_twin, half, gain, inject],
            [history_shape] + ([] if last else state_shapes),
            buffers,
            cost=step_cost,
        )
        arrays = [results[0], histories[phases - 1 - phase], states[phases - 1 - phase]]
        if last:
            sends = call(
                part(gradient_last, lay),
                (where,),
                arrays + [gradient],
                [f32(lay.cells, LANES)] * count,
                [pltpu.VMEM((lay.rows, LANES), jnp.float32)] * 2,
            )
            continue
        _, state, send = results
        from_next, from_twin = swap(send, send)
        half_way = count // 2
        state = after(state, parts[:half_way] if first else parts[half_way:])
        kernel = gradient_first if first else gradient_later
        (gradient,) = call(
            part(kernel, lay), (), arrays + ([] if first else [gradient]), [f32(lay.rows, LANES)], cost=side_cost
        )
    pieces = [lax.ppermute(send, axes, lay.to_slabs(turn)) for turn, send in enumerate(sends)]
    (gradient,) = call(part(finish, lay), (slab_int,), pieces, [f32(lay.width_x * lay.width_y, LANES)])
    return gradient.reshape(courant.shape), residual.reshape(observed.shape)


def local(courant, *rest):
    width_x, width_y, depth_z = courant.shape
    count_x, count_y = lax.axis_size("gx"), lax.axis_size("gy")
    if fits(count_x, count_y, width_x, width_y, depth_z):
        return local_tiles(Layout(count_x, count_y, width_x, width_y), courant, *rest)
    return local_blocks(courant, *rest)


def padded_2(cells, sides, width):
    for axis, dim in sides:
        count = lax.axis_size(axis)
        ends = count - 1
        head = lax.slice_in_dim(cells, 0, width, axis=dim)
        tail = lax.slice_in_dim(cells, cells.shape[dim] - width, cells.shape[dim], axis=dim)
        cells = jnp.concatenate(
            [
                lax.ppermute(tail, axis, [(i, (i + 1) % count) for i in range(ends)]),
                cells,
                lax.ppermute(head, axis, [((i + 1) % count, i) for i in range(ends)]),
            ],
            axis=dim,
        )
    return cells


def laplace(values):
    width_x, width_y, depth_z = values.shape
    padded = padded_2(values, (("gx", 0), ("gy", 1)), 4)
    z_padded = jnp.pad(values, ((0, 0), (0, 0), (4, 4)))
    summed = 3.0 * stencil[0] * values
    for offset in range(1, 5):
        paired = (
            padded[4 + offset : 4 + offset + width_x, 4 : 4 + width_y]
            + padded[4 - offset : 4 - offset + width_x, 4 : 4 + width_y]
        )
        paired = (
            paired
            + padded[4 : 4 + width_x, 4 + offset : 4 + offset + width_y]
            + padded[4 : 4 + width_x, 4 - offset : 4 - offset + width_y]
        )
        paired = (
            paired
            + z_padded[:, :, 4 + offset : 4 + offset + depth_z]
            + z_padded[:, :, 4 - offset : 4 - offset + depth_z]
        )
        summed = summed + stencil[offset] * paired
    return summed


def sponge(start, count, whole):
    position = start + jnp.arange(count, dtype=jnp.int32)
    edge_gap = jnp.minimum(position, whole - 1 - position)
    profile = jnp.maximum(SPONGE - edge_gap, 0).astype(jnp.float32) / SPONGE
    return profile * profile


def place_sum(indices, amounts, shape):
    flat = jnp.zeros((shape[0] * shape[1] * shape[2],), jnp.float32).at[indices].add(amounts)
    return flat.reshape(shape)


def local_blocks(
    courant,
    state_prev,
    state_now,
    adjoint_now,
    adjoint_next,
    source_cell,
    wavelet,
    observed,
    receiver_cell,
    receiver_count,
):
    shape = courant.shape
    width_x, width_y, depth_z = shape
    slab = lax.axis_index("gx")
    strip = lax.axis_index("gy")
    whole_x = width_x * lax.axis_size("gx")
    whole_y = width_y * lax.axis_size("gy")
    damping = damping_peak * (
        sponge(slab * width_x, width_x, whole_x)[:, None, None]
        + sponge(strip * width_y, width_y, whole_y)[None, :, None]
    )
    source_x = source_cell // (whole_y * depth_z) - slab * width_x
    source_y = source_cell // depth_z % whole_y - strip * width_y
    source_z = source_cell % depth_z
    inside = (source_x >= 0) & (source_x < width_x) & (source_y >= 0) & (source_y < width_y)
    source_flat = jnp.where(inside, (source_x * width_y + source_y) * depth_z + source_z, 0)
    source_weight = wavelet * inside.astype(jnp.float32)[None, :]
    senders = receiver_cell.shape[2]
    slots = receiver_cell.shape[3]
    cells = receiver_cell.reshape(-1)
    active = (
        jnp.arange(slots, dtype=jnp.int32)[None, :] < receiver_count.reshape(senders, 1)
    ).astype(jnp.float32)
    active_flat = active.reshape(-1)

    def advance(carry, weights):
        former, current = carry
        drive = laplace(current) + place_sum(source_flat, weights, shape)
        following = (2.0 * current - (1.0 - damping) * former + courant * drive) / (1.0 + damping)
        return (
            (current, following),
            (following - 2.0 * current + former, following.reshape(-1)[cells] * active_flat),
        )

    final_states, (accels, recorded) = lax.scan(advance, (state_prev, state_now), source_weight)
    recorded_tiles = recorded.reshape(STEPS, senders, 1, 1, slots)
    active_tiles = active.reshape(1, senders, 1, 1, slots)
    synthetic, mask_back = (
        lax.all_to_all(recorded_tiles, "gx", split_axis=1, concat_axis=3, tiled=True),
        lax.all_to_all(active_tiles, "gx", split_axis=1, concat_axis=3, tiled=True),
    )
    trace_residual = mask_back * (synthetic - observed)
    misfit = lax.all_to_all(trace_residual, "gx", split_axis=3, concat_axis=1, tiled=True)
    misfit_rows = misfit.reshape(STEPS, senders * slots)

    def retreat(carry, inputs):
        later, current, gradient = carry
        acceleration, residual_row = inputs
        drive = laplace(current) + place_sum(cells, residual_row, shape)
        earlier = (2.0 * current - (1.0 - damping) * later + courant * drive) / (1.0 + damping)
        return ((current, earlier, gradient + earlier * acceleration), None)

    start_gradient = jnp.zeros(shape, jnp.float32)
    (last_later, last_current, gradient), unused = lax.scan(
        retreat, (adjoint_next, adjoint_now, start_gradient), (accels, misfit_rows), reverse=True
    )
    return (gradient, trace_residual)


def solution(mesh):
    placed = (
        P("gx", "gy", None),
        P(("groups", "gx"), "gy", None),
        P(("groups", "gx"), "gy", None),
        P(("groups", "gx"), "gy", None),
        P(("groups", "gx"), "gy", None),
        P("groups"),
        P(None, "groups"),
        P("groups", "gx", "gy", None, None),
        P("gx", "gy", None, None),
        P("gx", "gy", None),
    )
    return jax.shard_map(
        local,
        mesh=mesh,
        in_specs=placed,
        out_specs=(P(("groups", "gx"), "gy", None), P("groups", "gx", "gy", None, None)),
        check_vma=False,
    )
```

```python
import functools

import jax
import jax.numpy as jnp
from jax import lax
from jax.experimental import pallas as pl
from jax.experimental.pallas import tpu as pltpu
from jax.sharding import PartitionSpec as P

STEPS = 12
SPONGE = 8
REACH = 4
DEPTH = 4
LANES = 128
ROWS = 8


stencil = (-205.0 / 72.0, 8.0 / 5.0, -1.0 / 5.0, 8.0 / 315.0, -1.0 / 560.0)
damping_peak = 0.3


class Layout:
    def __init__(self, count_x, count_y, width_x, width_y):
        self.count_x, self.count_y = count_x, count_y
        self.width_x, self.width_y = width_x, width_y
        self.chunk = width_y // count_x
        self.wide = width_x * count_x
        self.tiles = self.wide // ROWS
        self.whole_y = width_y * count_y
        self.margin = REACH * DEPTH
        self.extent = self.chunk + 2 * self.margin
        self.stride = self.tiles * 2 * ROWS
        self.padded_rows = self.extent * self.stride + ROWS
        self.kept = self.margin - REACH
        self.inner = self.extent - 2 * REACH
        self.rows = self.chunk * self.wide
        self.cells = self.chunk * width_x
        self.near = self.chunk + 2 * REACH
        self.state_rows = (self.chunk + self.near) * self.wide
        self.lacking = range(REACH, self.chunk - REACH)
        self.send_rows = (self.chunk + len(self.lacking)) * self.wide

    def at(self, place):
        pair, rest = divmod(place, 2 * self.count_x)
        chip, core = divmod(rest, 2)
        slab = chip if pair % 2 == 0 else self.count_x - 1 - chip
        return slab * self.count_y + 2 * pair + core

    def to_chunks(self, turn):
        moves = []
        for slab in range(self.count_x):
            for strip in range(self.count_y):
                moves.append((slab * self.count_y + strip, self.at(strip * self.count_x + (slab ^ turn))))
        return moves

    def to_slabs(self, turn):
        return [(target, source) for source, target in self.to_chunks(turn)]

    def swaps(self, first):
        moves = []
        for place in range(first, self.count_x * self.count_y - 1, 2):
            moves += [(self.at(place), self.at(place + 1)), (self.at(place + 1), self.at(place))]
        return moves


def fits(count_x, count_y, width_x, width_y, depth_z):
    return (
        count_x & (count_x - 1) == 0
        and count_y % 2 == 0
        and width_x == ROWS
        and width_x * count_x == ROWS * REACH
        and depth_z == LANES
        and width_y == count_x * REACH * DEPTH
    )


def f32(*shape):
    return jax.ShapeDtypeStruct(shape, jnp.float32)


def call(
    kernel, ints, arrays, outs, scratch=(), cost=1_000_000, space=pltpu.VMEM, aliases=None, limit=32 * 1024 * 1024
):
    return pl.pallas_call(
        kernel,
        out_shape=tuple(outs),
        in_specs=[pl.BlockSpec(memory_space=pltpu.SMEM)] * len(ints)
        + [pl.BlockSpec(memory_space=space)] * len(arrays),
        out_specs=tuple(pl.BlockSpec(memory_space=pltpu.VMEM) for _ in outs),
        scratch_shapes=list(scratch),
        input_output_aliases=aliases or {},
        compiler_params=pltpu.CompilerParams(vmem_limit_bytes=limit),
        cost_estimate=pl.CostEstimate(flops=cost, bytes_accessed=cost, transcendentals=0),
    )(*ints, *arrays)


def aligned(value, to=ROWS):
    return pl.multiple_of(value, to)


def cut_blocks(lay, slab_ref, count_ref, *refs):
    inputs, refs = refs[:7], refs[7:]
    sends, back_sends = refs[: lay.count_x], refs[lay.count_x : 2 * lay.count_x]
    held, held_cell, held_traces, done = refs[2 * lay.count_x :]
    targets = [held.at[index] for index in range(5)] + [held_cell, held_traces]
    copies = [
        pltpu.make_async_copy(source, target, done.at[index])
        for index, (source, target) in enumerate(zip(inputs, targets))
    ]
    for copy in copies:
        copy.start()
    for copy in copies:
        copy.wait()
    slab = slab_ref[0]
    slots = lax.broadcasted_iota(jnp.int32, (1, LANES), 1)
    used = []
    for tile in range(lay.count_x):
        cell = jnp.where(slots < count_ref[tile], held_cell[tile : tile + 1, :], -1)
        used.append(cell.astype(jnp.float32))
    for turn in range(lay.count_x):
        start = (slab ^ turn) * lay.chunk
        for index in range(5):
            target, first = (sends[turn], index) if index < 3 else (back_sends[turn], index - 3)
            for y in range(lay.chunk):
                row = (first * lay.chunk + y) * ROWS
                target[row : row + ROWS, :] = held[index, pl.ds(start + y, ROWS, stride=lay.width_y), :]
        for tile in range(lay.count_x):
            row = 3 * lay.cells + tile
            sends[turn][row : row + 1, :] = used[tile]
        row = 2 * lay.cells
        back_sends[turn][row : row + held_traces.shape[0], :] = held_traces[...]


def join_fields(lay, own_slot, odd, pieces, joined, state, courant, send_next, send_twin):
    fields = joined.shape[0]
    for turn, piece in enumerate(pieces):
        start_x = (own_slot ^ turn) * ROWS
        for field in range(fields):
            for y in range(lay.chunk):
                row = (field * lay.chunk + y) * ROWS
                joined[field, pl.ds(aligned(y * lay.wide + start_x), ROWS), :] = piece[row : row + ROWS, :]
    kept_rows = lay.kept * lay.wide
    for field in range(fields):
        target, first = (state, 0) if field == 0 else (state, (lay.chunk + REACH) * lay.wide)
        if field == 2:
            target, first = courant, 0
        for y in range(lay.chunk):
            for tile in range(lay.tiles):
                values = joined[field, pl.ds(y * lay.wide + tile, ROWS, stride=lay.tiles), :]
                row = y * lay.wide + tile * ROWS
                target[first + row : first + row + ROWS, :] = values
                if field == 0:
                    send_next[row : row + ROWS, :] = values
                    send_twin[row : row + ROWS, :] = values
    for field in range(1, fields):
        source, first = (state, (lay.chunk + REACH) * lay.wide) if field == 1 else (courant, 0)
        place = lay.rows + (field - 1) * kept_rows
        skipped = (lay.chunk - lay.kept) * lay.wide
        ahead = source[pl.ds(aligned(first + odd * skipped), kept_rows), :]
        send_next[place : place + kept_rows, :] = ahead
        behind = source[pl.ds(aligned(first + (1 - odd) * skipped), kept_rows), :]
        send_twin[place : place + kept_rows, :] = behind


def join_forward(lay, where_ref, *refs):
    pieces, (state, courant, send_next, send_twin, codes, joined) = refs[: lay.count_x], refs[lay.count_x :]
    own_slot = where_ref[0]
    join_fields(lay, own_slot, where_ref[1], pieces, joined, state, courant, send_next, send_twin)
    first = 3 * lay.cells
    strip_cells = lay.width_y * LANES
    slab_row = lax.broadcasted_iota(jnp.int32, codes.shape, 0)
    found = jnp.full(codes.shape, -1.0, jnp.float32)
    for turn, piece in enumerate(pieces):
        cell = piece[first : first + lay.count_x, :].astype(jnp.int32)
        used = cell >= 0
        cell = jnp.maximum(cell, 0)
        x = lax.div(cell, jnp.int32(strip_cells))
        y = lax.rem(lax.div(cell, jnp.int32(LANES)), jnp.int32(lay.width_y)) - own_slot * lay.chunk
        inside = used & (y >= 0) & (y < lay.chunk)
        code = jnp.where(inside, (y * ROWS + x) * LANES + lax.rem(cell, jnp.int32(LANES)), -1)
        code = code.astype(jnp.float32)
        line = jnp.concatenate([code[tile : tile + 1, :] for tile in range(lay.count_x)], axis=1)
        found = jnp.where(slab_row == (own_slot ^ turn), jnp.broadcast_to(line, codes.shape), found)
    codes[...] = found


def join_adjoint(lay, where_ref, *refs):
    pieces, (tie, state, send_next, send_twin, joined) = refs[: lay.count_x], refs[lay.count_x :]
    join_fields(lay, where_ref[0], where_ref[1], pieces, joined, state, None, send_next, send_twin)


def load_state(lay, odd, first, now, prev, state, from_next, from_twin):
    def put(buffer, layer, ref, source):
        for tile in range(lay.tiles):
            row = layer * lay.stride + (2 * tile + 1) * ROWS
            values = ref[source * lay.wide + tile * ROWS : source * lay.wide + (tile + 1) * ROWS, :]
            buffer[pl.ds(row if isinstance(row, int) else aligned(row), ROWS), :] = values

    ahead = lay.margin + lay.chunk
    for y in range(lay.chunk):
        put(now, lay.margin + y, state, y)
        put(now, odd * ahead + y, from_next, y)
        put(now, (1 - odd) * ahead + y, from_twin, y)
    if first:
        for y in range(lay.chunk):
            put(prev, lay.margin + y, state, lay.chunk + REACH + y)
        for y in range(lay.kept):
            put(prev, odd * ahead + (1 - odd) * REACH + y, from_next, lay.chunk + y)
            put(prev, (1 - odd) * ahead + odd * REACH + y, from_twin, lay.chunk + y)
        return
    for y in range(lay.near):
        put(prev, lay.margin - REACH + y, state, lay.chunk + y)
    for index, y in enumerate(lay.lacking):
        put(prev, odd * ahead + y, from_next, lay.chunk + index)
        put(prev, (1 - odd) * ahead + y, from_twin, lay.chunk + index)


def store_state(lay, now, prev, state, send):
    def put(refs, target, buffer, layer):
        for tile in range(lay.tiles):
            row = layer * lay.stride + (2 * tile + 1) * ROWS
            values = buffer[row : row + ROWS, :]
            for ref, place in refs:
                ref[place * lay.wide + tile * ROWS : place * lay.wide + (tile + 1) * ROWS, :] = values

    for y in range(lay.chunk):
        put([(state, y), (send, y)], y, now, lay.margin + y)
    for y in range(lay.near):
        refs = [(state, lay.chunk + y)]
        if y - REACH in lay.lacking:
            refs.append((send, lay.chunk + y - REACH - lay.lacking[0]))
        put(refs, y, prev, lay.margin - REACH + y)


def split(values):
    high = values.astype(jnp.bfloat16)
    rest = values - high.astype(jnp.float32)
    middle = rest.astype(jnp.bfloat16)
    low = (rest - middle.astype(jnp.float32)).astype(jnp.bfloat16)
    return high, middle, low


def fill_band(band):
    apart = lax.broadcasted_iota(jnp.int32, (LANES, LANES), 0) - lax.broadcasted_iota(
        jnp.int32, (LANES, LANES), 1
    )
    weights = jnp.where(apart == 0, 3.0 * stencil[0], 0.0).astype(jnp.float32)
    for k in range(1, REACH + 1):
        weights = jnp.where(jnp.abs(apart) == k, stencil[k], weights)
    high, middle, low = split(weights)
    for index, part in enumerate((high, high, high, middle, middle, low)):
        band[index * LANES : (index + 1) * LANES, :] = part


def sweep(lay, step, now, prev, following, half, gain, band, inject=None):
    first_layer = REACH * (step + 1)
    group = 8
    reach_rows = REACH * lay.stride

    def layers(block, carry):
        start = first_layer + group * block
        base = aligned((start - REACH) * lay.stride)
        around = now.at[pl.ds(base, (group + 2 * REACH) * lay.stride)]
        middle_rows = pl.ds(aligned(base + reach_rows), group * lay.stride)
        former_rows, target = prev.at[middle_rows], following.at[middle_rows]
        flat = aligned((start - REACH) * lay.wide)
        flat_rows = pl.ds(flat, group * lay.wide)
        half_rows, gain_rows = half.at[flat_rows], gain.at[flat_rows]
        added = None if inject is None else inject.at[step, flat_rows]

        def place(y, tile):
            return (y * lay.tiles + tile) * 2 * ROWS + ROWS

        def at(y, tile):
            row = place(y + REACH, tile)
            return around[row : row + ROWS, :]

        def beside(y, tile, shift):
            return now[pl.ds(base + (place(y + REACH, tile) + shift), ROWS), :]

        centers = [[at(y, tile) for tile in range(lay.tiles)] for y in range(group)]
        high, middle, low = split(jnp.concatenate([tile for layer in centers for tile in layer], axis=0))
        along_z = jnp.dot(
            jnp.concatenate([high, middle, low, high, middle, high], axis=1),
            band[...],
            preferred_element_type=jnp.float32,
        )
        for y in range(group):
            lower = [beside(y, tile, -1) for tile in range(lay.tiles)]
            upper = [beside(y, tile, 1) for tile in range(lay.tiles)]
            line = lower + centers[y] + upper
            for tile in range(lay.tiles):
                flat_at = (y * lay.tiles + tile) * ROWS
                total = along_z[flat_at : flat_at + ROWS, :]
                for k in range(1, REACH + 1):
                    pair = line[lay.tiles + tile - k] + line[lay.tiles + tile + k]
                    total = total + stencil[k] * (pair + (at(y - k, tile) + at(y + k, tile)))
                if added is not None:
                    total = total + added[pl.ds(y * lay.wide + tile, ROWS, stride=lay.tiles), :]
                row = place(y, tile)
                former = former_rows[row : row + ROWS, :]
                change = (centers[y][tile] - former) + half_rows[flat_at : flat_at + ROWS, :] * total
                target[row : row + ROWS, :] = former + gain_rows[flat_at : flat_at + ROWS, :] * change
        return carry

    lax.fori_loop(0, (lay.extent - 2 * first_layer) // group, layers, 0)


def zero_between(lay, step, buffer):
    zeros = jnp.zeros((ROWS, LANES), jnp.float32)
    first = REACH * (step + 1)
    for row in range(first * lay.stride, (lay.extent - first) * lay.stride + 1, 2 * ROWS):
        buffer[row : row + ROWS, :] = zeros


def zero_buffers(lay, now, prev, following):
    zero_between(lay, 0, now)
    zero_between(lay, 1, following)
    zero_between(lay, 2, prev)


def keep_own(lay, step, following, history):
    for y in range(lay.chunk):
        for tile in range(lay.tiles):
            row = (lay.margin + y) * lay.stride + (2 * tile + 1) * ROWS
            place = step * lay.rows + y * lay.wide + tile * ROWS
            history[place : place + ROWS, :] = following[row : row + ROWS, :]


def forward(lay, phase, sources, ints, state, from_next, from_twin, courant, gain, drive, *refs):
    first, last = phase == 0, phase == STEPS // DEPTH - 1
    refs = list(refs)
    history = refs.pop(0)
    half = refs.pop(0) if first else courant
    if not last:
        state_out, send, tie = [refs.pop(0) for _ in range(3)]
        tie[...] = jnp.zeros_like(tie)
    now, prev, following, band, pulse = refs
    odd = ints[0]

    fill_band(band)
    load_state(lay, odd, first, now, prev, state, from_next, from_twin)
    zero_buffers(lay, now, prev, following)
    if first:
        tail = (lay.chunk + lay.kept) * lay.wide
        part = lay.kept * lay.wide
        half[part : part + lay.rows, :] = 0.5 * courant[...]
        ahead = part + lay.rows
        half[pl.ds(aligned(odd * ahead), part), :] = 0.5 * from_next[tail : tail + part, :]
        half[pl.ds(aligned((1 - odd) * ahead), part), :] = 0.5 * from_twin[tail : tail + part, :]
    for source in range(sources):
        flat = pl.ds(ints[1 + sources + source], 1)
        pulse[source : source + 1, :] = half[flat, :] * gain[flat, :]

    for step in range(DEPTH):
        sweep(lay, step, now, prev, following, half, gain, band)
        added = pulse[...] * drive[phase * DEPTH + step]
        places = [pl.ds(ints[1 + source], 1) for source in range(sources)]
        lines = [following[place, :] for place in places]
        for source, (place, line) in enumerate(zip(places, lines)):
            following[place, :] = line + added[source : source + 1, :]
        keep_own(lay, step, following, history)
        now, prev, following = following, now, prev

    if not last:
        store_state(lay, now, prev, state_out, send)


def slot_rows(codes, slab):
    code = codes[slab : slab + 1, :].astype(jnp.int32)
    row = jnp.where(code >= 0, lax.shift_right_arithmetic(code, 7), -1)
    return row, jnp.where(code >= 0, code & (LANES - 1), -1)


def record_slots(lay, history, codes, plain, record):
    for step in range(DEPTH):
        for y in range(lay.chunk):
            for tile in range(lay.tiles):
                row = step * lay.rows + y * lay.wide
                values = history[row + tile * ROWS : row + (tile + 1) * ROWS, :]
                plain[pl.ds(row + tile, ROWS, stride=lay.tiles), :] = values
    slots = codes.shape[1]
    width = 2 * LANES
    for slab in range(lay.count_x):
        cell_row, cell_z = slot_rows(codes, slab)
        tiles = []
        for step in range(DEPTH):
            for y in range(lay.chunk):
                row = step * lay.rows + y * lay.wide + slab * ROWS
                tiles.append(plain[row : row + ROWS, :])
        parts = jnp.concatenate(split(jnp.concatenate(tiles, axis=0)), axis=1)
        for start in range(0, slots, width):
            here = slice(start, start + width)
            z = lax.broadcasted_iota(jnp.int32, (LANES, width), 0)
            pick = jnp.where(z == cell_z[:, here], 1.0, 0.0).astype(jnp.bfloat16)
            found = jnp.dot(parts, jnp.concatenate([pick] * 3, axis=0), preferred_element_type=jnp.float32)
            wanted = lax.broadcasted_iota(jnp.int32, (lay.cells, width), 0) == cell_row[:, here]
            for step in range(DEPTH):
                part = jnp.where(wanted, found[step * lay.cells : (step + 1) * lay.cells, :], 0.0)
                row = step * lay.count_x + slab
                record[row : row + 1, here] = jnp.sum(part, axis=0, keepdims=True)


def record_phase(lay, history, codes, record, plain):
    record_slots(lay, history, codes, plain, record)


def record_last(lay, phases, where_ref, history, codes, *refs):
    earlier, refs = refs[: phases - 1], refs[phases - 1 :]
    observed, (misfit, plain, record) = refs[: lay.count_x], refs[lay.count_x :]
    record_slots(lay, history, codes, plain, record)
    block = DEPTH * lay.count_x
    for index, part in enumerate(list(earlier) + [record]):
        misfit[index * block : (index + 1) * block, :] = part[...]
    total = STEPS * lay.count_x
    for slab in range(lay.count_x):
        misfit[total + slab : total + slab + 1, :] = codes[slab : slab + 1, :]
    for turn, piece in enumerate(observed):
        place = pl.ds(aligned((where_ref[0] ^ turn) * LANES, LANES), LANES)
        used = jnp.concatenate([codes[:, place]] * STEPS, axis=0) >= 0
        seen = piece[2 * lay.cells : 2 * lay.cells + total, :]
        misfit[0:total, place] = jnp.where(used, misfit[0:total, place] - seen, 0.0)


def spread(lay, phase, side, misfit, inject):
    codes = misfit[STEPS * lay.count_x : (STEPS + 1) * lay.count_x, :]
    for slab in range(lay.count_x):
        cell_row, cell_z = slot_rows(codes, slab)
        slots = cell_row.shape[1]
        z = lax.broadcasted_iota(jnp.int32, (LANES, slots), 0)
        pick = jnp.where(z == cell_z, 1.0, 0.0).astype(jnp.bfloat16)
        hit = lax.broadcasted_iota(jnp.int32, (lay.cells, slots), 0) == cell_row
        hit = jnp.where(hit, 1.0, 0.0).astype(jnp.bfloat16)
        left, spans = [], []
        for step in range(DEPTH):
            low, high = 0, lay.chunk
            if side < 0:
                low = REACH * (step + 1) - lay.margin + lay.chunk
            if side > 0:
                high = lay.margin - REACH * (step + 1)
            if low >= high:
                continue
            row = (STEPS - 1 - phase * DEPTH - step) * lay.count_x + slab
            parts = split(misfit[row : row + 1, :])
            left.append(jnp.concatenate([hit[low * ROWS : high * ROWS, :] * part for part in parts], axis=1))
            spans.append((step, low, high))
        placed = lax.dot_general(
            jnp.concatenate(left, axis=0),
            jnp.concatenate([pick] * 3, axis=1),
            (((1,), (1,)), ((), ())),
            preferred_element_type=jnp.float32,
        )
        at = 0
        for step, low, high in spans:
            for y in range(low, high):
                layer = lay.margin + side * lay.chunk + y - REACH
                target = layer * lay.wide + slab * ROWS
                inject[step, target : target + ROWS, :] = placed[at : at + ROWS, :]
                at += ROWS


def spread_own(lay, phase, misfit, inject):
    spread(lay, phase, 0, misfit, inject)


def spread_sides(lay, phase, where_ref, own, misfit_next, misfit_twin, inject):
    odd = where_ref[1]

    @pl.when(odd == 1)
    def ahead_is_next():
        spread(lay, phase, 1, misfit_next, inject)
        spread(lay, phase, -1, misfit_twin, inject)

    @pl.when(odd == 0)
    def behind_is_next():
        spread(lay, phase, -1, misfit_next, inject)
        spread(lay, phase, 1, misfit_twin, inject)


def backward(lay, phase, where_ref, state, from_next, from_twin, half, gain, inject, *refs):
    first, last = phase == 0, phase == STEPS // DEPTH - 1
    refs = list(refs)
    history = refs.pop(0)
    if not last:
        state_out, send = refs.pop(0), refs.pop(0)
    now, prev, following, band = refs

    fill_band(band)
    load_state(lay, where_ref[1], first, now, prev, state, from_next, from_twin)
    zero_buffers(lay, now, prev, following)
    for step in range(DEPTH):
        sweep(lay, step, now, prev, following, half, gain, band, inject)
        keep_own(lay, step, following, history)
        now, prev, following = following, now, prev
    if not last:
        store_state(lay, now, prev, state_out, send)


def add_gradient(lay, before, adjoint, history, state, gradient):
    def layer(y, carry):
        place = aligned(y * lay.wide)
        own = pl.ds(place, lay.wide)
        fields = [state[pl.ds(aligned(place + (lay.chunk + REACH) * lay.wide), lay.wide), :], state[own, :]]
        fields += [history[pl.ds(aligned(place + step * lay.rows), lay.wide), :] for step in range(DEPTH)]
        total = None if before is None else before[own, :]
        for step in range(DEPTH):
            index = DEPTH - 1 - step
            accel = (fields[index + 2] - fields[index + 1]) - (fields[index + 1] - fields[index])
            term = adjoint[pl.ds(aligned(place + step * lay.rows), lay.wide), :] * accel
            total = term if total is None else total + term
        gradient[own, :] = total
        return carry

    lax.fori_loop(0, lay.chunk, layer, 0)


def gradient_first(lay, adjoint, history, state, gradient):
    add_gradient(lay, None, adjoint, history, state, gradient)


def gradient_later(lay, adjoint, history, state, before, gradient):
    add_gradient(lay, before, adjoint, history, state, gradient)


def gradient_last(lay, where_ref, adjoint, history, state, before, misfit, *refs):
    sends, (gradient, plain) = refs[: lay.count_x], refs[lay.count_x :]
    add_gradient(lay, before, adjoint, history, state, gradient)
    for y in range(lay.chunk):
        for tile in range(lay.tiles):
            row = y * lay.wide + tile * ROWS
            plain[pl.ds(y * lay.wide + tile, ROWS, stride=lay.tiles), :] = gradient[row : row + ROWS, :]
    total = STEPS * lay.count_x
    for turn, send in enumerate(sends):
        other = where_ref[0] ^ turn
        for y in range(lay.chunk):
            source = pl.ds(aligned(y * lay.wide + other * ROWS), ROWS)
            send[y * ROWS : (y + 1) * ROWS, :] = plain[source, :]
        tile = pl.ds(aligned(other * LANES, LANES), LANES)
        send[lay.cells : lay.cells + total, :] = misfit[0:total, tile]


def finish(lay, slab_ref, *refs):
    pieces, (gradient, residual) = refs[: lay.count_x], refs[lay.count_x :]
    total = None
    for turn, piece in enumerate(pieces):
        start = (slab_ref[0] ^ turn) * lay.chunk
        for x in range(ROWS):
            target = pl.ds(aligned(x * lay.width_y + start), lay.chunk)
            gradient[target, :] = piece[pl.ds(x, lay.chunk, stride=ROWS), :]
        part = piece[lay.cells : lay.cells + residual.shape[0], :]
        total = part if total is None else total + part
    residual[...] = total


def gain_rows(lay, first_y):
    x = jnp.arange(ROWS)[None, :] * lay.tiles + jnp.arange(lay.tiles)[:, None]
    y = first_y + REACH + jnp.arange(lay.inner)

    def ramp(position, count):
        gap = jnp.minimum(position, count - 1 - position)
        profile = jnp.maximum(SPONGE - gap, 0).astype(jnp.float32) / SPONGE
        return profile * profile

    damping = damping_peak * (ramp(x, lay.wide)[None] + ramp(y, lay.whole_y)[:, None, None])
    gain = (2.0 / (1.0 + damping)).reshape(lay.inner * lay.wide, 1)
    return jnp.broadcast_to(gain, (lay.inner * lay.wide, LANES))


def source_rows(lay, first_y, source_cell, wavelet):
    x = source_cell // (lay.whole_y * LANES)
    y = source_cell // LANES % lay.whole_y - first_y
    z = source_cell % LANES
    inside = (y >= REACH) & (y < lay.extent - REACH)
    tile, row = x % lay.tiles, x // lay.tiles
    padded = jnp.where(inside, y * lay.stride + (2 * tile + 1) * ROWS + row, ROWS // 2)
    flat = jnp.where(inside, (y - REACH) * lay.wide + tile * ROWS + row, 0)
    same = (padded[:, None] == padded[None, :]) & inside[None, :]
    spot = (z[:, None] == jnp.arange(LANES)[None, :]).astype(jnp.float32)
    lines = jnp.where(same[None, :, :, None], wavelet[:, None, :, None] * spot[None, None], 0.0)
    return padded, flat, jnp.sum(lines, axis=2)


def local_tiles(
    lay,
    courant,
    state_prev,
    state_now,
    adjoint_now,
    adjoint_next,
    source_cell,
    wavelet,
    observed,
    receiver_cell,
    receiver_count,
):
    axes = ("gx", "gy")
    slab = lax.axis_index("gx")
    strip = lax.axis_index("gy")
    pair = strip // 2
    chip = jnp.where(pair % 2 == 0, slab, lay.count_x - 1 - slab)
    place = (pair * lay.count_x + chip) * 2 + strip % 2
    odd = strip % 2
    first_y = place * lay.chunk - lay.margin
    slab_int = slab.reshape(1).astype(jnp.int32)
    where = jnp.stack([place % lay.count_x, odd]).astype(jnp.int32)

    count = lay.count_x
    sources = source_cell.shape[0]
    slots = count * receiver_cell.shape[3]
    flat = lambda values: values.reshape(-1, LANES)
    part = functools.partial

    def swap(to_next, to_twin):
        return (
            lax.ppermute(to_next, axes, lay.swaps(1)),
            lax.ppermute(to_twin, axes, lay.swaps(0)),
        )

    def after(value, others):
        return lax.optimization_barrier((value, others))[0]

    padded, flat_row, drive = source_rows(lay, first_y, source_cell, wavelet)
    gain = gain_rows(lay, first_y)
    ints = jnp.concatenate([odd.reshape(1), padded, flat_row]).astype(jnp.int32)

    traces = flat(observed)
    forward_rows = 3 * lay.cells + -(-count // ROWS) * ROWS
    back_rows = 2 * lay.cells + traces.shape[0]
    cuts = call(
        part(cut_blocks, lay),
        (slab_int, receiver_count.reshape(-1)),
        [flat(field) for field in (state_now, state_prev, courant, adjoint_now, adjoint_next)]
        + [receiver_cell.reshape(count, LANES), traces],
        [f32(forward_rows, LANES)] * count + [f32(back_rows, LANES)] * count,
        [
            pltpu.VMEM((5, lay.width_x * lay.width_y, LANES), jnp.float32),
            pltpu.VMEM((count, LANES), jnp.int32),
            pltpu.VMEM(traces.shape, jnp.float32),
            pltpu.SemaphoreType.DMA((7,)),
        ],
        space=pltpu.HBM,
        limit=60 * 1024 * 1024,
    )
    cuts, back_cuts = cuts[:count], cuts[count:]
    pieces = [lax.ppermute(cut, axes, lay.to_chunks(turn)) for turn, cut in enumerate(cuts)]
    pieces, ints, gain, drive = lax.optimization_barrier((pieces, ints, gain, drive))
    kept_rows = lay.kept * lay.wide
    tie_shape = f32(ROWS, LANES)
    state, own_courant, to_next, to_twin, codes = call(
        part(join_forward, lay),
        (where,),
        pieces,
        [f32(lay.state_rows, LANES), f32(lay.rows, LANES)]
        + [f32(lay.rows + 2 * kept_rows, LANES)] * 2
        + [f32(count, slots)],
        [pltpu.VMEM((3, lay.rows, LANES), jnp.float32)],
    )
    from_next, from_twin = swap(to_next, to_twin)

    back_pieces = []

    def move_adjoint(turns, tie):
        for turn in turns:
            back_pieces.append(lax.ppermute(after(back_cuts[turn], tie), axes, lay.to_chunks(turn)))

    move_adjoint(range(count // 2), codes)

    phases = STEPS // DEPTH
    step_cost = 8_000_000
    side_cost = 4_000_000
    history_shape = f32(DEPTH * lay.rows, LANES)
    state_shapes = [f32(lay.state_rows, LANES), f32(lay.send_rows, LANES)]
    buffers = [pltpu.VMEM((lay.padded_rows, LANES), jnp.float32)] * 3
    buffers += [pltpu.VMEM((6 * LANES, LANES), jnp.bfloat16)]
    record_scratch = [pltpu.VMEM((DEPTH * lay.rows, LANES), jnp.float32)]
    record_shape = (DEPTH * count, slots)
    histories, states, records = [], [], []
    half = own_courant
    for phase in range(phases):
        first, last = phase == 0, phase == phases - 1
        outs = [history_shape]
        if first:
            outs.append(f32(lay.inner * lay.wide, LANES))
        if not last:
            outs += state_shapes + [tie_shape]
        results = list(
            call(
                part(forward, lay, phase, sources),
                (ints,),
                [state, from_next, from_twin, half, gain, drive],
                outs,
                buffers + [pltpu.VMEM((sources, LANES), jnp.float32)],
                cost=step_cost,
            )
        )
        histories.append(results.pop(0))
        states.append(state)
        if first:
            half = results.pop(0)
        if last:
            continue
        state, send, tie = results
        send = after(send, back_pieces[-(count // 2) :])
        from_next, from_twin = swap(send, send)
        if first:
            move_adjoint(range(count // 2, count), tie)
    back_state, to_next, to_twin = call(
        part(join_adjoint, lay),
        (where,),
        back_pieces + [tie],
        [f32(lay.state_rows, LANES)] + [f32(lay.rows + kept_rows, LANES)] * 2,
        [pltpu.VMEM((2, lay.rows, LANES), jnp.float32)],
    )
    for history in histories[:-1]:
        records += call(
            part(record_phase, lay),
            (),
            [history, codes],
            [f32(*record_shape)],
            record_scratch,
            cost=side_cost,
        )
    arrived = (from_next, from_twin, records)
    back_from_next, back_from_twin = swap(after(to_next, arrived), after(to_twin, arrived))
    (misfit,) = call(
        part(record_last, lay, phases),
        (where,),
        [histories[-1], codes] + records + back_pieces,
        [f32(-(-(STEPS + 1) * count // ROWS) * ROWS, slots)],
        record_scratch + [pltpu.VMEM(record_shape, jnp.float32)],
        cost=side_cost,
    )

    misfit = after(misfit, [back_from_next, back_from_twin])
    misfit_next, misfit_twin = swap(misfit, misfit)
    state, from_next, from_twin = back_state, back_from_next, back_from_twin
    gradient = None
    inject_shape = f32(DEPTH, lay.inner * lay.wide, LANES)
    for phase in range(phases):
        first, last = phase == 0, phase == phases - 1
        (inject,) = call(part(spread_own, lay, phase), (), [misfit], [inject_shape], cost=side_cost)
        (inject,) = call(
            part(spread_sides, lay, phase),
            (where,),
            [inject, misfit_next, misfit_twin],
            [inject_shape],
            cost=side_cost,
            aliases={1: 0},
        )
        results = call(
            part(backward, lay, phase),
            (where,),
            [state, from_next, from_twin, half, gain, inject],
            [history_shape] + ([] if last else state_shapes),
            buffers,
            cost=step_cost,
        )
        arrays = [results[0], histories[phases - 1 - phase], states[phases - 1 - phase]]
        if last:
            sends = call(
                part(gradient_last, lay),
                (where,),
                arrays + [gradient, misfit],
                [f32(lay.cells + traces.shape[0], LANES)] * count,
                [pltpu.VMEM((lay.rows, LANES), jnp.float32)] * 2,
            )
            continue
        _, state, send = results
        from_next, from_twin = swap(send, send)
        kernel = gradient_first if first else gradient_later
        (gradient,) = call(
            part(kernel, lay), (), arrays + ([] if first else [gradient]), [f32(lay.rows, LANES)], cost=side_cost
        )
    pieces = [lax.ppermute(send, axes, lay.to_slabs(turn)) for turn, send in enumerate(sends)]
    gradient, residual = call(
        part(finish, lay),
        (slab_int,),
        pieces,
        [f32(lay.width_x * lay.width_y, LANES), f32(*traces.shape)],
    )
    return gradient.reshape(courant.shape), residual.reshape(observed.shape)


def local(courant, *rest):
    width_x, width_y, depth_z = courant.shape
    count_x, count_y = lax.axis_size("gx"), lax.axis_size("gy")
    if fits(count_x, count_y, width_x, width_y, depth_z):
        return local_tiles(Layout(count_x, count_y, width_x, width_y), courant, *rest)
    return local_blocks(courant, *rest)


def padded_2(cells, sides, width):
    for axis, dim in sides:
        count = lax.axis_size(axis)
        ends = count - 1
        head = lax.slice_in_dim(cells, 0, width, axis=dim)
        tail = lax.slice_in_dim(cells, cells.shape[dim] - width, cells.shape[dim], axis=dim)
        cells = jnp.concatenate(
            [
                lax.ppermute(tail, axis, [(i, (i + 1) % count) for i in range(ends)]),
                cells,
                lax.ppermute(head, axis, [((i + 1) % count, i) for i in range(ends)]),
            ],
            axis=dim,
        )
    return cells


def laplace(values):
    width_x, width_y, depth_z = values.shape
    padded = padded_2(values, (("gx", 0), ("gy", 1)), 4)
    z_padded = jnp.pad(values, ((0, 0), (0, 0), (4, 4)))
    summed = 3.0 * stencil[0] * values
    for offset in range(1, 5):
        paired = (
            padded[4 + offset : 4 + offset + width_x, 4 : 4 + width_y]
            + padded[4 - offset : 4 - offset + width_x, 4 : 4 + width_y]
        )
        paired = (
            paired
            + padded[4 : 4 + width_x, 4 + offset : 4 + offset + width_y]
            + padded[4 : 4 + width_x, 4 - offset : 4 - offset + width_y]
        )
        paired = (
            paired
            + z_padded[:, :, 4 + offset : 4 + offset + depth_z]
            + z_padded[:, :, 4 - offset : 4 - offset + depth_z]
        )
        summed = summed + stencil[offset] * paired
    return summed


def sponge(start, count, whole):
    position = start + jnp.arange(count, dtype=jnp.int32)
    edge_gap = jnp.minimum(position, whole - 1 - position)
    profile = jnp.maximum(SPONGE - edge_gap, 0).astype(jnp.float32) / SPONGE
    return profile * profile


def place_sum(indices, amounts, shape):
    flat = jnp.zeros((shape[0] * shape[1] * shape[2],), jnp.float32).at[indices].add(amounts)
    return flat.reshape(shape)


def local_blocks(
    courant,
    state_prev,
    state_now,
    adjoint_now,
    adjoint_next,
    source_cell,
    wavelet,
    observed,
    receiver_cell,
    receiver_count,
):
    shape = courant.shape
    width_x, width_y, depth_z = shape
    slab = lax.axis_index("gx")
    strip = lax.axis_index("gy")
    whole_x = width_x * lax.axis_size("gx")
    whole_y = width_y * lax.axis_size("gy")
    damping = damping_peak * (
        sponge(slab * width_x, width_x, whole_x)[:, None, None]
        + sponge(strip * width_y, width_y, whole_y)[None, :, None]
    )
    source_x = source_cell // (whole_y * depth_z) - slab * width_x
    source_y = source_cell // depth_z % whole_y - strip * width_y
    source_z = source_cell % depth_z
    inside = (source_x >= 0) & (source_x < width_x) & (source_y >= 0) & (source_y < width_y)
    source_flat = jnp.where(inside, (source_x * width_y + source_y) * depth_z + source_z, 0)
    source_weight = wavelet * inside.astype(jnp.float32)[None, :]
    senders = receiver_cell.shape[2]
    slots = receiver_cell.shape[3]
    cells = receiver_cell.reshape(-1)
    active = (
        jnp.arange(slots, dtype=jnp.int32)[None, :] < receiver_count.reshape(senders, 1)
    ).astype(jnp.float32)
    active_flat = active.reshape(-1)

    def advance(carry, weights):
        former, current = carry
        drive = laplace(current) + place_sum(source_flat, weights, shape)
        following = (2.0 * current - (1.0 - damping) * former + courant * drive) / (1.0 + damping)
        return (
            (current, following),
            (following - 2.0 * current + former, following.reshape(-1)[cells] * active_flat),
        )

    final_states, (accels, recorded) = lax.scan(advance, (state_prev, state_now), source_weight)
    recorded_tiles = recorded.reshape(STEPS, senders, 1, 1, slots)
    active_tiles = active.reshape(1, senders, 1, 1, slots)
    synthetic, mask_back = (
        lax.all_to_all(recorded_tiles, "gx", split_axis=1, concat_axis=3, tiled=True),
        lax.all_to_all(active_tiles, "gx", split_axis=1, concat_axis=3, tiled=True),
    )
    trace_residual = mask_back * (synthetic - observed)
    misfit = lax.all_to_all(trace_residual, "gx", split_axis=3, concat_axis=1, tiled=True)
    misfit_rows = misfit.reshape(STEPS, senders * slots)

    def retreat(carry, inputs):
        later, current, gradient = carry
        acceleration, residual_row = inputs
        drive = laplace(current) + place_sum(cells, residual_row, shape)
        earlier = (2.0 * current - (1.0 - damping) * later + courant * drive) / (1.0 + damping)
        return ((current, earlier, gradient + earlier * acceleration), None)

    start_gradient = jnp.zeros(shape, jnp.float32)
    (last_later, last_current, gradient), unused = lax.scan(
        retreat, (adjoint_next, adjoint_now, start_gradient), (accels, misfit_rows), reverse=True
    )
    return (gradient, trace_residual)


def solution(mesh):
    placed = (
        P("gx", "gy", None),
        P(("groups", "gx"), "gy", None),
        P(("groups", "gx"), "gy", None),
        P(("groups", "gx"), "gy", None),
        P(("groups", "gx"), "gy", None),
        P("groups"),
        P(None, "groups"),
        P("groups", "gx", "gy", None, None),
        P("gx", "gy", None, None),
        P("gx", "gy", None),
    )
    return jax.shard_map(
        local,
        mesh=mesh,
        in_specs=placed,
        out_specs=(P(("groups", "gx"), "gy", None), P("groups", "gx", "gy", None, None)),
        check_vma=False,
    )
```

```python
import functools

import jax
import jax.numpy as jnp
from jax import lax
from jax.experimental import pallas as pl
from jax.experimental.pallas import tpu as pltpu
from jax.sharding import PartitionSpec as P

STEPS = 12
SPONGE = 8
REACH = 4
DEPTH = 4
LANES = 128
ROWS = 8


stencil = (-205.0 / 72.0, 8.0 / 5.0, -1.0 / 5.0, 8.0 / 315.0, -1.0 / 560.0)
damping_peak = 0.3
scale = 5040.0
weights = (3.0 * -14350.0, 8064.0, -1008.0, 128.0, -9.0)


class Layout:
    def __init__(self, count_x, count_y, width_x, width_y):
        self.count_x, self.count_y = count_x, count_y
        self.width_x, self.width_y = width_x, width_y
        self.chunk = width_y // count_x
        self.wide = width_x * count_x
        self.tiles = self.wide // ROWS
        self.whole_y = width_y * count_y
        self.margin = REACH * DEPTH
        self.extent = self.chunk + 2 * self.margin
        self.stride = self.tiles * 2 * ROWS
        self.padded_rows = self.extent * self.stride + ROWS
        self.kept = self.margin - REACH
        self.inner = self.extent - 2 * REACH
        self.rows = self.chunk * self.wide
        self.cells = self.chunk * width_x
        self.near = self.chunk + 2 * REACH
        self.state_rows = (self.chunk + self.near) * self.wide
        self.lacking = range(REACH, self.chunk - REACH)
        self.send_rows = (self.chunk + len(self.lacking)) * self.wide

    def at(self, place):
        pair, rest = divmod(place, 2 * self.count_x)
        chip, core = divmod(rest, 2)
        slab = chip if pair % 2 == 0 else self.count_x - 1 - chip
        return slab * self.count_y + 2 * pair + core

    def to_chunks(self, turn):
        moves = []
        for slab in range(self.count_x):
            for strip in range(self.count_y):
                moves.append((slab * self.count_y + strip, self.at(strip * self.count_x + (slab ^ turn))))
        return moves

    def to_slabs(self, turn):
        return [(target, source) for source, target in self.to_chunks(turn)]

    def swaps(self, first):
        moves = []
        for place in range(first, self.count_x * self.count_y - 1, 2):
            moves += [(self.at(place), self.at(place + 1)), (self.at(place + 1), self.at(place))]
        return moves


def fits(count_x, count_y, width_x, width_y, depth_z):
    return (
        count_x & (count_x - 1) == 0
        and count_y % 2 == 0
        and width_x == ROWS
        and width_x * count_x == ROWS * REACH
        and depth_z == LANES
        and width_y == count_x * REACH * DEPTH
    )


def f32(*shape):
    return jax.ShapeDtypeStruct(shape, jnp.float32)


def call(
    kernel, ints, arrays, outs, scratch=(), cost=1_000_000, space=pltpu.VMEM, aliases=None, limit=32 * 1024 * 1024
):
    return pl.pallas_call(
        kernel,
        out_shape=tuple(outs),
        in_specs=[pl.BlockSpec(memory_space=pltpu.SMEM)] * len(ints)
        + [pl.BlockSpec(memory_space=space)] * len(arrays),
        out_specs=tuple(pl.BlockSpec(memory_space=pltpu.VMEM) for _ in outs),
        scratch_shapes=list(scratch),
        input_output_aliases=aliases or {},
        compiler_params=pltpu.CompilerParams(vmem_limit_bytes=limit),
        cost_estimate=pl.CostEstimate(flops=cost, bytes_accessed=cost, transcendentals=0),
    )(*ints, *arrays)


def aligned(value, to=ROWS):
    return pl.multiple_of(value, to)


def cut_chunk(lay, slab, turn, fields, target):
    start = (slab ^ turn) * lay.chunk
    for index, field in enumerate(fields):
        for y in range(lay.chunk):
            row = (index * lay.chunk + y) * ROWS
            target[row : row + ROWS, :] = field[pl.ds(start + y, ROWS, stride=lay.width_y), :]


def cut_forward(lay, slab_ref, count_ref, *refs):
    inputs, sends, (held, held_cell, done) = refs[:4], refs[4 : 4 + lay.count_x], refs[4 + lay.count_x :]
    fields = [held.at[index] for index in range(3)]
    copies = [
        pltpu.make_async_copy(source, target, done.at[index])
        for index, (source, target) in enumerate(zip(inputs, fields + [held_cell]))
    ]
    for copy in copies:
        copy.start()
    for copy in copies:
        copy.wait()
    slots = lax.broadcasted_iota(jnp.int32, (1, LANES), 1)
    used = []
    for tile in range(lay.count_x):
        cell = jnp.where(slots < count_ref[tile], held_cell[tile : tile + 1, :], -1)
        used.append(cell.astype(jnp.float32))
    for turn, send in enumerate(sends):
        cut_chunk(lay, slab_ref[0], turn, fields, send)
        for tile in range(lay.count_x):
            row = 3 * lay.cells + tile
            send[row : row + 1, :] = used[tile]


def cut_adjoint(lay, slab_ref, now, prev, observed, *sends):
    for turn, send in enumerate(sends):
        cut_chunk(lay, slab_ref[0], turn, (now, prev), send)
        row = 2 * lay.cells
        send[row : row + observed.shape[0], :] = observed[...]


def join_fields(lay, own_slot, odd, pieces, joined, state, courant, send_next, send_twin):
    fields = joined.shape[0]
    for turn, piece in enumerate(pieces):
        start_x = (own_slot ^ turn) * ROWS
        for field in range(fields):
            for y in range(lay.chunk):
                row = (field * lay.chunk + y) * ROWS
                joined[field, pl.ds(aligned(y * lay.wide + start_x), ROWS), :] = piece[row : row + ROWS, :]
    kept_rows = lay.kept * lay.wide
    for field in range(fields):
        target, first = (state, 0) if field == 0 else (state, (lay.chunk + REACH) * lay.wide)
        if field == 2:
            target, first = courant, 0
        for y in range(lay.chunk):
            for tile in range(lay.tiles):
                values = joined[field, pl.ds(y * lay.wide + tile, ROWS, stride=lay.tiles), :]
                row = y * lay.wide + tile * ROWS
                target[first + row : first + row + ROWS, :] = values
                if field == 0:
                    send_next[row : row + ROWS, :] = values
                    send_twin[row : row + ROWS, :] = values
    for field in range(1, fields):
        source, first = (state, (lay.chunk + REACH) * lay.wide) if field == 1 else (courant, 0)
        place = lay.rows + (field - 1) * kept_rows
        skipped = (lay.chunk - lay.kept) * lay.wide
        ahead = source[pl.ds(aligned(first + odd * skipped), kept_rows), :]
        send_next[place : place + kept_rows, :] = ahead
        behind = source[pl.ds(aligned(first + (1 - odd) * skipped), kept_rows), :]
        send_twin[place : place + kept_rows, :] = behind


def join_forward(lay, where_ref, *refs):
    pieces, (state, courant, send_next, send_twin, codes, joined) = refs[: lay.count_x], refs[lay.count_x :]
    own_slot = where_ref[0]
    join_fields(lay, own_slot, where_ref[1], pieces, joined, state, courant, send_next, send_twin)
    first = 3 * lay.cells
    strip_cells = lay.width_y * LANES
    slab_row = lax.broadcasted_iota(jnp.int32, codes.shape, 0)
    found = jnp.full(codes.shape, -1.0, jnp.float32)
    for turn, piece in enumerate(pieces):
        cell = piece[first : first + lay.count_x, :].astype(jnp.int32)
        used = cell >= 0
        cell = jnp.maximum(cell, 0)
        x = lax.div(cell, jnp.int32(strip_cells))
        y = lax.rem(lax.div(cell, jnp.int32(LANES)), jnp.int32(lay.width_y)) - own_slot * lay.chunk
        inside = used & (y >= 0) & (y < lay.chunk)
        code = jnp.where(inside, (y * ROWS + x) * LANES + lax.rem(cell, jnp.int32(LANES)), -1)
        code = code.astype(jnp.float32)
        line = jnp.concatenate([code[tile : tile + 1, :] for tile in range(lay.count_x)], axis=1)
        found = jnp.where(slab_row == (own_slot ^ turn), jnp.broadcast_to(line, codes.shape), found)
    codes[...] = found


def join_adjoint(lay, where_ref, *refs):
    pieces, (state, send_next, send_twin, joined) = refs[: lay.count_x], refs[lay.count_x :]
    join_fields(lay, where_ref[0], where_ref[1], pieces, joined, state, None, send_next, send_twin)


def load_state(lay, odd, first, now, prev, state, from_next, from_twin):
    def put(buffer, layer, ref, source):
        for tile in range(lay.tiles):
            row = layer * lay.stride + (2 * tile + 1) * ROWS
            values = ref[source * lay.wide + tile * ROWS : source * lay.wide + (tile + 1) * ROWS, :]
            buffer[pl.ds(row if isinstance(row, int) else aligned(row), ROWS), :] = values

    ahead = lay.margin + lay.chunk
    for y in range(lay.chunk):
        put(now, lay.margin + y, state, y)
        put(now, odd * ahead + y, from_next, y)
        put(now, (1 - odd) * ahead + y, from_twin, y)
    if first:
        for y in range(lay.chunk):
            put(prev, lay.margin + y, state, lay.chunk + REACH + y)
        for y in range(lay.kept):
            put(prev, odd * ahead + (1 - odd) * REACH + y, from_next, lay.chunk + y)
            put(prev, (1 - odd) * ahead + odd * REACH + y, from_twin, lay.chunk + y)
        return
    for y in range(lay.near):
        put(prev, lay.margin - REACH + y, state, lay.chunk + y)
    for index, y in enumerate(lay.lacking):
        put(prev, odd * ahead + y, from_next, lay.chunk + index)
        put(prev, (1 - odd) * ahead + y, from_twin, lay.chunk + index)


def store_state(lay, now, prev, state, send):
    def put(refs, target, buffer, layer):
        for tile in range(lay.tiles):
            row = layer * lay.stride + (2 * tile + 1) * ROWS
            values = buffer[row : row + ROWS, :]
            for ref, place in refs:
                ref[place * lay.wide + tile * ROWS : place * lay.wide + (tile + 1) * ROWS, :] = values

    for y in range(lay.chunk):
        put([(state, y), (send, y)], y, now, lay.margin + y)
    for y in range(lay.near):
        refs = [(state, lay.chunk + y)]
        if y - REACH in lay.lacking:
            refs.append((send, lay.chunk + y - REACH - lay.lacking[0]))
        put(refs, y, prev, lay.margin - REACH + y)


def split(values):
    high = values.astype(jnp.bfloat16)
    rest = values - high.astype(jnp.float32)
    middle = rest.astype(jnp.bfloat16)
    low = (rest - middle.astype(jnp.float32)).astype(jnp.bfloat16)
    return high, middle, low


def fill_band(band):
    row = lax.broadcasted_iota(jnp.int32, (2 * LANES, 2 * LANES), 0)
    column = lax.broadcasted_iota(jnp.int32, (2 * LANES, 2 * LANES), 1)
    apart = jnp.where((row < LANES) == (column < LANES), jnp.abs(row - column), 0)
    values = jnp.zeros((2 * LANES, 2 * LANES), jnp.float32)
    for k in range(1, REACH + 1):
        values = jnp.where(apart == k, weights[k], values)
    values = values.astype(jnp.bfloat16)
    for part in range(3):
        band[part * 2 * LANES : (part + 1) * 2 * LANES, :] = values


def multiply_z(lay, first_layer, count, now, band, along_z):
    tiles = []
    for y in range(count):
        for tile in range(lay.tiles):
            row = (first_layer + y) * lay.stride + (2 * tile + 1) * ROWS
            tiles.append(now[row : row + ROWS, :])
    half = len(tiles) // 2
    parts = [split(jnp.concatenate(group, axis=0)) for group in (tiles[:half], tiles[half:])]
    both = [side[part] for part in range(3) for side in parts]
    found = jnp.dot(jnp.concatenate(both, axis=1), band[...], preferred_element_type=jnp.float32)
    along_z[0 : half * ROWS, :] = found[:, :LANES]
    along_z[half * ROWS : 2 * half * ROWS, :] = found[:, LANES:]


def sweep(lay, step, now, prev, following, half, gain, band, along_z, inject=None):
    first_layer = REACH * (step + 1)
    group = 8
    reach_rows = REACH * lay.stride
    multiply_z(lay, first_layer, lay.extent - 2 * first_layer, now, band, along_z)

    def layers(block, carry):
        start = first_layer + group * block
        base = aligned((start - REACH) * lay.stride)
        around = now.at[pl.ds(base, (group + 2 * REACH) * lay.stride)]
        middle_rows = pl.ds(aligned(base + reach_rows), group * lay.stride)
        former_rows, target = prev.at[middle_rows], following.at[middle_rows]
        flat = aligned((start - REACH) * lay.wide)
        flat_rows = pl.ds(flat, group * lay.wide)
        half_rows, gain_rows = half.at[flat_rows], gain.at[flat_rows]
        added = None if inject is None else inject.at[step, flat_rows]

        def place(y, tile):
            return (y * lay.tiles + tile) * 2 * ROWS + ROWS

        def at(y, tile):
            row = place(y + REACH, tile)
            return around[row : row + ROWS, :]

        def beside(y, tile, shift):
            return now[pl.ds(base + (place(y + REACH, tile) + shift), ROWS), :]

        z_rows = along_z.at[pl.ds(aligned(block * group * lay.wide), group * lay.wide)]
        for y in range(group):
            center = [at(y, tile) for tile in range(lay.tiles)]
            lower = [beside(y, tile, -1) for tile in range(lay.tiles)]
            upper = [beside(y, tile, 1) for tile in range(lay.tiles)]
            line = lower + center + upper
            for tile in range(lay.tiles):
                flat_at = (y * lay.tiles + tile) * ROWS
                total = z_rows[flat_at : flat_at + ROWS, :] + weights[0] * center[tile]
                for k in range(1, REACH + 1):
                    pair = line[lay.tiles + tile - k] + line[lay.tiles + tile + k]
                    total = total + weights[k] * (pair + (at(y - k, tile) + at(y + k, tile)))
                if added is not None:
                    total = total + added[pl.ds(y * lay.wide + tile, ROWS, stride=lay.tiles), :]
                row = place(y, tile)
                former = former_rows[row : row + ROWS, :]
                change = (center[tile] - former) + half_rows[flat_at : flat_at + ROWS, :] * total
                target[row : row + ROWS, :] = former + gain_rows[flat_at : flat_at + ROWS, :] * change
        return carry

    lax.fori_loop(0, (lay.extent - 2 * first_layer) // group, layers, 0)


def zero_between(lay, step, buffer):
    zeros = jnp.zeros((ROWS, LANES), jnp.float32)
    first = REACH * (step + 1)
    for row in range(first * lay.stride, (lay.extent - first) * lay.stride + 1, 2 * ROWS):
        buffer[row : row + ROWS, :] = zeros


def zero_buffers(lay, now, prev, following):
    zero_between(lay, 0, now)
    zero_between(lay, 1, following)
    zero_between(lay, 2, prev)


def keep_own(lay, step, following, history):
    for y in range(lay.chunk):
        for tile in range(lay.tiles):
            row = (lay.margin + y) * lay.stride + (2 * tile + 1) * ROWS
            place = step * lay.rows + y * lay.wide + tile * ROWS
            history[place : place + ROWS, :] = following[row : row + ROWS, :]


def forward(lay, phase, sources, ints, state, from_next, from_twin, courant, gain, drive, *refs):
    first, last = phase == 0, phase == STEPS // DEPTH - 1
    refs = list(refs)
    history = refs.pop(0)
    half = refs.pop(0) if first else courant
    if not last:
        state_out, send, tie = [refs.pop(0) for _ in range(3)]
        tie[...] = jnp.zeros_like(tie)
    now, prev, following, band, along_z, pulse = refs
    odd = ints[0]

    fill_band(band)
    load_state(lay, odd, first, now, prev, state, from_next, from_twin)
    zero_buffers(lay, now, prev, following)
    if first:
        tail = (lay.chunk + lay.kept) * lay.wide
        part = lay.kept * lay.wide
        half[part : part + lay.rows, :] = (0.5 / scale) * courant[...]
        ahead = part + lay.rows
        half[pl.ds(aligned(odd * ahead), part), :] = (0.5 / scale) * from_next[tail : tail + part, :]
        half[pl.ds(aligned((1 - odd) * ahead), part), :] = (0.5 / scale) * from_twin[tail : tail + part, :]
    for source in range(sources):
        flat = pl.ds(ints[1 + sources + source], 1)
        pulse[source : source + 1, :] = scale * (half[flat, :] * gain[flat, :])

    for step in range(DEPTH):
        sweep(lay, step, now, prev, following, half, gain, band, along_z)
        added = pulse[...] * drive[phase * DEPTH + step]
        places = [pl.ds(ints[1 + source], 1) for source in range(sources)]
        lines = [following[place, :] for place in places]
        for source, (place, line) in enumerate(zip(places, lines)):
            following[place, :] = line + added[source : source + 1, :]
        keep_own(lay, step, following, history)
        now, prev, following = following, now, prev

    if not last:
        store_state(lay, now, prev, state_out, send)


def slot_rows(codes, slab):
    code = codes[slab : slab + 1, :].astype(jnp.int32)
    row = jnp.where(code >= 0, lax.shift_right_arithmetic(code, 7), -1)
    return row, jnp.where(code >= 0, code & (LANES - 1), -1)


def record_slots(lay, history, codes, plain, record):
    for step in range(DEPTH):
        for y in range(lay.chunk):
            for tile in range(lay.tiles):
                row = step * lay.rows + y * lay.wide
                values = history[row + tile * ROWS : row + (tile + 1) * ROWS, :]
                plain[pl.ds(row + tile, ROWS, stride=lay.tiles), :] = values
    slots = codes.shape[1]
    width = 2 * LANES
    for slab in range(lay.count_x):
        cell_row, cell_z = slot_rows(codes, slab)
        tiles = []
        for step in range(DEPTH):
            for y in range(lay.chunk):
                row = step * lay.rows + y * lay.wide + slab * ROWS
                tiles.append(plain[row : row + ROWS, :])
        parts = jnp.concatenate(split(jnp.concatenate(tiles, axis=0)), axis=1)
        for start in range(0, slots, width):
            here = slice(start, start + width)
            z = lax.broadcasted_iota(jnp.int32, (LANES, width), 0)
            pick = jnp.where(z == cell_z[:, here], 1.0, 0.0).astype(jnp.bfloat16)
            found = jnp.dot(parts, jnp.concatenate([pick] * 3, axis=0), preferred_element_type=jnp.float32)
            wanted = lax.broadcasted_iota(jnp.int32, (lay.cells, width), 0) == cell_row[:, here]
            for step in range(DEPTH):
                part = jnp.where(wanted, found[step * lay.cells : (step + 1) * lay.cells, :], 0.0)
                row = step * lay.count_x + slab
                record[row : row + 1, here] = jnp.sum(part, axis=0, keepdims=True)


def record_phase(lay, history, codes, record, plain):
    record_slots(lay, history, codes, plain, record)


def record_last(lay, phases, where_ref, history, codes, *refs):
    earlier, refs = refs[: phases - 1], refs[phases - 1 :]
    observed, (misfit, plain, record) = refs[: lay.count_x], refs[lay.count_x :]
    record_slots(lay, history, codes, plain, record)
    block = DEPTH * lay.count_x
    for index, part in enumerate(list(earlier) + [record]):
        misfit[index * block : (index + 1) * block, :] = part[...]
    total = STEPS * lay.count_x
    for slab in range(lay.count_x):
        misfit[total + slab : total + slab + 1, :] = codes[slab : slab + 1, :]
    for turn, piece in enumerate(observed):
        place = pl.ds(aligned((where_ref[0] ^ turn) * LANES, LANES), LANES)
        used = jnp.concatenate([codes[:, place]] * STEPS, axis=0) >= 0
        seen = piece[2 * lay.cells : 2 * lay.cells + total, :]
        misfit[0:total, place] = jnp.where(used, misfit[0:total, place] - seen, 0.0)


def spread(lay, phase, side, misfit, inject):
    codes = misfit[STEPS * lay.count_x : (STEPS + 1) * lay.count_x, :]
    for slab in range(lay.count_x):
        cell_row, cell_z = slot_rows(codes, slab)
        slots = cell_row.shape[1]
        z = lax.broadcasted_iota(jnp.int32, (LANES, slots), 0)
        pick = jnp.where(z == cell_z, 1.0, 0.0).astype(jnp.bfloat16)
        hit = lax.broadcasted_iota(jnp.int32, (lay.cells, slots), 0) == cell_row
        hit = jnp.where(hit, 1.0, 0.0).astype(jnp.bfloat16)
        left, spans = [], []
        for step in range(DEPTH):
            low, high = 0, lay.chunk
            if side < 0:
                low = REACH * (step + 1) - lay.margin + lay.chunk
            if side > 0:
                high = lay.margin - REACH * (step + 1)
            if low >= high:
                continue
            row = (STEPS - 1 - phase * DEPTH - step) * lay.count_x + slab
            parts = split(scale * misfit[row : row + 1, :])
            left += [hit[low * ROWS : high * ROWS, :] * part for part in parts]
            spans.append((step, low, high))
        placed = lax.dot_general(
            jnp.concatenate(left, axis=0),
            pick,
            (((1,), (1,)), ((), ())),
            preferred_element_type=jnp.float32,
        )
        at = 0
        for step, low, high in spans:
            rows = (high - low) * ROWS
            total = placed[at : at + rows, :]
            for part in (1, 2):
                total = total + placed[at + part * rows : at + (part + 1) * rows, :]
            for y in range(low, high):
                layer = lay.margin + side * lay.chunk + y - REACH
                target = layer * lay.wide + slab * ROWS
                inject[step, target : target + ROWS, :] = total[(y - low) * ROWS : (y - low + 1) * ROWS, :]
            at += 3 * rows


def spread_own(lay, phase, misfit, inject):
    spread(lay, phase, 0, misfit, inject)


def spread_sides(lay, phase, where_ref, own, misfit_next, misfit_twin, inject):
    odd = where_ref[1]

    @pl.when(odd == 1)
    def ahead_is_next():
        spread(lay, phase, 1, misfit_next, inject)
        spread(lay, phase, -1, misfit_twin, inject)

    @pl.when(odd == 0)
    def behind_is_next():
        spread(lay, phase, -1, misfit_next, inject)
        spread(lay, phase, 1, misfit_twin, inject)


def backward(lay, phase, where_ref, state, from_next, from_twin, half, gain, inject, *refs):
    first, last = phase == 0, phase == STEPS // DEPTH - 1
    refs = list(refs)
    history = refs.pop(0)
    if not last:
        state_out, send = refs.pop(0), refs.pop(0)
    now, prev, following, band, along_z = refs

    fill_band(band)
    load_state(lay, where_ref[1], first, now, prev, state, from_next, from_twin)
    zero_buffers(lay, now, prev, following)
    for step in range(DEPTH):
        sweep(lay, step, now, prev, following, half, gain, band, along_z, inject)
        keep_own(lay, step, following, history)
        now, prev, following = following, now, prev
    if not last:
        store_state(lay, now, prev, state_out, send)


def add_gradient(lay, before, adjoint, history, state, gradient):
    def layer(y, carry):
        place = aligned(y * lay.wide)
        own = pl.ds(place, lay.wide)
        fields = [state[pl.ds(aligned(place + (lay.chunk + REACH) * lay.wide), lay.wide), :], state[own, :]]
        fields += [history[pl.ds(aligned(place + step * lay.rows), lay.wide), :] for step in range(DEPTH)]
        total = None if before is None else before[own, :]
        for step in range(DEPTH):
            index = DEPTH - 1 - step
            accel = (fields[index + 2] - fields[index + 1]) - (fields[index + 1] - fields[index])
            term = adjoint[pl.ds(aligned(place + step * lay.rows), lay.wide), :] * accel
            total = term if total is None else total + term
        gradient[own, :] = total
        return carry

    lax.fori_loop(0, lay.chunk, layer, 0)


def gradient_first(lay, adjoint, history, state, gradient):
    add_gradient(lay, None, adjoint, history, state, gradient)


def gradient_later(lay, adjoint, history, state, before, gradient):
    add_gradient(lay, before, adjoint, history, state, gradient)


def gradient_last(lay, where_ref, adjoint, history, state, before, misfit, *refs):
    sends, (gradient, plain) = refs[: lay.count_x], refs[lay.count_x :]
    add_gradient(lay, before, adjoint, history, state, gradient)
    for y in range(lay.chunk):
        for tile in range(lay.tiles):
            row = y * lay.wide + tile * ROWS
            plain[pl.ds(y * lay.wide + tile, ROWS, stride=lay.tiles), :] = gradient[row : row + ROWS, :]
    total = STEPS * lay.count_x
    for turn, send in enumerate(sends):
        other = where_ref[0] ^ turn
        for y in range(lay.chunk):
            source = pl.ds(aligned(y * lay.wide + other * ROWS), ROWS)
            send[y * ROWS : (y + 1) * ROWS, :] = plain[source, :]
        tile = pl.ds(aligned(other * LANES, LANES), LANES)
        send[lay.cells : lay.cells + total, :] = misfit[0:total, tile]


def finish(lay, slab_ref, *refs):
    pieces, (gradient, residual) = refs[: lay.count_x], refs[lay.count_x :]
    total = None
    for turn, piece in enumerate(pieces):
        start = (slab_ref[0] ^ turn) * lay.chunk
        for x in range(ROWS):
            target = pl.ds(aligned(x * lay.width_y + start), lay.chunk)
            gradient[target, :] = piece[pl.ds(x, lay.chunk, stride=ROWS), :]
        part = piece[lay.cells : lay.cells + residual.shape[0], :]
        total = part if total is None else total + part
    residual[...] = total


def gain_rows(lay, first_y):
    x = jnp.arange(ROWS)[None, :] * lay.tiles + jnp.arange(lay.tiles)[:, None]
    y = first_y + REACH + jnp.arange(lay.inner)

    def ramp(position, count):
        gap = jnp.minimum(position, count - 1 - position)
        profile = jnp.maximum(SPONGE - gap, 0).astype(jnp.float32) / SPONGE
        return profile * profile

    damping = damping_peak * (ramp(x, lay.wide)[None] + ramp(y, lay.whole_y)[:, None, None])
    gain = (2.0 / (1.0 + damping)).reshape(lay.inner * lay.wide, 1)
    return jnp.broadcast_to(gain, (lay.inner * lay.wide, LANES))


def source_rows(lay, first_y, source_cell, wavelet):
    x = source_cell // (lay.whole_y * LANES)
    y = source_cell // LANES % lay.whole_y - first_y
    z = source_cell % LANES
    inside = (y >= REACH) & (y < lay.extent - REACH)
    tile, row = x % lay.tiles, x // lay.tiles
    padded = jnp.where(inside, y * lay.stride + (2 * tile + 1) * ROWS + row, ROWS // 2)
    flat = jnp.where(inside, (y - REACH) * lay.wide + tile * ROWS + row, 0)
    same = (padded[:, None] == padded[None, :]) & inside[None, :]
    spot = (z[:, None] == jnp.arange(LANES)[None, :]).astype(jnp.float32)
    lines = jnp.where(same[None, :, :, None], wavelet[:, None, :, None] * spot[None, None], 0.0)
    return padded, flat, jnp.sum(lines, axis=2)


def local_tiles(
    lay,
    courant,
    state_prev,
    state_now,
    adjoint_now,
    adjoint_next,
    source_cell,
    wavelet,
    observed,
    receiver_cell,
    receiver_count,
):
    axes = ("gx", "gy")
    slab = lax.axis_index("gx")
    strip = lax.axis_index("gy")
    pair = strip // 2
    chip = jnp.where(pair % 2 == 0, slab, lay.count_x - 1 - slab)
    place = (pair * lay.count_x + chip) * 2 + strip % 2
    odd = strip % 2
    first_y = place * lay.chunk - lay.margin
    slab_int = slab.reshape(1).astype(jnp.int32)
    where = jnp.stack([place % lay.count_x, odd]).astype(jnp.int32)

    count = lay.count_x
    sources = source_cell.shape[0]
    slots = count * receiver_cell.shape[3]
    flat = lambda values: values.reshape(-1, LANES)
    part = functools.partial

    def swap(to_next, to_twin):
        return (
            lax.ppermute(to_next, axes, lay.swaps(1)),
            lax.ppermute(to_twin, axes, lay.swaps(0)),
        )

    def after(value, others):
        return lax.optimization_barrier((value, others))[0]

    padded, flat_row, drive = source_rows(lay, first_y, source_cell, wavelet)
    gain = gain_rows(lay, first_y)
    ints = jnp.concatenate([odd.reshape(1), padded, flat_row]).astype(jnp.int32)

    traces = flat(observed)
    forward_rows = 3 * lay.cells + -(-count // ROWS) * ROWS
    back_rows = 2 * lay.cells + traces.shape[0]
    cuts = call(
        part(cut_forward, lay),
        (slab_int, receiver_count.reshape(-1)),
        [flat(field) for field in (state_now, state_prev, courant)] + [receiver_cell.reshape(count, LANES)],
        [f32(forward_rows, LANES)] * count,
        [
            pltpu.VMEM((3, lay.width_x * lay.width_y, LANES), jnp.float32),
            pltpu.VMEM((count, LANES), jnp.int32),
            pltpu.SemaphoreType.DMA((4,)),
        ],
        space=pltpu.HBM,
        limit=60 * 1024 * 1024,
    )
    back_cuts = call(
        part(cut_adjoint, lay),
        (slab_int,),
        [flat(adjoint_now), flat(adjoint_next), traces],
        [f32(back_rows, LANES)] * count,
    )
    pieces = [lax.ppermute(cut, axes, lay.to_chunks(turn)) for turn, cut in enumerate(cuts)]
    pieces, ints, gain, drive, back_cuts = lax.optimization_barrier((pieces, ints, gain, drive, back_cuts))
    kept_rows = lay.kept * lay.wide
    tie_shape = f32(ROWS, LANES)
    state, own_courant, to_next, to_twin, codes = call(
        part(join_forward, lay),
        (where,),
        pieces,
        [f32(lay.state_rows, LANES), f32(lay.rows, LANES)]
        + [f32(lay.rows + 2 * kept_rows, LANES)] * 2
        + [f32(count, slots)],
        [pltpu.VMEM((3, lay.rows, LANES), jnp.float32)],
    )
    from_next, from_twin = swap(to_next, to_twin)

    back_pieces = []

    def move_adjoint(turns, tie):
        for turn in turns:
            back_pieces.append(lax.ppermute(after(back_cuts[turn], tie), axes, lay.to_chunks(turn)))

    move_adjoint(range(count), codes)

    phases = STEPS // DEPTH
    step_cost = 8_000_000
    side_cost = 4_000_000
    history_shape = f32(DEPTH * lay.rows, LANES)
    state_shapes = [f32(lay.state_rows, LANES), f32(lay.send_rows, LANES)]
    buffers = [pltpu.VMEM((lay.padded_rows, LANES), jnp.float32)] * 3
    buffers += [pltpu.VMEM((6 * LANES, 2 * LANES), jnp.bfloat16)]
    buffers += [pltpu.VMEM((lay.inner * lay.wide, LANES), jnp.float32)]
    record_scratch = [pltpu.VMEM((DEPTH * lay.rows, LANES), jnp.float32)]
    record_shape = (DEPTH * count, slots)
    histories, states, records = [], [], []
    half = own_courant
    for phase in range(phases):
        first, last = phase == 0, phase == phases - 1
        outs = [history_shape]
        if first:
            outs.append(f32(lay.inner * lay.wide, LANES))
        if not last:
            outs += state_shapes + [tie_shape]
        results = list(
            call(
                part(forward, lay, phase, sources),
                (ints,),
                [state, from_next, from_twin, half, gain, drive],
                outs,
                buffers + [pltpu.VMEM((sources, LANES), jnp.float32)],
                cost=step_cost,
            )
        )
        histories.append(results.pop(0))
        states.append(state)
        if first:
            half = results.pop(0)
        if last:
            continue
        state, send, tie = results
        if first:
            send = after(send, back_pieces)
        from_next, from_twin = swap(send, send)
    for history in histories[:-1]:
        records += call(
            part(record_phase, lay),
            (),
            [history, codes],
            [f32(*record_shape)],
            record_scratch,
            cost=side_cost,
        )
    back_state, to_next, to_twin = call(
        part(join_adjoint, lay),
        (where,),
        back_pieces,
        [f32(lay.state_rows, LANES)] + [f32(lay.rows + kept_rows, LANES)] * 2,
        [pltpu.VMEM((2, lay.rows, LANES), jnp.float32)],
    )
    back_from_next, back_from_twin = swap(to_next, to_twin)
    (misfit,) = call(
        part(record_last, lay, phases),
        (where,),
        [histories[-1], codes] + records + back_pieces,
        [f32(-(-(STEPS + 1) * count // ROWS) * ROWS, slots)],
        record_scratch + [pltpu.VMEM(record_shape, jnp.float32)],
        cost=side_cost,
    )

    misfit = after(misfit, [back_from_next, back_from_twin])
    misfit_next, misfit_twin = swap(misfit, misfit)
    state, from_next, from_twin = back_state, back_from_next, back_from_twin
    gradient = None
    inject_shape = f32(DEPTH, lay.inner * lay.wide, LANES)
    for phase in range(phases):
        first, last = phase == 0, phase == phases - 1
        (inject,) = call(part(spread_own, lay, phase), (), [misfit], [inject_shape], cost=side_cost)
        (inject,) = call(
            part(spread_sides, lay, phase),
            (where,),
            [inject, misfit_next, misfit_twin],
            [inject_shape],
            cost=side_cost,
            aliases={1: 0},
        )
        results = call(
            part(backward, lay, phase),
            (where,),
            [state, from_next, from_twin, half, gain, inject],
            [history_shape] + ([] if last else state_shapes),
            buffers,
            cost=step_cost,
        )
        arrays = [results[0], histories[phases - 1 - phase], states[phases - 1 - phase]]
        if last:
            sends = call(
                part(gradient_last, lay),
                (where,),
                arrays + [gradient, misfit],
                [f32(lay.cells + traces.shape[0], LANES)] * count,
                [pltpu.VMEM((lay.rows, LANES), jnp.float32)] * 2,
            )
            continue
        _, state, send = results
        from_next, from_twin = swap(send, send)
        kernel = gradient_first if first else gradient_later
        (gradient,) = call(
            part(kernel, lay), (), arrays + ([] if first else [gradient]), [f32(lay.rows, LANES)], cost=side_cost
        )
    pieces = [lax.ppermute(send, axes, lay.to_slabs(turn)) for turn, send in enumerate(sends)]
    gradient, residual = call(
        part(finish, lay),
        (slab_int,),
        pieces,
        [f32(lay.width_x * lay.width_y, LANES), f32(*traces.shape)],
    )
    return gradient.reshape(courant.shape), residual.reshape(observed.shape)


def local(courant, *rest):
    width_x, width_y, depth_z = courant.shape
    count_x, count_y = lax.axis_size("gx"), lax.axis_size("gy")
    if fits(count_x, count_y, width_x, width_y, depth_z):
        return local_tiles(Layout(count_x, count_y, width_x, width_y), courant, *rest)
    return local_blocks(courant, *rest)


def padded_2(cells, sides, width):
    for axis, dim in sides:
        count = lax.axis_size(axis)
        ends = count - 1
        head = lax.slice_in_dim(cells, 0, width, axis=dim)
        tail = lax.slice_in_dim(cells, cells.shape[dim] - width, cells.shape[dim], axis=dim)
        cells = jnp.concatenate(
            [
                lax.ppermute(tail, axis, [(i, (i + 1) % count) for i in range(ends)]),
                cells,
                lax.ppermute(head, axis, [((i + 1) % count, i) for i in range(ends)]),
            ],
            axis=dim,
        )
    return cells


def laplace(values):
    width_x, width_y, depth_z = values.shape
    padded = padded_2(values, (("gx", 0), ("gy", 1)), 4)
    z_padded = jnp.pad(values, ((0, 0), (0, 0), (4, 4)))
    summed = 3.0 * stencil[0] * values
    for offset in range(1, 5):
        paired = (
            padded[4 + offset : 4 + offset + width_x, 4 : 4 + width_y]
            + padded[4 - offset : 4 - offset + width_x, 4 : 4 + width_y]
        )
        paired = (
            paired
            + padded[4 : 4 + width_x, 4 + offset : 4 + offset + width_y]
            + padded[4 : 4 + width_x, 4 - offset : 4 - offset + width_y]
        )
        paired = (
            paired
            + z_padded[:, :, 4 + offset : 4 + offset + depth_z]
            + z_padded[:, :, 4 - offset : 4 - offset + depth_z]
        )
        summed = summed + stencil[offset] * paired
    return summed


def sponge(start, count, whole):
    position = start + jnp.arange(count, dtype=jnp.int32)
    edge_gap = jnp.minimum(position, whole - 1 - position)
    profile = jnp.maximum(SPONGE - edge_gap, 0).astype(jnp.float32) / SPONGE
    return profile * profile


def place_sum(indices, amounts, shape):
    flat = jnp.zeros((shape[0] * shape[1] * shape[2],), jnp.float32).at[indices].add(amounts)
    return flat.reshape(shape)


def local_blocks(
    courant,
    state_prev,
    state_now,
    adjoint_now,
    adjoint_next,
    source_cell,
    wavelet,
    observed,
    receiver_cell,
    receiver_count,
):
    shape = courant.shape
    width_x, width_y, depth_z = shape
    slab = lax.axis_index("gx")
    strip = lax.axis_index("gy")
    whole_x = width_x * lax.axis_size("gx")
    whole_y = width_y * lax.axis_size("gy")
    damping = damping_peak * (
        sponge(slab * width_x, width_x, whole_x)[:, None, None]
        + sponge(strip * width_y, width_y, whole_y)[None, :, None]
    )
    source_x = source_cell // (whole_y * depth_z) - slab * width_x
    source_y = source_cell // depth_z % whole_y - strip * width_y
    source_z = source_cell % depth_z
    inside = (source_x >= 0) & (source_x < width_x) & (source_y >= 0) & (source_y < width_y)
    source_flat = jnp.where(inside, (source_x * width_y + source_y) * depth_z + source_z, 0)
    source_weight = wavelet * inside.astype(jnp.float32)[None, :]
    senders = receiver_cell.shape[2]
    slots = receiver_cell.shape[3]
    cells = receiver_cell.reshape(-1)
    active = (
        jnp.arange(slots, dtype=jnp.int32)[None, :] < receiver_count.reshape(senders, 1)
    ).astype(jnp.float32)
    active_flat = active.reshape(-1)

    def advance(carry, weights):
        former, current = carry
        drive = laplace(current) + place_sum(source_flat, weights, shape)
        following = (2.0 * current - (1.0 - damping) * former + courant * drive) / (1.0 + damping)
        return (
            (current, following),
            (following - 2.0 * current + former, following.reshape(-1)[cells] * active_flat),
        )

    final_states, (accels, recorded) = lax.scan(advance, (state_prev, state_now), source_weight)
    recorded_tiles = recorded.reshape(STEPS, senders, 1, 1, slots)
    active_tiles = active.reshape(1, senders, 1, 1, slots)
    synthetic, mask_back = (
        lax.all_to_all(recorded_tiles, "gx", split_axis=1, concat_axis=3, tiled=True),
        lax.all_to_all(active_tiles, "gx", split_axis=1, concat_axis=3, tiled=True),
    )
    trace_residual = mask_back * (synthetic - observed)
    misfit = lax.all_to_all(trace_residual, "gx", split_axis=3, concat_axis=1, tiled=True)
    misfit_rows = misfit.reshape(STEPS, senders * slots)

    def retreat(carry, inputs):
        later, current, gradient = carry
        acceleration, residual_row = inputs
        drive = laplace(current) + place_sum(cells, residual_row, shape)
        earlier = (2.0 * current - (1.0 - damping) * later + courant * drive) / (1.0 + damping)
        return ((current, earlier, gradient + earlier * acceleration), None)

    start_gradient = jnp.zeros(shape, jnp.float32)
    (last_later, last_current, gradient), unused = lax.scan(
        retreat, (adjoint_next, adjoint_now, start_gradient), (accels, misfit_rows), reverse=True
    )
    return (gradient, trace_residual)


def solution(mesh):
    placed = (
        P("gx", "gy", None),
        P(("groups", "gx"), "gy", None),
        P(("groups", "gx"), "gy", None),
        P(("groups", "gx"), "gy", None),
        P(("groups", "gx"), "gy", None),
        P("groups"),
        P(None, "groups"),
        P("groups", "gx", "gy", None, None),
        P("gx", "gy", None, None),
        P("gx", "gy", None),
    )
    return jax.shard_map(
        local,
        mesh=mesh,
        in_specs=placed,
        out_specs=(P(("groups", "gx"), "gy", None), P("groups", "gx", "gy", None, None)),
        check_vma=False,
    )
```

```python
import functools

import jax
import jax.numpy as jnp
from jax import lax
from jax.experimental import pallas as pl
from jax.experimental.pallas import tpu as pltpu
from jax.sharding import PartitionSpec as P

STEPS = 12
SPONGE = 8
REACH = 4
DEPTH = 4
LANES = 128
ROWS = 8


stencil = (-205.0 / 72.0, 8.0 / 5.0, -1.0 / 5.0, 8.0 / 315.0, -1.0 / 560.0)
damping_peak = 0.3
scale = 5040.0
weights = (3.0 * -14350.0, 8064.0, -1008.0, 128.0, -9.0)


class Layout:
    def __init__(self, count_x, count_y, width_x, width_y):
        self.count_x, self.count_y = count_x, count_y
        self.width_x, self.width_y = width_x, width_y
        self.chunk = width_y // count_x
        self.wide = width_x * count_x
        self.tiles = self.wide // ROWS
        self.whole_y = width_y * count_y
        self.margin = REACH * DEPTH
        self.extent = self.chunk + 2 * self.margin
        self.stride = self.tiles * 2 * ROWS
        self.padded_rows = self.extent * self.stride + ROWS
        self.kept = self.margin - REACH
        self.inner = self.extent - 2 * REACH
        self.rows = self.chunk * self.wide
        self.cells = self.chunk * width_x
        self.near = self.chunk + 2 * REACH
        self.state_rows = (self.chunk + self.near) * self.wide
        self.lacking = range(REACH, self.chunk - REACH)
        self.send_rows = (self.chunk + len(self.lacking)) * self.wide

    def at(self, place):
        pair, rest = divmod(place, 2 * self.count_x)
        chip, core = divmod(rest, 2)
        slab = chip if pair % 2 == 0 else self.count_x - 1 - chip
        return slab * self.count_y + 2 * pair + core

    def to_chunks(self, turn):
        moves = []
        for slab in range(self.count_x):
            for strip in range(self.count_y):
                moves.append((slab * self.count_y + strip, self.at(strip * self.count_x + (slab ^ turn))))
        return moves

    def to_slabs(self, turn):
        return [(target, source) for source, target in self.to_chunks(turn)]

    def swaps(self, first):
        moves = []
        for place in range(first, self.count_x * self.count_y - 1, 2):
            moves += [(self.at(place), self.at(place + 1)), (self.at(place + 1), self.at(place))]
        return moves


def fits(count_x, count_y, width_x, width_y, depth_z):
    return (
        count_x & (count_x - 1) == 0
        and count_y % 2 == 0
        and width_x == ROWS
        and width_x * count_x == ROWS * REACH
        and depth_z == LANES
        and width_y == count_x * REACH * DEPTH
    )


def f32(*shape):
    return jax.ShapeDtypeStruct(shape, jnp.float32)


def call(
    kernel, ints, arrays, outs, scratch=(), cost=1_000_000, space=pltpu.VMEM, aliases=None,
    out_space=pltpu.VMEM, limit=32 * 1024 * 1024
):
    return pl.pallas_call(
        kernel,
        out_shape=tuple(outs),
        in_specs=[pl.BlockSpec(memory_space=pltpu.SMEM)] * len(ints)
        + [pl.BlockSpec(memory_space=space)] * len(arrays),
        out_specs=tuple(pl.BlockSpec(memory_space=out_space) for _ in outs),
        scratch_shapes=list(scratch),
        input_output_aliases=aliases or {},
        compiler_params=pltpu.CompilerParams(vmem_limit_bytes=limit),
        cost_estimate=pl.CostEstimate(flops=cost, bytes_accessed=cost, transcendentals=0),
    )(*ints, *arrays)


def aligned(value, to=ROWS):
    return pl.multiple_of(value, to)


def cut_forward(lay, slab_ref, count_ref, *refs):
    fields, cell, refs = refs[:3], refs[3], refs[4:]
    sends, (held_cell, used, done, cells_done) = refs[: lay.count_x], refs[lay.count_x :]
    copies = []
    for turn, send in enumerate(sends):
        chunk = pl.ds(aligned((slab_ref[0] ^ turn) * lay.chunk), lay.chunk)
        for index, field in enumerate(fields):
            source = field.at[:, chunk, :]
            target = send.at[pl.ds(index * lay.width_x, lay.width_x)]
            copies.append(pltpu.make_async_copy(source, target, done.at[turn, index]))
            copies[-1].start()
    loaded = pltpu.make_async_copy(cell, held_cell, cells_done.at[0])
    loaded.start()
    loaded.wait()
    slots = lax.broadcasted_iota(jnp.int32, (1, LANES), 1)
    used[...] = jnp.full(used.shape, -1.0, jnp.float32)
    for tile in range(lay.count_x):
        line = jnp.where(slots < count_ref[tile], held_cell[tile : tile + 1, :], -1)
        used[tile : tile + 1, :] = line.astype(jnp.float32)
    for turn, send in enumerate(sends):
        target = send.at[3 * lay.width_x]
        copies.append(pltpu.make_async_copy(used, target, done.at[turn, 3]))
        copies[-1].start()
    for copy in copies:
        copy.wait()


def cut_adjoint(lay, slab_ref, now, prev, observed, *sends):
    for turn, send in enumerate(sends):
        chunk = pl.ds(aligned((slab_ref[0] ^ turn) * lay.chunk), lay.chunk)
        for index, field in enumerate((now, prev)):
            send[index * lay.width_x : (index + 1) * lay.width_x] = field[:, chunk, :]
        for index in range(observed.shape[0] // lay.chunk):
            rows = observed[index * lay.chunk : (index + 1) * lay.chunk, :]
            send[2 * lay.width_x + index] = rows


def join_fields(lay, own_slot, odd, pieces, joined, state, courant, send_next, send_twin):
    fields = joined.shape[0]
    for turn, piece in enumerate(pieces):
        start_x = (own_slot ^ turn) * ROWS
        for field in range(fields):
            for y in range(lay.chunk):
                rows = pl.ds(field * lay.cells + y, ROWS, stride=lay.chunk)
                joined[field, pl.ds(aligned(y * lay.wide + start_x), ROWS), :] = piece[rows, :]
    kept_rows = lay.kept * lay.wide
    for field in range(fields):
        target, first = (state, 0) if field == 0 else (state, (lay.chunk + REACH) * lay.wide)
        if field == 2:
            target, first = courant, 0
        for y in range(lay.chunk):
            for tile in range(lay.tiles):
                values = joined[field, pl.ds(y * lay.wide + tile, ROWS, stride=lay.tiles), :]
                row = y * lay.wide + tile * ROWS
                target[first + row : first + row + ROWS, :] = values
                if field == 0:
                    send_next[row : row + ROWS, :] = values
                    send_twin[row : row + ROWS, :] = values
    for field in range(1, fields):
        source, first = (state, (lay.chunk + REACH) * lay.wide) if field == 1 else (courant, 0)
        place = lay.rows + (field - 1) * kept_rows
        skipped = (lay.chunk - lay.kept) * lay.wide
        ahead = source[pl.ds(aligned(first + odd * skipped), kept_rows), :]
        send_next[place : place + kept_rows, :] = ahead
        behind = source[pl.ds(aligned(first + (1 - odd) * skipped), kept_rows), :]
        send_twin[place : place + kept_rows, :] = behind


def join_forward(lay, where_ref, *refs):
    pieces, (state, courant, send_next, send_twin, codes, joined) = refs[: lay.count_x], refs[lay.count_x :]
    own_slot = where_ref[0]
    join_fields(lay, own_slot, where_ref[1], pieces, joined, state, courant, send_next, send_twin)
    first = 3 * lay.cells
    strip_cells = lay.width_y * LANES
    slab_row = lax.broadcasted_iota(jnp.int32, codes.shape, 0)
    found = jnp.full(codes.shape, -1.0, jnp.float32)
    for turn, piece in enumerate(pieces):
        cell = piece[first : first + lay.count_x, :].astype(jnp.int32)
        used = cell >= 0
        cell = jnp.maximum(cell, 0)
        x = lax.div(cell, jnp.int32(strip_cells))
        y = lax.rem(lax.div(cell, jnp.int32(LANES)), jnp.int32(lay.width_y)) - own_slot * lay.chunk
        inside = used & (y >= 0) & (y < lay.chunk)
        code = jnp.where(inside, (y * ROWS + x) * LANES + lax.rem(cell, jnp.int32(LANES)), -1)
        code = code.astype(jnp.float32)
        line = jnp.concatenate([code[tile : tile + 1, :] for tile in range(lay.count_x)], axis=1)
        found = jnp.where(slab_row == (own_slot ^ turn), jnp.broadcast_to(line, codes.shape), found)
    codes[...] = found


def join_adjoint(lay, where_ref, *refs):
    pieces, (state, send_next, send_twin, joined) = refs[: lay.count_x], refs[lay.count_x :]
    join_fields(lay, where_ref[0], where_ref[1], pieces, joined, state, None, send_next, send_twin)


def load_state(lay, odd, first, now, prev, state, from_next, from_twin):
    def put(buffer, layer, ref, source):
        for tile in range(lay.tiles):
            row = layer * lay.stride + (2 * tile + 1) * ROWS
            values = ref[source * lay.wide + tile * ROWS : source * lay.wide + (tile + 1) * ROWS, :]
            buffer[pl.ds(row if isinstance(row, int) else aligned(row), ROWS), :] = values

    ahead = lay.margin + lay.chunk
    for y in range(lay.chunk):
        put(now, lay.margin + y, state, y)
        put(now, odd * ahead + y, from_next, y)
        put(now, (1 - odd) * ahead + y, from_twin, y)
    if first:
        for y in range(lay.chunk):
            put(prev, lay.margin + y, state, lay.chunk + REACH + y)
        for y in range(lay.kept):
            put(prev, odd * ahead + (1 - odd) * REACH + y, from_next, lay.chunk + y)
            put(prev, (1 - odd) * ahead + odd * REACH + y, from_twin, lay.chunk + y)
        return
    for y in range(lay.near):
        put(prev, lay.margin - REACH + y, state, lay.chunk + y)
    for index, y in enumerate(lay.lacking):
        put(prev, odd * ahead + y, from_next, lay.chunk + index)
        put(prev, (1 - odd) * ahead + y, from_twin, lay.chunk + index)


def store_state(lay, now, prev, state, send):
    def put(refs, target, buffer, layer):
        for tile in range(lay.tiles):
            row = layer * lay.stride + (2 * tile + 1) * ROWS
            values = buffer[row : row + ROWS, :]
            for ref, place in refs:
                ref[place * lay.wide + tile * ROWS : place * lay.wide + (tile + 1) * ROWS, :] = values

    for y in range(lay.chunk):
        put([(state, y), (send, y)], y, now, lay.margin + y)
    for y in range(lay.near):
        refs = [(state, lay.chunk + y)]
        if y - REACH in lay.lacking:
            refs.append((send, lay.chunk + y - REACH - lay.lacking[0]))
        put(refs, y, prev, lay.margin - REACH + y)


def split(values):
    high = values.astype(jnp.bfloat16)
    rest = values - high.astype(jnp.float32)
    middle = rest.astype(jnp.bfloat16)
    low = (rest - middle.astype(jnp.float32)).astype(jnp.bfloat16)
    return high, middle, low


def fill_band(band):
    row = lax.broadcasted_iota(jnp.int32, (2 * LANES, 2 * LANES), 0)
    column = lax.broadcasted_iota(jnp.int32, (2 * LANES, 2 * LANES), 1)
    apart = jnp.where((row < LANES) == (column < LANES), jnp.abs(row - column), 0)
    values = jnp.zeros((2 * LANES, 2 * LANES), jnp.float32)
    for k in range(1, REACH + 1):
        values = jnp.where(apart == k, weights[k], values)
    values = values.astype(jnp.bfloat16)
    for part in range(3):
        band[part * 2 * LANES : (part + 1) * 2 * LANES, :] = values


def multiply_z(lay, first_layer, count, now, band, along_z):
    tiles = []
    for y in range(count):
        for tile in range(lay.tiles):
            row = (first_layer + y) * lay.stride + (2 * tile + 1) * ROWS
            tiles.append(now[row : row + ROWS, :])
    half = len(tiles) // 2
    parts = [split(jnp.concatenate(group, axis=0)) for group in (tiles[:half], tiles[half:])]
    both = [side[part] for part in range(3) for side in parts]
    found = jnp.dot(jnp.concatenate(both, axis=1), band[...], preferred_element_type=jnp.float32)
    along_z[0 : half * ROWS, :] = found[:, :LANES]
    along_z[half * ROWS : 2 * half * ROWS, :] = found[:, LANES:]


def sweep(lay, step, now, prev, following, half, gain, band, along_z, inject=None):
    first_layer = REACH * (step + 1)
    group, quad = 8, 4
    reach_rows = REACH * lay.stride
    multiply_z(lay, first_layer, lay.extent - 2 * first_layer, now, band, along_z)

    def layers(block, carry):
        start = first_layer + group * block
        base = aligned((start - REACH) * lay.stride)
        around = now.at[pl.ds(base, (group + 2 * REACH) * lay.stride)]
        middle_rows = pl.ds(aligned(base + reach_rows), group * lay.stride)
        former_rows, target = prev.at[middle_rows], following.at[middle_rows]
        flat = aligned((start - REACH) * lay.wide)
        flat_rows = pl.ds(flat, group * lay.wide)
        half_rows, gain_rows = half.at[flat_rows], gain.at[flat_rows]
        added = None if inject is None else inject.at[step, flat_rows]

        z_rows = along_z.at[pl.ds(aligned(block * group * lay.wide), group * lay.wide)]

        def place(y, tile):
            return (y * lay.tiles + tile) * 2 * ROWS + ROWS

        def at(y, tile):
            row = place(y + REACH, tile)
            return around[row : row + ROWS, :]

        def beside(y, tile, shift):
            return now[pl.ds(base + (place(y + REACH, tile) + shift), ROWS), :]

        def layers_from(first):
            inside = range(first, first + quad)
            centers = {y: [] for y in inside}
            totals = {y: [] for y in inside}
            for tile in range(lay.tiles):
                column = {y: at(y, tile) for y in range(first - REACH, first + quad + REACH)}
                for y in inside:
                    total = weights[0] * column[y]
                    for k in range(1, REACH + 1):
                        total = total + weights[k] * (column[y - k] + column[y + k])
                    centers[y].append(column[y])
                    totals[y].append(total)
            for y in inside:
                lower = [beside(y, tile, -1) for tile in range(lay.tiles)]
                upper = [beside(y, tile, 1) for tile in range(lay.tiles)]
                line = lower + centers[y] + upper
                for tile in range(lay.tiles):
                    total = totals[y][tile]
                    for k in range(1, REACH + 1):
                        pair = line[lay.tiles + tile - k] + line[lay.tiles + tile + k]
                        total = total + weights[k] * pair
                    flat_at = (y * lay.tiles + tile) * ROWS
                    total = total + z_rows[flat_at : flat_at + ROWS, :]
                    if added is not None:
                        total = total + added[pl.ds(y * lay.wide + tile, ROWS, stride=lay.tiles), :]
                    row = place(y, tile)
                    former = former_rows[row : row + ROWS, :]
                    change = (centers[y][tile] - former) + half_rows[flat_at : flat_at + ROWS, :] * total
                    target[row : row + ROWS, :] = former + gain_rows[flat_at : flat_at + ROWS, :] * change

        for first in range(0, group, quad):
            layers_from(first)
        return carry

    lax.fori_loop(0, (lay.extent - 2 * first_layer) // group, layers, 0)


def zero_between(lay, step, buffer):
    zeros = jnp.zeros((ROWS, LANES), jnp.float32)
    first = REACH * (step + 1)
    for row in range(first * lay.stride, (lay.extent - first) * lay.stride + 1, 2 * ROWS):
        buffer[row : row + ROWS, :] = zeros


def zero_buffers(lay, now, prev, following):
    zero_between(lay, 0, now)
    zero_between(lay, 1, following)
    zero_between(lay, 2, prev)


def keep_own(lay, step, following, history):
    for y in range(lay.chunk):
        for tile in range(lay.tiles):
            row = (lay.margin + y) * lay.stride + (2 * tile + 1) * ROWS
            place = step * lay.rows + y * lay.wide + tile * ROWS
            history[place : place + ROWS, :] = following[row : row + ROWS, :]


def forward(lay, phase, sources, ints, state, from_next, from_twin, courant, gain, drive, *refs):
    first, last = phase == 0, phase == STEPS // DEPTH - 1
    refs = list(refs)
    history = refs.pop(0)
    half = refs.pop(0) if first else courant
    if not last:
        state_out, send = refs.pop(0), refs.pop(0)
    now, prev, following, band, along_z, pulse = refs
    odd = ints[0]

    fill_band(band)
    load_state(lay, odd, first, now, prev, state, from_next, from_twin)
    zero_buffers(lay, now, prev, following)
    if first:
        tail = (lay.chunk + lay.kept) * lay.wide
        part = lay.kept * lay.wide
        half[part : part + lay.rows, :] = (0.5 / scale) * courant[...]
        ahead = part + lay.rows
        half[pl.ds(aligned(odd * ahead), part), :] = (0.5 / scale) * from_next[tail : tail + part, :]
        half[pl.ds(aligned((1 - odd) * ahead), part), :] = (0.5 / scale) * from_twin[tail : tail + part, :]
    for source in range(sources):
        flat = pl.ds(ints[1 + sources + source], 1)
        pulse[source : source + 1, :] = scale * (half[flat, :] * gain[flat, :])

    for step in range(DEPTH):
        sweep(lay, step, now, prev, following, half, gain, band, along_z)
        added = pulse[...] * drive[phase * DEPTH + step]
        places = [pl.ds(ints[1 + source], 1) for source in range(sources)]
        lines = [following[place, :] for place in places]
        for source, (place, line) in enumerate(zip(places, lines)):
            following[place, :] = line + added[source : source + 1, :]
        keep_own(lay, step, following, history)
        now, prev, following = following, now, prev

    if not last:
        store_state(lay, now, prev, state_out, send)


def slot_rows(codes, slab):
    code = codes[slab : slab + 1, :].astype(jnp.int32)
    row = jnp.where(code >= 0, lax.shift_right_arithmetic(code, 7), -1)
    return row, jnp.where(code >= 0, code & (LANES - 1), -1)


def record_slots(lay, history, codes, plain, record):
    for step in range(DEPTH):
        for y in range(lay.chunk):
            for tile in range(lay.tiles):
                row = step * lay.rows + y * lay.wide
                values = history[row + tile * ROWS : row + (tile + 1) * ROWS, :]
                plain[pl.ds(row + tile, ROWS, stride=lay.tiles), :] = values
    slots = codes.shape[1]
    width = 2 * LANES
    for slab in range(lay.count_x):
        cell_row, cell_z = slot_rows(codes, slab)
        tiles = []
        for step in range(DEPTH):
            for y in range(lay.chunk):
                row = step * lay.rows + y * lay.wide + slab * ROWS
                tiles.append(plain[row : row + ROWS, :])
        parts = jnp.concatenate(split(jnp.concatenate(tiles, axis=0)), axis=1)
        for start in range(0, slots, width):
            here = slice(start, start + width)
            z = lax.broadcasted_iota(jnp.int32, (LANES, width), 0)
            pick = jnp.where(z == cell_z[:, here], 1.0, 0.0).astype(jnp.bfloat16)
            found = jnp.dot(parts, jnp.concatenate([pick] * 3, axis=0), preferred_element_type=jnp.float32)
            wanted = lax.broadcasted_iota(jnp.int32, (lay.cells, width), 0) == cell_row[:, here]
            for step in range(DEPTH):
                part = jnp.where(wanted, found[step * lay.cells : (step + 1) * lay.cells, :], 0.0)
                row = step * lay.count_x + slab
                record[row : row + 1, here] = jnp.sum(part, axis=0, keepdims=True)


def record_phase(lay, history, codes, record, plain):
    record_slots(lay, history, codes, plain, record)


def record_last(lay, phases, where_ref, history, codes, *refs):
    earlier, refs = refs[: phases - 1], refs[phases - 1 :]
    observed, (misfit, plain, record) = refs[: lay.count_x], refs[lay.count_x :]
    record_slots(lay, history, codes, plain, record)
    block = DEPTH * lay.count_x
    for index, part in enumerate(list(earlier) + [record]):
        misfit[index * block : (index + 1) * block, :] = part[...]
    total = STEPS * lay.count_x
    for slab in range(lay.count_x):
        misfit[total + slab : total + slab + 1, :] = codes[slab : slab + 1, :]
    for turn, piece in enumerate(observed):
        place = pl.ds(aligned((where_ref[0] ^ turn) * LANES, LANES), LANES)
        used = jnp.concatenate([codes[:, place]] * STEPS, axis=0) >= 0
        seen = piece[2 * lay.cells : 2 * lay.cells + total, :]
        misfit[0:total, place] = jnp.where(used, misfit[0:total, place] - seen, 0.0)


def spread(lay, phase, side, misfit, inject):
    codes = misfit[STEPS * lay.count_x : (STEPS + 1) * lay.count_x, :]
    for slab in range(lay.count_x):
        cell_row, cell_z = slot_rows(codes, slab)
        slots = cell_row.shape[1]
        z = lax.broadcasted_iota(jnp.int32, (LANES, slots), 0)
        pick = jnp.where(z == cell_z, 1.0, 0.0).astype(jnp.bfloat16)
        hit = lax.broadcasted_iota(jnp.int32, (lay.cells, slots), 0) == cell_row
        hit = jnp.where(hit, 1.0, 0.0).astype(jnp.bfloat16)
        left, spans = [], []
        for step in range(DEPTH):
            low, high = 0, lay.chunk
            if side < 0:
                low = REACH * (step + 1) - lay.margin + lay.chunk
            if side > 0:
                high = lay.margin - REACH * (step + 1)
            if low >= high:
                continue
            row = (STEPS - 1 - phase * DEPTH - step) * lay.count_x + slab
            parts = split(scale * misfit[row : row + 1, :])
            left += [hit[low * ROWS : high * ROWS, :] * part for part in parts]
            spans.append((step, low, high))
        placed = lax.dot_general(
            jnp.concatenate(left, axis=0),
            pick,
            (((1,), (1,)), ((), ())),
            preferred_element_type=jnp.float32,
        )
        at = 0
        for step, low, high in spans:
            rows = (high - low) * ROWS
            total = placed[at : at + rows, :]
            for part in (1, 2):
                total = total + placed[at + part * rows : at + (part + 1) * rows, :]
            for y in range(low, high):
                layer = lay.margin + side * lay.chunk + y - REACH
                target = layer * lay.wide + slab * ROWS
                inject[step, target : target + ROWS, :] = total[(y - low) * ROWS : (y - low + 1) * ROWS, :]
            at += 3 * rows


def spread_own(lay, phase, misfit, inject):
    spread(lay, phase, 0, misfit, inject)


def spread_sides(lay, phase, where_ref, own, misfit_next, misfit_twin, inject):
    odd = where_ref[1]

    @pl.when(odd == 1)
    def ahead_is_next():
        spread(lay, phase, 1, misfit_next, inject)
        spread(lay, phase, -1, misfit_twin, inject)

    @pl.when(odd == 0)
    def behind_is_next():
        spread(lay, phase, -1, misfit_next, inject)
        spread(lay, phase, 1, misfit_twin, inject)


def backward(lay, phase, where_ref, state, from_next, from_twin, half, gain, inject, *refs):
    first, last = phase == 0, phase == STEPS // DEPTH - 1
    refs = list(refs)
    history = refs.pop(0)
    if not last:
        state_out, send = refs.pop(0), refs.pop(0)
    now, prev, following, band, along_z = refs

    fill_band(band)
    load_state(lay, where_ref[1], first, now, prev, state, from_next, from_twin)
    zero_buffers(lay, now, prev, following)
    for step in range(DEPTH):
        sweep(lay, step, now, prev, following, half, gain, band, along_z, inject)
        keep_own(lay, step, following, history)
        now, prev, following = following, now, prev
    if not last:
        store_state(lay, now, prev, state_out, send)


def add_gradient(lay, before, adjoint, history, state, gradient):
    def layer(y, carry):
        place = aligned(y * lay.wide)
        own = pl.ds(place, lay.wide)
        fields = [state[pl.ds(aligned(place + (lay.chunk + REACH) * lay.wide), lay.wide), :], state[own, :]]
        fields += [history[pl.ds(aligned(place + step * lay.rows), lay.wide), :] for step in range(DEPTH)]
        total = None if before is None else before[own, :]
        for step in range(DEPTH):
            index = DEPTH - 1 - step
            accel = (fields[index + 2] - fields[index + 1]) - (fields[index + 1] - fields[index])
            term = adjoint[pl.ds(aligned(place + step * lay.rows), lay.wide), :] * accel
            total = term if total is None else total + term
        gradient[own, :] = total
        return carry

    lax.fori_loop(0, lay.chunk, layer, 0)


def gradient_first(lay, adjoint, history, state, gradient):
    add_gradient(lay, None, adjoint, history, state, gradient)


def gradient_later(lay, adjoint, history, state, before, gradient):
    add_gradient(lay, before, adjoint, history, state, gradient)


def gradient_last(lay, where_ref, adjoint, history, state, before, misfit, *refs):
    sends, (gradient, plain) = refs[: lay.count_x], refs[lay.count_x :]
    add_gradient(lay, before, adjoint, history, state, gradient)
    for y in range(lay.chunk):
        for tile in range(lay.tiles):
            row = y * lay.wide + tile * ROWS
            plain[pl.ds(y * lay.wide + tile, ROWS, stride=lay.tiles), :] = gradient[row : row + ROWS, :]
    total = STEPS * lay.count_x
    for turn, send in enumerate(sends):
        other = where_ref[0] ^ turn
        for y in range(lay.chunk):
            source = pl.ds(aligned(y * lay.wide + other * ROWS), ROWS)
            send[y * ROWS : (y + 1) * ROWS, :] = plain[source, :]
        tile = pl.ds(aligned(other * LANES, LANES), LANES)
        send[lay.cells : lay.cells + total, :] = misfit[0:total, tile]


def finish(lay, slab_ref, *refs):
    pieces, (gradient, residual) = refs[: lay.count_x], refs[lay.count_x :]
    total = None
    for turn, piece in enumerate(pieces):
        start = (slab_ref[0] ^ turn) * lay.chunk
        for x in range(ROWS):
            target = pl.ds(aligned(x * lay.width_y + start), lay.chunk)
            gradient[target, :] = piece[pl.ds(x, lay.chunk, stride=ROWS), :]
        part = piece[lay.cells : lay.cells + residual.shape[0], :]
        total = part if total is None else total + part
    residual[...] = total


def gain_rows(lay, first_y):
    x = jnp.arange(ROWS)[None, :] * lay.tiles + jnp.arange(lay.tiles)[:, None]
    y = first_y + REACH + jnp.arange(lay.inner)

    def ramp(position, count):
        gap = jnp.minimum(position, count - 1 - position)
        profile = jnp.maximum(SPONGE - gap, 0).astype(jnp.float32) / SPONGE
        return profile * profile

    damping = damping_peak * (ramp(x, lay.wide)[None] + ramp(y, lay.whole_y)[:, None, None])
    gain = (2.0 / (1.0 + damping)).reshape(lay.inner * lay.wide, 1)
    return jnp.broadcast_to(gain, (lay.inner * lay.wide, LANES))


def source_rows(lay, first_y, source_cell, wavelet):
    x = source_cell // (lay.whole_y * LANES)
    y = source_cell // LANES % lay.whole_y - first_y
    z = source_cell % LANES
    inside = (y >= REACH) & (y < lay.extent - REACH)
    tile, row = x % lay.tiles, x // lay.tiles
    padded = jnp.where(inside, y * lay.stride + (2 * tile + 1) * ROWS + row, ROWS // 2)
    flat = jnp.where(inside, (y - REACH) * lay.wide + tile * ROWS + row, 0)
    same = (padded[:, None] == padded[None, :]) & inside[None, :]
    spot = (z[:, None] == jnp.arange(LANES)[None, :]).astype(jnp.float32)
    lines = jnp.where(same[None, :, :, None], wavelet[:, None, :, None] * spot[None, None], 0.0)
    return padded, flat, jnp.sum(lines, axis=2)


def local_tiles(
    lay,
    courant,
    state_prev,
    state_now,
    adjoint_now,
    adjoint_next,
    source_cell,
    wavelet,
    observed,
    receiver_cell,
    receiver_count,
):
    axes = ("gx", "gy")
    slab = lax.axis_index("gx")
    strip = lax.axis_index("gy")
    pair = strip // 2
    chip = jnp.where(pair % 2 == 0, slab, lay.count_x - 1 - slab)
    place = (pair * lay.count_x + chip) * 2 + strip % 2
    odd = strip % 2
    first_y = place * lay.chunk - lay.margin
    slab_int = slab.reshape(1).astype(jnp.int32)
    where = jnp.stack([place % lay.count_x, odd]).astype(jnp.int32)

    count = lay.count_x
    sources = source_cell.shape[0]
    slots = count * receiver_cell.shape[3]
    flat = lambda values: values.reshape(-1, LANES)
    part = functools.partial

    def swap(to_next, to_twin):
        return (
            lax.ppermute(to_next, axes, lay.swaps(1)),
            lax.ppermute(to_twin, axes, lay.swaps(0)),
        )

    def after(value, others):
        return lax.optimization_barrier((value, others))[0]

    padded, flat_row, drive = source_rows(lay, first_y, source_cell, wavelet)
    gain = gain_rows(lay, first_y)
    ints = jnp.concatenate([odd.reshape(1), padded, flat_row]).astype(jnp.int32)

    traces = flat(observed)
    forward_shape = f32(3 * lay.width_x + 1, lay.chunk, LANES)
    back_shape = f32(2 * lay.width_x + traces.shape[0] // lay.chunk, lay.chunk, LANES)
    cuts = call(
        part(cut_forward, lay),
        (slab_int, receiver_count.reshape(-1)),
        [state_now, state_prev, courant, receiver_cell.reshape(count, LANES)],
        [forward_shape] * count,
        [
            pltpu.VMEM((count, LANES), jnp.int32),
            pltpu.VMEM((lay.chunk, LANES), jnp.float32),
            pltpu.SemaphoreType.DMA((count, 4)),
            pltpu.SemaphoreType.DMA((1,)),
        ],
        space=pltpu.HBM,
        out_space=pltpu.HBM,
        limit=60 * 1024 * 1024,
    )
    back_cuts = call(
        part(cut_adjoint, lay),
        (slab_int,),
        [adjoint_now, adjoint_next, traces],
        [back_shape] * count,
    )
    pieces = [flat(lax.ppermute(cut, axes, lay.to_chunks(turn))) for turn, cut in enumerate(cuts)]
    pieces, ints, gain, drive, back_cuts = lax.optimization_barrier((pieces, ints, gain, drive, back_cuts))
    kept_rows = lay.kept * lay.wide
    state, own_courant, to_next, to_twin, codes = call(
        part(join_forward, lay),
        (where,),
        pieces,
        [f32(lay.state_rows, LANES), f32(lay.rows, LANES)]
        + [f32(lay.rows + 2 * kept_rows, LANES)] * 2
        + [f32(count, slots)],
        [pltpu.VMEM((3, lay.rows, LANES), jnp.float32)],
    )
    from_next, from_twin = swap(to_next, to_twin)

    back_pieces = []

    def move_adjoint(turns, earlier):
        for turn in turns:
            moved = lax.ppermute(after(back_cuts[turn], earlier), axes, lay.to_chunks(turn))
            back_pieces.append(flat(moved))

    move_adjoint(range(count - 2), codes)

    phases = STEPS // DEPTH
    step_cost = 8_000_000
    side_cost = 4_000_000
    history_shape = f32(DEPTH * lay.rows, LANES)
    state_shapes = [f32(lay.state_rows, LANES), f32(lay.send_rows, LANES)]
    buffers = [pltpu.VMEM((lay.padded_rows, LANES), jnp.float32)] * 3
    buffers += [pltpu.VMEM((6 * LANES, 2 * LANES), jnp.bfloat16)]
    buffers += [pltpu.VMEM((lay.inner * lay.wide, LANES), jnp.float32)]
    record_scratch = [pltpu.VMEM((DEPTH * lay.rows, LANES), jnp.float32)]
    record_shape = (DEPTH * count, slots)
    histories, states, records = [], [], []
    half = own_courant
    for phase in range(phases):
        first, last = phase == 0, phase == phases - 1
        if last:
            for history in histories:
                records += call(
                    part(record_phase, lay),
                    (),
                    [history, codes],
                    [f32(*record_shape)],
                    record_scratch,
                    cost=side_cost,
                )
            state = after(state, records)
        outs = [history_shape]
        if first:
            outs.append(f32(lay.inner * lay.wide, LANES))
        if not last:
            outs += state_shapes
        results = list(
            call(
                part(forward, lay, phase, sources),
                (ints,),
                [state, from_next, from_twin, half, gain, drive],
                outs,
                buffers + [pltpu.VMEM((sources, LANES), jnp.float32)],
                cost=step_cost,
            )
        )
        histories.append(results.pop(0))
        states.append(state)
        if first:
            half = results.pop(0)
        if last:
            continue
        state, send = results
        send = after(send, back_pieces)
        from_next, from_twin = swap(send, send)
        move_adjoint([count - 2 + phase], send)
    back_pieces = after(back_pieces, histories[-1])
    back_state, to_next, to_twin = call(
        part(join_adjoint, lay),
        (where,),
        back_pieces,
        [f32(lay.state_rows, LANES)] + [f32(lay.rows + kept_rows, LANES)] * 2,
        [pltpu.VMEM((2, lay.rows, LANES), jnp.float32)],
    )
    back_from_next, back_from_twin = swap(to_next, to_twin)
    (misfit,) = call(
        part(record_last, lay, phases),
        (where,),
        [histories[-1], codes] + records + back_pieces,
        [f32(-(-(STEPS + 1) * count // ROWS) * ROWS, slots)],
        record_scratch + [pltpu.VMEM(record_shape, jnp.float32)],
        cost=side_cost,
    )

    misfit_next, misfit_twin = swap(misfit, misfit)
    state, from_next, from_twin = back_state, back_from_next, back_from_twin
    gradient = None
    inject_shape = f32(DEPTH, lay.inner * lay.wide, LANES)
    for phase in range(phases):
        first, last = phase == 0, phase == phases - 1
        (inject,) = call(part(spread_own, lay, phase), (), [misfit], [inject_shape], cost=side_cost)
        (inject,) = call(
            part(spread_sides, lay, phase),
            (where,),
            [inject, misfit_next, misfit_twin],
            [inject_shape],
            cost=side_cost,
            aliases={1: 0},
        )
        results = call(
            part(backward, lay, phase),
            (where,),
            [state, from_next, from_twin, half, gain, inject],
            [history_shape] + ([] if last else state_shapes),
            buffers,
            cost=step_cost,
        )
        arrays = [results[0], histories[phases - 1 - phase], states[phases - 1 - phase]]
        if last:
            sends = call(
                part(gradient_last, lay),
                (where,),
                arrays + [gradient, misfit],
                [f32(lay.cells + traces.shape[0], LANES)] * count,
                [pltpu.VMEM((lay.rows, LANES), jnp.float32)] * 2,
            )
            continue
        _, state, send = results
        from_next, from_twin = swap(send, send)
        kernel = gradient_first if first else gradient_later
        (gradient,) = call(
            part(kernel, lay), (), arrays + ([] if first else [gradient]), [f32(lay.rows, LANES)], cost=side_cost
        )
    pieces = [lax.ppermute(send, axes, lay.to_slabs(turn)) for turn, send in enumerate(sends)]
    gradient, residual = call(
        part(finish, lay),
        (slab_int,),
        pieces,
        [f32(lay.width_x * lay.width_y, LANES), f32(*traces.shape)],
    )
    return gradient.reshape(courant.shape), residual.reshape(observed.shape)


def local(courant, *rest):
    width_x, width_y, depth_z = courant.shape
    count_x, count_y = lax.axis_size("gx"), lax.axis_size("gy")
    if fits(count_x, count_y, width_x, width_y, depth_z):
        return local_tiles(Layout(count_x, count_y, width_x, width_y), courant, *rest)
    return local_blocks(courant, *rest)


def padded_2(cells, sides, width):
    for axis, dim in sides:
        count = lax.axis_size(axis)
        ends = count - 1
        head = lax.slice_in_dim(cells, 0, width, axis=dim)
        tail = lax.slice_in_dim(cells, cells.shape[dim] - width, cells.shape[dim], axis=dim)
        cells = jnp.concatenate(
            [
                lax.ppermute(tail, axis, [(i, (i + 1) % count) for i in range(ends)]),
                cells,
                lax.ppermute(head, axis, [((i + 1) % count, i) for i in range(ends)]),
            ],
            axis=dim,
        )
    return cells


def laplace(values):
    width_x, width_y, depth_z = values.shape
    padded = padded_2(values, (("gx", 0), ("gy", 1)), 4)
    z_padded = jnp.pad(values, ((0, 0), (0, 0), (4, 4)))
    summed = 3.0 * stencil[0] * values
    for offset in range(1, 5):
        paired = (
            padded[4 + offset : 4 + offset + width_x, 4 : 4 + width_y]
            + padded[4 - offset : 4 - offset + width_x, 4 : 4 + width_y]
        )
        paired = (
            paired
            + padded[4 : 4 + width_x, 4 + offset : 4 + offset + width_y]
            + padded[4 : 4 + width_x, 4 - offset : 4 - offset + width_y]
        )
        paired = (
            paired
            + z_padded[:, :, 4 + offset : 4 + offset + depth_z]
            + z_padded[:, :, 4 - offset : 4 - offset + depth_z]
        )
        summed = summed + stencil[offset] * paired
    return summed


def sponge(start, count, whole):
    position = start + jnp.arange(count, dtype=jnp.int32)
    edge_gap = jnp.minimum(position, whole - 1 - position)
    profile = jnp.maximum(SPONGE - edge_gap, 0).astype(jnp.float32) / SPONGE
    return profile * profile


def place_sum(indices, amounts, shape):
    flat = jnp.zeros((shape[0] * shape[1] * shape[2],), jnp.float32).at[indices].add(amounts)
    return flat.reshape(shape)


def local_blocks(
    courant,
    state_prev,
    state_now,
    adjoint_now,
    adjoint_next,
    source_cell,
    wavelet,
    observed,
    receiver_cell,
    receiver_count,
):
    shape = courant.shape
    width_x, width_y, depth_z = shape
    slab = lax.axis_index("gx")
    strip = lax.axis_index("gy")
    whole_x = width_x * lax.axis_size("gx")
    whole_y = width_y * lax.axis_size("gy")
    damping = damping_peak * (
        sponge(slab * width_x, width_x, whole_x)[:, None, None]
        + sponge(strip * width_y, width_y, whole_y)[None, :, None]
    )
    source_x = source_cell // (whole_y * depth_z) - slab * width_x
    source_y = source_cell // depth_z % whole_y - strip * width_y
    source_z = source_cell % depth_z
    inside = (source_x >= 0) & (source_x < width_x) & (source_y >= 0) & (source_y < width_y)
    source_flat = jnp.where(inside, (source_x * width_y + source_y) * depth_z + source_z, 0)
    source_weight = wavelet * inside.astype(jnp.float32)[None, :]
    senders = receiver_cell.shape[2]
    slots = receiver_cell.shape[3]
    cells = receiver_cell.reshape(-1)
    active = (
        jnp.arange(slots, dtype=jnp.int32)[None, :] < receiver_count.reshape(senders, 1)
    ).astype(jnp.float32)
    active_flat = active.reshape(-1)

    def advance(carry, weights):
        former, current = carry
        drive = laplace(current) + place_sum(source_flat, weights, shape)
        following = (2.0 * current - (1.0 - damping) * former + courant * drive) / (1.0 + damping)
        return (
            (current, following),
            (following - 2.0 * current + former, following.reshape(-1)[cells] * active_flat),
        )

    final_states, (accels, recorded) = lax.scan(advance, (state_prev, state_now), source_weight)
    recorded_tiles = recorded.reshape(STEPS, senders, 1, 1, slots)
    active_tiles = active.reshape(1, senders, 1, 1, slots)
    synthetic, mask_back = (
        lax.all_to_all(recorded_tiles, "gx", split_axis=1, concat_axis=3, tiled=True),
        lax.all_to_all(active_tiles, "gx", split_axis=1, concat_axis=3, tiled=True),
    )
    trace_residual = mask_back * (synthetic - observed)
    misfit = lax.all_to_all(trace_residual, "gx", split_axis=3, concat_axis=1, tiled=True)
    misfit_rows = misfit.reshape(STEPS, senders * slots)

    def retreat(carry, inputs):
        later, current, gradient = carry
        acceleration, residual_row = inputs
        drive = laplace(current) + place_sum(cells, residual_row, shape)
        earlier = (2.0 * current - (1.0 - damping) * later + courant * drive) / (1.0 + damping)
        return ((current, earlier, gradient + earlier * acceleration), None)

    start_gradient = jnp.zeros(shape, jnp.float32)
    (last_later, last_current, gradient), unused = lax.scan(
        retreat, (adjoint_next, adjoint_now, start_gradient), (accels, misfit_rows), reverse=True
    )
    return (gradient, trace_residual)


def solution(mesh):
    placed = (
        P("gx", "gy", None),
        P(("groups", "gx"), "gy", None),
        P(("groups", "gx"), "gy", None),
        P(("groups", "gx"), "gy", None),
        P(("groups", "gx"), "gy", None),
        P("groups"),
        P(None, "groups"),
        P("groups", "gx", "gy", None, None),
        P("gx", "gy", None, None),
        P("gx", "gy", None),
    )
    return jax.shard_map(
        local,
        mesh=mesh,
        in_specs=placed,
        out_specs=(P(("groups", "gx"), "gy", None), P("groups", "gx", "gy", None, None)),
        check_vma=False,
    )
```

```python
import functools

import jax
import jax.numpy as jnp
from jax import lax
from jax.experimental import pallas as pl
from jax.experimental.pallas import tpu as pltpu
from jax.sharding import PartitionSpec as P

STEPS = 12
SPONGE = 8
REACH = 4
DEPTH = 4
LANES = 128
ROWS = 8


stencil = (-205.0 / 72.0, 8.0 / 5.0, -1.0 / 5.0, 8.0 / 315.0, -1.0 / 560.0)
damping_peak = 0.3
scale = 5040.0
weights = (3.0 * -14350.0, 8064.0, -1008.0, 128.0, -9.0)


class Layout:
    def __init__(self, count_x, count_y, width_x, width_y):
        self.count_x, self.count_y = count_x, count_y
        self.width_x, self.width_y = width_x, width_y
        self.chunk = width_y // count_x
        self.wide = width_x * count_x
        self.tiles = self.wide // ROWS
        self.whole_y = width_y * count_y
        self.margin = REACH * DEPTH
        self.extent = self.chunk + 2 * self.margin
        self.kept = self.margin - REACH
        self.inner = self.extent - 2 * REACH
        self.rows = self.chunk * self.wide
        self.cells = self.chunk * width_x
        self.near = self.chunk + 2 * REACH
        self.state_rows = (self.chunk + self.near) * self.wide
        self.lacking = range(REACH, self.chunk - REACH)
        self.send_rows = (self.chunk + len(self.lacking)) * self.wide

    def at(self, place):
        pair, rest = divmod(place, 2 * self.count_x)
        chip, core = divmod(rest, 2)
        slab = chip if pair % 2 == 0 else self.count_x - 1 - chip
        return slab * self.count_y + 2 * pair + core

    def to_chunks(self, turn):
        moves = []
        for slab in range(self.count_x):
            for strip in range(self.count_y):
                moves.append((slab * self.count_y + strip, self.at(strip * self.count_x + (slab ^ turn))))
        return moves

    def to_slabs(self, turn):
        return [(target, source) for source, target in self.to_chunks(turn)]

    def swaps(self, first):
        moves = []
        for place in range(first, self.count_x * self.count_y - 1, 2):
            moves += [(self.at(place), self.at(place + 1)), (self.at(place + 1), self.at(place))]
        return moves


def fits(count_x, count_y, width_x, width_y, depth_z):
    return (
        count_x & (count_x - 1) == 0
        and count_y % 2 == 0
        and width_x == ROWS
        and width_x * count_x == ROWS * REACH
        and depth_z == LANES
        and width_y == count_x * REACH * DEPTH
    )


def f32(*shape):
    return jax.ShapeDtypeStruct(shape, jnp.float32)


def call(
    kernel, ints, arrays, outs, scratch=(), cost=1_000_000, space=pltpu.VMEM, aliases=None, limit=32 * 1024 * 1024
):
    return pl.pallas_call(
        kernel,
        out_shape=tuple(outs),
        in_specs=[pl.BlockSpec(memory_space=pltpu.SMEM)] * len(ints)
        + [pl.BlockSpec(memory_space=space)] * len(arrays),
        out_specs=tuple(pl.BlockSpec(memory_space=pltpu.VMEM) for _ in outs),
        scratch_shapes=list(scratch),
        input_output_aliases=aliases or {},
        compiler_params=pltpu.CompilerParams(vmem_limit_bytes=limit),
        cost_estimate=pl.CostEstimate(flops=cost, bytes_accessed=cost, transcendentals=0),
    )(*ints, *arrays)


def aligned(value, to=ROWS):
    return pl.multiple_of(value, to)


def cut_chunk(lay, slab, turn, fields, target):
    start = (slab ^ turn) * lay.chunk
    for index, field in enumerate(fields):
        for y in range(lay.chunk):
            row = (index * lay.chunk + y) * ROWS
            target[row : row + ROWS, :] = field[pl.ds(start + y, ROWS, stride=lay.width_y), :]


def cut_forward(lay, slab_ref, count_ref, *refs):
    inputs, sends, (held, held_cell, done) = refs[:4], refs[4 : 4 + lay.count_x], refs[4 + lay.count_x :]
    fields = [held.at[index] for index in range(3)]
    copies = [
        pltpu.make_async_copy(source, target, done.at[index])
        for index, (source, target) in enumerate(zip(inputs, fields + [held_cell]))
    ]
    for copy in copies:
        copy.start()
    for copy in copies:
        copy.wait()
    slots = lax.broadcasted_iota(jnp.int32, (1, LANES), 1)
    used = []
    for tile in range(lay.count_x):
        cell = jnp.where(slots < count_ref[tile], held_cell[tile : tile + 1, :], -1)
        used.append(cell.astype(jnp.float32))
    for turn, send in enumerate(sends):
        cut_chunk(lay, slab_ref[0], turn, fields, send)
        for tile in range(lay.count_x):
            row = 3 * lay.cells + tile
            send[row : row + 1, :] = used[tile]


def cut_adjoint(lay, slab_ref, now, prev, observed, *sends):
    for turn, send in enumerate(sends):
        cut_chunk(lay, slab_ref[0], turn, (now, prev), send)
        row = 2 * lay.cells
        send[row : row + observed.shape[0], :] = observed[...]


def join_fields(lay, own_slot, odd, pieces, joined, state, courant, send_next, send_twin):
    fields = joined.shape[0]
    for turn, piece in enumerate(pieces):
        start_x = (own_slot ^ turn) * ROWS
        for field in range(fields):
            for y in range(lay.chunk):
                row = (field * lay.chunk + y) * ROWS
                joined[field, pl.ds(aligned(y * lay.wide + start_x), ROWS), :] = piece[row : row + ROWS, :]
    kept_rows = lay.kept * lay.wide
    for field in range(fields):
        target, first = (state, 0) if field == 0 else (state, (lay.chunk + REACH) * lay.wide)
        if field == 2:
            target, first = courant, 0
        for y in range(lay.chunk):
            for tile in range(lay.tiles):
                values = joined[field, pl.ds(y * lay.wide + tile, ROWS, stride=lay.tiles), :]
                row = y * lay.wide + tile * ROWS
                target[first + row : first + row + ROWS, :] = values
                if field == 0:
                    send_next[row : row + ROWS, :] = values
                    send_twin[row : row + ROWS, :] = values
    for field in range(1, fields):
        source, first = (state, (lay.chunk + REACH) * lay.wide) if field == 1 else (courant, 0)
        place = lay.rows + (field - 1) * kept_rows
        skipped = (lay.chunk - lay.kept) * lay.wide
        ahead = source[pl.ds(aligned(first + odd * skipped), kept_rows), :]
        send_next[place : place + kept_rows, :] = ahead
        behind = source[pl.ds(aligned(first + (1 - odd) * skipped), kept_rows), :]
        send_twin[place : place + kept_rows, :] = behind


def join_forward(lay, where_ref, *refs):
    pieces, (state, courant, send_next, send_twin, codes, joined) = refs[: lay.count_x], refs[lay.count_x :]
    own_slot = where_ref[0]
    join_fields(lay, own_slot, where_ref[1], pieces, joined, state, courant, send_next, send_twin)
    first = 3 * lay.cells
    strip_cells = lay.width_y * LANES
    slab_row = lax.broadcasted_iota(jnp.int32, codes.shape, 0)
    found = jnp.full(codes.shape, -1.0, jnp.float32)
    for turn, piece in enumerate(pieces):
        cell = piece[first : first + lay.count_x, :].astype(jnp.int32)
        used = cell >= 0
        cell = jnp.maximum(cell, 0)
        x = lax.div(cell, jnp.int32(strip_cells))
        y = lax.rem(lax.div(cell, jnp.int32(LANES)), jnp.int32(lay.width_y)) - own_slot * lay.chunk
        inside = used & (y >= 0) & (y < lay.chunk)
        code = jnp.where(inside, (y * ROWS + x) * LANES + lax.rem(cell, jnp.int32(LANES)), -1)
        code = code.astype(jnp.float32)
        line = jnp.concatenate([code[tile : tile + 1, :] for tile in range(lay.count_x)], axis=1)
        found = jnp.where(slab_row == (own_slot ^ turn), jnp.broadcast_to(line, codes.shape), found)
    codes[...] = found


def join_adjoint(lay, where_ref, *refs):
    pieces, (state, send_next, send_twin, joined) = refs[: lay.count_x], refs[lay.count_x :]
    join_fields(lay, where_ref[0], where_ref[1], pieces, joined, state, None, send_next, send_twin)


def load_state(lay, odd, first, now, prev, state, from_next, from_twin):
    wide = lay.wide

    def put(buffer, layer, ref, source, count):
        target = pl.ds(layer * wide if isinstance(layer, int) else aligned(layer * wide), count * wide)
        buffer[target, :] = ref[source * wide : (source + count) * wide, :]

    ahead = lay.margin + lay.chunk
    put(now, lay.margin, state, 0, lay.chunk)
    put(now, odd * ahead, from_next, 0, lay.chunk)
    put(now, (1 - odd) * ahead, from_twin, 0, lay.chunk)
    if first:
        put(prev, lay.margin, state, lay.chunk + REACH, lay.chunk)
        put(prev, odd * ahead + (1 - odd) * REACH, from_next, lay.chunk, lay.kept)
        put(prev, (1 - odd) * ahead + odd * REACH, from_twin, lay.chunk, lay.kept)
        return
    put(prev, lay.margin - REACH, state, lay.chunk, lay.near)
    put(prev, odd * ahead + lay.lacking[0], from_next, lay.chunk, len(lay.lacking))
    put(prev, (1 - odd) * ahead + lay.lacking[0], from_twin, lay.chunk, len(lay.lacking))


def store_state(lay, now, prev, state, send):
    wide = lay.wide

    def put(ref, target, buffer, layer, count):
        ref[target * wide : (target + count) * wide, :] = buffer[layer * wide : (layer + count) * wide, :]

    put(state, 0, now, lay.margin, lay.chunk)
    put(send, 0, now, lay.margin, lay.chunk)
    put(state, lay.chunk, prev, lay.margin - REACH, lay.near)
    put(send, lay.chunk, prev, lay.margin + lay.lacking[0], len(lay.lacking))


def split(values):
    high = values.astype(jnp.bfloat16)
    rest = values - high.astype(jnp.float32)
    middle = rest.astype(jnp.bfloat16)
    low = (rest - middle.astype(jnp.float32)).astype(jnp.bfloat16)
    return high, middle, low


def fill_band(band):
    row = lax.broadcasted_iota(jnp.int32, (2 * LANES, 2 * LANES), 0)
    column = lax.broadcasted_iota(jnp.int32, (2 * LANES, 2 * LANES), 1)
    apart = jnp.where((row < LANES) == (column < LANES), jnp.abs(row - column), 0)
    values = jnp.zeros((2 * LANES, 2 * LANES), jnp.float32)
    for k in range(1, REACH + 1):
        values = jnp.where(apart == k, weights[k], values)
    values = values.astype(jnp.bfloat16)
    for part in range(3):
        band[part * 2 * LANES : (part + 1) * 2 * LANES, :] = values


def multiply_z(lay, first_layer, count, now, band, along_z):
    half = count * lay.wide // 2
    first = first_layer * lay.wide
    parts = [split(now[start : start + half, :]) for start in (first, first + half)]
    both = [side[part] for part in range(3) for side in parts]
    found = jnp.dot(jnp.concatenate(both, axis=1), band[...], preferred_element_type=jnp.float32)
    along_z[0:half, :] = found[:, :LANES]
    along_z[half : 2 * half, :] = found[:, LANES:]


def sweep(lay, step, now, prev, following, half, gain, band, along_z, inject=None):
    first_layer = REACH * (step + 1)
    group = 8
    multiply_z(lay, first_layer, lay.extent - 2 * first_layer, now, band, along_z)
    row = lax.broadcasted_iota(jnp.int32, (ROWS, LANES), 0)
    top, bottom = row == 0, row == ROWS - 1

    def layers(block, carry):
        start = first_layer + group * block
        around = now.at[pl.ds(aligned((start - REACH) * lay.wide), (group + 2 * REACH) * lay.wide)]
        here = pl.ds(aligned(start * lay.wide), group * lay.wide)
        former_rows, target = prev.at[here], following.at[here]
        inner = pl.ds(aligned((start - REACH) * lay.wide), group * lay.wide)
        half_rows, gain_rows = half.at[inner], gain.at[inner]
        added = None if inject is None else inject.at[step, inner]
        z_rows = along_z.at[pl.ds(aligned(block * group * lay.wide), group * lay.wide)]

        def at(y, tile):
            first = ((y + REACH) * lay.tiles + tile) * ROWS
            return around[first : first + ROWS, :]

        for y in range(group):
            center = [at(y, tile) for tile in range(lay.tiles)]
            lower = [jnp.where(top, 0.0, pltpu.roll(tile, 1, 0)) for tile in center]
            upper = [jnp.where(bottom, 0.0, pltpu.roll(tile, ROWS - 1, 0)) for tile in center]
            line = lower + center + upper
            for tile in range(lay.tiles):
                place = (y * lay.tiles + tile) * ROWS
                place = slice(place, place + ROWS)
                total = z_rows[place, :] + weights[0] * center[tile]
                for k in range(1, REACH + 1):
                    pair = line[lay.tiles + tile - k] + line[lay.tiles + tile + k]
                    total = total + weights[k] * (pair + (at(y - k, tile) + at(y + k, tile)))
                if added is not None:
                    total = total + added[pl.ds(y * lay.wide + tile, ROWS, stride=lay.tiles), :]
                former = former_rows[place, :]
                change = (center[tile] - former) + half_rows[place, :] * total
                target[place, :] = former + gain_rows[place, :] * change
        return carry

    lax.fori_loop(0, (lay.extent - 2 * first_layer) // group, layers, 0)


def keep_own(lay, step, following, history):
    first = lay.margin * lay.wide
    history[step * lay.rows : (step + 1) * lay.rows, :] = following[first : first + lay.rows, :]


def forward(lay, phase, sources, ints, state, from_next, from_twin, courant, gain, drive, *refs):
    first, last = phase == 0, phase == STEPS // DEPTH - 1
    refs = list(refs)
    history = refs.pop(0)
    half = refs.pop(0) if first else courant
    if not last:
        state_out, send = refs.pop(0), refs.pop(0)
    now, prev, following, band, along_z, pulse = refs
    odd = ints[0]

    fill_band(band)
    load_state(lay, odd, first, now, prev, state, from_next, from_twin)
    if first:
        tail = (lay.chunk + lay.kept) * lay.wide
        part = lay.kept * lay.wide
        half[part : part + lay.rows, :] = (0.5 / scale) * courant[...]
        ahead = part + lay.rows
        half[pl.ds(aligned(odd * ahead), part), :] = (0.5 / scale) * from_next[tail : tail + part, :]
        half[pl.ds(aligned((1 - odd) * ahead), part), :] = (0.5 / scale) * from_twin[tail : tail + part, :]
    for source in range(sources):
        flat = pl.ds(ints[1 + sources + source], 1)
        pulse[source : source + 1, :] = scale * (half[flat, :] * gain[flat, :])

    for step in range(DEPTH):
        sweep(lay, step, now, prev, following, half, gain, band, along_z)
        added = pulse[...] * drive[phase * DEPTH + step]
        places = [pl.ds(ints[1 + source], 1) for source in range(sources)]
        lines = [following[place, :] for place in places]
        for source, (place, line) in enumerate(zip(places, lines)):
            following[place, :] = line + added[source : source + 1, :]
        keep_own(lay, step, following, history)
        now, prev, following = following, now, prev

    if not last:
        store_state(lay, now, prev, state_out, send)


def slot_rows(codes, slab):
    code = codes[slab : slab + 1, :].astype(jnp.int32)
    row = jnp.where(code >= 0, lax.shift_right_arithmetic(code, 7), -1)
    return row, jnp.where(code >= 0, code & (LANES - 1), -1)


def record_slots(lay, history, codes, plain, record):
    for step in range(DEPTH):
        for y in range(lay.chunk):
            for tile in range(lay.tiles):
                row = step * lay.rows + y * lay.wide
                values = history[row + tile * ROWS : row + (tile + 1) * ROWS, :]
                plain[pl.ds(row + tile, ROWS, stride=lay.tiles), :] = values
    slots = codes.shape[1]
    width = 2 * LANES
    for slab in range(lay.count_x):
        cell_row, cell_z = slot_rows(codes, slab)
        tiles = []
        for step in range(DEPTH):
            for y in range(lay.chunk):
                row = step * lay.rows + y * lay.wide + slab * ROWS
                tiles.append(plain[row : row + ROWS, :])
        parts = jnp.concatenate(split(jnp.concatenate(tiles, axis=0)), axis=1)
        for start in range(0, slots, width):
            here = slice(start, start + width)
            z = lax.broadcasted_iota(jnp.int32, (LANES, width), 0)
            pick = jnp.where(z == cell_z[:, here], 1.0, 0.0).astype(jnp.bfloat16)
            found = jnp.dot(parts, jnp.concatenate([pick] * 3, axis=0), preferred_element_type=jnp.float32)
            wanted = lax.broadcasted_iota(jnp.int32, (lay.cells, width), 0) == cell_row[:, here]
            for step in range(DEPTH):
                part = jnp.where(wanted, found[step * lay.cells : (step + 1) * lay.cells, :], 0.0)
                row = step * lay.count_x + slab
                record[row : row + 1, here] = jnp.sum(part, axis=0, keepdims=True)


def record_phase(lay, history, codes, record, plain):
    record_slots(lay, history, codes, plain, record)


def record_last(lay, phases, where_ref, history, codes, *refs):
    earlier, refs = refs[: phases - 1], refs[phases - 1 :]
    observed, (misfit, plain, record) = refs[: lay.count_x], refs[lay.count_x :]
    record_slots(lay, history, codes, plain, record)
    block = DEPTH * lay.count_x
    for index, part in enumerate(list(earlier) + [record]):
        misfit[index * block : (index + 1) * block, :] = part[...]
    total = STEPS * lay.count_x
    for slab in range(lay.count_x):
        misfit[total + slab : total + slab + 1, :] = codes[slab : slab + 1, :]
    for turn, piece in enumerate(observed):
        place = pl.ds(aligned((where_ref[0] ^ turn) * LANES, LANES), LANES)
        used = jnp.concatenate([codes[:, place]] * STEPS, axis=0) >= 0
        seen = piece[2 * lay.cells : 2 * lay.cells + total, :]
        misfit[0:total, place] = jnp.where(used, misfit[0:total, place] - seen, 0.0)


def spread(lay, phase, side, misfit, inject):
    codes = misfit[STEPS * lay.count_x : (STEPS + 1) * lay.count_x, :]
    for slab in range(lay.count_x):
        cell_row, cell_z = slot_rows(codes, slab)
        slots = cell_row.shape[1]
        z = lax.broadcasted_iota(jnp.int32, (LANES, slots), 0)
        pick = jnp.where(z == cell_z, 1.0, 0.0).astype(jnp.bfloat16)
        hit = lax.broadcasted_iota(jnp.int32, (lay.cells, slots), 0) == cell_row
        hit = jnp.where(hit, 1.0, 0.0).astype(jnp.bfloat16)
        left, spans = [], []
        for step in range(DEPTH):
            low, high = 0, lay.chunk
            if side < 0:
                low = REACH * (step + 1) - lay.margin + lay.chunk
            if side > 0:
                high = lay.margin - REACH * (step + 1)
            if low >= high:
                continue
            row = (STEPS - 1 - phase * DEPTH - step) * lay.count_x + slab
            parts = split(scale * misfit[row : row + 1, :])
            left += [hit[low * ROWS : high * ROWS, :] * part for part in parts]
            spans.append((step, low, high))
        placed = lax.dot_general(
            jnp.concatenate(left, axis=0),
            pick,
            (((1,), (1,)), ((), ())),
            preferred_element_type=jnp.float32,
        )
        at = 0
        for step, low, high in spans:
            rows = (high - low) * ROWS
            total = placed[at : at + rows, :]
            for part in (1, 2):
                total = total + placed[at + part * rows : at + (part + 1) * rows, :]
            for y in range(low, high):
                layer = lay.margin + side * lay.chunk + y - REACH
                target = layer * lay.wide + slab * ROWS
                inject[step, target : target + ROWS, :] = total[(y - low) * ROWS : (y - low + 1) * ROWS, :]
            at += 3 * rows


def spread_own(lay, phase, misfit, inject):
    spread(lay, phase, 0, misfit, inject)


def spread_sides(lay, phase, where_ref, own, misfit_next, misfit_twin, inject):
    odd = where_ref[1]

    @pl.when(odd == 1)
    def ahead_is_next():
        spread(lay, phase, 1, misfit_next, inject)
        spread(lay, phase, -1, misfit_twin, inject)

    @pl.when(odd == 0)
    def behind_is_next():
        spread(lay, phase, -1, misfit_next, inject)
        spread(lay, phase, 1, misfit_twin, inject)


def backward(lay, phase, where_ref, state, from_next, from_twin, half, gain, inject, *refs):
    first, last = phase == 0, phase == STEPS // DEPTH - 1
    refs = list(refs)
    history = refs.pop(0)
    if not last:
        state_out, send = refs.pop(0), refs.pop(0)
    now, prev, following, band, along_z = refs

    fill_band(band)
    load_state(lay, where_ref[1], first, now, prev, state, from_next, from_twin)
    for step in range(DEPTH):
        sweep(lay, step, now, prev, following, half, gain, band, along_z, inject)
        keep_own(lay, step, following, history)
        now, prev, following = following, now, prev
    if not last:
        store_state(lay, now, prev, state_out, send)


def add_gradient(lay, before, adjoint, history, state, gradient):
    def layer(y, carry):
        place = aligned(y * lay.wide)
        own = pl.ds(place, lay.wide)
        fields = [state[pl.ds(aligned(place + (lay.chunk + REACH) * lay.wide), lay.wide), :], state[own, :]]
        fields += [history[pl.ds(aligned(place + step * lay.rows), lay.wide), :] for step in range(DEPTH)]
        total = None if before is None else before[own, :]
        for step in range(DEPTH):
            index = DEPTH - 1 - step
            accel = (fields[index + 2] - fields[index + 1]) - (fields[index + 1] - fields[index])
            term = adjoint[pl.ds(aligned(place + step * lay.rows), lay.wide), :] * accel
            total = term if total is None else total + term
        gradient[own, :] = total
        return carry

    lax.fori_loop(0, lay.chunk, layer, 0)


def gradient_first(lay, adjoint, history, state, gradient):
    add_gradient(lay, None, adjoint, history, state, gradient)


def gradient_later(lay, adjoint, history, state, before, gradient):
    add_gradient(lay, before, adjoint, history, state, gradient)


def gradient_last(lay, where_ref, adjoint, history, state, before, misfit, *refs):
    sends, (gradient, plain) = refs[: lay.count_x], refs[lay.count_x :]
    add_gradient(lay, before, adjoint, history, state, gradient)
    for y in range(lay.chunk):
        for tile in range(lay.tiles):
            row = y * lay.wide + tile * ROWS
            plain[pl.ds(y * lay.wide + tile, ROWS, stride=lay.tiles), :] = gradient[row : row + ROWS, :]
    total = STEPS * lay.count_x
    for turn, send in enumerate(sends):
        other = where_ref[0] ^ turn
        for y in range(lay.chunk):
            source = pl.ds(aligned(y * lay.wide + other * ROWS), ROWS)
            send[y * ROWS : (y + 1) * ROWS, :] = plain[source, :]
        tile = pl.ds(aligned(other * LANES, LANES), LANES)
        send[lay.cells : lay.cells + total, :] = misfit[0:total, tile]


def finish(lay, slab_ref, *refs):
    pieces, (gradient, residual) = refs[: lay.count_x], refs[lay.count_x :]
    total = None
    for turn, piece in enumerate(pieces):
        start = (slab_ref[0] ^ turn) * lay.chunk
        for x in range(ROWS):
            target = pl.ds(aligned(x * lay.width_y + start), lay.chunk)
            gradient[target, :] = piece[pl.ds(x, lay.chunk, stride=ROWS), :]
        part = piece[lay.cells : lay.cells + residual.shape[0], :]
        total = part if total is None else total + part
    residual[...] = total


def gain_rows(lay, first_y):
    x = jnp.arange(ROWS)[None, :] * lay.tiles + jnp.arange(lay.tiles)[:, None]
    y = first_y + REACH + jnp.arange(lay.inner)

    def ramp(position, count):
        gap = jnp.minimum(position, count - 1 - position)
        profile = jnp.maximum(SPONGE - gap, 0).astype(jnp.float32) / SPONGE
        return profile * profile

    damping = damping_peak * (ramp(x, lay.wide)[None] + ramp(y, lay.whole_y)[:, None, None])
    gain = (2.0 / (1.0 + damping)).reshape(lay.inner * lay.wide, 1)
    return jnp.broadcast_to(gain, (lay.inner * lay.wide, LANES))


def source_rows(lay, first_y, source_cell, wavelet):
    x = source_cell // (lay.whole_y * LANES)
    y = source_cell // LANES % lay.whole_y - first_y
    z = source_cell % LANES
    inside = (y >= REACH) & (y < lay.extent - REACH)
    tile, row = x % lay.tiles, x // lay.tiles
    flat = jnp.where(inside, (y - REACH) * lay.wide + tile * ROWS + row, 0)
    buffer_row = jnp.where(inside, flat + REACH * lay.wide, 0)
    same = (buffer_row[:, None] == buffer_row[None, :]) & inside[None, :]
    spot = (z[:, None] == jnp.arange(LANES)[None, :]).astype(jnp.float32)
    lines = jnp.where(same[None, :, :, None], wavelet[:, None, :, None] * spot[None, None], 0.0)
    return buffer_row, flat, jnp.sum(lines, axis=2)


def local_tiles(
    lay,
    courant,
    state_prev,
    state_now,
    adjoint_now,
    adjoint_next,
    source_cell,
    wavelet,
    observed,
    receiver_cell,
    receiver_count,
):
    axes = ("gx", "gy")
    slab = lax.axis_index("gx")
    strip = lax.axis_index("gy")
    pair = strip // 2
    chip = jnp.where(pair % 2 == 0, slab, lay.count_x - 1 - slab)
    place = (pair * lay.count_x + chip) * 2 + strip % 2
    odd = strip % 2
    first_y = place * lay.chunk - lay.margin
    slab_int = slab.reshape(1).astype(jnp.int32)
    where = jnp.stack([place % lay.count_x, odd]).astype(jnp.int32)

    count = lay.count_x
    sources = source_cell.shape[0]
    slots = count * receiver_cell.shape[3]
    flat = lambda values: values.reshape(-1, LANES)
    part = functools.partial

    def swap(to_next, to_twin):
        return (
            lax.ppermute(to_next, axes, lay.swaps(1)),
            lax.ppermute(to_twin, axes, lay.swaps(0)),
        )

    def after(value, others):
        return lax.optimization_barrier((value, others))[0]

    buffer_row, flat_row, drive = source_rows(lay, first_y, source_cell, wavelet)
    gain = gain_rows(lay, first_y)
    ints = jnp.concatenate([odd.reshape(1), buffer_row, flat_row]).astype(jnp.int32)

    traces = flat(observed)
    forward_rows = 3 * lay.cells + -(-count // ROWS) * ROWS
    back_rows = 2 * lay.cells + traces.shape[0]
    cuts = call(
        part(cut_forward, lay),
        (slab_int, receiver_count.reshape(-1)),
        [flat(field) for field in (state_now, state_prev, courant)] + [receiver_cell.reshape(count, LANES)],
        [f32(forward_rows, LANES)] * count,
        [
            pltpu.VMEM((3, lay.width_x * lay.width_y, LANES), jnp.float32),
            pltpu.VMEM((count, LANES), jnp.int32),
            pltpu.SemaphoreType.DMA((4,)),
        ],
        space=pltpu.HBM,
        limit=60 * 1024 * 1024,
    )
    back_cuts = call(
        part(cut_adjoint, lay),
        (slab_int,),
        [flat(adjoint_now), flat(adjoint_next), traces],
        [f32(back_rows, LANES)] * count,
    )
    pieces = [lax.ppermute(cut, axes, lay.to_chunks(turn)) for turn, cut in enumerate(cuts)]
    pieces, ints, gain, drive, back_cuts = lax.optimization_barrier((pieces, ints, gain, drive, back_cuts))
    kept_rows = lay.kept * lay.wide
    state, own_courant, to_next, to_twin, codes = call(
        part(join_forward, lay),
        (where,),
        pieces,
        [f32(lay.state_rows, LANES), f32(lay.rows, LANES)]
        + [f32(lay.rows + 2 * kept_rows, LANES)] * 2
        + [f32(count, slots)],
        [pltpu.VMEM((3, lay.rows, LANES), jnp.float32)],
    )
    from_next, from_twin = swap(to_next, to_twin)

    back_pieces = [None] * count

    def move_adjoint(turns, earlier):
        for turn in turns:
            back_pieces[turn] = lax.ppermute(after(back_cuts[turn], earlier), axes, lay.to_chunks(turn))

    move_adjoint(range(1, count), codes)
    move_adjoint(range(1), from_twin)

    phases = STEPS // DEPTH
    step_cost = 8_000_000
    side_cost = 4_000_000
    history_shape = f32(DEPTH * lay.rows, LANES)
    state_shapes = [f32(lay.state_rows, LANES), f32(lay.send_rows, LANES)]
    buffers = [pltpu.VMEM((lay.extent * lay.wide, LANES), jnp.float32)] * 3
    buffers += [pltpu.VMEM((6 * LANES, 2 * LANES), jnp.bfloat16)]
    buffers += [pltpu.VMEM((lay.inner * lay.wide, LANES), jnp.float32)]
    record_scratch = [pltpu.VMEM((DEPTH * lay.rows, LANES), jnp.float32)]
    record_shape = (DEPTH * count, slots)
    histories, states, records = [], [], []
    half = own_courant
    for phase in range(phases):
        first, last = phase == 0, phase == phases - 1
        outs = [history_shape]
        if first:
            outs.append(f32(lay.inner * lay.wide, LANES))
        if not last:
            outs += state_shapes
        results = list(
            call(
                part(forward, lay, phase, sources),
                (ints,),
                [state, from_next, from_twin, half, gain, drive],
                outs,
                buffers + [pltpu.VMEM((sources, LANES), jnp.float32)],
                cost=step_cost,
            )
        )
        histories.append(results.pop(0))
        states.append(state)
        if first:
            half = results.pop(0)
        if last:
            continue
        state, send = results
        if first:
            send = after(send, back_pieces)
        from_next, from_twin = swap(send, send)
    for history in histories[:-1]:
        records += call(
            part(record_phase, lay),
            (),
            [history, codes],
            [f32(*record_shape)],
            record_scratch,
            cost=side_cost,
        )
    back_state, to_next, to_twin = call(
        part(join_adjoint, lay),
        (where,),
        back_pieces,
        [f32(lay.state_rows, LANES)] + [f32(lay.rows + kept_rows, LANES)] * 2,
        [pltpu.VMEM((2, lay.rows, LANES), jnp.float32)],
    )
    back_from_next, back_from_twin = swap(to_next, to_twin)
    (misfit,) = call(
        part(record_last, lay, phases),
        (where,),
        [histories[-1], codes] + records + back_pieces,
        [f32(-(-(STEPS + 1) * count // ROWS) * ROWS, slots)],
        record_scratch + [pltpu.VMEM(record_shape, jnp.float32)],
        cost=side_cost,
    )

    misfit = after(misfit, [back_from_next, back_from_twin])
    misfit_next, misfit_twin = swap(misfit, misfit)
    state, from_next, from_twin = back_state, back_from_next, back_from_twin
    gradient = None
    inject_shape = f32(DEPTH, lay.inner * lay.wide, LANES)
    for phase in range(phases):
        first, last = phase == 0, phase == phases - 1
        (inject,) = call(part(spread_own, lay, phase), (), [misfit], [inject_shape], cost=side_cost)
        (inject,) = call(
            part(spread_sides, lay, phase),
            (where,),
            [inject, misfit_next, misfit_twin],
            [inject_shape],
            cost=side_cost,
            aliases={1: 0},
        )
        results = call(
            part(backward, lay, phase),
            (where,),
            [state, from_next, from_twin, half, gain, inject],
            [history_shape] + ([] if last else state_shapes),
            buffers,
            cost=step_cost,
        )
        arrays = [results[0], histories[phases - 1 - phase], states[phases - 1 - phase]]
        if last:
            sends = call(
                part(gradient_last, lay),
                (where,),
                arrays + [gradient, misfit],
                [f32(lay.cells + traces.shape[0], LANES)] * count,
                [pltpu.VMEM((lay.rows, LANES), jnp.float32)] * 2,
            )
            continue
        _, state, send = results
        from_next, from_twin = swap(send, send)
        kernel = gradient_first if first else gradient_later
        (gradient,) = call(
            part(kernel, lay), (), arrays + ([] if first else [gradient]), [f32(lay.rows, LANES)], cost=side_cost
        )
    pieces = [lax.ppermute(send, axes, lay.to_slabs(turn)) for turn, send in enumerate(sends)]
    gradient, residual = call(
        part(finish, lay),
        (slab_int,),
        pieces,
        [f32(lay.width_x * lay.width_y, LANES), f32(*traces.shape)],
    )
    return gradient.reshape(courant.shape), residual.reshape(observed.shape)


def local(courant, *rest):
    width_x, width_y, depth_z = courant.shape
    count_x, count_y = lax.axis_size("gx"), lax.axis_size("gy")
    if fits(count_x, count_y, width_x, width_y, depth_z):
        return local_tiles(Layout(count_x, count_y, width_x, width_y), courant, *rest)
    return local_blocks(courant, *rest)


def padded_2(cells, sides, width):
    for axis, dim in sides:
        count = lax.axis_size(axis)
        ends = count - 1
        head = lax.slice_in_dim(cells, 0, width, axis=dim)
        tail = lax.slice_in_dim(cells, cells.shape[dim] - width, cells.shape[dim], axis=dim)
        cells = jnp.concatenate(
            [
                lax.ppermute(tail, axis, [(i, (i + 1) % count) for i in range(ends)]),
                cells,
                lax.ppermute(head, axis, [((i + 1) % count, i) for i in range(ends)]),
            ],
            axis=dim,
        )
    return cells


def laplace(values):
    width_x, width_y, depth_z = values.shape
    padded = padded_2(values, (("gx", 0), ("gy", 1)), 4)
    z_padded = jnp.pad(values, ((0, 0), (0, 0), (4, 4)))
    summed = 3.0 * stencil[0] * values
    for offset in range(1, 5):
        paired = (
            padded[4 + offset : 4 + offset + width_x, 4 : 4 + width_y]
            + padded[4 - offset : 4 - offset + width_x, 4 : 4 + width_y]
        )
        paired = (
            paired
            + padded[4 : 4 + width_x, 4 + offset : 4 + offset + width_y]
            + padded[4 : 4 + width_x, 4 - offset : 4 - offset + width_y]
        )
        paired = (
            paired
            + z_padded[:, :, 4 + offset : 4 + offset + depth_z]
            + z_padded[:, :, 4 - offset : 4 - offset + depth_z]
        )
        summed = summed + stencil[offset] * paired
    return summed


def sponge(start, count, whole):
    position = start + jnp.arange(count, dtype=jnp.int32)
    edge_gap = jnp.minimum(position, whole - 1 - position)
    profile = jnp.maximum(SPONGE - edge_gap, 0).astype(jnp.float32) / SPONGE
    return profile * profile


def place_sum(indices, amounts, shape):
    flat = jnp.zeros((shape[0] * shape[1] * shape[2],), jnp.float32).at[indices].add(amounts)
    return flat.reshape(shape)


def local_blocks(
    courant,
    state_prev,
    state_now,
    adjoint_now,
    adjoint_next,
    source_cell,
    wavelet,
    observed,
    receiver_cell,
    receiver_count,
):
    shape = courant.shape
    width_x, width_y, depth_z = shape
    slab = lax.axis_index("gx")
    strip = lax.axis_index("gy")
    whole_x = width_x * lax.axis_size("gx")
    whole_y = width_y * lax.axis_size("gy")
    damping = damping_peak * (
        sponge(slab * width_x, width_x, whole_x)[:, None, None]
        + sponge(strip * width_y, width_y, whole_y)[None, :, None]
    )
    source_x = source_cell // (whole_y * depth_z) - slab * width_x
    source_y = source_cell // depth_z % whole_y - strip * width_y
    source_z = source_cell % depth_z
    inside = (source_x >= 0) & (source_x < width_x) & (source_y >= 0) & (source_y < width_y)
    source_flat = jnp.where(inside, (source_x * width_y + source_y) * depth_z + source_z, 0)
    source_weight = wavelet * inside.astype(jnp.float32)[None, :]
    senders = receiver_cell.shape[2]
    slots = receiver_cell.shape[3]
    cells = receiver_cell.reshape(-1)
    active = (
        jnp.arange(slots, dtype=jnp.int32)[None, :] < receiver_count.reshape(senders, 1)
    ).astype(jnp.float32)
    active_flat = active.reshape(-1)

    def advance(carry, weights):
        former, current = carry
        drive = laplace(current) + place_sum(source_flat, weights, shape)
        following = (2.0 * current - (1.0 - damping) * former + courant * drive) / (1.0 + damping)
        return (
            (current, following),
            (following - 2.0 * current + former, following.reshape(-1)[cells] * active_flat),
        )

    final_states, (accels, recorded) = lax.scan(advance, (state_prev, state_now), source_weight)
    recorded_tiles = recorded.reshape(STEPS, senders, 1, 1, slots)
    active_tiles = active.reshape(1, senders, 1, 1, slots)
    synthetic, mask_back = (
        lax.all_to_all(recorded_tiles, "gx", split_axis=1, concat_axis=3, tiled=True),
        lax.all_to_all(active_tiles, "gx", split_axis=1, concat_axis=3, tiled=True),
    )
    trace_residual = mask_back * (synthetic - observed)
    misfit = lax.all_to_all(trace_residual, "gx", split_axis=3, concat_axis=1, tiled=True)
    misfit_rows = misfit.reshape(STEPS, senders * slots)

    def retreat(carry, inputs):
        later, current, gradient = carry
        acceleration, residual_row = inputs
        drive = laplace(current) + place_sum(cells, residual_row, shape)
        earlier = (2.0 * current - (1.0 - damping) * later + courant * drive) / (1.0 + damping)
        return ((current, earlier, gradient + earlier * acceleration), None)

    start_gradient = jnp.zeros(shape, jnp.float32)
    (last_later, last_current, gradient), unused = lax.scan(
        retreat, (adjoint_next, adjoint_now, start_gradient), (accels, misfit_rows), reverse=True
    )
    return (gradient, trace_residual)


def solution(mesh):
    placed = (
        P("gx", "gy", None),
        P(("groups", "gx"), "gy", None),
        P(("groups", "gx"), "gy", None),
        P(("groups", "gx"), "gy", None),
        P(("groups", "gx"), "gy", None),
        P("groups"),
        P(None, "groups"),
        P("groups", "gx", "gy", None, None),
        P("gx", "gy", None, None),
        P("gx", "gy", None),
    )
    return jax.shard_map(
        local,
        mesh=mesh,
        in_specs=placed,
        out_specs=(P(("groups", "gx"), "gy", None), P("groups", "gx", "gy", None, None)),
        check_vma=False,
    )
```

```python
import functools

import jax
import jax.numpy as jnp
from jax import lax
from jax.experimental import pallas as pl
from jax.experimental.pallas import tpu as pltpu
from jax.sharding import PartitionSpec as P

STEPS = 12
SPONGE = 8
REACH = 4
DEPTH = 4
LANES = 128
ROWS = 8
LAYERS = (4, 2, 1)


stencil = (-205.0 / 72.0, 8.0 / 5.0, -1.0 / 5.0, 8.0 / 315.0, -1.0 / 560.0)
damping_peak = 0.3
scale = 5040.0
weights = (3.0 * -14350.0, 8064.0, -1008.0, 128.0, -9.0)


class Layout:
    def __init__(self, count_x, count_y, width_x, width_y):
        self.count_x, self.count_y = count_x, count_y
        self.width_x, self.width_y = width_x, width_y
        self.chunk = width_y // count_x
        self.wide = width_x * count_x
        self.tiles = self.wide // ROWS
        self.whole_y = width_y * count_y
        self.margin = REACH * DEPTH
        self.extent = self.chunk + 2 * self.margin
        self.kept = self.margin - REACH
        self.inner = self.extent - 2 * REACH
        self.rows = self.chunk * self.wide
        self.cells = self.chunk * width_x
        self.near = self.chunk + 2 * REACH
        self.state_rows = (self.chunk + self.near) * self.wide
        self.lacking = range(REACH, self.chunk - REACH)
        self.send_rows = (self.chunk + len(self.lacking)) * self.wide

    def at(self, place):
        pair, rest = divmod(place, 2 * self.count_x)
        chip, core = divmod(rest, 2)
        slab = chip if pair % 2 == 0 else self.count_x - 1 - chip
        return slab * self.count_y + 2 * pair + core

    def to_chunks(self, turn):
        moves = []
        for slab in range(self.count_x):
            for strip in range(self.count_y):
                moves.append((slab * self.count_y + strip, self.at(strip * self.count_x + (slab ^ turn))))
        return moves

    def to_slabs(self, turn):
        return [(target, source) for source, target in self.to_chunks(turn)]

    def across(self):
        far = self.count_x // 2
        return [(self.at(place), self.at(place ^ far)) for place in range(self.count_x * self.count_y)]

    def home(self):
        moves = []
        for strip in range(self.count_y):
            for slot in range(self.count_x):
                moves.append((self.at(strip * self.count_x + slot), slot * self.count_y + strip))
        return moves

    def swaps(self, first):
        moves = []
        for place in range(first, self.count_x * self.count_y - 1, 2):
            moves += [(self.at(place), self.at(place + 1)), (self.at(place + 1), self.at(place))]
        return moves


def fits(count_x, count_y, width_x, width_y, depth_z):
    return (
        count_x & (count_x - 1) == 0
        and count_x == 4
        and count_y % 2 == 0
        and width_x == ROWS
        and width_x * count_x == ROWS * REACH
        and depth_z == LANES
        and width_y == count_x * REACH * DEPTH
    )


def f32(*shape):
    return jax.ShapeDtypeStruct(shape, jnp.float32)


def call(
    kernel, ints, arrays, outs, scratch=(), cost=1_000_000, space=pltpu.VMEM, aliases=None, limit=32 * 1024 * 1024
):
    return pl.pallas_call(
        kernel,
        out_shape=tuple(outs),
        in_specs=[pl.BlockSpec(memory_space=pltpu.SMEM)] * len(ints)
        + [pl.BlockSpec(memory_space=space)] * len(arrays),
        out_specs=tuple(pl.BlockSpec(memory_space=pltpu.VMEM) for _ in outs),
        scratch_shapes=list(scratch),
        input_output_aliases=aliases or {},
        compiler_params=pltpu.CompilerParams(vmem_limit_bytes=limit),
        cost_estimate=pl.CostEstimate(flops=cost, bytes_accessed=cost, transcendentals=0),
    )(*ints, *arrays)


def aligned(value, to=ROWS):
    return pl.multiple_of(value, to)


def cut_chunk(lay, slab, turn, fields, target):
    start = (slab ^ turn) * lay.chunk
    for index, field in enumerate(fields):
        for y in range(lay.chunk):
            row = (index * lay.chunk + y) * ROWS
            target[row : row + ROWS, :] = field[pl.ds(start + y, ROWS, stride=lay.width_y), :]


def cut_forward(lay, slab_ref, count_ref, *refs):
    inputs, sends, (held, held_cell, done) = refs[:4], refs[4 : 4 + lay.count_x], refs[4 + lay.count_x :]
    fields = [held.at[index] for index in range(3)]
    copies = [
        pltpu.make_async_copy(source, target, done.at[index])
        for index, (source, target) in enumerate(zip(inputs, fields + [held_cell]))
    ]
    for copy in copies:
        copy.start()
    for copy in copies:
        copy.wait()
    slots = lax.broadcasted_iota(jnp.int32, (1, LANES), 1)
    used = []
    for tile in range(lay.count_x):
        cell = jnp.where(slots < count_ref[tile], held_cell[tile : tile + 1, :], -1)
        used.append(cell.astype(jnp.float32))
    for turn, send in enumerate(sends):
        cut_chunk(lay, slab_ref[0], turn, fields, send)
        for tile in range(lay.count_x):
            row = 3 * lay.cells + tile
            send[row : row + 1, :] = used[tile]


def cut_adjoint(lay, slab_ref, now, prev, observed, *sends):
    for turn, send in enumerate(sends):
        cut_chunk(lay, slab_ref[0], turn, (now, prev), send)
        row = 2 * lay.cells
        send[row : row + observed.shape[0], :] = observed[...]


def join_fields(lay, own_slot, odd, pieces, joined, state, courant, send_next, send_twin):
    fields = joined.shape[0]
    for turn, piece in enumerate(pieces):
        start_x = (own_slot ^ turn) * ROWS
        for field in range(fields):
            for y in range(lay.chunk):
                row = (field * lay.chunk + y) * ROWS
                joined[field, pl.ds(aligned(y * lay.wide + start_x), ROWS), :] = piece[row : row + ROWS, :]
    kept_rows = lay.kept * lay.wide
    for field in range(fields):
        target, first = (state, 0) if field == 0 else (state, (lay.chunk + REACH) * lay.wide)
        if field == 2:
            target, first = courant, 0
        for y in range(lay.chunk):
            for tile in range(lay.tiles):
                values = joined[field, pl.ds(y * lay.wide + tile, ROWS, stride=lay.tiles), :]
                row = y * lay.wide + tile * ROWS
                target[first + row : first + row + ROWS, :] = values
                if field == 0:
                    send_next[row : row + ROWS, :] = values
                    send_twin[row : row + ROWS, :] = values
    for field in range(1, fields):
        source, first = (state, (lay.chunk + REACH) * lay.wide) if field == 1 else (courant, 0)
        place = lay.rows + (field - 1) * kept_rows
        skipped = (lay.chunk - lay.kept) * lay.wide
        ahead = source[pl.ds(aligned(first + odd * skipped), kept_rows), :]
        send_next[place : place + kept_rows, :] = ahead
        behind = source[pl.ds(aligned(first + (1 - odd) * skipped), kept_rows), :]
        send_twin[place : place + kept_rows, :] = behind


def join_forward(lay, where_ref, *refs):
    pieces, (state, courant, send_next, send_twin, codes, joined) = refs[: lay.count_x], refs[lay.count_x :]
    own_slot = where_ref[0]
    join_fields(lay, own_slot, where_ref[1], pieces, joined, state, courant, send_next, send_twin)
    first = 3 * lay.cells
    strip_cells = lay.width_y * LANES
    slab_row = lax.broadcasted_iota(jnp.int32, codes.shape, 0)
    found = jnp.full(codes.shape, -1.0, jnp.float32)
    for turn, piece in enumerate(pieces):
        cell = piece[first : first + lay.count_x, :].astype(jnp.int32)
        used = cell >= 0
        cell = jnp.maximum(cell, 0)
        x = lax.div(cell, jnp.int32(strip_cells))
        y = lax.rem(lax.div(cell, jnp.int32(LANES)), jnp.int32(lay.width_y)) - own_slot * lay.chunk
        inside = used & (y >= 0) & (y < lay.chunk)
        code = jnp.where(inside, (y * ROWS + x) * LANES + lax.rem(cell, jnp.int32(LANES)), -1)
        code = code.astype(jnp.float32)
        line = jnp.concatenate([code[tile : tile + 1, :] for tile in range(lay.count_x)], axis=1)
        found = jnp.where(slab_row == (own_slot ^ turn), jnp.broadcast_to(line, codes.shape), found)
    codes[...] = found


def join_adjoint(lay, where_ref, *refs):
    pieces, (state, send_next, send_twin, joined) = refs[: lay.count_x], refs[lay.count_x :]
    join_fields(lay, where_ref[0], where_ref[1], pieces, joined, state, None, send_next, send_twin)


def load_state(lay, odd, first, now, prev, state, from_next, from_twin):
    wide = lay.wide

    def put(buffer, layer, ref, source, count):
        target = pl.ds(layer * wide if isinstance(layer, int) else aligned(layer * wide), count * wide)
        buffer[target, :] = ref[source * wide : (source + count) * wide, :]

    ahead = lay.margin + lay.chunk
    put(now, lay.margin, state, 0, lay.chunk)
    put(now, odd * ahead, from_next, 0, lay.chunk)
    put(now, (1 - odd) * ahead, from_twin, 0, lay.chunk)
    if first:
        put(prev, lay.margin, state, lay.chunk + REACH, lay.chunk)
        put(prev, odd * ahead + (1 - odd) * REACH, from_next, lay.chunk, lay.kept)
        put(prev, (1 - odd) * ahead + odd * REACH, from_twin, lay.chunk, lay.kept)
        return
    put(prev, lay.margin - REACH, state, lay.chunk, lay.near)
    put(prev, odd * ahead + lay.lacking[0], from_next, lay.chunk, len(lay.lacking))
    put(prev, (1 - odd) * ahead + lay.lacking[0], from_twin, lay.chunk, len(lay.lacking))


def store_state(lay, now, prev, state, send):
    wide = lay.wide

    def put(ref, target, buffer, layer, count):
        ref[target * wide : (target + count) * wide, :] = buffer[layer * wide : (layer + count) * wide, :]

    put(state, 0, now, lay.margin, lay.chunk)
    put(send, 0, now, lay.margin, lay.chunk)
    put(state, lay.chunk, prev, lay.margin - REACH, lay.near)
    put(send, lay.chunk, prev, lay.margin + lay.lacking[0], len(lay.lacking))


def split(values):
    high = values.astype(jnp.bfloat16)
    rest = values - high.astype(jnp.float32)
    middle = rest.astype(jnp.bfloat16)
    low = (rest - middle.astype(jnp.float32)).astype(jnp.bfloat16)
    return high, middle, low


def fill_band(band):
    row = lax.broadcasted_iota(jnp.int32, (2 * LANES, 2 * LANES), 0)
    column = lax.broadcasted_iota(jnp.int32, (2 * LANES, 2 * LANES), 1)
    apart = jnp.where((row < LANES) == (column < LANES), jnp.abs(row - column), 0)
    values = jnp.zeros((2 * LANES, 2 * LANES), jnp.float32)
    for k in range(1, REACH + 1):
        values = jnp.where(apart == k, weights[k], values)
    values = values.astype(jnp.bfloat16)
    for part in range(3):
        band[part * 2 * LANES : (part + 1) * 2 * LANES, :] = values


def multiply_z(lay, first_layer, count, now, band, along_z):
    half = count * lay.wide // 2
    first = first_layer * lay.wide
    parts = [split(now[start : start + half, :]) for start in (first, first + half)]
    both = [side[part] for part in range(3) for side in parts]
    found = jnp.dot(jnp.concatenate(both, axis=1), band[...], preferred_element_type=jnp.float32)
    along_z[0:half, :] = found[:, :LANES]
    along_z[half : 2 * half, :] = found[:, LANES:]


def sweep(lay, step, group, now, prev, following, half, gain, band, along_z, inject=None):
    first_layer = REACH * (step + 1)
    multiply_z(lay, first_layer, lay.extent - 2 * first_layer, now, band, along_z)
    row = lax.broadcasted_iota(jnp.int32, (ROWS, LANES), 0)
    top, bottom = row == 0, row == ROWS - 1

    def layers(block, carry):
        start = first_layer + group * block
        around = now.at[pl.ds(aligned((start - REACH) * lay.wide), (group + 2 * REACH) * lay.wide)]
        here = pl.ds(aligned(start * lay.wide), group * lay.wide)
        former_rows, target = prev.at[here], following.at[here]
        inner = pl.ds(aligned((start - REACH) * lay.wide), group * lay.wide)
        half_rows, gain_rows = half.at[inner], gain.at[inner]
        added = None if inject is None else inject.at[step, inner]
        z_rows = along_z.at[pl.ds(aligned(block * group * lay.wide), group * lay.wide)]

        def at(y, tile):
            first = ((y + REACH) * lay.tiles + tile) * ROWS
            return around[first : first + ROWS, :]

        for y in range(group):
            center = [at(y, tile) for tile in range(lay.tiles)]
            lower = [jnp.where(top, 0.0, pltpu.roll(tile, 1, 0)) for tile in center]
            upper = [jnp.where(bottom, 0.0, pltpu.roll(tile, ROWS - 1, 0)) for tile in center]
            line = lower + center + upper
            for tile in range(lay.tiles):
                place = (y * lay.tiles + tile) * ROWS
                place = slice(place, place + ROWS)
                total = z_rows[place, :] + weights[0] * center[tile]
                for k in range(1, REACH + 1):
                    pair = line[lay.tiles + tile - k] + line[lay.tiles + tile + k]
                    total = total + weights[k] * (pair + (at(y - k, tile) + at(y + k, tile)))
                if added is not None:
                    total = total + added[pl.ds(y * lay.wide + tile, ROWS, stride=lay.tiles), :]
                former = former_rows[place, :]
                change = (center[tile] - former) + half_rows[place, :] * total
                target[place, :] = former + gain_rows[place, :] * change
        return carry

    lax.fori_loop(0, (lay.extent - 2 * first_layer) // group, layers, 0)


def keep_own(lay, step, following, history):
    first = lay.margin * lay.wide
    history[step * lay.rows : (step + 1) * lay.rows, :] = following[first : first + lay.rows, :]


def forward(lay, phase, sources, ints, state, from_next, from_twin, courant, gain, drive, *refs):
    first, last = phase == 0, phase == STEPS // DEPTH - 1
    refs = list(refs)
    history = refs.pop(0)
    half = refs.pop(0) if first else courant
    if not last:
        state_out, send = refs.pop(0), refs.pop(0)
    now, prev, following, band, along_z, pulse = refs
    odd = ints[0]

    fill_band(band)
    load_state(lay, odd, first, now, prev, state, from_next, from_twin)
    if first:
        tail = (lay.chunk + lay.kept) * lay.wide
        part = lay.kept * lay.wide
        half[part : part + lay.rows, :] = (0.5 / scale) * courant[...]
        ahead = part + lay.rows
        half[pl.ds(aligned(odd * ahead), part), :] = (0.5 / scale) * from_next[tail : tail + part, :]
        half[pl.ds(aligned((1 - odd) * ahead), part), :] = (0.5 / scale) * from_twin[tail : tail + part, :]
    for source in range(sources):
        flat = pl.ds(ints[1 + sources + source], 1)
        pulse[source : source + 1, :] = scale * (half[flat, :] * gain[flat, :])

    for step in range(DEPTH):
        sweep(lay, step, LAYERS[phase], now, prev, following, half, gain, band, along_z)
        added = pulse[...] * drive[phase * DEPTH + step]
        places = [pl.ds(ints[1 + source], 1) for source in range(sources)]
        lines = [following[place, :] for place in places]
        for source, (place, line) in enumerate(zip(places, lines)):
            following[place, :] = line + added[source : source + 1, :]
        keep_own(lay, step, following, history)
        now, prev, following = following, now, prev

    if not last:
        store_state(lay, now, prev, state_out, send)


def slot_rows(codes, slab):
    code = codes[slab : slab + 1, :].astype(jnp.int32)
    row = jnp.where(code >= 0, lax.shift_right_arithmetic(code, 7), -1)
    return row, jnp.where(code >= 0, code & (LANES - 1), -1)


def record_slots(lay, history, codes, plain, record):
    for step in range(DEPTH):
        for y in range(lay.chunk):
            for tile in range(lay.tiles):
                row = step * lay.rows + y * lay.wide
                values = history[row + tile * ROWS : row + (tile + 1) * ROWS, :]
                plain[pl.ds(row + tile, ROWS, stride=lay.tiles), :] = values
    slots = codes.shape[1]
    width = 2 * LANES
    for slab in range(lay.count_x):
        cell_row, cell_z = slot_rows(codes, slab)
        tiles = []
        for step in range(DEPTH):
            for y in range(lay.chunk):
                row = step * lay.rows + y * lay.wide + slab * ROWS
                tiles.append(plain[row : row + ROWS, :])
        parts = jnp.concatenate(split(jnp.concatenate(tiles, axis=0)), axis=1)
        for start in range(0, slots, width):
            here = slice(start, start + width)
            z = lax.broadcasted_iota(jnp.int32, (LANES, width), 0)
            pick = jnp.where(z == cell_z[:, here], 1.0, 0.0).astype(jnp.bfloat16)
            found = jnp.dot(parts, jnp.concatenate([pick] * 3, axis=0), preferred_element_type=jnp.float32)
            wanted = lax.broadcasted_iota(jnp.int32, (lay.cells, width), 0) == cell_row[:, here]
            for step in range(DEPTH):
                part = jnp.where(wanted, found[step * lay.cells : (step + 1) * lay.cells, :], 0.0)
                row = step * lay.count_x + slab
                record[row : row + 1, here] = jnp.sum(part, axis=0, keepdims=True)


def record_phase(lay, history, codes, record, plain):
    record_slots(lay, history, codes, plain, record)


def record_last(lay, phases, where_ref, history, codes, *refs):
    earlier, refs = refs[: phases - 1], refs[phases - 1 :]
    observed, (misfit, plain, record) = refs[: lay.count_x], refs[lay.count_x :]
    record_slots(lay, history, codes, plain, record)
    block = DEPTH * lay.count_x
    for index, part in enumerate(list(earlier) + [record]):
        misfit[index * block : (index + 1) * block, :] = part[...]
    total = STEPS * lay.count_x
    for slab in range(lay.count_x):
        misfit[total + slab : total + slab + 1, :] = codes[slab : slab + 1, :]
    for turn, piece in enumerate(observed):
        place = pl.ds(aligned((where_ref[0] ^ turn) * LANES, LANES), LANES)
        used = jnp.concatenate([codes[:, place]] * STEPS, axis=0) >= 0
        seen = piece[2 * lay.cells : 2 * lay.cells + total, :]
        misfit[0:total, place] = jnp.where(used, misfit[0:total, place] - seen, 0.0)


def spread(lay, phase, side, misfit, inject):
    codes = misfit[STEPS * lay.count_x : (STEPS + 1) * lay.count_x, :]
    for slab in range(lay.count_x):
        cell_row, cell_z = slot_rows(codes, slab)
        slots = cell_row.shape[1]
        z = lax.broadcasted_iota(jnp.int32, (LANES, slots), 0)
        pick = jnp.where(z == cell_z, 1.0, 0.0).astype(jnp.bfloat16)
        hit = lax.broadcasted_iota(jnp.int32, (lay.cells, slots), 0) == cell_row
        hit = jnp.where(hit, 1.0, 0.0).astype(jnp.bfloat16)
        left, spans = [], []
        for step in range(DEPTH):
            low, high = 0, lay.chunk
            if side < 0:
                low = REACH * (step + 1) - lay.margin + lay.chunk
            if side > 0:
                high = lay.margin - REACH * (step + 1)
            if low >= high:
                continue
            row = (STEPS - 1 - phase * DEPTH - step) * lay.count_x + slab
            parts = split(scale * misfit[row : row + 1, :])
            left += [hit[low * ROWS : high * ROWS, :] * part for part in parts]
            spans.append((step, low, high))
        placed = lax.dot_general(
            jnp.concatenate(left, axis=0),
            pick,
            (((1,), (1,)), ((), ())),
            preferred_element_type=jnp.float32,
        )
        at = 0
        for step, low, high in spans:
            rows = (high - low) * ROWS
            total = placed[at : at + rows, :]
            for part in (1, 2):
                total = total + placed[at + part * rows : at + (part + 1) * rows, :]
            for y in range(low, high):
                layer = lay.margin + side * lay.chunk + y - REACH
                target = layer * lay.wide + slab * ROWS
                inject[step, target : target + ROWS, :] = total[(y - low) * ROWS : (y - low + 1) * ROWS, :]
            at += 3 * rows


def spread_own(lay, phase, misfit, inject):
    spread(lay, phase, 0, misfit, inject)


def spread_sides(lay, phase, where_ref, own, misfit_next, misfit_twin, inject):
    odd = where_ref[1]

    @pl.when(odd == 1)
    def ahead_is_next():
        spread(lay, phase, 1, misfit_next, inject)
        spread(lay, phase, -1, misfit_twin, inject)

    @pl.when(odd == 0)
    def behind_is_next():
        spread(lay, phase, -1, misfit_next, inject)
        spread(lay, phase, 1, misfit_twin, inject)


def backward(lay, phase, where_ref, state, from_next, from_twin, half, gain, inject, *refs):
    first, last = phase == 0, phase == STEPS // DEPTH - 1
    refs = list(refs)
    history = refs.pop(0)
    if not last:
        state_out, send = refs.pop(0), refs.pop(0)
    now, prev, following, band, along_z = refs

    fill_band(band)
    load_state(lay, where_ref[1], first, now, prev, state, from_next, from_twin)
    for step in range(DEPTH):
        sweep(lay, step, LAYERS[phase], now, prev, following, half, gain, band, along_z, inject)
        keep_own(lay, step, following, history)
        now, prev, following = following, now, prev
    if not last:
        store_state(lay, now, prev, state_out, send)


def add_gradient(lay, before, adjoint, history, state, gradient):
    def layer(y, carry):
        place = aligned(y * lay.wide)
        own = pl.ds(place, lay.wide)
        fields = [state[pl.ds(aligned(place + (lay.chunk + REACH) * lay.wide), lay.wide), :], state[own, :]]
        fields += [history[pl.ds(aligned(place + step * lay.rows), lay.wide), :] for step in range(DEPTH)]
        total = None if before is None else before[own, :]
        for step in range(DEPTH):
            index = DEPTH - 1 - step
            accel = (fields[index + 2] - fields[index + 1]) - (fields[index + 1] - fields[index])
            term = adjoint[pl.ds(aligned(place + step * lay.rows), lay.wide), :] * accel
            total = term if total is None else total + term
        gradient[own, :] = total
        return carry

    lax.fori_loop(0, lay.chunk, layer, 0)


def gradient_first(lay, adjoint, history, state, gradient):
    add_gradient(lay, None, adjoint, history, state, gradient)


def gradient_later(lay, adjoint, history, state, before, gradient):
    add_gradient(lay, before, adjoint, history, state, gradient)


def gradient_last(lay, where_ref, adjoint, history, state, before, *refs):
    sends, (gradient, plain) = refs[: lay.count_x], refs[lay.count_x :]
    add_gradient(lay, before, adjoint, history, state, gradient)
    for y in range(lay.chunk):
        for tile in range(lay.tiles):
            row = y * lay.wide + tile * ROWS
            plain[pl.ds(y * lay.wide + tile, ROWS, stride=lay.tiles), :] = gradient[row : row + ROWS, :]
    for turn, send in enumerate(sends):
        other = where_ref[0] ^ turn
        for y in range(lay.chunk):
            source = pl.ds(aligned(y * lay.wide + other * ROWS), ROWS)
            send[y * ROWS : (y + 1) * ROWS, :] = plain[source, :]


def finish(lay, slab_ref, *refs):
    pieces, gradient = refs[: lay.count_x], refs[lay.count_x]
    for turn, piece in enumerate(pieces):
        start = (slab_ref[0] ^ turn) * lay.chunk
        for x in range(ROWS):
            target = pl.ds(aligned(x * lay.width_y + start), lay.chunk)
            gradient[target, :] = piece[pl.ds(x, lay.chunk, stride=ROWS), :]


def gain_rows(lay, first_y):
    x = jnp.arange(ROWS)[None, :] * lay.tiles + jnp.arange(lay.tiles)[:, None]
    y = first_y + REACH + jnp.arange(lay.inner)

    def ramp(position, count):
        gap = jnp.minimum(position, count - 1 - position)
        profile = jnp.maximum(SPONGE - gap, 0).astype(jnp.float32) / SPONGE
        return profile * profile

    damping = damping_peak * (ramp(x, lay.wide)[None] + ramp(y, lay.whole_y)[:, None, None])
    gain = (2.0 / (1.0 + damping)).reshape(lay.inner * lay.wide, 1)
    return jnp.broadcast_to(gain, (lay.inner * lay.wide, LANES))


def source_rows(lay, first_y, source_cell, wavelet):
    x = source_cell // (lay.whole_y * LANES)
    y = source_cell // LANES % lay.whole_y - first_y
    z = source_cell % LANES
    inside = (y >= REACH) & (y < lay.extent - REACH)
    tile, row = x % lay.tiles, x // lay.tiles
    flat = jnp.where(inside, (y - REACH) * lay.wide + tile * ROWS + row, 0)
    buffer_row = jnp.where(inside, flat + REACH * lay.wide, 0)
    same = (buffer_row[:, None] == buffer_row[None, :]) & inside[None, :]
    spot = (z[:, None] == jnp.arange(LANES)[None, :]).astype(jnp.float32)
    lines = jnp.where(same[None, :, :, None], wavelet[:, None, :, None] * spot[None, None], 0.0)
    return buffer_row, flat, jnp.sum(lines, axis=2)


def local_tiles(
    lay,
    courant,
    state_prev,
    state_now,
    adjoint_now,
    adjoint_next,
    source_cell,
    wavelet,
    observed,
    receiver_cell,
    receiver_count,
):
    axes = ("gx", "gy")
    slab = lax.axis_index("gx")
    strip = lax.axis_index("gy")
    pair = strip // 2
    chip = jnp.where(pair % 2 == 0, slab, lay.count_x - 1 - slab)
    place = (pair * lay.count_x + chip) * 2 + strip % 2
    odd = strip % 2
    first_y = place * lay.chunk - lay.margin
    slab_int = slab.reshape(1).astype(jnp.int32)
    where = jnp.stack([place % lay.count_x, odd]).astype(jnp.int32)

    count = lay.count_x
    sources = source_cell.shape[0]
    slots = count * receiver_cell.shape[3]
    flat = lambda values: values.reshape(-1, LANES)
    part = functools.partial

    def swap(to_next, to_twin):
        return (
            lax.ppermute(to_next, axes, lay.swaps(1)),
            lax.ppermute(to_twin, axes, lay.swaps(0)),
        )

    def after(value, others):
        return lax.optimization_barrier((value, others))[0]

    buffer_row, flat_row, drive = source_rows(lay, first_y, source_cell, wavelet)
    gain = gain_rows(lay, first_y)
    ints = jnp.concatenate([odd.reshape(1), buffer_row, flat_row]).astype(jnp.int32)

    traces = flat(observed)
    forward_rows = 3 * lay.cells + -(-count // ROWS) * ROWS
    back_rows = 2 * lay.cells + traces.shape[0]
    cuts = call(
        part(cut_forward, lay),
        (slab_int, receiver_count.reshape(-1)),
        [flat(field) for field in (state_now, state_prev, courant)] + [receiver_cell.reshape(count, LANES)],
        [f32(forward_rows, LANES)] * count,
        [
            pltpu.VMEM((3, lay.width_x * lay.width_y, LANES), jnp.float32),
            pltpu.VMEM((count, LANES), jnp.int32),
            pltpu.SemaphoreType.DMA((4,)),
        ],
        space=pltpu.HBM,
        limit=60 * 1024 * 1024,
    )
    back_cuts = call(
        part(cut_adjoint, lay),
        (slab_int,),
        [flat(adjoint_now), flat(adjoint_next), traces],
        [f32(back_rows, LANES)] * count,
    )
    pieces = [lax.ppermute(cut, axes, lay.to_chunks(turn)) for turn, cut in enumerate(cuts)]
    pieces, ints, gain, drive, back_cuts = lax.optimization_barrier((pieces, ints, gain, drive, back_cuts))
    kept_rows = lay.kept * lay.wide
    state, own_courant, to_next, to_twin, codes = call(
        part(join_forward, lay),
        (where,),
        pieces,
        [f32(lay.state_rows, LANES), f32(lay.rows, LANES)]
        + [f32(lay.rows + 2 * kept_rows, LANES)] * 2
        + [f32(count, slots)],
        [pltpu.VMEM((3, lay.rows, LANES), jnp.float32)],
    )
    from_next, from_twin = swap(to_next, to_twin)

    back_pieces = [None] * count

    def move_adjoint(turns, earlier):
        for turn in turns:
            back_pieces[turn] = lax.ppermute(after(back_cuts[turn], earlier), axes, lay.to_chunks(turn))

    move_adjoint(range(1, count), codes)
    move_adjoint(range(1), from_twin)

    phases = STEPS // DEPTH
    step_cost = 8_000_000
    side_cost = 4_000_000
    history_shape = f32(DEPTH * lay.rows, LANES)
    state_shapes = [f32(lay.state_rows, LANES), f32(lay.send_rows, LANES)]
    buffers = [pltpu.VMEM((lay.extent * lay.wide, LANES), jnp.float32)] * 3
    buffers += [pltpu.VMEM((6 * LANES, 2 * LANES), jnp.bfloat16)]
    buffers += [pltpu.VMEM((lay.inner * lay.wide, LANES), jnp.float32)]
    record_scratch = [pltpu.VMEM((DEPTH * lay.rows, LANES), jnp.float32)]
    record_shape = (DEPTH * count, slots)
    histories, states, records = [], [], []
    half = own_courant
    for phase in range(phases):
        first, last = phase == 0, phase == phases - 1
        outs = [history_shape]
        if first:
            outs.append(f32(lay.inner * lay.wide, LANES))
        if not last:
            outs += state_shapes
        results = list(
            call(
                part(forward, lay, phase, sources),
                (ints,),
                [state, from_next, from_twin, half, gain, drive],
                outs,
                buffers + [pltpu.VMEM((sources, LANES), jnp.float32)],
                cost=step_cost,
            )
        )
        histories.append(results.pop(0))
        states.append(state)
        if first:
            half = results.pop(0)
        if last:
            continue
        state, send = results
        to_twin = after(send, back_pieces) if first else send
        from_next, from_twin = swap(send, to_twin)
    for history in histories[:-1]:
        records += call(
            part(record_phase, lay),
            (),
            [history, codes],
            [f32(*record_shape)],
            record_scratch,
            cost=side_cost,
        )
    back_state, to_next, to_twin = call(
        part(join_adjoint, lay),
        (where,),
        back_pieces,
        [f32(lay.state_rows, LANES)] + [f32(lay.rows + kept_rows, LANES)] * 2,
        [pltpu.VMEM((2, lay.rows, LANES), jnp.float32)],
    )
    back_from_next, back_from_twin = swap(to_next, to_twin)
    (misfit,) = call(
        part(record_last, lay, phases),
        (where,),
        [histories[-1], codes] + records + back_pieces,
        [f32(-(-(STEPS + 1) * count // ROWS) * ROWS, slots)],
        record_scratch + [pltpu.VMEM(record_shape, jnp.float32)],
        cost=side_cost,
    )

    misfit = after(misfit, [back_from_next, back_from_twin])
    misfit_next, misfit_twin = swap(misfit, misfit)

    total = STEPS * count
    twins = after(misfit[:total] + misfit_twin[:total], state)
    state, from_next, from_twin = back_state, back_from_next, back_from_twin
    gradient = None
    inject_shape = f32(DEPTH, lay.inner * lay.wide, LANES)
    for phase in range(phases):
        first, last = phase == 0, phase == phases - 1
        (inject,) = call(part(spread_own, lay, phase), (), [misfit], [inject_shape], cost=side_cost)
        (inject,) = call(
            part(spread_sides, lay, phase),
            (where,),
            [inject, misfit_next, misfit_twin],
            [inject_shape],
            cost=side_cost,
            aliases={1: 0},
        )
        results = call(
            part(backward, lay, phase),
            (where,),
            [state, from_next, from_twin, half, gain, inject],
            [history_shape] + ([] if last else state_shapes),
            buffers,
            cost=step_cost,
        )
        arrays = [results[0], histories[phases - 1 - phase], states[phases - 1 - phase]]
        if last:
            sends = call(
                part(gradient_last, lay),
                (where,),
                arrays + [gradient],
                [f32(lay.cells, LANES)] * count,
                [pltpu.VMEM((lay.rows, LANES), jnp.float32)] * 2,
            )
            continue
        _, state, send = results
        from_next, from_twin = swap(send, send)
        if first:
            others = lax.ppermute(after(twins, send), axes, lay.across())
            state = after(state, others)
        else:
            tile = lax.dynamic_slice_in_dim(twins + others, where[0] * LANES, LANES, axis=1)
            residual = lax.ppermute(tile, axes, lay.home())
            state = after(state, residual)
        kernel = gradient_first if first else gradient_later
        (gradient,) = call(
            part(kernel, lay), (), arrays + ([] if first else [gradient]), [f32(lay.rows, LANES)], cost=side_cost
        )
    pieces = [lax.ppermute(send, axes, lay.to_slabs(turn)) for turn, send in enumerate(sends)]
    (gradient,) = call(part(finish, lay), (slab_int,), pieces, [f32(lay.width_x * lay.width_y, LANES)])
    return gradient.reshape(courant.shape), residual.reshape(observed.shape)


def local(courant, *rest):
    width_x, width_y, depth_z = courant.shape
    count_x, count_y = lax.axis_size("gx"), lax.axis_size("gy")
    if fits(count_x, count_y, width_x, width_y, depth_z):
        return local_tiles(Layout(count_x, count_y, width_x, width_y), courant, *rest)
    return local_blocks(courant, *rest)


def padded_2(cells, sides, width):
    for axis, dim in sides:
        count = lax.axis_size(axis)
        ends = count - 1
        head = lax.slice_in_dim(cells, 0, width, axis=dim)
        tail = lax.slice_in_dim(cells, cells.shape[dim] - width, cells.shape[dim], axis=dim)
        cells = jnp.concatenate(
            [
                lax.ppermute(tail, axis, [(i, (i + 1) % count) for i in range(ends)]),
                cells,
                lax.ppermute(head, axis, [((i + 1) % count, i) for i in range(ends)]),
            ],
            axis=dim,
        )
    return cells


def laplace(values):
    width_x, width_y, depth_z = values.shape
    padded = padded_2(values, (("gx", 0), ("gy", 1)), 4)
    z_padded = jnp.pad(values, ((0, 0), (0, 0), (4, 4)))
    summed = 3.0 * stencil[0] * values
    for offset in range(1, 5):
        paired = (
            padded[4 + offset : 4 + offset + width_x, 4 : 4 + width_y]
            + padded[4 - offset : 4 - offset + width_x, 4 : 4 + width_y]
        )
        paired = (
            paired
            + padded[4 : 4 + width_x, 4 + offset : 4 + offset + width_y]
            + padded[4 : 4 + width_x, 4 - offset : 4 - offset + width_y]
        )
        paired = (
            paired
            + z_padded[:, :, 4 + offset : 4 + offset + depth_z]
            + z_padded[:, :, 4 - offset : 4 - offset + depth_z]
        )
        summed = summed + stencil[offset] * paired
    return summed


def sponge(start, count, whole):
    position = start + jnp.arange(count, dtype=jnp.int32)
    edge_gap = jnp.minimum(position, whole - 1 - position)
    profile = jnp.maximum(SPONGE - edge_gap, 0).astype(jnp.float32) / SPONGE
    return profile * profile


def place_sum(indices, amounts, shape):
    flat = jnp.zeros((shape[0] * shape[1] * shape[2],), jnp.float32).at[indices].add(amounts)
    return flat.reshape(shape)


def local_blocks(
    courant,
    state_prev,
    state_now,
    adjoint_now,
    adjoint_next,
    source_cell,
    wavelet,
    observed,
    receiver_cell,
    receiver_count,
):
    shape = courant.shape
    width_x, width_y, depth_z = shape
    slab = lax.axis_index("gx")
    strip = lax.axis_index("gy")
    whole_x = width_x * lax.axis_size("gx")
    whole_y = width_y * lax.axis_size("gy")
    damping = damping_peak * (
        sponge(slab * width_x, width_x, whole_x)[:, None, None]
        + sponge(strip * width_y, width_y, whole_y)[None, :, None]
    )
    source_x = source_cell // (whole_y * depth_z) - slab * width_x
    source_y = source_cell // depth_z % whole_y - strip * width_y
    source_z = source_cell % depth_z
    inside = (source_x >= 0) & (source_x < width_x) & (source_y >= 0) & (source_y < width_y)
    source_flat = jnp.where(inside, (source_x * width_y + source_y) * depth_z + source_z, 0)
    source_weight = wavelet * inside.astype(jnp.float32)[None, :]
    senders = receiver_cell.shape[2]
    slots = receiver_cell.shape[3]
    cells = receiver_cell.reshape(-1)
    active = (
        jnp.arange(slots, dtype=jnp.int32)[None, :] < receiver_count.reshape(senders, 1)
    ).astype(jnp.float32)
    active_flat = active.reshape(-1)

    def advance(carry, weights):
        former, current = carry
        drive = laplace(current) + place_sum(source_flat, weights, shape)
        following = (2.0 * current - (1.0 - damping) * former + courant * drive) / (1.0 + damping)
        return (
            (current, following),
            (following - 2.0 * current + former, following.reshape(-1)[cells] * active_flat),
        )

    final_states, (accels, recorded) = lax.scan(advance, (state_prev, state_now), source_weight)
    recorded_tiles = recorded.reshape(STEPS, senders, 1, 1, slots)
    active_tiles = active.reshape(1, senders, 1, 1, slots)
    synthetic, mask_back = (
        lax.all_to_all(recorded_tiles, "gx", split_axis=1, concat_axis=3, tiled=True),
        lax.all_to_all(active_tiles, "gx", split_axis=1, concat_axis=3, tiled=True),
    )
    trace_residual = mask_back * (synthetic - observed)
    misfit = lax.all_to_all(trace_residual, "gx", split_axis=3, concat_axis=1, tiled=True)
    misfit_rows = misfit.reshape(STEPS, senders * slots)

    def retreat(carry, inputs):
        later, current, gradient = carry
        acceleration, residual_row = inputs
        drive = laplace(current) + place_sum(cells, residual_row, shape)
        earlier = (2.0 * current - (1.0 - damping) * later + courant * drive) / (1.0 + damping)
        return ((current, earlier, gradient + earlier * acceleration), None)

    start_gradient = jnp.zeros(shape, jnp.float32)
    (last_later, last_current, gradient), unused = lax.scan(
        retreat, (adjoint_next, adjoint_now, start_gradient), (accels, misfit_rows), reverse=True
    )
    return (gradient, trace_residual)


def solution(mesh):
    placed = (
        P("gx", "gy", None),
        P(("groups", "gx"), "gy", None),
        P(("groups", "gx"), "gy", None),
        P(("groups", "gx"), "gy", None),
        P(("groups", "gx"), "gy", None),
        P("groups"),
        P(None, "groups"),
        P("groups", "gx", "gy", None, None),
        P("gx", "gy", None, None),
        P("gx", "gy", None),
    )
    return jax.shard_map(
        local,
        mesh=mesh,
        in_specs=placed,
        out_specs=(P(("groups", "gx"), "gy", None), P("groups", "gx", "gy", None, None)),
        check_vma=False,
    )
```

```python
import functools

import jax
import jax.numpy as jnp
from jax import lax
from jax.experimental import pallas as pl
from jax.experimental.pallas import tpu as pltpu
from jax.sharding import PartitionSpec as P

STEPS = 12
SPONGE = 8
REACH = 4
DEPTH = 4
LANES = 128
ROWS = 8
LAYERS = 8


stencil = (-205.0 / 72.0, 8.0 / 5.0, -1.0 / 5.0, 8.0 / 315.0, -1.0 / 560.0)
damping_peak = 0.3
scale = 5040.0
weights = (3.0 * -14350.0, 8064.0, -1008.0, 128.0, -9.0)


class Layout:
    def __init__(self, count_x, count_y, width_x, width_y):
        self.count_x, self.count_y = count_x, count_y
        self.width_x, self.width_y = width_x, width_y
        self.chunk = width_y // count_x
        self.wide = width_x * count_x
        self.tiles = self.wide // ROWS
        self.whole_y = width_y * count_y
        self.margin = REACH * DEPTH
        self.extent = self.chunk + 2 * self.margin
        self.kept = self.margin - REACH
        self.inner = self.extent - 2 * REACH
        self.rows = self.chunk * self.wide
        self.cells = self.chunk * width_x
        self.near = self.chunk + 2 * REACH
        self.state_rows = (self.chunk + self.near) * self.wide
        self.lacking = range(REACH, self.chunk - REACH)
        self.send_rows = (self.chunk + len(self.lacking)) * self.wide

    def at(self, place):
        pair, rest = divmod(place, 2 * self.count_x)
        chip, core = divmod(rest, 2)
        slab = chip if pair % 2 == 0 else self.count_x - 1 - chip
        return slab * self.count_y + 2 * pair + core

    def to_chunks(self, turn):
        moves = []
        for slab in range(self.count_x):
            for strip in range(self.count_y):
                moves.append((slab * self.count_y + strip, self.at(strip * self.count_x + (slab ^ turn))))
        return moves

    def to_slabs(self, turn):
        return [(target, source) for source, target in self.to_chunks(turn)]

    def swaps(self, first):
        moves = []
        for place in range(first, self.count_x * self.count_y - 1, 2):
            moves += [(self.at(place), self.at(place + 1)), (self.at(place + 1), self.at(place))]
        return moves


def fits(count_x, count_y, width_x, width_y, depth_z):
    return (
        count_x & (count_x - 1) == 0
        and count_y % 2 == 0
        and width_x == ROWS
        and width_x * count_x == ROWS * REACH
        and depth_z == LANES
        and width_y == count_x * REACH * DEPTH
    )


def f32(*shape):
    return jax.ShapeDtypeStruct(shape, jnp.float32)


def call(
    kernel, ints, arrays, outs, scratch=(), cost=1_000_000, space=pltpu.VMEM, aliases=None, limit=32 * 1024 * 1024
):
    return pl.pallas_call(
        kernel,
        out_shape=tuple(outs),
        in_specs=[pl.BlockSpec(memory_space=pltpu.SMEM)] * len(ints)
        + [pl.BlockSpec(memory_space=space)] * len(arrays),
        out_specs=tuple(pl.BlockSpec(memory_space=pltpu.VMEM) for _ in outs),
        scratch_shapes=list(scratch),
        input_output_aliases=aliases or {},
        compiler_params=pltpu.CompilerParams(vmem_limit_bytes=limit),
        cost_estimate=pl.CostEstimate(flops=cost, bytes_accessed=cost, transcendentals=0),
    )(*ints, *arrays)


def aligned(value, to=ROWS):
    return pl.multiple_of(value, to)


def cut_chunk(lay, slab, turn, fields, target):
    start = (slab ^ turn) * lay.chunk
    for index, field in enumerate(fields):
        for y in range(lay.chunk):
            row = (index * lay.chunk + y) * ROWS
            target[row : row + ROWS, :] = field[pl.ds(start + y, ROWS, stride=lay.width_y), :]


def cut_forward(lay, slab_ref, count_ref, *refs):
    inputs, sends, (held, held_cell, done) = refs[:4], refs[4 : 4 + lay.count_x], refs[4 + lay.count_x :]
    fields = [held.at[index] for index in range(3)]
    copies = [
        pltpu.make_async_copy(source, target, done.at[index])
        for index, (source, target) in enumerate(zip(inputs, fields + [held_cell]))
    ]
    for copy in copies:
        copy.start()
    for copy in copies:
        copy.wait()
    slots = lax.broadcasted_iota(jnp.int32, (1, LANES), 1)
    used = []
    for tile in range(lay.count_x):
        cell = jnp.where(slots < count_ref[tile], held_cell[tile : tile + 1, :], -1)
        used.append(cell.astype(jnp.float32))
    for turn, send in enumerate(sends):
        cut_chunk(lay, slab_ref[0], turn, fields, send)
        for tile in range(lay.count_x):
            row = 3 * lay.cells + tile
            send[row : row + 1, :] = used[tile]


def cut_adjoint(lay, slab_ref, now, prev, observed, *sends):
    for turn, send in enumerate(sends):
        cut_chunk(lay, slab_ref[0], turn, (now, prev), send)
        row = 2 * lay.cells
        send[row : row + observed.shape[0], :] = observed[...]


def join_fields(lay, own_slot, odd, pieces, joined, state, courant, send_next, send_twin):
    fields = joined.shape[0]
    for turn, piece in enumerate(pieces):
        start_x = (own_slot ^ turn) * ROWS
        for field in range(fields):
            for y in range(lay.chunk):
                row = (field * lay.chunk + y) * ROWS
                joined[field, pl.ds(aligned(y * lay.wide + start_x), ROWS), :] = piece[row : row + ROWS, :]
    kept_rows = lay.kept * lay.wide
    for field in range(fields):
        target, first = (state, 0) if field == 0 else (state, (lay.chunk + REACH) * lay.wide)
        if field == 2:
            target, first = courant, 0
        for y in range(lay.chunk):
            for tile in range(lay.tiles):
                values = joined[field, pl.ds(y * lay.wide + tile, ROWS, stride=lay.tiles), :]
                row = y * lay.wide + tile * ROWS
                target[first + row : first + row + ROWS, :] = values
                if field == 0:
                    send_next[row : row + ROWS, :] = values
                    send_twin[row : row + ROWS, :] = values
    for field in range(1, fields):
        source, first = (state, (lay.chunk + REACH) * lay.wide) if field == 1 else (courant, 0)
        place = lay.rows + (field - 1) * kept_rows
        skipped = (lay.chunk - lay.kept) * lay.wide
        ahead = source[pl.ds(aligned(first + odd * skipped), kept_rows), :]
        send_next[place : place + kept_rows, :] = ahead
        behind = source[pl.ds(aligned(first + (1 - odd) * skipped), kept_rows), :]
        send_twin[place : place + kept_rows, :] = behind


def join_forward(lay, where_ref, *refs):
    pieces, (state, courant, send_next, send_twin, codes, joined) = refs[: lay.count_x], refs[lay.count_x :]
    own_slot = where_ref[0]
    join_fields(lay, own_slot, where_ref[1], pieces, joined, state, courant, send_next, send_twin)
    first = 3 * lay.cells
    strip_cells = lay.width_y * LANES
    slab_row = lax.broadcasted_iota(jnp.int32, codes.shape, 0)
    found = jnp.full(codes.shape, -1.0, jnp.float32)
    for turn, piece in enumerate(pieces):
        cell = piece[first : first + lay.count_x, :].astype(jnp.int32)
        used = cell >= 0
        cell = jnp.maximum(cell, 0)
        x = lax.div(cell, jnp.int32(strip_cells))
        y = lax.rem(lax.div(cell, jnp.int32(LANES)), jnp.int32(lay.width_y)) - own_slot * lay.chunk
        inside = used & (y >= 0) & (y < lay.chunk)
        code = jnp.where(inside, (y * ROWS + x) * LANES + lax.rem(cell, jnp.int32(LANES)), -1)
        code = code.astype(jnp.float32)
        line = jnp.concatenate([code[tile : tile + 1, :] for tile in range(lay.count_x)], axis=1)
        found = jnp.where(slab_row == (own_slot ^ turn), jnp.broadcast_to(line, codes.shape), found)
    codes[...] = found


def join_adjoint(lay, where_ref, *refs):
    pieces, (state, send_next, send_twin, joined) = refs[: lay.count_x], refs[lay.count_x :]
    join_fields(lay, where_ref[0], where_ref[1], pieces, joined, state, None, send_next, send_twin)


def load_state(lay, odd, first, now, prev, state, from_next, from_twin):
    wide = lay.wide

    def put(buffer, layer, ref, source, count):
        target = pl.ds(layer * wide if isinstance(layer, int) else aligned(layer * wide), count * wide)
        buffer[target, :] = ref[source * wide : (source + count) * wide, :]

    ahead = lay.margin + lay.chunk
    put(now, lay.margin, state, 0, lay.chunk)
    put(now, odd * ahead, from_next, 0, lay.chunk)
    put(now, (1 - odd) * ahead, from_twin, 0, lay.chunk)
    if first:
        put(prev, lay.margin, state, lay.chunk + REACH, lay.chunk)
        put(prev, odd * ahead + (1 - odd) * REACH, from_next, lay.chunk, lay.kept)
        put(prev, (1 - odd) * ahead + odd * REACH, from_twin, lay.chunk, lay.kept)
        return
    put(prev, lay.margin - REACH, state, lay.chunk, lay.near)
    put(prev, odd * ahead + lay.lacking[0], from_next, lay.chunk, len(lay.lacking))
    put(prev, (1 - odd) * ahead + lay.lacking[0], from_twin, lay.chunk, len(lay.lacking))


def store_state(lay, now, prev, state, send):
    wide = lay.wide

    def put(ref, target, buffer, layer, count):
        ref[target * wide : (target + count) * wide, :] = buffer[layer * wide : (layer + count) * wide, :]

    put(state, 0, now, lay.margin, lay.chunk)
    put(send, 0, now, lay.margin, lay.chunk)
    put(state, lay.chunk, prev, lay.margin - REACH, lay.near)
    put(send, lay.chunk, prev, lay.margin + lay.lacking[0], len(lay.lacking))


def split(values):
    high = values.astype(jnp.bfloat16)
    rest = values - high.astype(jnp.float32)
    middle = rest.astype(jnp.bfloat16)
    low = (rest - middle.astype(jnp.float32)).astype(jnp.bfloat16)
    return high, middle, low


def fill_band(band):
    row = lax.broadcasted_iota(jnp.int32, (2 * LANES, 2 * LANES), 0)
    column = lax.broadcasted_iota(jnp.int32, (2 * LANES, 2 * LANES), 1)
    apart = jnp.where((row < LANES) == (column < LANES), jnp.abs(row - column), 0)
    values = jnp.zeros((2 * LANES, 2 * LANES), jnp.float32)
    for k in range(1, REACH + 1):
        values = jnp.where(apart == k, weights[k], values)
    values = values.astype(jnp.bfloat16)
    for part in range(3):
        band[part * 2 * LANES : (part + 1) * 2 * LANES, :] = values


def multiply_z(lay, first_layer, count, now, band, along_z):
    half = count * lay.wide // 2
    first = first_layer * lay.wide
    parts = [split(now[start : start + half, :]) for start in (first, first + half)]
    both = [side[part] for part in range(3) for side in parts]
    found = jnp.dot(jnp.concatenate(both, axis=1), band[...], preferred_element_type=jnp.float32)
    along_z[0:half, :] = found[:, :LANES]
    along_z[half : 2 * half, :] = found[:, LANES:]


def sweep(lay, step, group, now, prev, following, half, gain, band, along_z, inject=None):
    first_layer = REACH * (step + 1)
    multiply_z(lay, first_layer, lay.extent - 2 * first_layer, now, band, along_z)
    row = lax.broadcasted_iota(jnp.int32, (ROWS, LANES), 0)
    top, bottom = row == 0, row == ROWS - 1

    def layers(block, carry):
        start = first_layer + group * block
        around = now.at[pl.ds(aligned((start - REACH) * lay.wide), (group + 2 * REACH) * lay.wide)]
        here = pl.ds(aligned(start * lay.wide), group * lay.wide)
        former_rows, target = prev.at[here], following.at[here]
        inner = pl.ds(aligned((start - REACH) * lay.wide), group * lay.wide)
        half_rows, gain_rows = half.at[inner], gain.at[inner]
        added = None if inject is None else inject.at[step, inner]
        z_rows = along_z.at[pl.ds(aligned(block * group * lay.wide), group * lay.wide)]

        def at(y, tile):
            first = ((y + REACH) * lay.tiles + tile) * ROWS
            return around[first : first + ROWS, :]

        for y in range(group):
            center = [at(y, tile) for tile in range(lay.tiles)]
            lower = [jnp.where(top, 0.0, pltpu.roll(tile, 1, 0)) for tile in center]
            upper = [jnp.where(bottom, 0.0, pltpu.roll(tile, ROWS - 1, 0)) for tile in center]
            line = lower + center + upper
            for tile in range(lay.tiles):
                place = (y * lay.tiles + tile) * ROWS
                place = slice(place, place + ROWS)
                total = z_rows[place, :] + weights[0] * center[tile]
                for k in range(1, REACH + 1):
                    pair = line[lay.tiles + tile - k] + line[lay.tiles + tile + k]
                    total = total + weights[k] * (pair + (at(y - k, tile) + at(y + k, tile)))
                if added is not None:
                    total = total + added[pl.ds(y * lay.wide + tile, ROWS, stride=lay.tiles), :]
                former = former_rows[place, :]
                change = (center[tile] - former) + half_rows[place, :] * total
                target[place, :] = former + gain_rows[place, :] * change
        return carry

    lax.fori_loop(0, (lay.extent - 2 * first_layer) // group, layers, 0)


def keep_own(lay, step, following, history):
    first = lay.margin * lay.wide
    history[step * lay.rows : (step + 1) * lay.rows, :] = following[first : first + lay.rows, :]


def forward(lay, phase, sources, ints, state, from_next, from_twin, courant, gain, drive, *refs):
    first, last = phase == 0, phase == STEPS // DEPTH - 1
    refs = list(refs)
    history = refs.pop(0)
    half = refs.pop(0) if first else courant
    if not last:
        state_out, send = refs.pop(0), refs.pop(0)
    now, prev, following, band, along_z, pulse = refs
    odd = ints[0]

    fill_band(band)
    load_state(lay, odd, first, now, prev, state, from_next, from_twin)
    if first:
        tail = (lay.chunk + lay.kept) * lay.wide
        part = lay.kept * lay.wide
        half[part : part + lay.rows, :] = (0.5 / scale) * courant[...]
        ahead = part + lay.rows
        half[pl.ds(aligned(odd * ahead), part), :] = (0.5 / scale) * from_next[tail : tail + part, :]
        half[pl.ds(aligned((1 - odd) * ahead), part), :] = (0.5 / scale) * from_twin[tail : tail + part, :]
    for source in range(sources):
        flat = pl.ds(ints[1 + sources + source], 1)
        pulse[source : source + 1, :] = scale * (half[flat, :] * gain[flat, :])

    for step in range(DEPTH):
        sweep(lay, step, LAYERS, now, prev, following, half, gain, band, along_z)
        added = pulse[...] * drive[phase * DEPTH + step]
        places = [pl.ds(ints[1 + source], 1) for source in range(sources)]
        lines = [following[place, :] for place in places]
        for source, (place, line) in enumerate(zip(places, lines)):
            following[place, :] = line + added[source : source + 1, :]
        keep_own(lay, step, following, history)
        now, prev, following = following, now, prev

    if not last:
        store_state(lay, now, prev, state_out, send)


def slot_rows(codes, slab):
    code = codes[slab : slab + 1, :].astype(jnp.int32)
    row = jnp.where(code >= 0, lax.shift_right_arithmetic(code, 7), -1)
    return row, jnp.where(code >= 0, code & (LANES - 1), -1)


def record_slots(lay, history, codes, plain, record):
    for step in range(DEPTH):
        for y in range(lay.chunk):
            for tile in range(lay.tiles):
                row = step * lay.rows + y * lay.wide
                values = history[row + tile * ROWS : row + (tile + 1) * ROWS, :]
                plain[pl.ds(row + tile, ROWS, stride=lay.tiles), :] = values
    slots = codes.shape[1]
    width = 2 * LANES
    for slab in range(lay.count_x):
        cell_row, cell_z = slot_rows(codes, slab)
        tiles = []
        for step in range(DEPTH):
            for y in range(lay.chunk):
                row = step * lay.rows + y * lay.wide + slab * ROWS
                tiles.append(plain[row : row + ROWS, :])
        parts = jnp.concatenate(split(jnp.concatenate(tiles, axis=0)), axis=1)
        for start in range(0, slots, width):
            here = slice(start, start + width)
            z = lax.broadcasted_iota(jnp.int32, (LANES, width), 0)
            pick = jnp.where(z == cell_z[:, here], 1.0, 0.0).astype(jnp.bfloat16)
            found = jnp.dot(parts, jnp.concatenate([pick] * 3, axis=0), preferred_element_type=jnp.float32)
            wanted = lax.broadcasted_iota(jnp.int32, (lay.cells, width), 0) == cell_row[:, here]
            for step in range(DEPTH):
                part = jnp.where(wanted, found[step * lay.cells : (step + 1) * lay.cells, :], 0.0)
                row = step * lay.count_x + slab
                record[row : row + 1, here] = jnp.sum(part, axis=0, keepdims=True)


def record_phase(lay, history, codes, record, plain):
    record_slots(lay, history, codes, plain, record)


def record_last(lay, phases, where_ref, history, codes, *refs):
    earlier, refs = refs[: phases - 1], refs[phases - 1 :]
    observed, (misfit, plain, record) = refs[: lay.count_x], refs[lay.count_x :]
    record_slots(lay, history, codes, plain, record)
    block = DEPTH * lay.count_x
    for index, part in enumerate(list(earlier) + [record]):
        misfit[index * block : (index + 1) * block, :] = part[...]
    total = STEPS * lay.count_x
    for slab in range(lay.count_x):
        misfit[total + slab : total + slab + 1, :] = codes[slab : slab + 1, :]
    for turn, piece in enumerate(observed):
        place = pl.ds(aligned((where_ref[0] ^ turn) * LANES, LANES), LANES)
        used = jnp.concatenate([codes[:, place]] * STEPS, axis=0) >= 0
        seen = piece[2 * lay.cells : 2 * lay.cells + total, :]
        misfit[0:total, place] = jnp.where(used, misfit[0:total, place] - seen, 0.0)


def spread(lay, phase, side, misfit, inject):
    codes = misfit[STEPS * lay.count_x : (STEPS + 1) * lay.count_x, :]
    for slab in range(lay.count_x):
        cell_row, cell_z = slot_rows(codes, slab)
        slots = cell_row.shape[1]
        z = lax.broadcasted_iota(jnp.int32, (LANES, slots), 0)
        pick = jnp.where(z == cell_z, 1.0, 0.0).astype(jnp.bfloat16)
        hit = lax.broadcasted_iota(jnp.int32, (lay.cells, slots), 0) == cell_row
        hit = jnp.where(hit, 1.0, 0.0).astype(jnp.bfloat16)
        left, spans = [], []
        for step in range(DEPTH):
            low, high = 0, lay.chunk
            if side < 0:
                low = REACH * (step + 1) - lay.margin + lay.chunk
            if side > 0:
                high = lay.margin - REACH * (step + 1)
            if low >= high:
                continue
            row = (STEPS - 1 - phase * DEPTH - step) * lay.count_x + slab
            parts = split(scale * misfit[row : row + 1, :])
            left += [hit[low * ROWS : high * ROWS, :] * part for part in parts]
            spans.append((step, low, high))
        placed = lax.dot_general(
            jnp.concatenate(left, axis=0),
            pick,
            (((1,), (1,)), ((), ())),
            preferred_element_type=jnp.float32,
        )
        at = 0
        for step, low, high in spans:
            rows = (high - low) * ROWS
            total = placed[at : at + rows, :]
            for part in (1, 2):
                total = total + placed[at + part * rows : at + (part + 1) * rows, :]
            for y in range(low, high):
                layer = lay.margin + side * lay.chunk + y - REACH
                target = layer * lay.wide + slab * ROWS
                inject[step, target : target + ROWS, :] = total[(y - low) * ROWS : (y - low + 1) * ROWS, :]
            at += 3 * rows


def spread_own(lay, phase, misfit, inject):
    spread(lay, phase, 0, misfit, inject)


def spread_sides(lay, phase, where_ref, own, misfit_next, misfit_twin, inject):
    odd = where_ref[1]

    @pl.when(odd == 1)
    def ahead_is_next():
        spread(lay, phase, 1, misfit_next, inject)
        spread(lay, phase, -1, misfit_twin, inject)

    @pl.when(odd == 0)
    def behind_is_next():
        spread(lay, phase, -1, misfit_next, inject)
        spread(lay, phase, 1, misfit_twin, inject)


def backward(lay, phase, where_ref, state, from_next, from_twin, half, gain, inject, *refs):
    first, last = phase == 0, phase == STEPS // DEPTH - 1
    refs = list(refs)
    history = refs.pop(0)
    if not last:
        state_out, send = refs.pop(0), refs.pop(0)
    now, prev, following, band, along_z = refs

    fill_band(band)
    load_state(lay, where_ref[1], first, now, prev, state, from_next, from_twin)
    for step in range(DEPTH):
        sweep(lay, step, LAYERS, now, prev, following, half, gain, band, along_z, inject)
        keep_own(lay, step, following, history)
        now, prev, following = following, now, prev
    if not last:
        store_state(lay, now, prev, state_out, send)


def add_gradient(lay, before, adjoint, history, state, gradient):
    def layer(y, carry):
        place = aligned(y * lay.wide)
        own = pl.ds(place, lay.wide)
        fields = [state[pl.ds(aligned(place + (lay.chunk + REACH) * lay.wide), lay.wide), :], state[own, :]]
        fields += [history[pl.ds(aligned(place + step * lay.rows), lay.wide), :] for step in range(DEPTH)]
        total = None if before is None else before[own, :]
        for step in range(DEPTH):
            index = DEPTH - 1 - step
            accel = (fields[index + 2] - fields[index + 1]) - (fields[index + 1] - fields[index])
            term = adjoint[pl.ds(aligned(place + step * lay.rows), lay.wide), :] * accel
            total = term if total is None else total + term
        gradient[own, :] = total
        return carry

    lax.fori_loop(0, lay.chunk, layer, 0)


def gradient_first(lay, adjoint, history, state, gradient):
    add_gradient(lay, None, adjoint, history, state, gradient)


def gradient_later(lay, adjoint, history, state, before, gradient):
    add_gradient(lay, before, adjoint, history, state, gradient)


def gradient_last(lay, where_ref, adjoint, history, state, before, misfit, *refs):
    sends, (gradient, plain) = refs[: lay.count_x], refs[lay.count_x :]
    add_gradient(lay, before, adjoint, history, state, gradient)
    for y in range(lay.chunk):
        for tile in range(lay.tiles):
            row = y * lay.wide + tile * ROWS
            plain[pl.ds(y * lay.wide + tile, ROWS, stride=lay.tiles), :] = gradient[row : row + ROWS, :]
    total = STEPS * lay.count_x
    for turn, send in enumerate(sends):
        other = where_ref[0] ^ turn
        for y in range(lay.chunk):
            source = pl.ds(aligned(y * lay.wide + other * ROWS), ROWS)
            send[y * ROWS : (y + 1) * ROWS, :] = plain[source, :]
        tile = pl.ds(aligned(other * LANES, LANES), LANES)
        send[lay.cells : lay.cells + total, :] = misfit[0:total, tile]


def finish(lay, slab_ref, *refs):
    pieces, (gradient, residual) = refs[: lay.count_x], refs[lay.count_x :]
    total = None
    for turn, piece in enumerate(pieces):
        start = (slab_ref[0] ^ turn) * lay.chunk
        for x in range(ROWS):
            target = pl.ds(aligned(x * lay.width_y + start), lay.chunk)
            gradient[target, :] = piece[pl.ds(x, lay.chunk, stride=ROWS), :]
        part = piece[lay.cells : lay.cells + residual.shape[0], :]
        total = part if total is None else total + part
    residual[...] = total


def gain_rows(lay, first_y):
    x = jnp.arange(ROWS)[None, :] * lay.tiles + jnp.arange(lay.tiles)[:, None]
    y = first_y + REACH + jnp.arange(lay.inner)

    def ramp(position, count):
        gap = jnp.minimum(position, count - 1 - position)
        profile = jnp.maximum(SPONGE - gap, 0).astype(jnp.float32) / SPONGE
        return profile * profile

    damping = damping_peak * (ramp(x, lay.wide)[None] + ramp(y, lay.whole_y)[:, None, None])
    gain = (2.0 / (1.0 + damping)).reshape(lay.inner * lay.wide, 1)
    return jnp.broadcast_to(gain, (lay.inner * lay.wide, LANES))


def source_rows(lay, first_y, source_cell, wavelet):
    x = source_cell // (lay.whole_y * LANES)
    y = source_cell // LANES % lay.whole_y - first_y
    z = source_cell % LANES
    inside = (y >= REACH) & (y < lay.extent - REACH)
    tile, row = x % lay.tiles, x // lay.tiles
    flat = jnp.where(inside, (y - REACH) * lay.wide + tile * ROWS + row, 0)
    buffer_row = jnp.where(inside, flat + REACH * lay.wide, 0)
    same = (buffer_row[:, None] == buffer_row[None, :]) & inside[None, :]
    spot = (z[:, None] == jnp.arange(LANES)[None, :]).astype(jnp.float32)
    lines = jnp.where(same[None, :, :, None], wavelet[:, None, :, None] * spot[None, None], 0.0)
    return buffer_row, flat, jnp.sum(lines, axis=2)


def local_tiles(
    lay,
    courant,
    state_prev,
    state_now,
    adjoint_now,
    adjoint_next,
    source_cell,
    wavelet,
    observed,
    receiver_cell,
    receiver_count,
):
    axes = ("gx", "gy")
    slab = lax.axis_index("gx")
    strip = lax.axis_index("gy")
    pair = strip // 2
    chip = jnp.where(pair % 2 == 0, slab, lay.count_x - 1 - slab)
    place = (pair * lay.count_x + chip) * 2 + strip % 2
    odd = strip % 2
    first_y = place * lay.chunk - lay.margin
    slab_int = slab.reshape(1).astype(jnp.int32)
    where = jnp.stack([place % lay.count_x, odd]).astype(jnp.int32)

    count = lay.count_x
    sources = source_cell.shape[0]
    slots = count * receiver_cell.shape[3]
    flat = lambda values: values.reshape(-1, LANES)
    part = functools.partial

    def swap(to_next, to_twin):
        return (
            lax.ppermute(to_next, axes, lay.swaps(1)),
            lax.ppermute(to_twin, axes, lay.swaps(0)),
        )

    def after(value, others):
        return lax.optimization_barrier((value, others))[0]

    buffer_row, flat_row, drive = source_rows(lay, first_y, source_cell, wavelet)
    gain = gain_rows(lay, first_y)
    ints = jnp.concatenate([odd.reshape(1), buffer_row, flat_row]).astype(jnp.int32)

    traces = flat(observed)
    forward_rows = 3 * lay.cells + -(-count // ROWS) * ROWS
    back_rows = 2 * lay.cells + traces.shape[0]
    cuts = call(
        part(cut_forward, lay),
        (slab_int, receiver_count.reshape(-1)),
        [flat(field) for field in (state_now, state_prev, courant)] + [receiver_cell.reshape(count, LANES)],
        [f32(forward_rows, LANES)] * count,
        [
            pltpu.VMEM((3, lay.width_x * lay.width_y, LANES), jnp.float32),
            pltpu.VMEM((count, LANES), jnp.int32),
            pltpu.SemaphoreType.DMA((4,)),
        ],
        space=pltpu.HBM,
        limit=60 * 1024 * 1024,
    )
    back_cuts = call(
        part(cut_adjoint, lay),
        (slab_int,),
        [flat(adjoint_now), flat(adjoint_next), traces],
        [f32(back_rows, LANES)] * count,
    )
    pieces = [lax.ppermute(cut, axes, lay.to_chunks(turn)) for turn, cut in enumerate(cuts)]
    pieces, ints, gain, drive, back_cuts = lax.optimization_barrier((pieces, ints, gain, drive, back_cuts))
    kept_rows = lay.kept * lay.wide
    state, own_courant, to_next, to_twin, codes = call(
        part(join_forward, lay),
        (where,),
        pieces,
        [f32(lay.state_rows, LANES), f32(lay.rows, LANES)]
        + [f32(lay.rows + 2 * kept_rows, LANES)] * 2
        + [f32(count, slots)],
        [pltpu.VMEM((3, lay.rows, LANES), jnp.float32)],
    )
    from_next, from_twin = swap(to_next, to_twin)

    back_pieces = [None] * count

    def move_adjoint(turns, earlier):
        for turn in turns:
            back_pieces[turn] = lax.ppermute(after(back_cuts[turn], earlier), axes, lay.to_chunks(turn))

    move_adjoint(range(1, count), codes)
    move_adjoint(range(1), from_twin)

    phases = STEPS // DEPTH
    step_cost = 8_000_000
    side_cost = 4_000_000
    history_shape = f32(DEPTH * lay.rows, LANES)
    state_shapes = [f32(lay.state_rows, LANES), f32(lay.send_rows, LANES)]
    buffers = [pltpu.VMEM((lay.extent * lay.wide, LANES), jnp.float32)] * 3
    buffers += [pltpu.VMEM((6 * LANES, 2 * LANES), jnp.bfloat16)]
    buffers += [pltpu.VMEM((lay.inner * lay.wide, LANES), jnp.float32)]
    record_scratch = [pltpu.VMEM((DEPTH * lay.rows, LANES), jnp.float32)]
    record_shape = (DEPTH * count, slots)
    histories, states, records = [], [], []
    half = own_courant
    for phase in range(phases):
        first, last = phase == 0, phase == phases - 1
        outs = [history_shape]
        if first:
            outs.append(f32(lay.inner * lay.wide, LANES))
        if not last:
            outs += state_shapes
        results = list(
            call(
                part(forward, lay, phase, sources),
                (ints,),
                [state, from_next, from_twin, half, gain, drive],
                outs,
                buffers + [pltpu.VMEM((sources, LANES), jnp.float32)],
                cost=step_cost,
            )
        )
        histories.append(results.pop(0))
        states.append(state)
        if first:
            half = results.pop(0)
        if last:
            continue
        state, send = results
        to_twin = after(send, back_pieces) if first else send
        from_next, from_twin = swap(send, to_twin)
    for history in histories[:-1]:
        records += call(
            part(record_phase, lay),
            (),
            [history, codes],
            [f32(*record_shape)],
            record_scratch,
            cost=side_cost,
        )
    back_state, to_next, to_twin = call(
        part(join_adjoint, lay),
        (where,),
        back_pieces,
        [f32(lay.state_rows, LANES)] + [f32(lay.rows + kept_rows, LANES)] * 2,
        [pltpu.VMEM((2, lay.rows, LANES), jnp.float32)],
    )
    back_from_next, back_from_twin = swap(to_next, to_twin)
    (misfit,) = call(
        part(record_last, lay, phases),
        (where,),
        [histories[-1], codes] + records + back_pieces,
        [f32(-(-(STEPS + 1) * count // ROWS) * ROWS, slots)],
        record_scratch + [pltpu.VMEM(record_shape, jnp.float32)],
        cost=side_cost,
    )

    misfit = after(misfit, [back_from_next, back_from_twin])
    misfit_next, misfit_twin = swap(misfit, misfit)
    state, from_next, from_twin = back_state, back_from_next, back_from_twin
    gradient = None
    inject_shape = f32(DEPTH, lay.inner * lay.wide, LANES)
    for phase in range(phases):
        first, last = phase == 0, phase == phases - 1
        (inject,) = call(part(spread_own, lay, phase), (), [misfit], [inject_shape], cost=side_cost)
        (inject,) = call(
            part(spread_sides, lay, phase),
            (where,),
            [inject, misfit_next, misfit_twin],
            [inject_shape],
            cost=side_cost,
            aliases={1: 0},
        )
        results = call(
            part(backward, lay, phase),
            (where,),
            [state, from_next, from_twin, half, gain, inject],
            [history_shape] + ([] if last else state_shapes),
            buffers,
            cost=step_cost,
        )
        arrays = [results[0], histories[phases - 1 - phase], states[phases - 1 - phase]]
        if last:
            sends = call(
                part(gradient_last, lay),
                (where,),
                arrays + [gradient, misfit],
                [f32(lay.cells + traces.shape[0], LANES)] * count,
                [pltpu.VMEM((lay.rows, LANES), jnp.float32)] * 2,
            )
            continue
        _, state, send = results
        from_next, from_twin = swap(send, send)
        kernel = gradient_first if first else gradient_later
        (gradient,) = call(
            part(kernel, lay), (), arrays + ([] if first else [gradient]), [f32(lay.rows, LANES)], cost=side_cost
        )
    pieces = [lax.ppermute(send, axes, lay.to_slabs(turn)) for turn, send in enumerate(sends)]
    gradient, residual = call(
        part(finish, lay),
        (slab_int,),
        pieces,
        [f32(lay.width_x * lay.width_y, LANES), f32(*traces.shape)],
    )
    return gradient.reshape(courant.shape), residual.reshape(observed.shape)


def local(courant, *rest):
    width_x, width_y, depth_z = courant.shape
    count_x, count_y = lax.axis_size("gx"), lax.axis_size("gy")
    if fits(count_x, count_y, width_x, width_y, depth_z):
        return local_tiles(Layout(count_x, count_y, width_x, width_y), courant, *rest)
    return local_blocks(courant, *rest)


def padded_2(cells, sides, width):
    for axis, dim in sides:
        count = lax.axis_size(axis)
        ends = count - 1
        head = lax.slice_in_dim(cells, 0, width, axis=dim)
        tail = lax.slice_in_dim(cells, cells.shape[dim] - width, cells.shape[dim], axis=dim)
        cells = jnp.concatenate(
            [
                lax.ppermute(tail, axis, [(i, (i + 1) % count) for i in range(ends)]),
                cells,
                lax.ppermute(head, axis, [((i + 1) % count, i) for i in range(ends)]),
            ],
            axis=dim,
        )
    return cells


def laplace(values):
    width_x, width_y, depth_z = values.shape
    padded = padded_2(values, (("gx", 0), ("gy", 1)), 4)
    z_padded = jnp.pad(values, ((0, 0), (0, 0), (4, 4)))
    summed = 3.0 * stencil[0] * values
    for offset in range(1, 5):
        paired = (
            padded[4 + offset : 4 + offset + width_x, 4 : 4 + width_y]
            + padded[4 - offset : 4 - offset + width_x, 4 : 4 + width_y]
        )
        paired = (
            paired
            + padded[4 : 4 + width_x, 4 + offset : 4 + offset + width_y]
            + padded[4 : 4 + width_x, 4 - offset : 4 - offset + width_y]
        )
        paired = (
            paired
            + z_padded[:, :, 4 + offset : 4 + offset + depth_z]
            + z_padded[:, :, 4 - offset : 4 - offset + depth_z]
        )
        summed = summed + stencil[offset] * paired
    return summed


def sponge(start, count, whole):
    position = start + jnp.arange(count, dtype=jnp.int32)
    edge_gap = jnp.minimum(position, whole - 1 - position)
    profile = jnp.maximum(SPONGE - edge_gap, 0).astype(jnp.float32) / SPONGE
    return profile * profile


def place_sum(indices, amounts, shape):
    flat = jnp.zeros((shape[0] * shape[1] * shape[2],), jnp.float32).at[indices].add(amounts)
    return flat.reshape(shape)


def local_blocks(
    courant,
    state_prev,
    state_now,
    adjoint_now,
    adjoint_next,
    source_cell,
    wavelet,
    observed,
    receiver_cell,
    receiver_count,
):
    shape = courant.shape
    width_x, width_y, depth_z = shape
    slab = lax.axis_index("gx")
    strip = lax.axis_index("gy")
    whole_x = width_x * lax.axis_size("gx")
    whole_y = width_y * lax.axis_size("gy")
    damping = damping_peak * (
        sponge(slab * width_x, width_x, whole_x)[:, None, None]
        + sponge(strip * width_y, width_y, whole_y)[None, :, None]
    )
    source_x = source_cell // (whole_y * depth_z) - slab * width_x
    source_y = source_cell // depth_z % whole_y - strip * width_y
    source_z = source_cell % depth_z
    inside = (source_x >= 0) & (source_x < width_x) & (source_y >= 0) & (source_y < width_y)
    source_flat = jnp.where(inside, (source_x * width_y + source_y) * depth_z + source_z, 0)
    source_weight = wavelet * inside.astype(jnp.float32)[None, :]
    senders = receiver_cell.shape[2]
    slots = receiver_cell.shape[3]
    cells = receiver_cell.reshape(-1)
    active = (
        jnp.arange(slots, dtype=jnp.int32)[None, :] < receiver_count.reshape(senders, 1)
    ).astype(jnp.float32)
    active_flat = active.reshape(-1)

    def advance(carry, weights):
        former, current = carry
        drive = laplace(current) + place_sum(source_flat, weights, shape)
        following = (2.0 * current - (1.0 - damping) * former + courant * drive) / (1.0 + damping)
        return (
            (current, following),
            (following - 2.0 * current + former, following.reshape(-1)[cells] * active_flat),
        )

    final_states, (accels, recorded) = lax.scan(advance, (state_prev, state_now), source_weight)
    recorded_tiles = recorded.reshape(STEPS, senders, 1, 1, slots)
    active_tiles = active.reshape(1, senders, 1, 1, slots)
    synthetic, mask_back = (
        lax.all_to_all(recorded_tiles, "gx", split_axis=1, concat_axis=3, tiled=True),
        lax.all_to_all(active_tiles, "gx", split_axis=1, concat_axis=3, tiled=True),
    )
    trace_residual = mask_back * (synthetic - observed)
    misfit = lax.all_to_all(trace_residual, "gx", split_axis=3, concat_axis=1, tiled=True)
    misfit_rows = misfit.reshape(STEPS, senders * slots)

    def retreat(carry, inputs):
        later, current, gradient = carry
        acceleration, residual_row = inputs
        drive = laplace(current) + place_sum(cells, residual_row, shape)
        earlier = (2.0 * current - (1.0 - damping) * later + courant * drive) / (1.0 + damping)
        return ((current, earlier, gradient + earlier * acceleration), None)

    start_gradient = jnp.zeros(shape, jnp.float32)
    (last_later, last_current, gradient), unused = lax.scan(
        retreat, (adjoint_next, adjoint_now, start_gradient), (accels, misfit_rows), reverse=True
    )
    return (gradient, trace_residual)


def solution(mesh):
    placed = (
        P("gx", "gy", None),
        P(("groups", "gx"), "gy", None),
        P(("groups", "gx"), "gy", None),
        P(("groups", "gx"), "gy", None),
        P(("groups", "gx"), "gy", None),
        P("groups"),
        P(None, "groups"),
        P("groups", "gx", "gy", None, None),
        P("gx", "gy", None, None),
        P("gx", "gy", None),
    )
    return jax.shard_map(
        local,
        mesh=mesh,
        in_specs=placed,
        out_specs=(P(("groups", "gx"), "gy", None), P("groups", "gx", "gy", None, None)),
        check_vma=False,
    )
```

```python
import functools

import jax
import jax.numpy as jnp
from jax import lax
from jax.experimental import pallas as pl
from jax.experimental.pallas import tpu as pltpu
from jax.sharding import PartitionSpec as P

STEPS = 12
SPONGE = 8
REACH = 4
DEPTH = 4
LANES = 128
ROWS = 8
LAYERS = 8


stencil = (-205.0 / 72.0, 8.0 / 5.0, -1.0 / 5.0, 8.0 / 315.0, -1.0 / 560.0)
damping_peak = 0.3
scale = 5040.0
weights = (3.0 * -14350.0, 8064.0, -1008.0, 128.0, -9.0)


class Layout:
    def __init__(self, count_x, count_y, width_x, width_y):
        self.count_x, self.count_y = count_x, count_y
        self.width_x, self.width_y = width_x, width_y
        self.chunk = width_y // count_x
        self.wide = width_x * count_x
        self.tiles = self.wide // ROWS
        self.whole_y = width_y * count_y
        self.margin = REACH * DEPTH
        self.extent = self.chunk + 2 * self.margin
        self.kept = self.margin - REACH
        self.inner = self.extent - 2 * REACH
        self.rows = self.chunk * self.wide
        self.cells = self.chunk * width_x
        self.near = self.chunk + 2 * REACH
        self.state_rows = (self.chunk + self.near) * self.wide
        self.lacking = range(REACH, self.chunk - REACH)
        self.send_rows = (self.chunk + len(self.lacking)) * self.wide

    def at(self, place):
        pair, rest = divmod(place, 2 * self.count_x)
        chip, core = divmod(rest, 2)
        slab = chip if pair % 2 == 0 else self.count_x - 1 - chip
        return slab * self.count_y + 2 * pair + core

    def to_chunks(self, turn):
        moves = []
        for slab in range(self.count_x):
            for strip in range(self.count_y):
                moves.append((slab * self.count_y + strip, self.at(strip * self.count_x + (slab ^ turn))))
        return moves

    def to_slabs(self, turn):
        return [(target, source) for source, target in self.to_chunks(turn)]

    def swaps(self, first):
        moves = []
        for place in range(first, self.count_x * self.count_y - 1, 2):
            moves += [(self.at(place), self.at(place + 1)), (self.at(place + 1), self.at(place))]
        return moves


def fits(count_x, count_y, width_x, width_y, depth_z):
    return (
        count_x & (count_x - 1) == 0
        and count_y % 2 == 0
        and width_x == ROWS
        and width_x * count_x == ROWS * REACH
        and depth_z == LANES
        and width_y == count_x * REACH * DEPTH
    )


def f32(*shape):
    return jax.ShapeDtypeStruct(shape, jnp.float32)


def call(
    kernel, ints, arrays, outs, scratch=(), cost=1_000_000, space=pltpu.VMEM, aliases=None, limit=32 * 1024 * 1024
):
    return pl.pallas_call(
        kernel,
        out_shape=tuple(outs),
        in_specs=[pl.BlockSpec(memory_space=pltpu.SMEM)] * len(ints)
        + [pl.BlockSpec(memory_space=space)] * len(arrays),
        out_specs=tuple(pl.BlockSpec(memory_space=pltpu.VMEM) for _ in outs),
        scratch_shapes=list(scratch),
        input_output_aliases=aliases or {},
        compiler_params=pltpu.CompilerParams(vmem_limit_bytes=limit),
        cost_estimate=pl.CostEstimate(flops=cost, bytes_accessed=cost, transcendentals=0),
    )(*ints, *arrays)


def aligned(value, to=ROWS):
    return pl.multiple_of(value, to)


def cut_chunk(lay, slab, turn, fields, target):
    start = (slab ^ turn) * lay.chunk
    for index, field in enumerate(fields):
        for y in range(lay.chunk):
            row = (index * lay.chunk + y) * ROWS
            target[row : row + ROWS, :] = field[pl.ds(start + y, ROWS, stride=lay.width_y), :]


def cut_forward(lay, slab_ref, count_ref, *refs):
    inputs, sends, (held, held_cell, done) = refs[:4], refs[4 : 4 + lay.count_x], refs[4 + lay.count_x :]
    fields = [held.at[index] for index in range(3)]
    copies = [
        pltpu.make_async_copy(source, target, done.at[index])
        for index, (source, target) in enumerate(zip(inputs, fields + [held_cell]))
    ]
    for copy in copies:
        copy.start()
    for copy in copies:
        copy.wait()
    slots = lax.broadcasted_iota(jnp.int32, (1, LANES), 1)
    used = []
    for tile in range(lay.count_x):
        cell = jnp.where(slots < count_ref[tile], held_cell[tile : tile + 1, :], -1)
        used.append(cell.astype(jnp.float32))
    for turn, send in enumerate(sends):
        cut_chunk(lay, slab_ref[0], turn, fields, send)
        for tile in range(lay.count_x):
            row = 3 * lay.cells + tile
            send[row : row + 1, :] = used[tile]


def cut_adjoint(lay, slab_ref, now, prev, observed, *sends):
    for turn, send in enumerate(sends):
        cut_chunk(lay, slab_ref[0], turn, (now, prev), send)
        row = 2 * lay.cells
        send[row : row + observed.shape[0], :] = observed[...]


def join_fields(lay, own_slot, odd, pieces, joined, state, courant, send_next, send_twin):
    fields = joined.shape[0]
    for turn, piece in enumerate(pieces):
        start_x = (own_slot ^ turn) * ROWS
        for field in range(fields):
            for y in range(lay.chunk):
                row = (field * lay.chunk + y) * ROWS
                joined[field, pl.ds(aligned(y * lay.wide + start_x), ROWS), :] = piece[row : row + ROWS, :]
    kept_rows = lay.kept * lay.wide
    for field in range(fields):
        target, first = (state, 0) if field == 0 else (state, (lay.chunk + REACH) * lay.wide)
        if field == 2:
            target, first = courant, 0
        for y in range(lay.chunk):
            for tile in range(lay.tiles):
                values = joined[field, pl.ds(y * lay.wide + tile, ROWS, stride=lay.tiles), :]
                row = y * lay.wide + tile * ROWS
                target[first + row : first + row + ROWS, :] = values
                if field == 0:
                    send_next[row : row + ROWS, :] = values
                    send_twin[row : row + ROWS, :] = values
    for field in range(1, fields):
        source, first = (state, (lay.chunk + REACH) * lay.wide) if field == 1 else (courant, 0)
        place = lay.rows + (field - 1) * kept_rows
        skipped = (lay.chunk - lay.kept) * lay.wide
        ahead = source[pl.ds(aligned(first + odd * skipped), kept_rows), :]
        send_next[place : place + kept_rows, :] = ahead
        behind = source[pl.ds(aligned(first + (1 - odd) * skipped), kept_rows), :]
        send_twin[place : place + kept_rows, :] = behind


def join_forward(lay, where_ref, *refs):
    pieces, (state, courant, send_next, send_twin, codes, joined) = refs[: lay.count_x], refs[lay.count_x :]
    own_slot = where_ref[0]
    join_fields(lay, own_slot, where_ref[1], pieces, joined, state, courant, send_next, send_twin)
    first = 3 * lay.cells
    strip_cells = lay.width_y * LANES
    slab_row = lax.broadcasted_iota(jnp.int32, codes.shape, 0)
    found = jnp.full(codes.shape, -1.0, jnp.float32)
    for turn, piece in enumerate(pieces):
        cell = piece[first : first + lay.count_x, :].astype(jnp.int32)
        used = cell >= 0
        cell = jnp.maximum(cell, 0)
        x = lax.div(cell, jnp.int32(strip_cells))
        y = lax.rem(lax.div(cell, jnp.int32(LANES)), jnp.int32(lay.width_y)) - own_slot * lay.chunk
        inside = used & (y >= 0) & (y < lay.chunk)
        code = jnp.where(inside, (y * ROWS + x) * LANES + lax.rem(cell, jnp.int32(LANES)), -1)
        code = code.astype(jnp.float32)
        line = jnp.concatenate([code[tile : tile + 1, :] for tile in range(lay.count_x)], axis=1)
        found = jnp.where(slab_row == (own_slot ^ turn), jnp.broadcast_to(line, codes.shape), found)
    codes[...] = found


def join_adjoint(lay, where_ref, *refs):
    pieces, (state, send_next, send_twin, joined) = refs[: lay.count_x], refs[lay.count_x :]
    join_fields(lay, where_ref[0], where_ref[1], pieces, joined, state, None, send_next, send_twin)


def load_state(lay, odd, first, now, prev, state, from_next, from_twin):
    wide = lay.wide

    def put(buffer, layer, ref, source, count):
        target = pl.ds(layer * wide if isinstance(layer, int) else aligned(layer * wide), count * wide)
        buffer[target, :] = ref[source * wide : (source + count) * wide, :]

    ahead = lay.margin + lay.chunk
    put(now, lay.margin, state, 0, lay.chunk)
    put(now, odd * ahead, from_next, 0, lay.chunk)
    put(now, (1 - odd) * ahead, from_twin, 0, lay.chunk)
    if first:
        put(prev, lay.margin, state, lay.chunk + REACH, lay.chunk)
        put(prev, odd * ahead + (1 - odd) * REACH, from_next, lay.chunk, lay.kept)
        put(prev, (1 - odd) * ahead + odd * REACH, from_twin, lay.chunk, lay.kept)
        return
    put(prev, lay.margin - REACH, state, lay.chunk, lay.near)
    put(prev, odd * ahead + lay.lacking[0], from_next, lay.chunk, len(lay.lacking))
    put(prev, (1 - odd) * ahead + lay.lacking[0], from_twin, lay.chunk, len(lay.lacking))


def store_state(lay, now, prev, state, send):
    wide = lay.wide

    def put(ref, target, buffer, layer, count):
        ref[target * wide : (target + count) * wide, :] = buffer[layer * wide : (layer + count) * wide, :]

    put(state, 0, now, lay.margin, lay.chunk)
    put(send, 0, now, lay.margin, lay.chunk)
    put(state, lay.chunk, prev, lay.margin - REACH, lay.near)
    put(send, lay.chunk, prev, lay.margin + lay.lacking[0], len(lay.lacking))


def split(values):
    high = values.astype(jnp.bfloat16)
    rest = values - high.astype(jnp.float32)
    middle = rest.astype(jnp.bfloat16)
    low = (rest - middle.astype(jnp.float32)).astype(jnp.bfloat16)
    return high, middle, low


def fill_band(band):
    row = lax.broadcasted_iota(jnp.int32, (2 * LANES, 2 * LANES), 0)
    column = lax.broadcasted_iota(jnp.int32, (2 * LANES, 2 * LANES), 1)
    apart = jnp.where((row < LANES) == (column < LANES), jnp.abs(row - column), 0)
    values = jnp.zeros((2 * LANES, 2 * LANES), jnp.float32)
    for k in range(1, REACH + 1):
        values = jnp.where(apart == k, weights[k], values)
    values = values.astype(jnp.bfloat16)
    for part in range(3):
        band[part * 2 * LANES : (part + 1) * 2 * LANES, :] = values


def multiply_z(lay, first_layer, count, now, band, along_z):
    half = count * lay.wide // 2
    first = first_layer * lay.wide
    parts = [split(now[start : start + half, :]) for start in (first, first + half)]
    both = [side[part] for part in range(3) for side in parts]
    found = jnp.dot(jnp.concatenate(both, axis=1), band[...], preferred_element_type=jnp.float32)
    along_z[0:half, :] = found[:, :LANES]
    along_z[half : 2 * half, :] = found[:, LANES:]


def sweep(lay, step, group, now, prev, following, half, gain, band, along_z, inject=None):
    first_layer = REACH * (step + 1)
    multiply_z(lay, first_layer, lay.extent - 2 * first_layer, now, band, along_z)
    row = lax.broadcasted_iota(jnp.int32, (ROWS, LANES), 0)
    top, bottom = row == 0, row == ROWS - 1

    def layers(block, carry):
        start = first_layer + group * block
        around = now.at[pl.ds(aligned((start - REACH) * lay.wide), (group + 2 * REACH) * lay.wide)]
        here = pl.ds(aligned(start * lay.wide), group * lay.wide)
        former_rows, target = prev.at[here], following.at[here]
        inner = pl.ds(aligned((start - REACH) * lay.wide), group * lay.wide)
        half_rows, gain_rows = half.at[inner], gain.at[inner]
        added = None if inject is None else inject.at[step, inner]
        z_rows = along_z.at[pl.ds(aligned(block * group * lay.wide), group * lay.wide)]

        def at(y, tile):
            first = ((y + REACH) * lay.tiles + tile) * ROWS
            return around[first : first + ROWS, :]

        for y in range(group):
            center = [at(y, tile) for tile in range(lay.tiles)]
            lower = [jnp.where(top, 0.0, pltpu.roll(tile, 1, 0)) for tile in center]
            upper = [jnp.where(bottom, 0.0, pltpu.roll(tile, ROWS - 1, 0)) for tile in center]
            line = lower + center + upper
            for tile in range(lay.tiles):
                place = (y * lay.tiles + tile) * ROWS
                place = slice(place, place + ROWS)
                total = z_rows[place, :] + weights[0] * center[tile]
                for k in range(1, REACH + 1):
                    pair = line[lay.tiles + tile - k] + line[lay.tiles + tile + k]
                    total = total + weights[k] * (pair + (at(y - k, tile) + at(y + k, tile)))
                if added is not None:
                    total = total + added[pl.ds(y * lay.wide + tile, ROWS, stride=lay.tiles), :]
                former = former_rows[place, :]
                change = (center[tile] - former) + half_rows[place, :] * total
                target[place, :] = former + gain_rows[place, :] * change
        return carry

    lax.fori_loop(0, (lay.extent - 2 * first_layer) // group, layers, 0)


def keep_own(lay, step, following, history):
    first = lay.margin * lay.wide
    history[step * lay.rows : (step + 1) * lay.rows, :] = following[first : first + lay.rows, :]


def forward(lay, phase, sources, ints, state, from_next, from_twin, courant, gain, drive, *refs):
    first, last = phase == 0, phase == STEPS // DEPTH - 1
    refs = list(refs)
    history = refs.pop(0)
    half = refs.pop(0) if first else courant
    if not last:
        state_out, send = refs.pop(0), refs.pop(0)
    now, prev, following, band, along_z, pulse = refs
    odd = ints[0]

    fill_band(band)
    load_state(lay, odd, first, now, prev, state, from_next, from_twin)
    if first:
        tail = (lay.chunk + lay.kept) * lay.wide
        part = lay.kept * lay.wide
        half[part : part + lay.rows, :] = (0.5 / scale) * courant[...]
        ahead = part + lay.rows
        half[pl.ds(aligned(odd * ahead), part), :] = (0.5 / scale) * from_next[tail : tail + part, :]
        half[pl.ds(aligned((1 - odd) * ahead), part), :] = (0.5 / scale) * from_twin[tail : tail + part, :]
    for source in range(sources):
        flat = pl.ds(ints[1 + sources + source], 1)
        pulse[source : source + 1, :] = scale * (half[flat, :] * gain[flat, :])

    for step in range(DEPTH):
        sweep(lay, step, LAYERS, now, prev, following, half, gain, band, along_z)
        added = pulse[...] * drive[phase * DEPTH + step]
        places = [pl.ds(ints[1 + source], 1) for source in range(sources)]
        lines = [following[place, :] for place in places]
        for source, (place, line) in enumerate(zip(places, lines)):
            following[place, :] = line + added[source : source + 1, :]
        keep_own(lay, step, following, history)
        now, prev, following = following, now, prev

    if not last:
        store_state(lay, now, prev, state_out, send)


def slot_rows(codes, slab):
    code = codes[slab : slab + 1, :].astype(jnp.int32)
    row = jnp.where(code >= 0, lax.shift_right_arithmetic(code, 7), -1)
    return row, jnp.where(code >= 0, code & (LANES - 1), -1)


def record_slots(lay, history, codes, plain, record):
    for step in range(DEPTH):
        for y in range(lay.chunk):
            for tile in range(lay.tiles):
                row = step * lay.rows + y * lay.wide
                values = history[row + tile * ROWS : row + (tile + 1) * ROWS, :]
                plain[pl.ds(row + tile, ROWS, stride=lay.tiles), :] = values
    slots = codes.shape[1]
    width = 2 * LANES
    for slab in range(lay.count_x):
        cell_row, cell_z = slot_rows(codes, slab)
        tiles = []
        for step in range(DEPTH):
            for y in range(lay.chunk):
                row = step * lay.rows + y * lay.wide + slab * ROWS
                tiles.append(plain[row : row + ROWS, :])
        parts = jnp.concatenate(split(jnp.concatenate(tiles, axis=0)), axis=1)
        for start in range(0, slots, width):
            here = slice(start, start + width)
            z = lax.broadcasted_iota(jnp.int32, (LANES, width), 0)
            pick = jnp.where(z == cell_z[:, here], 1.0, 0.0).astype(jnp.bfloat16)
            found = jnp.dot(parts, jnp.concatenate([pick] * 3, axis=0), preferred_element_type=jnp.float32)
            wanted = lax.broadcasted_iota(jnp.int32, (lay.cells, width), 0) == cell_row[:, here]
            for step in range(DEPTH):
                part = jnp.where(wanted, found[step * lay.cells : (step + 1) * lay.cells, :], 0.0)
                row = step * lay.count_x + slab
                record[row : row + 1, here] = jnp.sum(part, axis=0, keepdims=True)


def record_phase(lay, history, codes, record, plain):
    record_slots(lay, history, codes, plain, record)


def record_last(lay, phases, where_ref, history, codes, *refs):
    earlier, refs = refs[: phases - 1], refs[phases - 1 :]
    observed, (misfit, plain, record) = refs[: lay.count_x], refs[lay.count_x :]
    record_slots(lay, history, codes, plain, record)
    block = DEPTH * lay.count_x
    for index, part in enumerate(list(earlier) + [record]):
        misfit[index * block : (index + 1) * block, :] = part[...]
    total = STEPS * lay.count_x
    for slab in range(lay.count_x):
        misfit[total + slab : total + slab + 1, :] = codes[slab : slab + 1, :]
    for turn, piece in enumerate(observed):
        place = pl.ds(aligned((where_ref[0] ^ turn) * LANES, LANES), LANES)
        used = jnp.concatenate([codes[:, place]] * STEPS, axis=0) >= 0
        seen = piece[2 * lay.cells : 2 * lay.cells + total, :]
        misfit[0:total, place] = jnp.where(used, misfit[0:total, place] - seen, 0.0)


def spread(lay, phase, side, misfit, inject):
    codes = misfit[STEPS * lay.count_x : (STEPS + 1) * lay.count_x, :]
    for slab in range(lay.count_x):
        cell_row, cell_z = slot_rows(codes, slab)
        slots = cell_row.shape[1]
        z = lax.broadcasted_iota(jnp.int32, (LANES, slots), 0)
        pick = jnp.where(z == cell_z, 1.0, 0.0).astype(jnp.bfloat16)
        hit = lax.broadcasted_iota(jnp.int32, (lay.cells, slots), 0) == cell_row
        hit = jnp.where(hit, 1.0, 0.0).astype(jnp.bfloat16)
        left, spans = [], []
        for step in range(DEPTH):
            low, high = 0, lay.chunk
            if side < 0:
                low = REACH * (step + 1) - lay.margin + lay.chunk
            if side > 0:
                high = lay.margin - REACH * (step + 1)
            if low >= high:
                continue
            row = (STEPS - 1 - phase * DEPTH - step) * lay.count_x + slab
            parts = split(scale * misfit[row : row + 1, :])
            left += [hit[low * ROWS : high * ROWS, :] * part for part in parts]
            spans.append((step, low, high))
        placed = lax.dot_general(
            jnp.concatenate(left, axis=0),
            pick,
            (((1,), (1,)), ((), ())),
            preferred_element_type=jnp.float32,
        )
        at = 0
        for step, low, high in spans:
            rows = (high - low) * ROWS
            total = placed[at : at + rows, :]
            for part in (1, 2):
                total = total + placed[at + part * rows : at + (part + 1) * rows, :]
            for y in range(low, high):
                layer = lay.margin + side * lay.chunk + y - REACH
                target = layer * lay.wide + slab * ROWS
                inject[step, target : target + ROWS, :] = total[(y - low) * ROWS : (y - low + 1) * ROWS, :]
            at += 3 * rows


def spread_own(lay, phase, misfit, inject):
    spread(lay, phase, 0, misfit, inject)


def spread_sides(lay, phase, where_ref, own, misfit_next, misfit_twin, inject):
    odd = where_ref[1]

    @pl.when(odd == 1)
    def ahead_is_next():
        spread(lay, phase, 1, misfit_next, inject)
        spread(lay, phase, -1, misfit_twin, inject)

    @pl.when(odd == 0)
    def behind_is_next():
        spread(lay, phase, -1, misfit_next, inject)
        spread(lay, phase, 1, misfit_twin, inject)


def backward(lay, phase, where_ref, state, from_next, from_twin, half, gain, inject, *refs):
    first, last = phase == 0, phase == STEPS // DEPTH - 1
    refs = list(refs)
    history = refs.pop(0)
    if not last:
        state_out, send = refs.pop(0), refs.pop(0)
    now, prev, following, band, along_z = refs

    fill_band(band)
    load_state(lay, where_ref[1], first, now, prev, state, from_next, from_twin)
    for step in range(DEPTH):
        sweep(lay, step, LAYERS, now, prev, following, half, gain, band, along_z, inject)
        keep_own(lay, step, following, history)
        now, prev, following = following, now, prev
    if not last:
        store_state(lay, now, prev, state_out, send)


def add_gradient(lay, before, adjoint, history, state, gradient):
    def layer(y, carry):
        place = aligned(y * lay.wide)
        own = pl.ds(place, lay.wide)
        fields = [state[pl.ds(aligned(place + (lay.chunk + REACH) * lay.wide), lay.wide), :], state[own, :]]
        fields += [history[pl.ds(aligned(place + step * lay.rows), lay.wide), :] for step in range(DEPTH)]
        total = None if before is None else before[own, :]
        for step in range(DEPTH):
            index = DEPTH - 1 - step
            accel = (fields[index + 2] - fields[index + 1]) - (fields[index + 1] - fields[index])
            term = adjoint[pl.ds(aligned(place + step * lay.rows), lay.wide), :] * accel
            total = term if total is None else total + term
        gradient[own, :] = total
        return carry

    lax.fori_loop(0, lay.chunk, layer, 0)


def gradient_first(lay, adjoint, history, state, gradient):
    add_gradient(lay, None, adjoint, history, state, gradient)


def gradient_later(lay, adjoint, history, state, before, gradient):
    add_gradient(lay, before, adjoint, history, state, gradient)


def gradient_last(lay, where_ref, adjoint, history, state, before, *refs):
    sends, (gradient, plain) = refs[: lay.count_x], refs[lay.count_x :]
    add_gradient(lay, before, adjoint, history, state, gradient)
    for y in range(lay.chunk):
        for tile in range(lay.tiles):
            row = y * lay.wide + tile * ROWS
            plain[pl.ds(y * lay.wide + tile, ROWS, stride=lay.tiles), :] = gradient[row : row + ROWS, :]
    for turn, send in enumerate(sends):
        other = where_ref[0] ^ turn
        for y in range(lay.chunk):
            source = pl.ds(aligned(y * lay.wide + other * ROWS), ROWS)
            send[y * ROWS : (y + 1) * ROWS, :] = plain[source, :]


def place_residual(lay, strip_ref, misfit, placed):
    total = STEPS * lay.count_x
    placed[...] = jnp.zeros_like(placed)
    for tile in range(lay.count_x):
        placed[tile, strip_ref[0]] = misfit[0:total, tile * LANES : (tile + 1) * LANES]


def finish(lay, slab_ref, *refs):
    pieces, gradient = refs[: lay.count_x], refs[lay.count_x]
    for turn, piece in enumerate(pieces):
        start = (slab_ref[0] ^ turn) * lay.chunk
        for x in range(ROWS):
            target = pl.ds(aligned(x * lay.width_y + start), lay.chunk)
            gradient[target, :] = piece[pl.ds(x, lay.chunk, stride=ROWS), :]


def gain_rows(lay, first_y):
    x = jnp.arange(ROWS)[None, :] * lay.tiles + jnp.arange(lay.tiles)[:, None]
    y = first_y + REACH + jnp.arange(lay.inner)

    def ramp(position, count):
        gap = jnp.minimum(position, count - 1 - position)
        profile = jnp.maximum(SPONGE - gap, 0).astype(jnp.float32) / SPONGE
        return profile * profile

    damping = damping_peak * (ramp(x, lay.wide)[None] + ramp(y, lay.whole_y)[:, None, None])
    gain = (2.0 / (1.0 + damping)).reshape(lay.inner * lay.wide, 1)
    return jnp.broadcast_to(gain, (lay.inner * lay.wide, LANES))


def source_rows(lay, first_y, source_cell, wavelet):
    x = source_cell // (lay.whole_y * LANES)
    y = source_cell // LANES % lay.whole_y - first_y
    z = source_cell % LANES
    inside = (y >= REACH) & (y < lay.extent - REACH)
    tile, row = x % lay.tiles, x // lay.tiles
    flat = jnp.where(inside, (y - REACH) * lay.wide + tile * ROWS + row, 0)
    buffer_row = jnp.where(inside, flat + REACH * lay.wide, 0)
    same = (buffer_row[:, None] == buffer_row[None, :]) & inside[None, :]
    spot = (z[:, None] == jnp.arange(LANES)[None, :]).astype(jnp.float32)
    lines = jnp.where(same[None, :, :, None], wavelet[:, None, :, None] * spot[None, None], 0.0)
    return buffer_row, flat, jnp.sum(lines, axis=2)


def local_tiles(
    lay,
    courant,
    state_prev,
    state_now,
    adjoint_now,
    adjoint_next,
    source_cell,
    wavelet,
    observed,
    receiver_cell,
    receiver_count,
):
    axes = ("gx", "gy")
    slab = lax.axis_index("gx")
    strip = lax.axis_index("gy")
    pair = strip // 2
    chip = jnp.where(pair % 2 == 0, slab, lay.count_x - 1 - slab)
    place = (pair * lay.count_x + chip) * 2 + strip % 2
    odd = strip % 2
    first_y = place * lay.chunk - lay.margin
    slab_int = slab.reshape(1).astype(jnp.int32)
    where = jnp.stack([place % lay.count_x, odd]).astype(jnp.int32)

    count = lay.count_x
    sources = source_cell.shape[0]
    slots = count * receiver_cell.shape[3]
    flat = lambda values: values.reshape(-1, LANES)
    part = functools.partial

    def swap(to_next, to_twin):
        return (
            lax.ppermute(to_next, axes, lay.swaps(1)),
            lax.ppermute(to_twin, axes, lay.swaps(0)),
        )

    def after(value, others):
        return lax.optimization_barrier((value, others))[0]

    buffer_row, flat_row, drive = source_rows(lay, first_y, source_cell, wavelet)
    gain = gain_rows(lay, first_y)
    ints = jnp.concatenate([odd.reshape(1), buffer_row, flat_row]).astype(jnp.int32)

    traces = flat(observed)
    forward_rows = 3 * lay.cells + -(-count // ROWS) * ROWS
    back_rows = 2 * lay.cells + traces.shape[0]
    cuts = call(
        part(cut_forward, lay),
        (slab_int, receiver_count.reshape(-1)),
        [flat(field) for field in (state_now, state_prev, courant)] + [receiver_cell.reshape(count, LANES)],
        [f32(forward_rows, LANES)] * count,
        [
            pltpu.VMEM((3, lay.width_x * lay.width_y, LANES), jnp.float32),
            pltpu.VMEM((count, LANES), jnp.int32),
            pltpu.SemaphoreType.DMA((4,)),
        ],
        space=pltpu.HBM,
        limit=60 * 1024 * 1024,
    )
    back_cuts = call(
        part(cut_adjoint, lay),
        (slab_int,),
        [flat(adjoint_now), flat(adjoint_next), traces],
        [f32(back_rows, LANES)] * count,
    )
    pieces = [lax.ppermute(cut, axes, lay.to_chunks(turn)) for turn, cut in enumerate(cuts)]
    pieces, ints, gain, drive, back_cuts = lax.optimization_barrier((pieces, ints, gain, drive, back_cuts))
    kept_rows = lay.kept * lay.wide
    state, own_courant, to_next, to_twin, codes = call(
        part(join_forward, lay),
        (where,),
        pieces,
        [f32(lay.state_rows, LANES), f32(lay.rows, LANES)]
        + [f32(lay.rows + 2 * kept_rows, LANES)] * 2
        + [f32(count, slots)],
        [pltpu.VMEM((3, lay.rows, LANES), jnp.float32)],
    )
    from_next, from_twin = swap(to_next, to_twin)

    back_pieces = [None] * count

    def move_adjoint(turns, earlier):
        for turn in turns:
            back_pieces[turn] = lax.ppermute(after(back_cuts[turn], earlier), axes, lay.to_chunks(turn))

    move_adjoint(range(1, count), codes)
    move_adjoint(range(1), from_twin)

    phases = STEPS // DEPTH
    step_cost = 8_000_000
    side_cost = 4_000_000
    history_shape = f32(DEPTH * lay.rows, LANES)
    state_shapes = [f32(lay.state_rows, LANES), f32(lay.send_rows, LANES)]
    buffers = [pltpu.VMEM((lay.extent * lay.wide, LANES), jnp.float32)] * 3
    buffers += [pltpu.VMEM((6 * LANES, 2 * LANES), jnp.bfloat16)]
    buffers += [pltpu.VMEM((lay.inner * lay.wide, LANES), jnp.float32)]
    record_scratch = [pltpu.VMEM((DEPTH * lay.rows, LANES), jnp.float32)]
    record_shape = (DEPTH * count, slots)
    histories, states, records = [], [], []
    half = own_courant
    for phase in range(phases):
        first, last = phase == 0, phase == phases - 1
        outs = [history_shape]
        if first:
            outs.append(f32(lay.inner * lay.wide, LANES))
        if not last:
            outs += state_shapes
        results = list(
            call(
                part(forward, lay, phase, sources),
                (ints,),
                [state, from_next, from_twin, half, gain, drive],
                outs,
                buffers + [pltpu.VMEM((sources, LANES), jnp.float32)],
                cost=step_cost,
            )
        )
        histories.append(results.pop(0))
        states.append(state)
        if first:
            half = results.pop(0)
        if last:
            continue
        state, send = results
        to_twin = after(send, back_pieces) if first else send
        from_next, from_twin = swap(send, to_twin)
    for history in histories[:-1]:
        records += call(
            part(record_phase, lay),
            (),
            [history, codes],
            [f32(*record_shape)],
            record_scratch,
            cost=side_cost,
        )
    back_state, to_next, to_twin = call(
        part(join_adjoint, lay),
        (where,),
        back_pieces,
        [f32(lay.state_rows, LANES)] + [f32(lay.rows + kept_rows, LANES)] * 2,
        [pltpu.VMEM((2, lay.rows, LANES), jnp.float32)],
    )
    back_from_next, back_from_twin = swap(to_next, to_twin)
    (misfit,) = call(
        part(record_last, lay, phases),
        (where,),
        [histories[-1], codes] + records + back_pieces,
        [f32(-(-(STEPS + 1) * count // ROWS) * ROWS, slots)],
        record_scratch + [pltpu.VMEM(record_shape, jnp.float32)],
        cost=side_cost,
    )

    misfit = after(misfit, [back_from_next, back_from_twin])
    misfit_next, misfit_twin = swap(misfit, misfit)
    state, from_next, from_twin = back_state, back_from_next, back_from_twin
    gradient = None
    inject_shape = f32(DEPTH, lay.inner * lay.wide, LANES)
    for phase in range(phases):
        first, last = phase == 0, phase == phases - 1
        (inject,) = call(part(spread_own, lay, phase), (), [misfit], [inject_shape], cost=side_cost)
        (inject,) = call(
            part(spread_sides, lay, phase),
            (where,),
            [inject, misfit_next, misfit_twin],
            [inject_shape],
            cost=side_cost,
            aliases={1: 0},
        )
        results = call(
            part(backward, lay, phase),
            (where,),
            [state, from_next, from_twin, half, gain, inject],
            [history_shape] + ([] if last else state_shapes),
            buffers,
            cost=step_cost,
        )
        arrays = [results[0], histories[phases - 1 - phase], states[phases - 1 - phase]]
        if first:
            (placed,) = call(
                part(place_residual, lay),
                ((place // count).reshape(1).astype(jnp.int32),),
                [after(misfit, results[0])],
                [f32(count, lay.count_y, *traces.shape)],
            )
            placed = placed.reshape(-1, *traces.shape)
            residual = lax.psum_scatter(placed, axes, scatter_dimension=0, tiled=False)
        if last:
            arrays[0] = after(arrays[0], residual)
            sends = call(
                part(gradient_last, lay),
                (where,),
                arrays + [gradient],
                [f32(lay.cells, LANES)] * count,
                [pltpu.VMEM((lay.rows, LANES), jnp.float32)] * 2,
            )
            continue
        _, state, send = results
        from_next, from_twin = swap(send, send)
        kernel = gradient_first if first else gradient_later
        (gradient,) = call(
            part(kernel, lay), (), arrays + ([] if first else [gradient]), [f32(lay.rows, LANES)], cost=side_cost
        )
    pieces = [lax.ppermute(send, axes, lay.to_slabs(turn)) for turn, send in enumerate(sends)]
    (gradient,) = call(part(finish, lay), (slab_int,), pieces, [f32(lay.width_x * lay.width_y, LANES)])
    return gradient.reshape(courant.shape), residual.reshape(observed.shape)


def local(courant, *rest):
    width_x, width_y, depth_z = courant.shape
    count_x, count_y = lax.axis_size("gx"), lax.axis_size("gy")
    if fits(count_x, count_y, width_x, width_y, depth_z):
        return local_tiles(Layout(count_x, count_y, width_x, width_y), courant, *rest)
    return local_blocks(courant, *rest)


def padded_2(cells, sides, width):
    for axis, dim in sides:
        count = lax.axis_size(axis)
        ends = count - 1
        head = lax.slice_in_dim(cells, 0, width, axis=dim)
        tail = lax.slice_in_dim(cells, cells.shape[dim] - width, cells.shape[dim], axis=dim)
        cells = jnp.concatenate(
            [
                lax.ppermute(tail, axis, [(i, (i + 1) % count) for i in range(ends)]),
                cells,
                lax.ppermute(head, axis, [((i + 1) % count, i) for i in range(ends)]),
            ],
            axis=dim,
        )
    return cells


def laplace(values):
    width_x, width_y, depth_z = values.shape
    padded = padded_2(values, (("gx", 0), ("gy", 1)), 4)
    z_padded = jnp.pad(values, ((0, 0), (0, 0), (4, 4)))
    summed = 3.0 * stencil[0] * values
    for offset in range(1, 5):
        paired = (
            padded[4 + offset : 4 + offset + width_x, 4 : 4 + width_y]
            + padded[4 - offset : 4 - offset + width_x, 4 : 4 + width_y]
        )
        paired = (
            paired
            + padded[4 : 4 + width_x, 4 + offset : 4 + offset + width_y]
            + padded[4 : 4 + width_x, 4 - offset : 4 - offset + width_y]
        )
        paired = (
            paired
            + z_padded[:, :, 4 + offset : 4 + offset + depth_z]
            + z_padded[:, :, 4 - offset : 4 - offset + depth_z]
        )
        summed = summed + stencil[offset] * paired
    return summed


def sponge(start, count, whole):
    position = start + jnp.arange(count, dtype=jnp.int32)
    edge_gap = jnp.minimum(position, whole - 1 - position)
    profile = jnp.maximum(SPONGE - edge_gap, 0).astype(jnp.float32) / SPONGE
    return profile * profile


def place_sum(indices, amounts, shape):
    flat = jnp.zeros((shape[0] * shape[1] * shape[2],), jnp.float32).at[indices].add(amounts)
    return flat.reshape(shape)


def local_blocks(
    courant,
    state_prev,
    state_now,
    adjoint_now,
    adjoint_next,
    source_cell,
    wavelet,
    observed,
    receiver_cell,
    receiver_count,
):
    shape = courant.shape
    width_x, width_y, depth_z = shape
    slab = lax.axis_index("gx")
    strip = lax.axis_index("gy")
    whole_x = width_x * lax.axis_size("gx")
    whole_y = width_y * lax.axis_size("gy")
    damping = damping_peak * (
        sponge(slab * width_x, width_x, whole_x)[:, None, None]
        + sponge(strip * width_y, width_y, whole_y)[None, :, None]
    )
    source_x = source_cell // (whole_y * depth_z) - slab * width_x
    source_y = source_cell // depth_z % whole_y - strip * width_y
    source_z = source_cell % depth_z
    inside = (source_x >= 0) & (source_x < width_x) & (source_y >= 0) & (source_y < width_y)
    source_flat = jnp.where(inside, (source_x * width_y + source_y) * depth_z + source_z, 0)
    source_weight = wavelet * inside.astype(jnp.float32)[None, :]
    senders = receiver_cell.shape[2]
    slots = receiver_cell.shape[3]
    cells = receiver_cell.reshape(-1)
    active = (
        jnp.arange(slots, dtype=jnp.int32)[None, :] < receiver_count.reshape(senders, 1)
    ).astype(jnp.float32)
    active_flat = active.reshape(-1)

    def advance(carry, weights):
        former, current = carry
        drive = laplace(current) + place_sum(source_flat, weights, shape)
        following = (2.0 * current - (1.0 - damping) * former + courant * drive) / (1.0 + damping)
        return (
            (current, following),
            (following - 2.0 * current + former, following.reshape(-1)[cells] * active_flat),
        )

    final_states, (accels, recorded) = lax.scan(advance, (state_prev, state_now), source_weight)
    recorded_tiles = recorded.reshape(STEPS, senders, 1, 1, slots)
    active_tiles = active.reshape(1, senders, 1, 1, slots)
    synthetic, mask_back = (
        lax.all_to_all(recorded_tiles, "gx", split_axis=1, concat_axis=3, tiled=True),
        lax.all_to_all(active_tiles, "gx", split_axis=1, concat_axis=3, tiled=True),
    )
    trace_residual = mask_back * (synthetic - observed)
    misfit = lax.all_to_all(trace_residual, "gx", split_axis=3, concat_axis=1, tiled=True)
    misfit_rows = misfit.reshape(STEPS, senders * slots)

    def retreat(carry, inputs):
        later, current, gradient = carry
        acceleration, residual_row = inputs
        drive = laplace(current) + place_sum(cells, residual_row, shape)
        earlier = (2.0 * current - (1.0 - damping) * later + courant * drive) / (1.0 + damping)
        return ((current, earlier, gradient + earlier * acceleration), None)

    start_gradient = jnp.zeros(shape, jnp.float32)
    (last_later, last_current, gradient), unused = lax.scan(
        retreat, (adjoint_next, adjoint_now, start_gradient), (accels, misfit_rows), reverse=True
    )
    return (gradient, trace_residual)


def solution(mesh):
    placed = (
        P("gx", "gy", None),
        P(("groups", "gx"), "gy", None),
        P(("groups", "gx"), "gy", None),
        P(("groups", "gx"), "gy", None),
        P(("groups", "gx"), "gy", None),
        P("groups"),
        P(None, "groups"),
        P("groups", "gx", "gy", None, None),
        P("gx", "gy", None, None),
        P("gx", "gy", None),
    )
    return jax.shard_map(
        local,
        mesh=mesh,
        in_specs=placed,
        out_specs=(P(("groups", "gx"), "gy", None), P("groups", "gx", "gy", None, None)),
        check_vma=False,
    )
```

```python
import functools

import jax
import jax.numpy as jnp
from jax import lax
from jax.experimental import pallas as pl
from jax.experimental.pallas import tpu as pltpu
from jax.sharding import PartitionSpec as P

STEPS = 12
SPONGE = 8
REACH = 4
DEPTH = 4
LANES = 128
ROWS = 8
LAYERS = 8


stencil = (-205.0 / 72.0, 8.0 / 5.0, -1.0 / 5.0, 8.0 / 315.0, -1.0 / 560.0)
damping_peak = 0.3
scale = 5040.0
weights = (3.0 * -14350.0, 8064.0, -1008.0, 128.0, -9.0)


class Layout:
    def __init__(self, count_x, count_y, width_x, width_y):
        self.count_x, self.count_y = count_x, count_y
        self.width_x, self.width_y = width_x, width_y
        self.chunk = width_y // count_x
        self.wide = width_x * count_x
        self.tiles = self.wide // ROWS
        self.whole_y = width_y * count_y
        self.margin = REACH * DEPTH
        self.extent = self.chunk + 2 * self.margin
        self.kept = self.margin - REACH
        self.inner = self.extent - 2 * REACH
        self.rows = self.chunk * self.wide
        self.cells = self.chunk * width_x
        self.near = self.chunk + 2 * REACH
        self.state_rows = (self.chunk + self.near) * self.wide
        self.lacking = range(REACH, self.chunk - REACH)
        self.send_rows = (self.chunk + len(self.lacking)) * self.wide

    def at(self, place):
        pair, rest = divmod(place, 2 * self.count_x)
        chip, core = divmod(rest, 2)
        slab = chip if pair % 2 == 0 else self.count_x - 1 - chip
        return slab * self.count_y + 2 * pair + core

    def to_chunks(self, turn):
        moves = []
        for slab in range(self.count_x):
            for strip in range(self.count_y):
                moves.append((slab * self.count_y + strip, self.at(strip * self.count_x + (slab ^ turn))))
        return moves

    def to_slabs(self, turn):
        return [(target, source) for source, target in self.to_chunks(turn)]

    def swaps(self, first):
        moves = []
        for place in range(first, self.count_x * self.count_y - 1, 2):
            moves += [(self.at(place), self.at(place + 1)), (self.at(place + 1), self.at(place))]
        return moves


def fits(count_x, count_y, width_x, width_y, depth_z):
    return (
        count_x & (count_x - 1) == 0
        and count_y % 2 == 0
        and width_x == ROWS
        and width_x * count_x == ROWS * REACH
        and depth_z == LANES
        and width_y == count_x * REACH * DEPTH
    )


def f32(*shape):
    return jax.ShapeDtypeStruct(shape, jnp.float32)


def call(
    kernel, ints, arrays, outs, scratch=(), cost=1_000_000, space=pltpu.VMEM, aliases=None, limit=32 * 1024 * 1024
):
    return pl.pallas_call(
        kernel,
        out_shape=tuple(outs),
        in_specs=[pl.BlockSpec(memory_space=pltpu.SMEM)] * len(ints)
        + [pl.BlockSpec(memory_space=space)] * len(arrays),
        out_specs=tuple(pl.BlockSpec(memory_space=pltpu.VMEM) for _ in outs),
        scratch_shapes=list(scratch),
        input_output_aliases=aliases or {},
        compiler_params=pltpu.CompilerParams(vmem_limit_bytes=limit),
        cost_estimate=pl.CostEstimate(flops=cost, bytes_accessed=cost, transcendentals=0),
    )(*ints, *arrays)


def aligned(value, to=ROWS):
    return pl.multiple_of(value, to)


def cut_field(lay, slab, turn, index, field, target):
    start = (slab ^ turn) * lay.chunk
    for y in range(lay.chunk):
        row = (index * lay.chunk + y) * ROWS
        target[row : row + ROWS, :] = field[pl.ds(start + y, ROWS, stride=lay.width_y), :]


def cut_forward(lay, slab_ref, count_ref, *refs):
    inputs, sends, (held, held_cell, done) = refs[:4], refs[4 : 4 + lay.count_x], refs[4 + lay.count_x :]
    fields = [held.at[index] for index in range(3)]
    copies = [
        pltpu.make_async_copy(source, target, done.at[index])
        for index, (source, target) in enumerate(zip(inputs, fields + [held_cell]))
    ]
    for copy in copies:
        copy.start()
    for index, (copy, field) in enumerate(zip(copies, fields)):
        copy.wait()
        for turn, send in enumerate(sends):
            cut_field(lay, slab_ref[0], turn, index, field, send)
    copies[-1].wait()
    slots = lax.broadcasted_iota(jnp.int32, (1, LANES), 1)
    used = []
    for tile in range(lay.count_x):
        cell = jnp.where(slots < count_ref[tile], held_cell[tile : tile + 1, :], -1)
        used.append(cell.astype(jnp.float32))
    for send in sends:
        for tile in range(lay.count_x):
            row = 3 * lay.cells + tile
            send[row : row + 1, :] = used[tile]


def cut_adjoint(lay, slab_ref, now, prev, observed, *sends):
    for turn, send in enumerate(sends):
        for index, field in enumerate((now, prev)):
            cut_field(lay, slab_ref[0], turn, index, field, send)
        row = 2 * lay.cells
        send[row : row + observed.shape[0], :] = observed[...]


def join_fields(lay, own_slot, odd, pieces, joined, state, courant, send_next, send_twin):
    fields = joined.shape[0]
    for turn, piece in enumerate(pieces):
        start_x = (own_slot ^ turn) * ROWS
        for field in range(fields):
            for y in range(lay.chunk):
                row = (field * lay.chunk + y) * ROWS
                joined[field, pl.ds(aligned(y * lay.wide + start_x), ROWS), :] = piece[row : row + ROWS, :]
    kept_rows = lay.kept * lay.wide
    for field in range(fields):
        target, first = (state, 0) if field == 0 else (state, (lay.chunk + REACH) * lay.wide)
        if field == 2:
            target, first = courant, 0
        for y in range(lay.chunk):
            for tile in range(lay.tiles):
                values = joined[field, pl.ds(y * lay.wide + tile, ROWS, stride=lay.tiles), :]
                row = y * lay.wide + tile * ROWS
                target[first + row : first + row + ROWS, :] = values
                if field == 0:
                    send_next[row : row + ROWS, :] = values
                    send_twin[row : row + ROWS, :] = values
    for field in range(1, fields):
        source, first = (state, (lay.chunk + REACH) * lay.wide) if field == 1 else (courant, 0)
        place = lay.rows + (field - 1) * kept_rows
        skipped = (lay.chunk - lay.kept) * lay.wide
        ahead = source[pl.ds(aligned(first + odd * skipped), kept_rows), :]
        send_next[place : place + kept_rows, :] = ahead
        behind = source[pl.ds(aligned(first + (1 - odd) * skipped), kept_rows), :]
        send_twin[place : place + kept_rows, :] = behind


def join_forward(lay, where_ref, *refs):
    pieces, (state, courant, send_next, send_twin, codes, joined) = refs[: lay.count_x], refs[lay.count_x :]
    own_slot = where_ref[0]
    join_fields(lay, own_slot, where_ref[1], pieces, joined, state, courant, send_next, send_twin)
    first = 3 * lay.cells
    strip_cells = lay.width_y * LANES
    slab_row = lax.broadcasted_iota(jnp.int32, codes.shape, 0)
    found = jnp.full(codes.shape, -1.0, jnp.float32)
    for turn, piece in enumerate(pieces):
        cell = piece[first : first + lay.count_x, :].astype(jnp.int32)
        used = cell >= 0
        cell = jnp.maximum(cell, 0)
        x = lax.div(cell, jnp.int32(strip_cells))
        y = lax.rem(lax.div(cell, jnp.int32(LANES)), jnp.int32(lay.width_y)) - own_slot * lay.chunk
        inside = used & (y >= 0) & (y < lay.chunk)
        code = jnp.where(inside, (y * ROWS + x) * LANES + lax.rem(cell, jnp.int32(LANES)), -1)
        code = code.astype(jnp.float32)
        line = jnp.concatenate([code[tile : tile + 1, :] for tile in range(lay.count_x)], axis=1)
        found = jnp.where(slab_row == (own_slot ^ turn), jnp.broadcast_to(line, codes.shape), found)
    codes[...] = found


def join_adjoint(lay, where_ref, *refs):
    pieces, (state, send_next, send_twin, joined) = refs[: lay.count_x], refs[lay.count_x :]
    join_fields(lay, where_ref[0], where_ref[1], pieces, joined, state, None, send_next, send_twin)


def load_state(lay, odd, first, now, prev, state, from_next, from_twin):
    wide = lay.wide

    def put(buffer, layer, ref, source, count):
        target = pl.ds(layer * wide if isinstance(layer, int) else aligned(layer * wide), count * wide)
        buffer[target, :] = ref[source * wide : (source + count) * wide, :]

    ahead = lay.margin + lay.chunk
    put(now, lay.margin, state, 0, lay.chunk)
    put(now, odd * ahead, from_next, 0, lay.chunk)
    put(now, (1 - odd) * ahead, from_twin, 0, lay.chunk)
    if first:
        put(prev, lay.margin, state, lay.chunk + REACH, lay.chunk)
        put(prev, odd * ahead + (1 - odd) * REACH, from_next, lay.chunk, lay.kept)
        put(prev, (1 - odd) * ahead + odd * REACH, from_twin, lay.chunk, lay.kept)
        return
    put(prev, lay.margin - REACH, state, lay.chunk, lay.near)
    put(prev, odd * ahead + lay.lacking[0], from_next, lay.chunk, len(lay.lacking))
    put(prev, (1 - odd) * ahead + lay.lacking[0], from_twin, lay.chunk, len(lay.lacking))


def store_state(lay, now, prev, state, send):
    wide = lay.wide

    def put(ref, target, buffer, layer, count):
        ref[target * wide : (target + count) * wide, :] = buffer[layer * wide : (layer + count) * wide, :]

    put(state, 0, now, lay.margin, lay.chunk)
    put(send, 0, now, lay.margin, lay.chunk)
    put(state, lay.chunk, prev, lay.margin - REACH, lay.near)
    put(send, lay.chunk, prev, lay.margin + lay.lacking[0], len(lay.lacking))


def split(values):
    high = values.astype(jnp.bfloat16)
    rest = values - high.astype(jnp.float32)
    middle = rest.astype(jnp.bfloat16)
    low = (rest - middle.astype(jnp.float32)).astype(jnp.bfloat16)
    return high, middle, low


def fill_band(band):
    row = lax.broadcasted_iota(jnp.int32, (2 * LANES, 2 * LANES), 0)
    column = lax.broadcasted_iota(jnp.int32, (2 * LANES, 2 * LANES), 1)
    apart = jnp.where((row < LANES) == (column < LANES), jnp.abs(row - column), 0)
    values = jnp.zeros((2 * LANES, 2 * LANES), jnp.float32)
    for k in range(1, REACH + 1):
        values = jnp.where(apart == k, weights[k], values)
    values = values.astype(jnp.bfloat16)
    for part in range(3):
        band[part * 2 * LANES : (part + 1) * 2 * LANES, :] = values


def multiply_z(lay, first_layer, count, now, band, along_z):
    half = count * lay.wide // 2
    first = first_layer * lay.wide
    parts = [split(now[start : start + half, :]) for start in (first, first + half)]
    both = [side[part] for part in range(3) for side in parts]
    found = jnp.dot(jnp.concatenate(both, axis=1), band[...], preferred_element_type=jnp.float32)
    along_z[0:half, :] = found[:, :LANES]
    along_z[half : 2 * half, :] = found[:, LANES:]


def sweep(lay, step, group, now, prev, following, half, gain, band, along_z, inject=None):
    first_layer = REACH * (step + 1)
    multiply_z(lay, first_layer, lay.extent - 2 * first_layer, now, band, along_z)
    row = lax.broadcasted_iota(jnp.int32, (ROWS, LANES), 0)
    top, bottom = row == 0, row == ROWS - 1

    def layers(block, carry):
        start = first_layer + group * block
        around = now.at[pl.ds(aligned((start - REACH) * lay.wide), (group + 2 * REACH) * lay.wide)]
        here = pl.ds(aligned(start * lay.wide), group * lay.wide)
        former_rows, target = prev.at[here], following.at[here]
        inner = pl.ds(aligned((start - REACH) * lay.wide), group * lay.wide)
        half_rows, gain_rows = half.at[inner], gain.at[inner]
        added = None if inject is None else inject.at[step, inner]
        z_rows = along_z.at[pl.ds(aligned(block * group * lay.wide), group * lay.wide)]

        def at(y, tile):
            first = ((y + REACH) * lay.tiles + tile) * ROWS
            return around[first : first + ROWS, :]

        for y in range(group):
            center = [at(y, tile) for tile in range(lay.tiles)]
            lower = [jnp.where(top, 0.0, pltpu.roll(tile, 1, 0)) for tile in center]
            upper = [jnp.where(bottom, 0.0, pltpu.roll(tile, ROWS - 1, 0)) for tile in center]
            line = lower + center + upper
            for tile in range(lay.tiles):
                place = (y * lay.tiles + tile) * ROWS
                place = slice(place, place + ROWS)
                total = z_rows[place, :] + weights[0] * center[tile]
                for k in range(1, REACH + 1):
                    pair = line[lay.tiles + tile - k] + line[lay.tiles + tile + k]
                    total = total + weights[k] * (pair + (at(y - k, tile) + at(y + k, tile)))
                if added is not None:
                    total = total + added[pl.ds(y * lay.wide + tile, ROWS, stride=lay.tiles), :]
                former = former_rows[place, :]
                change = (center[tile] - former) + half_rows[place, :] * total
                target[place, :] = former + gain_rows[place, :] * change
        return carry

    lax.fori_loop(0, (lay.extent - 2 * first_layer) // group, layers, 0)


def keep_own(lay, step, following, history):
    first = lay.margin * lay.wide
    history[step * lay.rows : (step + 1) * lay.rows, :] = following[first : first + lay.rows, :]


def forward(lay, phase, sources, ints, state, from_next, from_twin, courant, gain, drive, *refs):
    first, last = phase == 0, phase == STEPS // DEPTH - 1
    refs = list(refs)
    history = refs.pop(0)
    half = refs.pop(0) if first else courant
    if not last:
        state_out, send = refs.pop(0), refs.pop(0)
    now, prev, following, band, along_z, pulse = refs
    odd = ints[0]

    fill_band(band)
    load_state(lay, odd, first, now, prev, state, from_next, from_twin)
    if first:
        tail = (lay.chunk + lay.kept) * lay.wide
        part = lay.kept * lay.wide
        half[part : part + lay.rows, :] = (0.5 / scale) * courant[...]
        ahead = part + lay.rows
        half[pl.ds(aligned(odd * ahead), part), :] = (0.5 / scale) * from_next[tail : tail + part, :]
        half[pl.ds(aligned((1 - odd) * ahead), part), :] = (0.5 / scale) * from_twin[tail : tail + part, :]
    for source in range(sources):
        flat = pl.ds(ints[1 + sources + source], 1)
        pulse[source : source + 1, :] = scale * (half[flat, :] * gain[flat, :])

    for step in range(DEPTH):
        sweep(lay, step, LAYERS, now, prev, following, half, gain, band, along_z)
        added = pulse[...] * drive[phase * DEPTH + step]
        places = [pl.ds(ints[1 + source], 1) for source in range(sources)]
        lines = [following[place, :] for place in places]
        for source, (place, line) in enumerate(zip(places, lines)):
            following[place, :] = line + added[source : source + 1, :]
        keep_own(lay, step, following, history)
        now, prev, following = following, now, prev

    if not last:
        store_state(lay, now, prev, state_out, send)


def slot_rows(codes, slab):
    code = codes[slab : slab + 1, :].astype(jnp.int32)
    row = jnp.where(code >= 0, lax.shift_right_arithmetic(code, 7), -1)
    return row, jnp.where(code >= 0, code & (LANES - 1), -1)


def record_slots(lay, history, codes, plain, record):
    for step in range(DEPTH):
        for y in range(lay.chunk):
            for tile in range(lay.tiles):
                row = step * lay.rows + y * lay.wide
                values = history[row + tile * ROWS : row + (tile + 1) * ROWS, :]
                plain[pl.ds(row + tile, ROWS, stride=lay.tiles), :] = values
    slots = codes.shape[1]
    width = 2 * LANES
    for slab in range(lay.count_x):
        cell_row, cell_z = slot_rows(codes, slab)
        tiles = []
        for step in range(DEPTH):
            for y in range(lay.chunk):
                row = step * lay.rows + y * lay.wide + slab * ROWS
                tiles.append(plain[row : row + ROWS, :])
        parts = jnp.concatenate(split(jnp.concatenate(tiles, axis=0)), axis=1)
        for start in range(0, slots, width):
            here = slice(start, start + width)
            z = lax.broadcasted_iota(jnp.int32, (LANES, width), 0)
            pick = jnp.where(z == cell_z[:, here], 1.0, 0.0).astype(jnp.bfloat16)
            found = jnp.dot(parts, jnp.concatenate([pick] * 3, axis=0), preferred_element_type=jnp.float32)
            wanted = lax.broadcasted_iota(jnp.int32, (lay.cells, width), 0) == cell_row[:, here]
            for step in range(DEPTH):
                part = jnp.where(wanted, found[step * lay.cells : (step + 1) * lay.cells, :], 0.0)
                row = step * lay.count_x + slab
                record[row : row + 1, here] = jnp.sum(part, axis=0, keepdims=True)


def record_phase(lay, history, codes, record, plain):
    record_slots(lay, history, codes, plain, record)


def record_last(lay, phases, where_ref, history, codes, *refs):
    earlier, refs = refs[: phases - 1], refs[phases - 1 :]
    observed, (misfit, plain, record) = refs[: lay.count_x], refs[lay.count_x :]
    record_slots(lay, history, codes, plain, record)
    block = DEPTH * lay.count_x
    for index, part in enumerate(list(earlier) + [record]):
        misfit[index * block : (index + 1) * block, :] = part[...]
    total = STEPS * lay.count_x
    for slab in range(lay.count_x):
        misfit[total + slab : total + slab + 1, :] = codes[slab : slab + 1, :]
    for turn, piece in enumerate(observed):
        place = pl.ds(aligned((where_ref[0] ^ turn) * LANES, LANES), LANES)
        used = jnp.concatenate([codes[:, place]] * STEPS, axis=0) >= 0
        seen = piece[2 * lay.cells : 2 * lay.cells + total, :]
        misfit[0:total, place] = jnp.where(used, misfit[0:total, place] - seen, 0.0)


def spread(lay, phase, side, misfit, inject):
    codes = misfit[STEPS * lay.count_x : (STEPS + 1) * lay.count_x, :]
    for slab in range(lay.count_x):
        cell_row, cell_z = slot_rows(codes, slab)
        slots = cell_row.shape[1]
        z = lax.broadcasted_iota(jnp.int32, (LANES, slots), 0)
        pick = jnp.where(z == cell_z, 1.0, 0.0).astype(jnp.bfloat16)
        hit = lax.broadcasted_iota(jnp.int32, (lay.cells, slots), 0) == cell_row
        hit = jnp.where(hit, 1.0, 0.0).astype(jnp.bfloat16)
        left, spans = [], []
        for step in range(DEPTH):
            low, high = 0, lay.chunk
            if side < 0:
                low = REACH * (step + 1) - lay.margin + lay.chunk
            if side > 0:
                high = lay.margin - REACH * (step + 1)
            if low >= high:
                continue
            row = (STEPS - 1 - phase * DEPTH - step) * lay.count_x + slab
            parts = split(scale * misfit[row : row + 1, :])
            left += [hit[low * ROWS : high * ROWS, :] * part for part in parts]
            spans.append((step, low, high))
        placed = lax.dot_general(
            jnp.concatenate(left, axis=0),
            pick,
            (((1,), (1,)), ((), ())),
            preferred_element_type=jnp.float32,
        )
        at = 0
        for step, low, high in spans:
            rows = (high - low) * ROWS
            total = placed[at : at + rows, :]
            for part in (1, 2):
                total = total + placed[at + part * rows : at + (part + 1) * rows, :]
            for y in range(low, high):
                layer = lay.margin + side * lay.chunk + y - REACH
                target = layer * lay.wide + slab * ROWS
                inject[step, target : target + ROWS, :] = total[(y - low) * ROWS : (y - low + 1) * ROWS, :]
            at += 3 * rows


def spread_own(lay, phase, misfit, inject):
    spread(lay, phase, 0, misfit, inject)


def spread_sides(lay, phase, where_ref, own, misfit_next, misfit_twin, inject):
    odd = where_ref[1]

    @pl.when(odd == 1)
    def ahead_is_next():
        spread(lay, phase, 1, misfit_next, inject)
        spread(lay, phase, -1, misfit_twin, inject)

    @pl.when(odd == 0)
    def behind_is_next():
        spread(lay, phase, -1, misfit_next, inject)
        spread(lay, phase, 1, misfit_twin, inject)


def backward(lay, phase, where_ref, state, from_next, from_twin, half, gain, inject, *refs):
    first, last = phase == 0, phase == STEPS // DEPTH - 1
    refs = list(refs)
    history = refs.pop(0)
    if not last:
        state_out, send = refs.pop(0), refs.pop(0)
    now, prev, following, band, along_z = refs

    fill_band(band)
    load_state(lay, where_ref[1], first, now, prev, state, from_next, from_twin)
    for step in range(DEPTH):
        sweep(lay, step, LAYERS, now, prev, following, half, gain, band, along_z, inject)
        keep_own(lay, step, following, history)
        now, prev, following = following, now, prev
    if not last:
        store_state(lay, now, prev, state_out, send)


def add_gradient(lay, before, adjoint, history, state, gradient, natural=False):
    def layer(y, carry):
        place = aligned(y * lay.wide)
        own = pl.ds(place, lay.wide)
        fields = [state[pl.ds(aligned(place + (lay.chunk + REACH) * lay.wide), lay.wide), :], state[own, :]]
        fields += [history[pl.ds(aligned(place + step * lay.rows), lay.wide), :] for step in range(DEPTH)]
        total = None if before is None else before[own, :]
        for step in range(DEPTH):
            index = DEPTH - 1 - step
            accel = (fields[index + 2] - fields[index + 1]) - (fields[index + 1] - fields[index])
            term = adjoint[pl.ds(aligned(place + step * lay.rows), lay.wide), :] * accel
            total = term if total is None else total + term
        if natural:
            for tile in range(lay.tiles):
                rows = pl.ds(place + tile, ROWS, stride=lay.tiles)
                gradient[rows, :] = total[tile * ROWS : (tile + 1) * ROWS, :]
        else:
            gradient[own, :] = total
        return carry

    lax.fori_loop(0, lay.chunk, layer, 0)


def gradient_first(lay, adjoint, history, state, gradient):
    add_gradient(lay, None, adjoint, history, state, gradient)


def gradient_later(lay, adjoint, history, state, before, gradient):
    add_gradient(lay, before, adjoint, history, state, gradient)


def gradient_last(lay, where_ref, adjoint, history, state, before, misfit, *refs):
    sends, plain = refs[: lay.count_x], refs[lay.count_x]
    add_gradient(lay, before, adjoint, history, state, plain, natural=True)
    total = STEPS * lay.count_x
    for turn, send in enumerate(sends):
        other = where_ref[0] ^ turn
        for y in range(lay.chunk):
            source = pl.ds(aligned(y * lay.wide + other * ROWS), ROWS)
            send[y * ROWS : (y + 1) * ROWS, :] = plain[source, :]
        tile = pl.ds(aligned(other * LANES, LANES), LANES)
        send[lay.cells : lay.cells + total, :] = misfit[0:total, tile]


def finish(lay, slab_ref, *refs):
    pieces, (gradient, residual) = refs[: lay.count_x], refs[lay.count_x :]
    total = None
    for turn, piece in enumerate(pieces):
        start = (slab_ref[0] ^ turn) * lay.chunk
        for x in range(ROWS):
            target = pl.ds(aligned(x * lay.width_y + start), lay.chunk)
            gradient[target, :] = piece[pl.ds(x, lay.chunk, stride=ROWS), :]
        part = piece[lay.cells : lay.cells + residual.shape[0], :]
        total = part if total is None else total + part
    residual[...] = total


def gain_rows(lay, first_y):
    x = jnp.arange(ROWS)[None, :] * lay.tiles + jnp.arange(lay.tiles)[:, None]
    y = first_y + REACH + jnp.arange(lay.inner)

    def ramp(position, count):
        gap = jnp.minimum(position, count - 1 - position)
        profile = jnp.maximum(SPONGE - gap, 0).astype(jnp.float32) / SPONGE
        return profile * profile

    damping = damping_peak * (ramp(x, lay.wide)[None] + ramp(y, lay.whole_y)[:, None, None])
    gain = (2.0 / (1.0 + damping)).reshape(lay.inner * lay.wide, 1)
    return jnp.broadcast_to(gain, (lay.inner * lay.wide, LANES))


def source_rows(lay, first_y, source_cell, wavelet):
    x = source_cell // (lay.whole_y * LANES)
    y = source_cell // LANES % lay.whole_y - first_y
    z = source_cell % LANES
    inside = (y >= REACH) & (y < lay.extent - REACH)
    tile, row = x % lay.tiles, x // lay.tiles
    flat = jnp.where(inside, (y - REACH) * lay.wide + tile * ROWS + row, 0)
    buffer_row = jnp.where(inside, flat + REACH * lay.wide, 0)
    same = (buffer_row[:, None] == buffer_row[None, :]) & inside[None, :]
    spot = (z[:, None] == jnp.arange(LANES)[None, :]).astype(jnp.float32)
    lines = jnp.where(same[None, :, :, None], wavelet[:, None, :, None] * spot[None, None], 0.0)
    return buffer_row, flat, jnp.sum(lines, axis=2)


def local_tiles(
    lay,
    courant,
    state_prev,
    state_now,
    adjoint_now,
    adjoint_next,
    source_cell,
    wavelet,
    observed,
    receiver_cell,
    receiver_count,
):
    axes = ("gx", "gy")
    slab = lax.axis_index("gx")
    strip = lax.axis_index("gy")
    pair = strip // 2
    chip = jnp.where(pair % 2 == 0, slab, lay.count_x - 1 - slab)
    place = (pair * lay.count_x + chip) * 2 + strip % 2
    odd = strip % 2
    first_y = place * lay.chunk - lay.margin
    slab_int = slab.reshape(1).astype(jnp.int32)
    where = jnp.stack([place % lay.count_x, odd]).astype(jnp.int32)

    count = lay.count_x
    sources = source_cell.shape[0]
    slots = count * receiver_cell.shape[3]
    flat = lambda values: values.reshape(-1, LANES)
    part = functools.partial

    def swap(to_next, to_twin):
        return (
            lax.ppermute(to_next, axes, lay.swaps(1)),
            lax.ppermute(to_twin, axes, lay.swaps(0)),
        )

    def after(value, others):
        return lax.optimization_barrier((value, others))[0]

    buffer_row, flat_row, drive = source_rows(lay, first_y, source_cell, wavelet)
    gain = gain_rows(lay, first_y)
    ints = jnp.concatenate([odd.reshape(1), buffer_row, flat_row]).astype(jnp.int32)

    traces = flat(observed)
    forward_rows = 3 * lay.cells + -(-count // ROWS) * ROWS
    back_rows = 2 * lay.cells + traces.shape[0]
    cuts = call(
        part(cut_forward, lay),
        (slab_int, receiver_count.reshape(-1)),
        [flat(field) for field in (state_now, state_prev, courant)] + [receiver_cell.reshape(count, LANES)],
        [f32(forward_rows, LANES)] * count,
        [
            pltpu.VMEM((3, lay.width_x * lay.width_y, LANES), jnp.float32),
            pltpu.VMEM((count, LANES), jnp.int32),
            pltpu.SemaphoreType.DMA((4,)),
        ],
        space=pltpu.HBM,
        limit=60 * 1024 * 1024,
    )
    back_cuts = call(
        part(cut_adjoint, lay),
        (slab_int,),
        [flat(adjoint_now), flat(adjoint_next), traces],
        [f32(back_rows, LANES)] * count,
    )
    pieces = [lax.ppermute(cut, axes, lay.to_chunks(turn)) for turn, cut in enumerate(cuts)]
    pieces, ints, gain, drive, back_cuts = lax.optimization_barrier((pieces, ints, gain, drive, back_cuts))
    kept_rows = lay.kept * lay.wide
    state, own_courant, to_next, to_twin, codes = call(
        part(join_forward, lay),
        (where,),
        pieces,
        [f32(lay.state_rows, LANES), f32(lay.rows, LANES)]
        + [f32(lay.rows + 2 * kept_rows, LANES)] * 2
        + [f32(count, slots)],
        [pltpu.VMEM((3, lay.rows, LANES), jnp.float32)],
    )
    from_next, from_twin = swap(to_next, to_twin)

    back_pieces = [None] * count

    def move_adjoint(turns, earlier):
        for turn in turns:
            back_pieces[turn] = lax.ppermute(after(back_cuts[turn], earlier), axes, lay.to_chunks(turn))

    move_adjoint(range(1, count), codes)
    move_adjoint(range(1), from_twin)

    phases = STEPS // DEPTH
    step_cost = 8_000_000
    side_cost = 4_000_000
    history_shape = f32(DEPTH * lay.rows, LANES)
    state_shapes = [f32(lay.state_rows, LANES), f32(lay.send_rows, LANES)]
    buffers = [pltpu.VMEM((lay.extent * lay.wide, LANES), jnp.float32)] * 3
    buffers += [pltpu.VMEM((6 * LANES, 2 * LANES), jnp.bfloat16)]
    buffers += [pltpu.VMEM((lay.inner * lay.wide, LANES), jnp.float32)]
    record_scratch = [pltpu.VMEM((DEPTH * lay.rows, LANES), jnp.float32)]
    record_shape = (DEPTH * count, slots)
    histories, states, records = [], [], []
    half = own_courant
    for phase in range(phases):
        first, last = phase == 0, phase == phases - 1
        outs = [history_shape]
        if first:
            outs.append(f32(lay.inner * lay.wide, LANES))
        if not last:
            outs += state_shapes
        results = list(
            call(
                part(forward, lay, phase, sources),
                (ints,),
                [state, from_next, from_twin, half, gain, drive],
                outs,
                buffers + [pltpu.VMEM((sources, LANES), jnp.float32)],
                cost=step_cost,
            )
        )
        histories.append(results.pop(0))
        states.append(state)
        if first:
            half = results.pop(0)
        if last:
            continue
        state, send = results
        to_twin = after(send, back_pieces) if first else send
        from_next, from_twin = swap(send, to_twin)
    for history in histories[:-1]:
        records += call(
            part(record_phase, lay),
            (),
            [history, codes],
            [f32(*record_shape)],
            record_scratch,
            cost=side_cost,
        )
    back_state, to_next, to_twin = call(
        part(join_adjoint, lay),
        (where,),
        back_pieces,
        [f32(lay.state_rows, LANES)] + [f32(lay.rows + kept_rows, LANES)] * 2,
        [pltpu.VMEM((2, lay.rows, LANES), jnp.float32)],
    )
    back_from_next, back_from_twin = swap(to_next, to_twin)
    (misfit,) = call(
        part(record_last, lay, phases),
        (where,),
        [histories[-1], codes] + records + back_pieces,
        [f32(-(-(STEPS + 1) * count // ROWS) * ROWS, slots)],
        record_scratch + [pltpu.VMEM(record_shape, jnp.float32)],
        cost=side_cost,
    )

    misfit = after(misfit, [back_from_next, back_from_twin])
    misfit_next, misfit_twin = swap(misfit, misfit)
    state, from_next, from_twin = back_state, back_from_next, back_from_twin
    gradient = None
    inject_shape = f32(DEPTH, lay.inner * lay.wide, LANES)
    for phase in range(phases):
        first, last = phase == 0, phase == phases - 1
        (inject,) = call(part(spread_own, lay, phase), (), [misfit], [inject_shape], cost=side_cost)
        (inject,) = call(
            part(spread_sides, lay, phase),
            (where,),
            [inject, misfit_next, misfit_twin],
            [inject_shape],
            cost=side_cost,
            aliases={1: 0},
        )
        results = call(
            part(backward, lay, phase),
            (where,),
            [state, from_next, from_twin, half, gain, inject],
            [history_shape] + ([] if last else state_shapes),
            buffers,
            cost=step_cost,
        )
        arrays = [results[0], histories[phases - 1 - phase], states[phases - 1 - phase]]
        if last:
            sends = call(
                part(gradient_last, lay),
                (where,),
                arrays + [gradient, misfit],
                [f32(lay.cells + traces.shape[0], LANES)] * count,
                [pltpu.VMEM((lay.rows, LANES), jnp.float32)],
            )
            continue
        _, state, send = results
        from_next, from_twin = swap(send, send)
        kernel = gradient_first if first else gradient_later
        (gradient,) = call(
            part(kernel, lay), (), arrays + ([] if first else [gradient]), [f32(lay.rows, LANES)], cost=side_cost
        )
    pieces = [lax.ppermute(send, axes, lay.to_slabs(turn)) for turn, send in enumerate(sends)]
    gradient, residual = call(
        part(finish, lay),
        (slab_int,),
        pieces,
        [f32(lay.width_x * lay.width_y, LANES), f32(*traces.shape)],
    )
    return gradient.reshape(courant.shape), residual.reshape(observed.shape)


def local(courant, *rest):
    width_x, width_y, depth_z = courant.shape
    count_x, count_y = lax.axis_size("gx"), lax.axis_size("gy")
    if fits(count_x, count_y, width_x, width_y, depth_z):
        return local_tiles(Layout(count_x, count_y, width_x, width_y), courant, *rest)
    return local_blocks(courant, *rest)


def padded_2(cells, sides, width):
    for axis, dim in sides:
        count = lax.axis_size(axis)
        ends = count - 1
        head = lax.slice_in_dim(cells, 0, width, axis=dim)
        tail = lax.slice_in_dim(cells, cells.shape[dim] - width, cells.shape[dim], axis=dim)
        cells = jnp.concatenate(
            [
                lax.ppermute(tail, axis, [(i, (i + 1) % count) for i in range(ends)]),
                cells,
                lax.ppermute(head, axis, [((i + 1) % count, i) for i in range(ends)]),
            ],
            axis=dim,
        )
    return cells


def laplace(values):
    width_x, width_y, depth_z = values.shape
    padded = padded_2(values, (("gx", 0), ("gy", 1)), 4)
    z_padded = jnp.pad(values, ((0, 0), (0, 0), (4, 4)))
    summed = 3.0 * stencil[0] * values
    for offset in range(1, 5):
        paired = (
            padded[4 + offset : 4 + offset + width_x, 4 : 4 + width_y]
            + padded[4 - offset : 4 - offset + width_x, 4 : 4 + width_y]
        )
        paired = (
            paired
            + padded[4 : 4 + width_x, 4 + offset : 4 + offset + width_y]
            + padded[4 : 4 + width_x, 4 - offset : 4 - offset + width_y]
        )
        paired = (
            paired
            + z_padded[:, :, 4 + offset : 4 + offset + depth_z]
            + z_padded[:, :, 4 - offset : 4 - offset + depth_z]
        )
        summed = summed + stencil[offset] * paired
    return summed


def sponge(start, count, whole):
    position = start + jnp.arange(count, dtype=jnp.int32)
    edge_gap = jnp.minimum(position, whole - 1 - position)
    profile = jnp.maximum(SPONGE - edge_gap, 0).astype(jnp.float32) / SPONGE
    return profile * profile


def place_sum(indices, amounts, shape):
    flat = jnp.zeros((shape[0] * shape[1] * shape[2],), jnp.float32).at[indices].add(amounts)
    return flat.reshape(shape)


def local_blocks(
    courant,
    state_prev,
    state_now,
    adjoint_now,
    adjoint_next,
    source_cell,
    wavelet,
    observed,
    receiver_cell,
    receiver_count,
):
    shape = courant.shape
    width_x, width_y, depth_z = shape
    slab = lax.axis_index("gx")
    strip = lax.axis_index("gy")
    whole_x = width_x * lax.axis_size("gx")
    whole_y = width_y * lax.axis_size("gy")
    damping = damping_peak * (
        sponge(slab * width_x, width_x, whole_x)[:, None, None]
        + sponge(strip * width_y, width_y, whole_y)[None, :, None]
    )
    source_x = source_cell // (whole_y * depth_z) - slab * width_x
    source_y = source_cell // depth_z % whole_y - strip * width_y
    source_z = source_cell % depth_z
    inside = (source_x >= 0) & (source_x < width_x) & (source_y >= 0) & (source_y < width_y)
    source_flat = jnp.where(inside, (source_x * width_y + source_y) * depth_z + source_z, 0)
    source_weight = wavelet * inside.astype(jnp.float32)[None, :]
    senders = receiver_cell.shape[2]
    slots = receiver_cell.shape[3]
    cells = receiver_cell.reshape(-1)
    active = (
        jnp.arange(slots, dtype=jnp.int32)[None, :] < receiver_count.reshape(senders, 1)
    ).astype(jnp.float32)
    active_flat = active.reshape(-1)

    def advance(carry, weights):
        former, current = carry
        drive = laplace(current) + place_sum(source_flat, weights, shape)
        following = (2.0 * current - (1.0 - damping) * former + courant * drive) / (1.0 + damping)
        return (
            (current, following),
            (following - 2.0 * current + former, following.reshape(-1)[cells] * active_flat),
        )

    final_states, (accels, recorded) = lax.scan(advance, (state_prev, state_now), source_weight)
    recorded_tiles = recorded.reshape(STEPS, senders, 1, 1, slots)
    active_tiles = active.reshape(1, senders, 1, 1, slots)
    synthetic, mask_back = (
        lax.all_to_all(recorded_tiles, "gx", split_axis=1, concat_axis=3, tiled=True),
        lax.all_to_all(active_tiles, "gx", split_axis=1, concat_axis=3, tiled=True),
    )
    trace_residual = mask_back * (synthetic - observed)
    misfit = lax.all_to_all(trace_residual, "gx", split_axis=3, concat_axis=1, tiled=True)
    misfit_rows = misfit.reshape(STEPS, senders * slots)

    def retreat(carry, inputs):
        later, current, gradient = carry
        acceleration, residual_row = inputs
        drive = laplace(current) + place_sum(cells, residual_row, shape)
        earlier = (2.0 * current - (1.0 - damping) * later + courant * drive) / (1.0 + damping)
        return ((current, earlier, gradient + earlier * acceleration), None)

    start_gradient = jnp.zeros(shape, jnp.float32)
    (last_later, last_current, gradient), unused = lax.scan(
        retreat, (adjoint_next, adjoint_now, start_gradient), (accels, misfit_rows), reverse=True
    )
    return (gradient, trace_residual)


def solution(mesh):
    placed = (
        P("gx", "gy", None),
        P(("groups", "gx"), "gy", None),
        P(("groups", "gx"), "gy", None),
        P(("groups", "gx"), "gy", None),
        P(("groups", "gx"), "gy", None),
        P("groups"),
        P(None, "groups"),
        P("groups", "gx", "gy", None, None),
        P("gx", "gy", None, None),
        P("gx", "gy", None),
    )
    return jax.shard_map(
        local,
        mesh=mesh,
        in_specs=placed,
        out_specs=(P(("groups", "gx"), "gy", None), P("groups", "gx", "gy", None, None)),
        check_vma=False,
    )
```
